32 devices in a mesh: seq: 16 (over z, y, x), head: 2 (over core).
Axes of the slice: x: 2, y: 2, z: 4, core: 2. Of those that a mesh axis runs over, the one named last changes fastest.
Arguments:
- resid_in: bfloat16 [1, 4096, 1536], P(None, 'seq'), may hold values from -6 to 6
- cotangent: bfloat16 [1, 4096, 1536], P(None, 'seq'), may hold values from -6 to 6
- norm_gain: bfloat16 [2, 1536], replicated, may hold values from 0.5 to 1.5
- w_zx: bfloat16 [2, 2, 1536, 3072], P(None, None, 'seq', 'head'), may hold values from -0.15625 to 0.15625
- w_dt: bfloat16 [2, 1536, 48], P(None, 'seq', 'head'), may hold values from -0.15625 to 0.15625
- w_bc: bfloat16 [2, 1536, 256], P(None, 'seq'), may hold values from -0.15625 to 0.15625
- conv_x: bfloat16 [2, 5, 3072], P(None, None, 'head'), may hold values from -0.5 to 0.5
- conv_bc: bfloat16 [2, 5, 256], replicated, may hold values from -0.5 to 0.5
- head_params: float32 [2, 3, 48], P(None, None, 'head'), may hold values from -15 to 3, as said below
- gated_gain: bfloat16 [2, 3072], P(None, 'head'), may hold values from 0.5 to 1.5
- w_out: bfloat16 [2, 3072, 1536], P(None, 'head', 'seq'), may hold values from -0.109375 to 0.109375
Outputs:
- block_out: bfloat16 [1, 4096, 1536], P(None, 'seq')
- grad_input: bfloat16 [1, 4096, 1536], P(None, 'seq')
- grad_norm_gain: bfloat16 [2, 1536], replicated
- grad_w_zx: bfloat16 [2, 2, 1536, 3072], P(None, None, 'seq', 'head')
- grad_w_dt: bfloat16 [2, 1536, 48], P(None, 'seq', 'head')
- grad_w_bc: bfloat16 [2, 1536, 256], P(None, 'seq')
- grad_conv_x: bfloat16 [2, 5, 3072], P(None, None, 'head')
- grad_conv_bc: bfloat16 [2, 5, 256], replicated
- grad_head_params: bfloat16 [2, 3, 48], P(None, None, 'head')
- grad_gated_gain: bfloat16 [2, 3072], P(None, 'head')
- grad_w_out: bfloat16 [2, 3072, 1536], P(None, 'head', 'seq')
The draws below stay inside these ranges and needn't reach their ends.
Inputs may be any that keep to these rules, and one draw needn't show every extreme that they name: `head_params`: row 0 of each layer holds the logarithm of each head's decay rate, which lies between 0 and log(16); row 1 holds the time-step biases; row 2 the skip gains, between 0.2 and 1.
All inputs are finite; a program needn't handle non-finite values.
Results may differ from the reference program's by a relative error of at most 0.03.
Values may be sent and summed in bfloat16 or wider, within the bound.
A program may use at most 256 MiB of HBM per device.

```python
import jax
import jax.numpy as jnp
from jax import lax

D = 1536
HEADS = 48
HEADDIM = 64
STATE = 128
CONV = 4
SPAN = 256
LAYERS = 2
SEQS = 1
INNER = 3072
LENGTH = 4096


def draw_head_params(key, part):
    key = jax.random.fold_in(key, 7)
    key_list = jax.random.split(key, 5)
    slow_share = 0.5
    slow_heads = jax.random.bernoulli(key_list[0], slow_share, (LAYERS, HEADS))
    rate_size = jnp.exp(jax.random.uniform(key_list[1], (LAYERS, HEADS), jnp.float32, 0.0, jnp.log(16.0)))
    fast_step = jnp.exp(jax.random.uniform(key_list[2], (LAYERS, HEADS), jnp.float32, jnp.log(1.0 / 60.0), jnp.log(1.0 / 25.0))) / rate_size
    slow_step = jnp.exp(jax.random.uniform(key_list[3], (LAYERS, HEADS), jnp.float32, jnp.log(0.3), 0.0)) / (LENGTH * rate_size)
    step_base = jnp.where(slow_heads, slow_step, fast_step)
    step_bias = jnp.log(jnp.expm1(step_base))
    skip_gain = jax.random.uniform(key_list[4], (LAYERS, HEADS), jnp.float32, 0.2, 1.0)
    return jnp.stack([jnp.log(rate_size), step_bias, skip_gain], axis=1).astype(jnp.float32)


def spiked(result, rng, source, target, shards_of, factor):
    def block_of(position):
        return (jnp.arange(result.shape[position]) // (result.shape[position] // shards_of)).reshape((-1,) + (1,) * (result.ndim - 1 - position))

    one_side = jax.random.permutation(rng, shards_of)[block_of(target)]
    far = (block_of(target) + shards_of // 2) % shards_of
    return jnp.where((block_of(source) == one_side) | (block_of(source) == far), factor * result, result)


def block_levels(own_key, shape, shards, least, top_value):
    loudness, own = 1.0, jax.random.fold_in(own_key, 6)
    for axis_at, blocks in shards:
        heights = jnp.exp(jax.random.uniform(jax.random.fold_in(own, axis_at), (blocks,), jnp.float32, least / len(shards), top_value / len(shards)))
        loudness = loudness * jnp.repeat(heights, shape[axis_at] // blocks).reshape([-1 if axis == axis_at else 1 for axis in range(len(shape))])
    return loudness


def normal_values(rng, shape, scale, bound, pieces=(), held_as=jnp.bfloat16):
    drawn = scale * jax.random.normal(rng, shape, jnp.float32)
    if pieces:
        drawn = drawn * block_levels(rng, shape, pieces, -0.22, 0.18)
    return jnp.clip(drawn, -bound, bound).astype(held_as)


def noise_with(rng, dims, spread, most, pieces, heavy, dtype=jnp.bfloat16):
    result = spread * jax.random.normal(rng, dims, jnp.float32)
    if pieces:
        result = result * block_levels(rng, dims, pieces, -0.22, 0.18)
    return jnp.clip(spiked(result, jax.random.fold_in(rng, 3), *heavy), -most, most).astype(dtype)


def setup_inputs(seed: int = 0) -> dict:
    streams_of = jax.random.split(jax.random.key(seed), 12)
    return {
        "resid_in": noise_with(streams_of[0], (SEQS, LENGTH, D), 1.0, 6.0, ((1, 16),), (1, 2, 16, 2.0)),
        "cotangent": noise_with(streams_of[1], (SEQS, LENGTH, D), 1.0, 6.0, ((1, 16),), (1, 2, 16, 2.0)),
        "norm_gain": jnp.clip(1.0 + 0.1 * jax.random.normal(streams_of[2], (LAYERS, D), jnp.float32), 0.5, 1.5).astype(jnp.bfloat16),
        "w_zx": normal_values(streams_of[3], (LAYERS, 2, D, INNER), D ** -0.5, 0.15625, ((2, 16), (3, 2))),
        "w_dt": normal_values(streams_of[4], (LAYERS, D, HEADS), D ** -0.5, 0.15625, ((1, 16), (2, 2))),
        "w_bc": normal_values(streams_of[5], (LAYERS, D, 2 * STATE), D ** -0.5, 0.15625, ((1, 16),)),
        "conv_x": jnp.clip(jax.random.uniform(streams_of[6], (LAYERS, CONV + 1, INNER), jnp.float32, -0.5, 0.5) * block_levels(streams_of[6], (LAYERS, CONV + 1, INNER), ((2, 2),), -0.4, 0.0), -0.5, 0.5).astype(jnp.bfloat16),
        "conv_bc": jnp.clip(jax.random.uniform(streams_of[7], (LAYERS, CONV + 1, 2 * STATE), jnp.float32, -0.5, 0.5), -0.5, 0.5).astype(jnp.bfloat16),
        "head_params": draw_head_params(jax.random.fold_in(streams_of[11], 71), 0),
        "gated_gain": jnp.clip(1.0 + 0.1 * jax.random.normal(streams_of[9], (LAYERS, INNER), jnp.float32), 0.5, 1.5).astype(jnp.bfloat16),
        "w_out": normal_values(streams_of[10], (LAYERS, INNER, D), INNER ** -0.5, 0.109375, ((1, 2), (2, 16))),
    }


epsilon = 1e-05
highest = lax.Precision.HIGHEST

@jax.custom_vjp
def low(v):
    return lax.optimization_barrier(v.astype(jnp.bfloat16)).astype(jnp.float32)

@jax.custom_vjp
def low_back(v):
    return v

def low_keep(v):
    return (low(v), None)

def low_pass(kept, grad):
    return (grad,)

def back_keep(v):
    return (v, None)

def back_low(kept, grad):
    return (low(grad),)
low.defvjp(low_keep, low_pass)
low_back.defvjp(back_keep, back_low)

def matmul(left, right):
    return jnp.dot(left, right, precision=highest, preferred_element_type=jnp.float32)

def causal_conv(values, weights):
    length = values.shape[0]
    padded = jnp.pad(values, ((CONV - 1, 0), (0, 0)))
    running = jnp.broadcast_to(weights[CONV], values.shape)
    for offset in range(CONV):
        running = running + weights[offset] * padded[offset:offset + length]
    return running

def mixer_spans(x_heads, b_vals, c_vals, step_size, decay_rate):
    span_count = x_heads.shape[0] // SPAN

    def to_blocks(values):
        return values.reshape((span_count, SPAN) + values.shape[1:])

    def one_span(state_now, block_in):
        x_block, b_block, c_block, step_block = block_in
        cum_log = jnp.cumsum(step_block * decay_rate, axis=0)
        row_ids = lax.broadcasted_iota(jnp.int32, (SPAN, SPAN), 0)
        col_ids = lax.broadcasted_iota(jnp.int32, (SPAN, SPAN), 1)
        causal = (col_ids <= row_ids)[:, :, None]
        log_gap = cum_log[:, None, :] - cum_log[None, :, :]
        decay_in = jnp.where(causal, jnp.exp(jnp.where(causal, log_gap, 0.0)), 0.0)
        weights_tk = decay_in * step_block[None, :, :]
        inner_cb = matmul(c_block, b_block.T)
        scores = low(inner_cb[:, :, None] * weights_tk)
        y_local = jnp.einsum('tkh,khp->thp', scores, x_block, precision=highest)
        state_weight = jnp.exp(cum_log[-1:] - cum_log) * step_block
        weighted = low(x_block * state_weight[:, :, None])
        local_state = low_back(jnp.einsum('khp,kn->hpn', weighted, b_block, precision=highest))
        c_decay = low(jnp.exp(cum_log)[:, :, None] * c_block[:, None, :])
        y_carry = jnp.einsum('thn,hpn->thp', c_decay, low(state_now), precision=highest)
        total_decay = jnp.exp(cum_log[-1])
        state_next = total_decay[:, None, None] * state_now + local_state
        return (state_next, low_back(y_local + y_carry))
    start_state = jnp.zeros((HEADS, HEADDIM, STATE), jnp.float32)
    final_state, outputs = lax.scan(jax.checkpoint(one_span), start_state, (to_blocks(x_heads), to_blocks(b_vals), to_blocks(c_vals), to_blocks(step_size)))
    return outputs.reshape(x_heads.shape)

def mixer_layer(residual, params):
    gain_in, w_zx, w_dt, w_bc, conv_xw, conv_bcw, head_vals, gate_gain, w_out = params
    inv_rms = lax.rsqrt(lax.optimization_barrier(jnp.mean(residual * residual, axis=-1, keepdims=True)) + epsilon)
    normed = low(residual * inv_rms * gain_in)
    z_proj = low_back(low(matmul(normed, w_zx[0])))
    x_proj = low_back(low(matmul(normed, w_zx[1])))
    dt_raw = low_back(low(matmul(normed, w_dt)))
    bc_proj = low_back(low(matmul(normed, w_bc)))
    x_conv = low(jax.nn.silu(causal_conv(x_proj, conv_xw)))
    bc_conv = low(jax.nn.silu(causal_conv(bc_proj, conv_bcw)))
    step_size = jax.nn.softplus(dt_raw + head_vals[1])
    decay_rate = -jnp.exp(head_vals[0])
    length = residual.shape[0]
    x_heads = x_conv.reshape(length, HEADS, HEADDIM)
    y_ssd = mixer_spans(x_heads, bc_conv[:, :STATE], bc_conv[:, STATE:], step_size, decay_rate)
    y_full = (y_ssd + head_vals[2][None, :, None] * x_heads).reshape(length, INNER)
    gated_vals = y_full * jax.nn.silu(z_proj)
    inv_gate = lax.rsqrt(lax.optimization_barrier(jnp.mean(gated_vals * gated_vals, axis=-1, keepdims=True)) + epsilon)
    normed_out = low(gated_vals * inv_gate * gate_gain)
    return residual + low_back(matmul(normed_out, w_out))

def add_up(left_val, right_val):
    return left_val + right_val

def reference(resid_in, cotangent, norm_gain, w_zx, w_dt, w_bc, conv_x, conv_bc, head_params, gated_gain, w_out):
    params = tuple((member.astype(jnp.float32) for member in (norm_gain, w_zx, w_dt, w_bc, conv_x, conv_bc, head_params, gated_gain, w_out)))

    def forward(param_set, residual):
        for layer_index in range(LAYERS):
            residual = mixer_layer(residual, tuple((member[layer_index] for member in param_set)))
        return residual

    def per_sequence(totals, pair_in):
        seq_in, seq_cot = pair_in
        seq_out, pullback = jax.vjp(forward, params, seq_in.astype(jnp.float32))
        grad_set, grad_seq = pullback(seq_cot.astype(jnp.float32))
        totals = jax.tree.map(add_up, totals, grad_set)
        return (totals, (seq_out.astype(jnp.bfloat16), grad_seq.astype(jnp.bfloat16)))
    zero_set = jax.tree.map(jnp.zeros_like, params)
    totals, (outputs, grad_rows) = lax.scan(per_sequence, zero_set, (resid_in, cotangent))
    return (outputs, grad_rows, totals[0].astype(jnp.bfloat16), totals[1].astype(jnp.bfloat16), totals[2].astype(jnp.bfloat16), totals[3].astype(jnp.bfloat16), totals[4].astype(jnp.bfloat16), totals[5].astype(jnp.bfloat16), totals[6].astype(jnp.bfloat16), totals[7].astype(jnp.bfloat16), totals[8].astype(jnp.bfloat16))
```

```python
import functools

import jax
import jax.numpy as jnp
from jax import lax
from jax.experimental import pallas as pl
from jax.experimental.pallas import tpu as pltpu
from jax.sharding import Mesh, PartitionSpec as P

HEADDIM = 64
STATE = 128
CONV = 4
SPAN = 256
GROUP = 4
EDGE = 16
EPS = 1e-05
HIGH = lax.Precision.HIGHEST
F32, BF16 = jnp.float32, jnp.bfloat16
NN = (((1,), (0,)), ((), ()))
NT = (((1,), (1,)), ((), ()))
TN = (((0,), (0,)), ((), ()))
VMEM_BYTES = 58 << 20


def dot(a, b, dims=NN):
    return lax.dot_general(a, b, dims, preferred_element_type=F32)


def dot_exact(a, b, dims=NN):
    return lax.dot_general(a, b, dims, precision=HIGH, preferred_element_type=F32)


def dot_split(a, b, dims=NN):
    high = a.astype(BF16)
    rest = (a - high.astype(F32)).astype(BF16)
    return dot(high, b, dims) + dot(rest, b, dims)


def sigmoid(v):
    return 1.0 / (1.0 + jnp.exp(-v))


def softplus(v):
    return jnp.maximum(v, 0.0) + jnp.log1p(jnp.exp(-jnp.abs(v)))


def silu_slope(v):
    sig = sigmoid(v)
    return sig * (1.0 + v * (1.0 - sig))


def iota(shape, dim):
    return lax.broadcasted_iota(jnp.int32, shape, dim)


def head_spread(inner):
    return (iota((128, inner), 0) == lax.shift_right_logical(iota((128, inner), 1), 6)).astype(BF16)


def triangle(lower):
    rows, cols = iota((SPAN, SPAN), 0), iota((SPAN, SPAN), 1)
    return ((cols <= rows) if lower else (cols >= rows)).astype(F32)


def half_masks():
    lane = iota((SPAN, 128), 1)
    return (lane < HEADDIM).astype(BF16), (lane >= HEADDIM).astype(BF16)


def conv_taps(window, taps):
    total = jnp.broadcast_to(taps[CONV : CONV + 1], (SPAN, window.shape[1]))
    for j in range(CONV):
        total = total + taps[j : j + 1] * window[EDGE - 3 + j : EDGE - 3 + j + SPAN]
    return total


def forward_local(
    normed, wx, wz, wbc, wdt, rowp, bcp, headp,
    z_out, xin_out, bcin_out, x_out, bc_out, dtraw_out, dt_out, s_out, y_out, local_out, decay_out, sum_out,
    ext,
):
    inner = x_out.shape[1]
    spans = x_out.shape[0] // SPAN

    edge = normed[0:EDGE]
    edge_x = dot(edge, wx[...]).astype(BF16)
    edge_bc = dot(edge, wbc[...]).astype(BF16)
    xin_out[0:EDGE] = edge_x
    bcin_out[0:EDGE] = edge_bc
    ext[0:EDGE, 0:inner] = edge_x.astype(F32)
    ext[0:EDGE, inner:] = edge_bc.astype(F32)
    spread = head_spread(inner)
    low_tri = triangle(True)
    rate = -jnp.exp(headp[0:1])
    bias = headp[1:2]

    def block(q, carry):
        state_sum, decay_all = carry
        at = pl.multiple_of(q * SPAN, SPAN)
        tok = pl.ds(at, SPAN)
        after = pl.ds(pl.multiple_of(at + EDGE, EDGE), SPAN)
        rows = normed[after, :]
        z_out[tok, :] = dot(rows, wz[...]).astype(BF16)
        xin = dot(rows, wx[...]).astype(BF16)
        bcin = dot(rows, wbc[...]).astype(BF16)
        dtraw = dot(rows, wdt[...]).astype(BF16)
        xin_out[after, :] = xin
        bcin_out[after, :] = bcin
        dtraw_out[tok, :] = dtraw
        ext[after, 0:inner] = xin.astype(F32)
        ext[after, inner:] = bcin.astype(F32)
        window = pl.ds(at, SPAN + EDGE)
        pre_x = conv_taps(ext[window, 0:inner], rowp)
        x = (pre_x * sigmoid(pre_x)).astype(BF16)
        x_out[tok, :] = x
        pre_bc = conv_taps(ext[window, inner:], bcp)
        bc = (pre_bc * sigmoid(pre_bc)).astype(BF16)
        bc_out[tok, :] = bc
        b, c = bc[:, :STATE], bc[:, STATE:]
        dt = softplus(dtraw.astype(F32) + bias)
        s = dot_exact(low_tri, dt * rate)
        dt_out[tok, :] = dt
        s_out[tok, :] = s
        s_row, dt_row = s.T, dt.T
        cb = dot(c, b, NT)
        causal = iota((SPAN, SPAN), 1) <= iota((SPAN, SPAN), 0)
        masks = half_masks()
        for pair in range(inner // 128):
            lanes = slice(pair * 128, pair * 128 + 128)
            x_pair = x[:, lanes]
            total = None
            for e in range(2):
                h = pair * 2 + e
                gap = jnp.where(causal, s[:, h : h + 1] - s_row[h : h + 1, :], -1e30)
                scores = (cb * (jnp.exp(gap) * dt_row[h : h + 1, :])).astype(BF16)
                term = dot(scores, x_pair * masks[e])
                total = term if total is None else total + term
            y_out[tok, lanes] = total
        to_end = jnp.exp(s[SPAN - 1 : SPAN] - s) * dt
        weighted = (x.astype(F32) * dot_split(to_end, spread)).astype(BF16)
        local = dot(b, weighted, TN)
        decay = dot_split(jnp.exp(s[SPAN - 8 : SPAN]), spread)[7:8]
        local_out[q] = local
        decay_out[q] = jnp.broadcast_to(decay, (8, inner))
        return state_sum * decay + local, decay_all * decay

    state_sum, decay_all = lax.fori_loop(
        0, spans, block, (jnp.zeros((STATE, inner), F32), jnp.ones((1, inner), F32))
    )
    sum_out[0:STATE] = state_sum
    sum_out[STATE : STATE + 8] = jnp.broadcast_to(decay_all, (8, inner))


def entering_state(place, count, sums, backward):
    inner = sums.shape[2]
    state = jnp.zeros((STATE, inner), F32)
    for turn in range(count):
        other = count - 1 - turn if backward else turn
        ahead = (place < other) if backward else (other < place)
        state = jnp.where(ahead, sums[other, STATE : STATE + 1] * state + sums[other, 0:STATE], state)
    return state


def forward_carried(count, sums, local, decay, y_local, x, bc, z, s, wo, rowp, y_out, states_out, part_out, sq_out):
    inner = x.shape[1]
    spans = x.shape[0] // SPAN
    spread = head_spread(inner)
    gain, skip = rowp[5:6], rowp[6:7]
    ones = jnp.ones((8, inner), F32)

    def block(q, state):
        tok = pl.ds(pl.multiple_of(q * SPAN, SPAN), SPAN)
        states_out[q] = state
        c = bc[tok, STATE:]
        carried = dot_split(jnp.exp(s[tok, :]), spread) * dot(c, state.astype(BF16))
        y = y_local[tok, :] + carried + skip * x[tok, :].astype(F32)
        y_out[tok, :] = y
        zf = z[tok, :].astype(F32)
        gated = y * (zf * sigmoid(zf))
        sq_out[:, tok] = dot_exact(ones, gated * gated, NT)
        part_out[tok, :] = dot((gated * gain).astype(BF16), wo[...], NT).astype(BF16)
        return decay[q, 0:1] * state + local[q]

    lax.fori_loop(0, spans, block, entering_state(lax.axis_index("z"), count, sums, False))


def backward_gate(
    inner_all, dmix, wo, y_in, z, x, bc, s, decay, token_scalars, rowp,
    dz_out, dy_out, gwo_out, prior_out, sum_out, small_out,
    normed_out,
):
    inner = x.shape[1]
    spans = x.shape[0] // SPAN
    spread = head_spread(inner)
    gain = rowp[5:6]

    def block(i, carry):
        grad_sum, gain_sum, skip_sum = carry
        q = spans - 1 - i
        tok = pl.ds(pl.multiple_of(q * SPAN, SPAN), SPAN)
        columns = token_scalars[:, tok].T
        inv, total_dot = columns[:, 0:1], columns[:, 1:2]
        zf = z[tok, :].astype(F32)
        sig = sigmoid(zf)
        act = zf * sig
        y = y_in[tok, :]
        gated = y * act
        d_no = dot(dmix[tok, :], wo[...])
        scaled = gated * inv
        normed_out[tok, :] = (scaled * gain).astype(BF16)
        gain_sum = gain_sum + jnp.sum(d_no * scaled, axis=0, keepdims=True)
        d_gated = inv * (d_no * gain) - gated * (inv * inv * inv * total_dot * (1.0 / inner_all))
        dz_out[tok, :] = (d_gated * y * (sig * (1.0 + zf * (1.0 - sig)))).astype(BF16)
        dy = d_gated * act
        xf = x[tok, :].astype(F32)
        skip_sum = skip_sum + jnp.sum(dy * xf, axis=0, keepdims=True)
        dy_low = dy.astype(BF16)
        dy_out[tok, :] = dy_low
        scaled_dy = (dy_low.astype(F32) * dot_split(jnp.exp(s[tok, :]), spread)).astype(BF16)
        prior = dot(bc[tok, STATE:], scaled_dy, TN)
        prior_out[q] = prior
        return prior + decay[q, 0:1] * grad_sum, gain_sum, skip_sum

    zero = jnp.zeros((1, inner), F32)
    grad_sum, gain_sum, skip_sum = lax.fori_loop(
        0, spans, block, (jnp.zeros((STATE, inner), F32), zero, zero)
    )
    decay_all = decay[0, 0:1]
    for q in range(1, spans):
        decay_all = decay_all * decay[q, 0:1]
    sum_out[0:STATE] = grad_sum
    sum_out[STATE : STATE + 8] = jnp.broadcast_to(decay_all, (8, inner))
    small_out[0:1] = gain_sum
    small_out[1:2] = skip_sum
    small_out[2:8] = jnp.zeros((6, inner), F32)

    def out_grad(i, _):
        rows = pl.ds(pl.multiple_of(i * SPAN, SPAN), SPAN)
        gwo_out[rows, :] = dot(dmix[:, rows], normed_out[...], TN).astype(BF16)
        return 0

    lax.fori_loop(0, dmix.shape[1] // SPAN, out_grad, 0)


def backward_ssd(
    count, sums, prior, decay, states, dy_in, x, bc, s_in, dt_in, dtraw, xin, bcin, rowp, bcp, headp,
    dcat_out, row_out, bcrow_out, head_out,
    dpre, dend,
):
    inner = x.shape[1]
    spans = x.shape[0] // SPAN
    spread = head_spread(inner)
    up_tri = triangle(False)
    skip = rowp[6:7]
    rate = -jnp.exp(headp[0:1])
    bias = headp[1:2]
    width = inner + 2 * STATE

    def chain(i, grad):
        q = spans - 1 - i
        dend[q] = grad
        return prior[q] + decay[q, 0:1] * grad

    lax.fori_loop(0, spans, chain, entering_state(lax.axis_index("z"), count, sums, True))
    dpre[0:EDGE] = jnp.zeros((EDGE, width), F32)
    dpre[EDGE + spans * SPAN :] = jnp.zeros((EDGE, width), F32)
    row_out[...] = jnp.zeros_like(row_out)
    bcrow_out[...] = jnp.zeros_like(bcrow_out)
    head_out[...] = jnp.zeros_like(head_out)
    dcat_out[0:EDGE, width:] = jnp.zeros((EDGE, 128), BF16)

    def block(q, _):
        at = pl.multiple_of(q * SPAN, SPAN)
        tok = pl.ds(at, SPAN)
        after = pl.ds(pl.multiple_of(at + EDGE, EDGE), SPAN)
        window = pl.ds(at, SPAN + EDGE)
        x_low, dy = x[tok, :], dy_in[tok, :]
        xf, dyf = x_low.astype(F32), dy.astype(F32)
        b, c = bc[tok, :STATE], bc[tok, STATE:]
        s, dt = s_in[tok, :], dt_in[tok, :]
        exp_s = jnp.exp(s)
        to_end = jnp.exp(s[SPAN - 1 : SPAN] - s)
        w = to_end * dt
        w_all, s_all = dot_split(w, spread), dot_split(exp_s, spread)
        state, grad = states[q], dend[q]
        state_low, grad_low = state.astype(BF16), grad.astype(BF16)
        carried = s_all * dot(c, state_low)
        ds = dot_split(dyf * carried, spread, NT)
        d_c = dot((dyf * s_all).astype(BF16), state_low, NT)
        d_w = dot(b, grad_low)
        d_b = dot((xf * w_all).astype(BF16), grad_low, NT)
        dx = dyf * skip + d_w * w_all
        dsw = dot_split(d_w * xf, spread, NT)
        s_row = s.T
        cb = dot(b, c, NT)
        seen = iota((SPAN, SPAN), 0) <= iota((SPAN, SPAN), 1)
        masks = half_masks()
        d_cb = jnp.zeros((SPAN, SPAN), F32)
        lane = iota((SPAN, 128), 1)
        row_id = iota((128, SPAN), 0)
        sum_k = jnp.zeros((128, SPAN), F32)
        sum_t = jnp.zeros((SPAN, 128), F32)
        dx_pairs = []
        for pair in range(inner // 128):
            lanes = slice(pair * 128, pair * 128 + 128)
            x_pair, dy_pair = x_low[:, lanes], dy[:, lanes]
            total = dx[:, lanes]
            for e in range(2):
                h = pair * 2 + e
                d_scores = dot(x_pair * masks[e], dy_pair, NT)
                fade = jnp.exp(jnp.where(seen, s_row[h : h + 1, :] - s[:, h : h + 1], -1e30))
                dt_h = dt[:, h : h + 1]
                fade_cb = cb * fade
                total = total + dot((fade_cb * dt_h).astype(BF16), dy_pair * masks[e])
                d_cb = d_cb + d_scores * (fade * dt_h)
                flow = d_scores * fade_cb
                sum_t = jnp.where(lane == h, jnp.sum(flow, axis=1, keepdims=True), sum_t)
                sum_k = jnp.where(row_id == h, jnp.sum(flow * dt_h, axis=0, keepdims=True), sum_k)
            dx_pairs.append(total)
        d_cb_low = d_cb.astype(BF16)
        d_b = d_b + dot(d_cb_low, c)
        d_c = d_c + dot(d_cb_low, b, TN)
        end = dsw * w
        ds = ds + sum_k.T - sum_t * dt - end
        held = dot_split(jnp.broadcast_to(jnp.sum(grad * state, axis=0, keepdims=True), (8, inner)), spread, NT)[0:1]
        last = jnp.sum(end, axis=0, keepdims=True) + held * exp_s[SPAN - 1 : SPAN]
        ds = ds + jnp.where(iota((SPAN, 128), 0) == SPAN - 1, last, 0.0)
        da = dot_exact(up_tri, ds)
        d_dt = sum_t + dsw * to_end + da * rate
        d_raw = d_dt * sigmoid(dtraw[tok, :].astype(F32) + bias)
        d_raw = jnp.where(lane < inner // HEADDIM, d_raw, 0.0)
        head_out[0:1] += jnp.sum(da * (dt * rate), axis=0, keepdims=True)
        head_out[1:2] += jnp.sum(d_raw, axis=0, keepdims=True)
        dcat_out[after, width:] = d_raw.astype(BF16)

        win_x = xin[window, :].astype(F32)
        d_x = jnp.concatenate(dx_pairs, axis=1) * silu_slope(conv_taps(win_x, rowp))
        dpre[after, 0:inner] = d_x
        for j in range(CONV):
            row_out[j : j + 1] += jnp.sum(d_x * win_x[EDGE - 3 + j : EDGE - 3 + j + SPAN], axis=0, keepdims=True)
        row_out[CONV : CONV + 1] += jnp.sum(d_x, axis=0, keepdims=True)
        win_bc = bcin[window, :].astype(F32)
        d_bc = jnp.concatenate([d_b, d_c], axis=1) * silu_slope(conv_taps(win_bc, bcp))
        dpre[after, inner:] = d_bc
        for j in range(CONV):
            bcrow_out[j : j + 1] += jnp.sum(d_bc * win_bc[EDGE - 3 + j : EDGE - 3 + j + SPAN], axis=0, keepdims=True)
        bcrow_out[CONV : CONV + 1] += jnp.sum(d_bc, axis=0, keepdims=True)
        return 0

    lax.fori_loop(0, spans, block, 0)

    def back(window, taps, rows):
        total = None
        for j in range(CONV):
            term = taps[j : j + 1] * window[CONV - 1 - j : CONV - 1 - j + rows]
            total = term if total is None else total + term
        return total.astype(BF16)

    dcat_out[0:EDGE, 0:inner] = back(dpre[0 : 2 * EDGE, 0:inner], rowp, EDGE)
    dcat_out[0:EDGE, inner:width] = back(dpre[0 : 2 * EDGE, inner:], bcp, EDGE)

    def conv_block(q, _):
        at = pl.multiple_of(q * SPAN, SPAN)
        after = pl.ds(pl.multiple_of(at + EDGE, EDGE), SPAN)
        window = pl.ds(pl.multiple_of(at + EDGE, EDGE), SPAN + EDGE)
        dcat_out[after, 0:inner] = back(dpre[window, 0:inner], rowp, SPAN)
        dcat_out[after, inner:width] = back(dpre[window, inner:], bcp, SPAN)
        return 0

    lax.fori_loop(0, spans, conv_block, 0)


def backward_project(dcat, dz, normed, wx, wz, wbc, wdt, dn_out, gxz_out, gbc_out, gdt_out):
    inner = dz.shape[1]
    width = inner + 2 * STATE
    spans = dz.shape[0] // SPAN
    d_edge = dcat[0:EDGE]
    dn_out[0:EDGE] = (
        dot(d_edge[:, 0:inner], wx[...], NT)
        + dot(d_edge[:, inner:width], wbc[...], NT)
    ).astype(BF16)

    def rows_of(q, _):
        at = pl.multiple_of(q * SPAN, SPAN)
        tok = pl.ds(at, SPAN)
        after = pl.ds(pl.multiple_of(at + EDGE, EDGE), SPAN)
        dn_out[after, :] = (
            dot(dz[tok, :], wz[...], NT)
            + dot(dcat[after, 0:inner], wx[...], NT)
            + dot(dcat[after, inner:width], wbc[...], NT)
            + dot(dcat[after, width:], wdt[...], NT)
        ).astype(BF16)
        return 0

    lax.fori_loop(0, spans, rows_of, 0)

    def grads_of(i, _):
        cols = pl.ds(pl.multiple_of(i * SPAN, SPAN), SPAN)
        part = normed[:, cols]
        both = dot(part, dcat[...], TN).astype(BF16)
        gxz_out[cols, 0:inner] = both[:, 0:inner]
        gbc_out[cols, :] = both[:, inner:width]
        gdt_out[cols, :] = both[:, width:]
        gxz_out[cols, inner:] = dot(part[EDGE:], dz[...], TN).astype(BF16)
        return 0

    lax.fori_loop(0, normed.shape[1] // SPAN, grads_of, 0)


def call(body, outs, *args, scratch=()):
    vmem = pl.BlockSpec(memory_space=pltpu.VMEM)
    return pl.pallas_call(
        body,
        out_shape=tuple(jax.ShapeDtypeStruct(shape, kind) for shape, kind in outs),
        in_specs=[vmem] * len(args),
        out_specs=tuple([vmem] * len(outs)),
        scratch_shapes=list(scratch),
        compiler_params=pltpu.CompilerParams(vmem_limit_bytes=VMEM_BYTES),
    )(*args)


def on_device(resid_in, cotangent, norm_gain, w_zx, w_dt, w_bc, conv_x, conv_bc, head_params, gated_gain, w_out):
    layers, model = norm_gain.shape
    groups = lax.axis_size("z")
    place = lax.axis_index("p")
    shard = w_dt.shape[1]
    inner_core = conv_x.shape[2]
    inner = inner_core // GROUP
    heads_core = head_params.shape[2]
    heads = heads_core // GROUP
    inner_all = inner_core * lax.axis_size("head")
    length = resid_in.shape[1]
    tokens = GROUP * length
    spans = tokens // SPAN

    def my_part(array, size):
        return lax.dynamic_slice_in_dim(array, place * size, size, array.ndim - 1)

    row_all, bc_all, head_all, weights = [], [], [], []
    conv_mine = my_part(conv_x, inner).astype(F32)
    gain_mine = my_part(gated_gain, inner).astype(F32)
    head_mine = my_part(head_params, heads)
    for layer in range(layers):
        skip = jnp.repeat(head_mine[layer, 2], HEADDIM)
        row_all.append(
            jnp.concatenate([conv_mine[layer], gain_mine[layer][None], skip[None], jnp.zeros((1, inner), F32)])
        )
        bc_all.append(jnp.pad(conv_bc[layer].astype(F32), ((0, 3), (0, 0))))
        head_all.append(jnp.pad(head_mine[layer], ((0, 5), (0, 128 - heads))))
        stacked = jnp.stack([w_zx[layer, 1], w_zx[layer, 0], w_out[layer].T])
        sliced = stacked.reshape(3, shard, GROUP, inner)
        swapped = lax.all_to_all(sliced, "p", 2, 1)
        gathered = lax.all_gather(swapped.reshape(3, GROUP * shard, inner), "z", axis=1, tiled=True)
        dt_full = lax.all_gather(w_dt[layer], ("z", "p"), axis=0, tiled=True)
        bc_full = lax.all_gather(w_bc[layer], ("z", "p"), axis=0, tiled=True)
        dt_mine = jnp.pad(my_part(dt_full, heads), ((0, 0), (0, 128 - heads)))
        weights.append((gathered[0], gathered[1], gathered[2], bc_full, dt_mine))

    def gather_rows(block):
        return lax.all_gather(block, "p", axis=0, tiled=True)

    def scatter_rows(partial):
        return lax.psum(lax.psum_scatter(partial, "p", scatter_dimension=0, tiled=True), "head")

    resid = resid_in[0].astype(F32)
    saved = []
    for layer in range(layers):
        wx, wz, wo, wbc, wdt = weights[layer]
        rowp, bcp, headp = row_all[layer], bc_all[layer], head_all[layer]
        inv_rms = lax.rsqrt(jnp.mean(resid * resid, axis=-1, keepdims=True) + EPS)
        own = (resid * inv_rms * norm_gain[layer].astype(F32)).astype(BF16)
        normed = gather_rows(own)
        edge = lax.ppermute(normed[tokens - EDGE :], "z", [(i, i + 1) for i in range(groups - 1)])
        normed = jnp.concatenate([edge, normed])
        z, xin, bcin, x, bc, dtraw, dt, s, y_local, local, decay, sums = call(
            forward_local,
            [
                ((tokens, inner), BF16),
                ((tokens + EDGE, inner), BF16),
                ((tokens + EDGE, 2 * STATE), BF16),
                ((tokens, inner), BF16),
                ((tokens, 2 * STATE), BF16),
                ((tokens, 128), BF16),
                ((tokens, 128), F32),
                ((tokens, 128), F32),
                ((tokens, inner), F32),
                ((spans, STATE, inner), F32),
                ((spans, 8, inner), F32),
                ((STATE + 8, inner), F32),
            ],
            normed, wx, wz, wbc, wdt, rowp, bcp, headp,
            scratch=[pltpu.VMEM((tokens + EDGE, inner + 2 * STATE), F32)],
        )
        all_sums = lax.all_gather(sums, "z")
        y, states, part, squares = call(
            functools.partial(forward_carried, groups),
            [
                ((tokens, inner), F32),
                ((spans, STATE, inner), F32),
                ((tokens, model), BF16),
                ((8, tokens), F32),
            ],
            all_sums, local, decay, y_local, x, bc, z, s, wo, rowp,
        )
        mixed = scatter_rows(part).astype(F32)
        total_sq = lax.psum(squares[0], ("p", "head"))
        inv_all = lax.rsqrt(total_sq / inner_all + EPS)
        inv_own = lax.dynamic_slice_in_dim(inv_all, place * length, length)[:, None]
        saved.append((resid, inv_rms, normed, z, xin, bcin, x, bc, dtraw, dt, s, y, states, decay, mixed, inv_all))
        resid = resid + inv_own * mixed
    block_out = resid.astype(BF16)[None]

    d_resid = cotangent[0].astype(F32)
    big, small = [None] * layers, [None] * layers
    for layer in reversed(range(layers)):
        wx, wz, wo, wbc, wdt = weights[layer]
        rowp, bcp, headp = row_all[layer], bc_all[layer], head_all[layer]
        resid, inv_rms, normed, z, xin, bcin, x, bc, dtraw, dt, s, y, states, decay, mixed, inv_all = saved[layer]
        d_mix_own = d_resid.astype(BF16)
        dots = jnp.sum(d_mix_own.astype(F32) * mixed, axis=-1)
        d_mix = gather_rows(d_mix_own)
        token_scalars = jnp.pad(jnp.stack([inv_all, gather_rows(dots)]), ((0, 6), (0, 0)))
        dz, dy, gwo, prior, sums, gate_small = call(
            functools.partial(backward_gate, inner_all),
            [
                ((tokens, inner), BF16),
                ((tokens, inner), BF16),
                ((model, inner), BF16),
                ((spans, STATE, inner), F32),
                ((STATE + 8, inner), F32),
                ((8, inner), F32),
            ],
            d_mix, wo, y, z, x, bc, s, decay, token_scalars, rowp,
            scratch=[pltpu.VMEM((tokens, inner), BF16)],
        )
        all_sums = lax.all_gather(sums, "z")
        dcat, row_small, bc_small, head_small = call(
            functools.partial(backward_ssd, groups),
            [
                ((tokens + EDGE, inner + 2 * STATE + 128), BF16),
                ((8, inner), F32),
                ((8, 2 * STATE), F32),
                ((8, 128), F32),
            ],
            all_sums, prior, decay, states, dy, x, bc, s, dt, dtraw, xin, bcin, rowp, bcp, headp,
            scratch=[
                pltpu.VMEM((tokens + 2 * EDGE, inner + 2 * STATE), F32),
                pltpu.VMEM((spans, STATE, inner), F32),
            ],
        )
        d_normed_part, gxz, gbc, gdt = call(
            backward_project,
            [
                ((tokens + EDGE, model), BF16),
                ((model, 2 * inner), BF16),
                ((model, 2 * STATE), BF16),
                ((model, 128), BF16),
            ],
            dcat, dz, normed, wx, wz, wbc, wdt,
        )
        d_normed = scatter_rows(d_normed_part[EDGE:]).astype(F32)
        edge = lax.psum(d_normed_part[:EDGE], ("p", "head"))
        edge = lax.ppermute(edge, "z", [(i + 1, i) for i in range(groups - 1)]).astype(F32)
        edge = jnp.where(place == GROUP - 1, edge, 0.0)
        d_normed = d_normed.at[length - EDGE :].add(edge)
        gain_grad = jnp.sum(d_normed * resid * inv_rms, axis=0)
        d_hidden = d_normed * norm_gain[layer].astype(F32)
        d_resid = (
            d_resid
            + inv_rms * d_hidden
            - resid * inv_rms**3 * jnp.mean(d_hidden * resid, axis=-1, keepdims=True)
        )

        grads = jnp.stack([gxz[:, :inner], gxz[:, inner:], gwo])
        grads = lax.psum_scatter(grads, "z", scatter_dimension=1, tiled=True)
        grads = lax.all_to_all(grads.reshape(3, GROUP, shard, inner), "p", 1, 2)
        grads = grads.reshape(3, shard, inner_core)
        g_zx = jnp.stack([grads[1], grads[0]])
        g_out = grads[2].T
        g_bc = lax.psum(lax.psum_scatter(gbc, ("z", "p"), scatter_dimension=0, tiled=True), "head")
        g_dt = lax.psum_scatter(gdt[:, :heads], "z", scatter_dimension=0, tiled=True)
        g_dt = lax.all_to_all(g_dt.reshape(GROUP, shard, heads), "p", 0, 1).reshape(shard, heads_core)
        big[layer] = (g_zx, g_dt, g_bc, g_out)
        skip_grad = jnp.sum(gate_small[1].reshape(heads, HEADDIM), axis=1)
        wide = jnp.concatenate([row_small[: CONV + 1], gate_small[0:1]])
        wide = jnp.zeros((CONV + 2, GROUP, inner), F32).at[:, place].set(wide).reshape(CONV + 2, inner_core)
        tall = jnp.concatenate([head_small[:2, :heads], skip_grad[None]])
        tall = jnp.zeros((3, GROUP, heads), F32).at[:, place].set(tall).reshape(3, heads_core)
        shared = lax.psum(bc_small[: CONV + 1], "head")
        small[layer] = lax.psum((gain_grad, wide, shared, tall), ("z", "p"))

    grad_input = d_resid.astype(BF16)[None]
    stack = lambda pick: jnp.stack([pick(layer) for layer in range(layers)]).astype(BF16)
    return (
        block_out,
        grad_input,
        stack(lambda l: small[l][0]),
        stack(lambda l: big[l][0]),
        stack(lambda l: big[l][1]),
        stack(lambda l: big[l][2]),
        stack(lambda l: small[l][1][: CONV + 1]),
        stack(lambda l: small[l][2]),
        stack(lambda l: small[l][3]),
        stack(lambda l: small[l][1][CONV + 1]),
        stack(lambda l: big[l][3]),
    )


def solution(mesh):
    seq, head = mesh.shape["seq"], mesh.shape["head"]
    split = Mesh(mesh.devices.reshape(seq // GROUP, GROUP, head), ("z", "p", "head"))
    seq_axes = ("z", "p")
    specs = (
        P(None, seq_axes, None),
        P(None, seq_axes, None),
        P(),
        P(None, None, seq_axes, "head"),
        P(None, seq_axes, "head"),
        P(None, seq_axes, None),
        P(None, None, "head"),
        P(),
        P(None, None, "head"),
        P(None, "head"),
        P(None, "head", seq_axes),
    )
    return jax.shard_map(on_device, mesh=split, in_specs=specs, out_specs=specs, check_vma=False)
```

```python
import functools

import jax
import jax.numpy as jnp
from jax import lax
from jax.experimental import pallas as pl
from jax.experimental.pallas import tpu as pltpu
from jax.sharding import Mesh, PartitionSpec as P

HEADDIM = 64
STATE = 128
CONV = 4
SPAN = 256
GROUP = 4
EDGE = 16
EPS = 1e-05
HIGH = lax.Precision.HIGHEST
F32, BF16 = jnp.float32, jnp.bfloat16
NN = (((1,), (0,)), ((), ()))
NT = (((1,), (1,)), ((), ()))
TN = (((0,), (0,)), ((), ()))
VMEM_BYTES = 58 << 20


def dot(a, b, dims=NN):
    return lax.dot_general(a, b, dims, preferred_element_type=F32)


def dot_exact(a, b, dims=NN):
    return lax.dot_general(a, b, dims, precision=HIGH, preferred_element_type=F32)


def dot_split(a, b, dims=NN):
    high = a.astype(BF16)
    rest = (a - high.astype(F32)).astype(BF16)
    return dot(high, b, dims) + dot(rest, b, dims)


def sigmoid(v):
    return 1.0 / (1.0 + jnp.exp(-v))


def softplus(v):
    return jnp.maximum(v, 0.0) + jnp.log1p(jnp.exp(-jnp.abs(v)))


def silu_slope(v):
    sig = sigmoid(v)
    return sig * (1.0 + v * (1.0 - sig))


def iota(shape, dim):
    return lax.broadcasted_iota(jnp.int32, shape, dim)


def head_spread(inner):
    return (iota((128, inner), 0) == lax.shift_right_logical(iota((128, inner), 1), 6)).astype(BF16)


def triangle(lower):
    rows, cols = iota((SPAN, SPAN), 0), iota((SPAN, SPAN), 1)
    return ((cols <= rows) if lower else (cols >= rows)).astype(F32)


def half_masks():
    lane = iota((SPAN, 128), 1)
    return (lane < HEADDIM).astype(BF16), (lane >= HEADDIM).astype(BF16)


def conv_taps(window, taps):
    total = jnp.broadcast_to(taps[CONV : CONV + 1], (SPAN, window.shape[1]))
    for j in range(CONV):
        total = total + taps[j : j + 1] * window[EDGE - 3 + j : EDGE - 3 + j + SPAN]
    return total


def forward_local(
    normed, wx, wz, wbc, wdt, rowp, bcp, headp,
    z_out, xin_out, bcin_out, x_out, bc_out, dtraw_out, dt_out, s_out, y_out, local_out, decay_out, sum_out, all_decay_out,
    ext,
):
    inner = x_out.shape[1]
    spans = x_out.shape[0] // SPAN

    edge = normed[0:EDGE]
    edge_x = dot(edge, wx[...]).astype(BF16)
    edge_bc = dot(edge, wbc[...]).astype(BF16)
    xin_out[0:EDGE] = edge_x
    bcin_out[0:EDGE] = edge_bc
    ext[0:EDGE, 0:inner] = edge_x.astype(F32)
    ext[0:EDGE, inner:] = edge_bc.astype(F32)
    spread = head_spread(inner)
    low_tri = triangle(True)
    rate = -jnp.exp(headp[0:1])
    bias = headp[1:2]

    def block(q, carry):
        state_sum, decay_all = carry
        at = pl.multiple_of(q * SPAN, SPAN)
        tok = pl.ds(at, SPAN)
        after = pl.ds(pl.multiple_of(at + EDGE, EDGE), SPAN)
        rows = normed[after, :]
        z_out[tok, :] = dot(rows, wz[...]).astype(BF16)
        xin = dot(rows, wx[...]).astype(BF16)
        bcin = dot(rows, wbc[...]).astype(BF16)
        dtraw = dot(rows, wdt[...]).astype(BF16)
        xin_out[after, :] = xin
        bcin_out[after, :] = bcin
        dtraw_out[tok, :] = dtraw
        ext[after, 0:inner] = xin.astype(F32)
        ext[after, inner:] = bcin.astype(F32)
        window = pl.ds(at, SPAN + EDGE)
        pre_x = conv_taps(ext[window, 0:inner], rowp)
        x = (pre_x * sigmoid(pre_x)).astype(BF16)
        x_out[tok, :] = x
        pre_bc = conv_taps(ext[window, inner:], bcp)
        bc = (pre_bc * sigmoid(pre_bc)).astype(BF16)
        bc_out[tok, :] = bc
        b, c = bc[:, :STATE], bc[:, STATE:]
        dt = softplus(dtraw.astype(F32) + bias)
        s = dot_exact(low_tri, dt * rate)
        dt_out[tok, :] = dt
        s_out[tok, :] = s
        s_row, dt_row = s.T, dt.T
        cb = dot(c, b, NT)
        causal = iota((SPAN, SPAN), 1) <= iota((SPAN, SPAN), 0)
        masks = half_masks()
        for pair in range(inner // 128):
            lanes = slice(pair * 128, pair * 128 + 128)
            x_pair = x[:, lanes]
            total = None
            for e in range(2):
                h = pair * 2 + e
                gap = jnp.where(causal, s[:, h : h + 1] - s_row[h : h + 1, :], -1e30)
                scores = (cb * (jnp.exp(gap) * dt_row[h : h + 1, :])).astype(BF16)
                term = dot(scores, x_pair * masks[e])
                total = term if total is None else total + term
            y_out[tok, lanes] = total
        to_end = jnp.exp(s[SPAN - 1 : SPAN] - s) * dt
        weighted = (x.astype(F32) * dot_split(to_end, spread)).astype(BF16)
        local = dot(b, weighted, TN)
        decay = dot_split(jnp.exp(s[SPAN - 8 : SPAN]), spread)[7:8]
        local_out[q] = local
        decay_out[q] = jnp.broadcast_to(decay, (8, inner))
        return state_sum * decay + local, decay_all * decay

    state_sum, decay_all = lax.fori_loop(
        0, spans, block, (jnp.zeros((STATE, inner), F32), jnp.ones((1, inner), F32))
    )
    sum_out[...] = state_sum.astype(BF16)
    all_decay_out[...] = jnp.broadcast_to(decay_all, (8, inner))


def entering_state(place, count, sums, decays, backward):
    inner = sums.shape[2]
    state = jnp.zeros((STATE, inner), F32)
    for turn in range(count):
        other = count - 1 - turn if backward else turn
        ahead = (place < other) if backward else (other < place)
        state = jnp.where(ahead, decays[other, 0:1] * state + sums[other].astype(F32), state)
    return state


def forward_carried(count, sums, decays, local, decay, y_local, x, bc, z, s, wo, rowp, y_out, states_out, part_out, sq_out):
    inner = x.shape[1]
    spans = x.shape[0] // SPAN
    spread = head_spread(inner)
    gain, skip = rowp[5:6], rowp[6:7]
    ones = jnp.ones((8, inner), F32)

    def block(q, state):
        tok = pl.ds(pl.multiple_of(q * SPAN, SPAN), SPAN)
        states_out[q] = state
        c = bc[tok, STATE:]
        carried = dot_split(jnp.exp(s[tok, :]), spread) * dot(c, state.astype(BF16))
        y = y_local[tok, :] + carried + skip * x[tok, :].astype(F32)
        y_out[tok, :] = y
        zf = z[tok, :].astype(F32)
        gated = y * (zf * sigmoid(zf))
        sq_out[:, tok] = dot_exact(ones, gated * gated, NT)
        part_out[tok, :] = dot((gated * gain).astype(BF16), wo[...], NT).astype(BF16)
        return decay[q, 0:1] * state + local[q]

    lax.fori_loop(0, spans, block, entering_state(lax.axis_index("z"), count, sums, decays, False))


def backward_gate(
    inner_all, dmix, wo, y_in, z, x, bc, s, decay, token_scalars, rowp,
    dz_out, dy_out, gwo_out, prior_out, sum_out, all_decay_out, small_out,
    normed_out,
):
    inner = x.shape[1]
    spans = x.shape[0] // SPAN
    spread = head_spread(inner)
    gain = rowp[5:6]

    def block(i, carry):
        grad_sum, gain_sum, skip_sum = carry
        q = spans - 1 - i
        tok = pl.ds(pl.multiple_of(q * SPAN, SPAN), SPAN)
        columns = token_scalars[:, tok].T
        inv, total_dot = columns[:, 0:1], columns[:, 1:2]
        zf = z[tok, :].astype(F32)
        sig = sigmoid(zf)
        act = zf * sig
        y = y_in[tok, :]
        gated = y * act
        d_no = dot(dmix[tok, :], wo[...])
        scaled = gated * inv
        normed_out[tok, :] = (scaled * gain).astype(BF16)
        gain_sum = gain_sum + jnp.sum(d_no * scaled, axis=0, keepdims=True)
        d_gated = inv * (d_no * gain) - gated * (inv * inv * inv * total_dot * (1.0 / inner_all))
        dz_out[tok, :] = (d_gated * y * (sig * (1.0 + zf * (1.0 - sig)))).astype(BF16)
        dy = d_gated * act
        xf = x[tok, :].astype(F32)
        skip_sum = skip_sum + jnp.sum(dy * xf, axis=0, keepdims=True)
        dy_low = dy.astype(BF16)
        dy_out[tok, :] = dy_low
        scaled_dy = (dy_low.astype(F32) * dot_split(jnp.exp(s[tok, :]), spread)).astype(BF16)
        prior = dot(bc[tok, STATE:], scaled_dy, TN)
        prior_out[q] = prior
        return prior + decay[q, 0:1] * grad_sum, gain_sum, skip_sum

    zero = jnp.zeros((1, inner), F32)
    grad_sum, gain_sum, skip_sum = lax.fori_loop(
        0, spans, block, (jnp.zeros((STATE, inner), F32), zero, zero)
    )
    decay_all = decay[0, 0:1]
    for q in range(1, spans):
        decay_all = decay_all * decay[q, 0:1]
    sum_out[...] = grad_sum.astype(BF16)
    all_decay_out[...] = jnp.broadcast_to(decay_all, (8, inner))
    small_out[0:1] = gain_sum
    small_out[1:2] = skip_sum
    small_out[2:8] = jnp.zeros((6, inner), F32)

    def out_grad(i, _):
        rows = pl.ds(pl.multiple_of(i * SPAN, SPAN), SPAN)
        gwo_out[rows, :] = dot(dmix[:, rows], normed_out[...], TN).astype(BF16)
        return 0

    lax.fori_loop(0, dmix.shape[1] // SPAN, out_grad, 0)


def backward_ssd(
    count, sums, decays, prior, decay, states, dy_in, x, bc, s_in, dt_in, dtraw, xin, bcin, rowp, bcp, headp,
    dcat_out, row_out, bcrow_out, head_out,
    dpre, dend,
):
    inner = x.shape[1]
    spans = x.shape[0] // SPAN
    spread = head_spread(inner)
    up_tri = triangle(False)
    skip = rowp[6:7]
    rate = -jnp.exp(headp[0:1])
    bias = headp[1:2]
    width = inner + 2 * STATE

    def chain(i, grad):
        q = spans - 1 - i
        dend[q] = grad
        return prior[q] + decay[q, 0:1] * grad

    lax.fori_loop(0, spans, chain, entering_state(lax.axis_index("z"), count, sums, decays, True))
    dpre[0:EDGE] = jnp.zeros((EDGE, width), F32)
    dpre[EDGE + spans * SPAN :] = jnp.zeros((EDGE, width), F32)
    row_out[...] = jnp.zeros_like(row_out)
    bcrow_out[...] = jnp.zeros_like(bcrow_out)
    head_out[...] = jnp.zeros_like(head_out)
    dcat_out[0:EDGE, width:] = jnp.zeros((EDGE, 128), BF16)

    def block(q, _):
        at = pl.multiple_of(q * SPAN, SPAN)
        tok = pl.ds(at, SPAN)
        after = pl.ds(pl.multiple_of(at + EDGE, EDGE), SPAN)
        window = pl.ds(at, SPAN + EDGE)
        x_low, dy = x[tok, :], dy_in[tok, :]
        xf, dyf = x_low.astype(F32), dy.astype(F32)
        b, c = bc[tok, :STATE], bc[tok, STATE:]
        s, dt = s_in[tok, :], dt_in[tok, :]
        exp_s = jnp.exp(s)
        to_end = jnp.exp(s[SPAN - 1 : SPAN] - s)
        w = to_end * dt
        w_all, s_all = dot_split(w, spread), dot_split(exp_s, spread)
        state, grad = states[q], dend[q]
        state_low, grad_low = state.astype(BF16), grad.astype(BF16)
        carried = s_all * dot(c, state_low)
        ds = dot_split(dyf * carried, spread, NT)
        d_c = dot((dyf * s_all).astype(BF16), state_low, NT)
        d_w = dot(b, grad_low)
        d_b = dot((xf * w_all).astype(BF16), grad_low, NT)
        dx = dyf * skip + d_w * w_all
        dsw = dot_split(d_w * xf, spread, NT)
        s_row = s.T
        cb = dot(b, c, NT)
        seen = iota((SPAN, SPAN), 0) <= iota((SPAN, SPAN), 1)
        masks = half_masks()
        d_cb = jnp.zeros((SPAN, SPAN), F32)
        lane = iota((SPAN, 128), 1)
        row_id = iota((128, SPAN), 0)
        sum_k = jnp.zeros((128, SPAN), F32)
        sum_t = jnp.zeros((SPAN, 128), F32)
        dx_pairs = []
        for pair in range(inner // 128):
            lanes = slice(pair * 128, pair * 128 + 128)
            x_pair, dy_pair = x_low[:, lanes], dy[:, lanes]
            total = dx[:, lanes]
            for e in range(2):
                h = pair * 2 + e
                d_scores = dot(x_pair * masks[e], dy_pair, NT)
                fade = jnp.exp(jnp.where(seen, s_row[h : h + 1, :] - s[:, h : h + 1], -1e30))
                dt_h = dt[:, h : h + 1]
                fade_cb = cb * fade
                total = total + dot((fade_cb * dt_h).astype(BF16), dy_pair * masks[e])
                d_cb = d_cb + d_scores * (fade * dt_h)
                flow = d_scores * fade_cb
                sum_t = jnp.where(lane == h, jnp.sum(flow, axis=1, keepdims=True), sum_t)
                sum_k = jnp.where(row_id == h, jnp.sum(flow * dt_h, axis=0, keepdims=True), sum_k)
            dx_pairs.append(total)
        d_cb_low = d_cb.astype(BF16)
        d_b = d_b + dot(d_cb_low, c)
        d_c = d_c + dot(d_cb_low, b, TN)
        end = dsw * w
        ds = ds + sum_k.T - sum_t * dt - end
        held = dot_split(jnp.broadcast_to(jnp.sum(grad * state, axis=0, keepdims=True), (8, inner)), spread, NT)[0:1]
        last = jnp.sum(end, axis=0, keepdims=True) + held * exp_s[SPAN - 1 : SPAN]
        ds = ds + jnp.where(iota((SPAN, 128), 0) == SPAN - 1, last, 0.0)
        da = dot_exact(up_tri, ds)
        d_dt = sum_t + dsw * to_end + da * rate
        d_raw = d_dt * sigmoid(dtraw[tok, :].astype(F32) + bias)
        d_raw = jnp.where(lane < inner // HEADDIM, d_raw, 0.0)
        head_out[0:1] += jnp.sum(da * (dt * rate), axis=0, keepdims=True)
        head_out[1:2] += jnp.sum(d_raw, axis=0, keepdims=True)
        dcat_out[after, width:] = d_raw.astype(BF16)

        win_x = xin[window, :].astype(F32)
        d_x = jnp.concatenate(dx_pairs, axis=1) * silu_slope(conv_taps(win_x, rowp))
        dpre[after, 0:inner] = d_x
        for j in range(CONV):
            row_out[j : j + 1] += jnp.sum(d_x * win_x[EDGE - 3 + j : EDGE - 3 + j + SPAN], axis=0, keepdims=True)
        row_out[CONV : CONV + 1] += jnp.sum(d_x, axis=0, keepdims=True)
        win_bc = bcin[window, :].astype(F32)
        d_bc = jnp.concatenate([d_b, d_c], axis=1) * silu_slope(conv_taps(win_bc, bcp))
        dpre[after, inner:] = d_bc
        for j in range(CONV):
            bcrow_out[j : j + 1] += jnp.sum(d_bc * win_bc[EDGE - 3 + j : EDGE - 3 + j + SPAN], axis=0, keepdims=True)
        bcrow_out[CONV : CONV + 1] += jnp.sum(d_bc, axis=0, keepdims=True)
        return 0

    lax.fori_loop(0, spans, block, 0)

    def back(window, taps, rows):
        total = None
        for j in range(CONV):
            term = taps[j : j + 1] * window[CONV - 1 - j : CONV - 1 - j + rows]
            total = term if total is None else total + term
        return total.astype(BF16)

    dcat_out[0:EDGE, 0:inner] = back(dpre[0 : 2 * EDGE, 0:inner], rowp, EDGE)
    dcat_out[0:EDGE, inner:width] = back(dpre[0 : 2 * EDGE, inner:], bcp, EDGE)

    def conv_block(q, _):
        at = pl.multiple_of(q * SPAN, SPAN)
        after = pl.ds(pl.multiple_of(at + EDGE, EDGE), SPAN)
        window = pl.ds(pl.multiple_of(at + EDGE, EDGE), SPAN + EDGE)
        dcat_out[after, 0:inner] = back(dpre[window, 0:inner], rowp, SPAN)
        dcat_out[after, inner:width] = back(dpre[window, inner:], bcp, SPAN)
        return 0

    lax.fori_loop(0, spans, conv_block, 0)


def backward_project(dcat, dz, normed, wx, wz, wbc, wdt, dn_out, gx_out, gz_out, gbc_out, gdt_out):
    inner = dz.shape[1]
    width = inner + 2 * STATE
    spans = dz.shape[0] // SPAN
    d_edge = dcat[0:EDGE]
    dn_out[0:EDGE] = (
        dot(d_edge[:, 0:inner], wx[...], NT)
        + dot(d_edge[:, inner:width], wbc[...], NT)
    ).astype(BF16)

    def rows_of(q, _):
        at = pl.multiple_of(q * SPAN, SPAN)
        tok = pl.ds(at, SPAN)
        after = pl.ds(pl.multiple_of(at + EDGE, EDGE), SPAN)
        dn_out[after, :] = (
            dot(dz[tok, :], wz[...], NT)
            + dot(dcat[after, 0:inner], wx[...], NT)
            + dot(dcat[after, inner:width], wbc[...], NT)
            + dot(dcat[after, width:], wdt[...], NT)
        ).astype(BF16)
        return 0

    lax.fori_loop(0, spans, rows_of, 0)

    def grads_of(i, _):
        cols = pl.ds(pl.multiple_of(i * SPAN, SPAN), SPAN)
        part = normed[:, cols]
        both = dot(part, dcat[:, 0:width], TN).astype(BF16)
        gx_out[cols, :] = both[:, 0:inner]
        gbc_out[cols, :] = both[:, inner:]
        gdt_out[:, cols] = dot(dcat[:, width:], part, TN)[0:EDGE].astype(BF16)
        gz_out[cols, :] = dot(part[EDGE:], dz[...], TN).astype(BF16)
        return 0

    lax.fori_loop(0, normed.shape[1] // SPAN, grads_of, 0)


HALF = 128
MESH = pl.DeviceIdType.MESH


class Links:
    def __init__(self, sends, recvs):
        self.z, self.p, self.c = lax.axis_index("z"), lax.axis_index("p"), lax.axis_index("head")
        self.groups = lax.axis_size("z")
        self.sends, self.recvs, self.used = sends, recvs, 0

    def copy(self, src, dst, device):
        i = self.used
        self.used += 1
        return pltpu.make_async_remote_copy(
            src_ref=src, dst_ref=dst, send_sem=self.sends.at[i], recv_sem=self.recvs.at[i],
            device_id=device, device_id_type=MESH,
        )

    def local(self, src, dst):
        i = self.used
        self.used += 1
        return pltpu.make_async_copy(src, dst, self.sends.at[i])

    def at(self, k, e):
        return (self.z, lax.bitwise_xor(self.p, jnp.int32(k)), lax.bitwise_xor(self.c, jnp.int32(e)))

    def last_of_plane(self):
        return jnp.logical_and(self.p == GROUP - 1, self.c == 1)

    def start_barrier(self, plane=False, lines=False, edge=0):
        barrier = pltpu.get_barrier_semaphore()
        z, groups = self.z, self.groups

        def signal(device):
            pl.semaphore_signal(barrier, 1, device_id=device, device_id_type=MESH)

        if plane:
            for k in range(GROUP):
                for e in range(2):
                    if k or e:
                        signal(self.at(k, e))
        has_below, has_above = z > 0, z < groups - 1
        if lines:
            pl.when(has_below)(lambda: signal((z - 1, self.p, self.c)))
            pl.when(has_above)(lambda: signal((z + 1, self.p, self.c)))
        if edge == 1:
            pl.when(has_below)(lambda: signal((z - 1, jnp.int32(GROUP - 1), jnp.int32(1))))
        if edge == -1:

            @pl.when(jnp.logical_and(self.last_of_plane(), has_above))
            def _():
                for p in range(GROUP):
                    for c in range(2):
                        signal((z + 1, jnp.int32(p), jnp.int32(c)))

        count = jnp.int32(2 * GROUP - 1 if plane else 0)
        if lines:
            count = count + has_below.astype(jnp.int32) + has_above.astype(jnp.int32)
        if edge == 1:
            sending = jnp.logical_and(self.last_of_plane(), has_above)
            count = count + 2 * GROUP * sending.astype(jnp.int32)
        if edge == -1:
            count = count + has_below.astype(jnp.int32)
        pl.semaphore_wait(barrier, count)


class Gather:
    def __init__(self, links, out, base):
        self.links, self.out, self.base = links, out, base

        def place(k, c):
            row = base + lax.bitwise_xor(links.p, jnp.int32(k)) * (2 * HALF) + c * HALF
            return out.at[pl.ds(pl.multiple_of(row, EDGE), HALF), :]

        own = place(0, links.c)
        self.out_copies = [links.copy(own, own, links.at(k, 0)) for k in (3, 1, 2)]
        self.shared = [links.copy(own, own, links.at(0, 1))]
        self.shared += [links.copy(place(k, links.c), place(k, links.c), links.at(0, 1)) for k in (1, 2, 3)]
        self.arrivals = [self.out_copies[1], self.out_copies[2], self.out_copies[0]]

    def own(self, start, size):
        row = self.base + self.links.p * (2 * HALF) + self.links.c * HALF + start
        return pl.ds(pl.multiple_of(row, EDGE), size)

    def start(self):
        for copy in self.out_copies:
            copy.start()
        self.shared[0].start()

    def pass_on(self):
        for k in range(3):
            self.arrivals[k].wait_recv()
            self.shared[k + 1].start()

    def finish(self):
        for copy in self.shared:
            copy.wait_recv()
        for copy in self.shared + self.out_copies:
            copy.wait_send()


class EdgeForward:
    def __init__(self, links, gather):
        self.links = links
        tail = gather.out.at[gather.own(HALF - EDGE, EDGE), :]
        first = links.used
        links.used += 2 * GROUP + 1
        recv = links.recvs.at[first + 2 * GROUP]
        self.out = gather.out
        self.copies = [
            pltpu.make_async_remote_copy(
                src_ref=tail, dst_ref=gather.out.at[0:EDGE, :], send_sem=links.sends.at[first + p * 2 + c], recv_sem=recv,
                device_id=(links.z + 1, jnp.int32(p), jnp.int32(c)), device_id_type=MESH,
            )
            for p in range(GROUP)
            for c in range(2)
        ]
        self.sending = jnp.logical_and(links.last_of_plane(), links.z < links.groups - 1)

    def start(self):
        @pl.when(self.sending)
        def _():
            for copy in self.copies:
                copy.start()

        @pl.when(self.links.z == 0)
        def _():
            self.out[0:EDGE, :] = jnp.zeros((EDGE, self.out.shape[1]), self.out.dtype)

    def finish(self):
        pl.when(self.links.z > 0)(self.copies[0].wait_recv)

        @pl.when(self.sending)
        def _():
            for copy in self.copies:
                copy.wait_send()


class Scatter:
    def __init__(self, links, part, base, sib, total, peer):
        self.links, self.part, self.base = links, part, base
        self.sib, self.total, self.peer = sib, total, peer
        other = 1 - links.c
        self.to_sibling = {
            k: links.copy(part.at[self.rows(k, other, 0, HALF), :], sib.at[k], links.at(0, 1)) for k in (3, 1, 2, 0)
        }
        self.to_peer = {k: links.copy(total.at[k - 1], peer.at[k - 1], links.at(k, 0)) for k in (3, 1, 2)}

    def rows(self, k, c, start, size):
        row = self.base + lax.bitwise_xor(self.links.p, jnp.int32(k)) * (2 * HALF) + c * HALF + start
        return pl.ds(pl.multiple_of(row, EDGE), size)

    def start(self):
        for copy in self.to_sibling.values():
            copy.start()

    def reduce(self):
        for k in (3, 1, 2):
            self.to_sibling[k].wait_recv()

            def add(i, _, k=k):
                at = pl.ds(pl.multiple_of(i * 32, 32), 32)
                mine = self.part[self.rows(k, self.links.c, i * 32, 32), :].astype(F32)
                self.total[k - 1, at, :] = (mine + self.sib[k, at, :].astype(F32)).astype(BF16)
                return 0

            lax.fori_loop(0, HALF // 32, add, 0)
            self.to_peer[k].start()
        self.to_sibling[0].wait_recv()
        for copy in self.to_peer.values():
            copy.wait_recv()

    def own(self, start, size):
        at = pl.ds(start, size)
        total = self.part[self.rows(0, self.links.c, start, size), :].astype(F32) + self.sib[0, at, :].astype(F32)
        for k in range(3):
            total = total + self.peer[k, at, :].astype(F32)
        return total

    def finish(self):
        for copy in list(self.to_sibling.values()) + list(self.to_peer.values()):
            copy.wait_send()


class SmallSum:
    def __init__(self, links, squares, slots):
        self.links, self.squares, self.slots = links, squares, slots
        self.copies = [
            links.copy(squares.at[:, self.lanes(k, e)], slots.at[2 * k + e - 1], links.at(k, e))
            for k in range(GROUP)
            for e in range(2)
            if k or e
        ]

    def lanes(self, k, e):
        links = self.links
        column = lax.bitwise_xor(links.p, jnp.int32(k)) * (2 * HALF) + lax.bitwise_xor(links.c, jnp.int32(e)) * HALF
        return pl.ds(pl.multiple_of(column, HALF), HALF)

    def start(self):
        for copy in self.copies:
            copy.start()

    def total(self):
        for copy in self.copies:
            copy.wait_recv()
        total = self.squares[:, self.lanes(0, 0)]
        for i in range(len(self.copies)):
            total = total + self.slots[i]
        return total

    def finish(self):
        for copy in self.copies:
            copy.wait_send()


class SmallGather:
    def __init__(self, links, out):
        self.out = out
        self.lanes = pl.ds(pl.multiple_of(links.p * (2 * HALF) + links.c * HALF, HALF), HALF)
        self.copies = [
            links.copy(out.at[:, self.lanes], out.at[:, self.lanes], links.at(k, e))
            for k in range(GROUP)
            for e in range(2)
            if k or e
        ]

    def start(self):
        for copy in self.copies:
            copy.start()

    def finish(self):
        for copy in self.copies:
            copy.wait()


def row_chunks(size=32):
    return [(start, size) for start in range(0, HALF, size)]


def rms_of(rows):
    return lax.rsqrt(jnp.mean(rows * rows, axis=-1, keepdims=True) + EPS)


def as_tile(columns):
    lane = iota((HALF, HALF), 1)
    wide = jnp.zeros((HALF, HALF), F32)
    for i, column in enumerate(columns):
        wide = jnp.where(lane == i, column, wide)
    return wide.T[0:8]


def begin_kernel(
    resid, cot, gain, wx, wz, wo, wbd, normed_out, dmix_out, wx_out, wz_out, wo_out, wbd_out, resid_out, cot_out,
    sends, recvs,
):
    links = Links(sends, recvs)
    z, p, c = links.z, links.p, links.c
    inner = wx_out.shape[2]
    groups = links.groups

    def columns(k):
        return pl.ds(pl.multiple_of(lax.bitwise_xor(p, jnp.int32(k)) * inner, 128), inner)

    mine = z * GROUP + p
    pairs = ((wx, wx_out), (wz, wz_out), (wo, wo_out))
    swaps = [[links.copy(w.at[:, columns(k)], out.at[mine], links.at(k, 0)) for k in (1, 2, 3)] for w, out in pairs]
    swaps.append([links.copy(wbd, wbd_out.at[c, mine], links.at(k, 0)) for k in (1, 2, 3)])
    keeps = [links.local(w.at[:, columns(0)], out.at[mine]) for w, out in pairs]
    keeps.append(links.local(wbd, wbd_out.at[c, mine]))
    for copy in keeps:
        copy.start()

    gather = Gather(links, normed_out, EDGE)
    other = Gather(links, dmix_out, 0)
    edge = EdgeForward(links, gather)
    for start, size in row_chunks():
        rows = pl.ds(pl.multiple_of(c * HALF + start, EDGE), size)
        part = resid[rows, :].astype(F32)
        resid_out[start : start + size] = part
        normed_out[gather.own(start, size), :] = (part * rms_of(part) * gain[...]).astype(BF16)
        part = cot[rows, :]
        cot_out[start : start + size] = part.astype(F32)
        dmix_out[other.own(start, size), :] = part

    links.start_barrier(plane=True, lines=True, edge=1)
    for group in swaps:
        for copy in group:
            copy.start()
    gather.start()
    edge.start()

    def piece(i, index):
        at = pl.ds(index * GROUP, GROUP)
        return wbd_out.at[c, at] if i == 3 else pairs[i][1].at[at]

    def lines(step):
        found = []
        up, down = z - step + 1, z + step - 1
        for i in range(4):
            block = piece(i, jnp.maximum(up, 0))
            sending = jnp.logical_and(up >= 0, z < groups - 1)
            found.append((sending, z - step >= 0, links.copy(block, block, (z + 1, p, c))))
            block = piece(i, jnp.minimum(down, groups - 1))
            sending = jnp.logical_and(down < groups, z > 0)
            found.append((sending, z + step < groups, links.copy(block, block, (z - 1, p, c))))
        return found

    steps = [lines(step) for step in range(1, groups)]
    share = links.copy(wbd_out.at[c], wbd_out.at[c], links.at(0, 1))
    for i in range(4):
        keeps[i].wait()
        for copy in swaps[i]:
            copy.wait_recv()
        for can_send, _, copy in steps[0][2 * i : 2 * i + 2]:
            pl.when(can_send)(copy.start)
    gather.pass_on()
    other.start()
    for step in range(1, len(steps)):
        for i in range(8):
            pl.when(steps[step - 1][i][1])(steps[step - 1][i][2].wait_recv)
            pl.when(steps[step][i][0])(steps[step][i][2].start)
        if step == 1:
            other.pass_on()
    for i in range(8):
        pl.when(steps[-1][i][1])(steps[-1][i][2].wait_recv)
    share.start()
    gather.finish()
    other.finish()
    edge.finish()
    for group in swaps:
        for copy in group:
            copy.wait_send()
    for found in steps:
        for can_send, _, copy in found:
            pl.when(can_send)(copy.wait_send)
    share.wait()


def exchange_kernel(backward, state, decay, states_out, decays_out, sends, recvs):
    links = Links(sends, recvs)
    z, groups = links.z, links.groups
    states_out[z] = state[...]
    decays_out[z] = decay[...]
    barrier = pltpu.get_barrier_semaphore()
    found = []
    for k in range(1, groups):
        to, source = (z - k, z + k) if backward else (z + k, z - k)
        sending, receiving = (to >= 0, source < groups) if backward else (to < groups, source >= 0)
        device = (jnp.clip(to, 0, groups - 1), links.p, links.c)
        pair = [
            links.copy(states_out.at[z], states_out.at[z], device),
            links.copy(decays_out.at[z], decays_out.at[z], device),
        ]
        found.append((sending, receiving, pair))

        @pl.when(receiving)
        def _(source=source):
            pl.semaphore_signal(barrier, 1, device_id=(source, links.p, links.c), device_id_type=MESH)

    count = z if backward else groups - 1 - z
    pl.when(count > 0)(lambda: pl.semaphore_wait(barrier, count))
    for sending, _, pair in found:

        @pl.when(sending)
        def _(pair=pair):
            for copy in pair:
                copy.start()

    for sending, receiving, pair in found:

        @pl.when(receiving)
        def _(pair=pair):
            for copy in pair:
                copy.wait_recv()

        @pl.when(sending)
        def _(pair=pair):
            for copy in pair:
                copy.wait_send()


class SmallSums:
    def __init__(self, links, bc, vec, dt, wide, bc_out, vec_out, dt_out, wide_out, bufs):
        self.links = links
        self.bc, self.vec, self.dt, self.wide = bc, vec, dt, wide
        self.bc_out, self.vec_out, self.dt_out, self.wide_out = bc_out, vec_out, dt_out, wide_out
        self.bc_in, self.bc_sum, self.bc_far, self.vec_in, self.vec_far, self.dt_far, self.wide_far = bufs
        z, p, c, groups = links.z, links.p, links.c, links.groups
        self.first, self.second, self.third = [], [], []
        for k in range(GROUP):
            for e in range(2):
                if not (k or e):
                    continue
                slot = 2 * k + e
                to_p, to_c = lax.bitwise_xor(p, jnp.int32(k)), lax.bitwise_xor(c, jnp.int32(e))
                device = links.at(k, e)
                for layer in range(bc.shape[0]):
                    src = bc.at[layer, :, to_p, :, pl.ds(pl.multiple_of(to_c * STATE, STATE), STATE)]
                    self.first.append(links.copy(src, self.bc_in.at[layer, slot - 1], device))
                self.first.append(links.copy(vec.at[to_p * 2 + to_c], self.vec_in.at[slot - 1], device))
                self.third.append(links.copy(vec_out.at[p * 2 + c], vec_out.at[p * 2 + c], device))
        for k in range(1, groups):
            to = lax.rem(z + k, groups)
            device = (to, p, c)
            for layer in range(bc.shape[0]):
                self.second.append(links.copy(self.bc_sum.at[layer, to], self.bc_far.at[layer, k - 1], device))
            self.second.append(links.copy(self.vec_in.at[7], self.vec_far.at[k - 1], device))
            self.second.append(links.copy(dt.at[to], self.dt_far.at[k - 1], device))
            self.second.append(links.copy(wide, self.wide_far.at[k - 1], device))
        for k in range(1, GROUP):
            device = links.at(k, 0)
            self.third.append(links.copy(dt_out.at[p], dt_out.at[p], device))
            self.third.append(links.copy(wide_out.at[p], wide_out.at[p], device))
        lanes = pl.ds(pl.multiple_of(c * STATE, STATE), STATE)
        self.third.append(links.copy(bc_out.at[:, :, lanes], bc_out.at[:, :, lanes], links.at(0, 1)))

    def round_one(self):
        for copy in self.first:
            copy.start()

    def round_two(self):
        links = self.links
        for copy in self.first:
            copy.wait_recv()
        own_lanes = pl.ds(pl.multiple_of(links.c * STATE, STATE), STATE)
        for layer in range(self.bc.shape[0]):

            def add(i, _, layer=layer):
                total = self.bc[layer, i, links.p, :, own_lanes].astype(F32)
                for slot in range(2 * GROUP - 1):
                    total = total + self.bc_in[layer, slot, i].astype(F32)
                self.bc_sum[layer, i] = total.astype(BF16)
                return 0

            lax.fori_loop(0, links.groups, add, 0)
        total = self.vec[links.p * 2 + links.c]
        for slot in range(2 * GROUP - 1):
            total = total + self.vec_in[slot]
        self.vec_in[7] = total
        for copy in self.second:
            copy.start()

    def round_three(self):
        links = self.links
        z, p, c = links.z, links.p, links.c
        for copy in self.second:
            copy.wait_recv()
        far = links.groups - 1
        lanes = pl.ds(pl.multiple_of(c * STATE, STATE), STATE)
        for layer in range(self.bc.shape[0]):
            total = self.bc_sum[layer, z].astype(F32)
            for k in range(far):
                total = total + self.bc_far[layer, k].astype(F32)
            self.bc_out[layer, :, lanes] = total.astype(BF16)
        total = self.vec_in[7]
        dt_total = self.dt[z].astype(F32)
        wide_total = self.wide[...]
        for k in range(far):
            total = total + self.vec_far[k]
            dt_total = dt_total + self.dt_far[k].astype(F32)
            wide_total = wide_total + self.wide_far[k]
        self.vec_out[p * 2 + c] = total
        self.dt_out[p] = dt_total.astype(BF16)
        self.wide_out[p] = wide_total
        for copy in self.third:
            copy.start()

    def finish(self):
        for copy in self.third:
            copy.wait_recv()
        for copy in self.first + self.second + self.third:
            copy.wait_send()


def grads_kernel(
    gx, gz, go, bc, vec, dt, wide, gx_out, gz_out, go_out, bc_out, vec_out, dt_out, wide_out,
    up_buf, down_buf, total, final, bc_in, bc_sum, bc_far, vec_in, vec_far, dt_far, wide_far, sends, recvs,
):
    links = Links(sends, recvs)
    z, p, c, groups = links.z, links.p, links.c, links.groups
    inner = gx.shape[2]
    parts, outs = (gx, gz, go), (gx_out, gz_out, go_out)
    small = SmallSums(
        links, bc, vec, dt, wide, bc_out, vec_out, dt_out, wide_out,
        (bc_in, bc_sum, bc_far, vec_in, vec_far, dt_far, wide_far),
    )
    barrier = pltpu.get_barrier_semaphore()
    for k in range(GROUP):
        for e in range(2):
            if k or e:
                pl.semaphore_signal(barrier, 1, device_id=links.at(k, e), device_id_type=MESH)
    for k in range(1, groups):
        pl.semaphore_signal(barrier, 1, device_id=(lax.rem(z + k, groups), p, c), device_id_type=MESH)
    pl.semaphore_wait(barrier, 2 * GROUP - 1 + groups - 1)

    def block(i, index):
        return parts[i].at[pl.ds(index * GROUP, GROUP)]

    def add_own(i, index, buf):
        def add(j, _):
            buf[j] = (buf[j].astype(F32) + parts[i][index * GROUP + j].astype(F32)).astype(BF16)
            return 0

        lax.fori_loop(0, GROUP, add, 0)

    small.round_one()
    waits = []
    for s in range(groups - 1):
        for i in range(3):
            for up in (True, False):
                target = groups - 1 - s if up else s
                buf = (up_buf if up else down_buf).at[s, i]
                if up:
                    first, passing, ends, to = z == 0, jnp.logical_and(z > 0, z < target), z == target, z + 1
                else:
                    first, passing, ends, to = z == groups - 1, jnp.logical_and(z < groups - 1, z > target), z == target, z - 1
                index = links.used
                links.used += 1

                def copy_from(src, index=index, buf=buf, to=to):
                    return pltpu.make_async_remote_copy(
                        src_ref=src, dst_ref=buf, send_sem=links.sends.at[index], recv_sem=links.recvs.at[index],
                        device_id=(to, p, c), device_id_type=MESH,
                    )

                here = block(i, target)

                @pl.when(first)
                def _(copy_from=copy_from, here=here):
                    copy_from(here).start()

                @pl.when(passing)
                def _(copy_from=copy_from, buf=buf, i=i, target=target):
                    copy_from(buf).wait_recv()
                    add_own(i, target, buf)
                    copy_from(buf).start()

                pl.when(ends)(copy_from(buf).wait_recv)
                waits.append((jnp.logical_or(first, passing), copy_from(buf)))
        if s == 0:
            small.round_two()
        if s == 1:
            small.round_three()
    swaps = []
    for i in range(3):
        mine = pl.ds(pl.multiple_of(p * inner, 128), inner)

        def own(j, _, i=i):
            total[j] = parts[i][z * GROUP + j].astype(F32)
            return 0

        lax.fori_loop(0, GROUP, own, 0)

        @pl.when(z > 0)
        def _(i=i):
            def add(j, _):
                total[j] = total[j] + up_buf[groups - 1 - z, i, j].astype(F32)
                return 0

            lax.fori_loop(0, GROUP, add, 0)

        @pl.when(z < groups - 1)
        def _(i=i):
            def add(j, _):
                total[j] = total[j] + down_buf[z, i, j].astype(F32)
                return 0

            lax.fori_loop(0, GROUP, add, 0)

        def store(j, _, i=i):
            final[i, j] = total[j].astype(BF16)
            return 0

        lax.fori_loop(0, GROUP, store, 0)
        outs[i][:, mine] = final[i, p]
        for k in (1, 2, 3):
            swaps.append(links.copy(final.at[i, lax.bitwise_xor(p, jnp.int32(k))], outs[i].at[:, mine], links.at(k, 0)))
            swaps[-1].start()
    for copy in swaps:
        copy.wait()
    small.finish()
    for sent, copy in waits:
        pl.when(sent)(copy.wait_send)


def next_layer_kernel(
    inner_all, part, squares, resid, gain, normed_out, resid_out, mixed_out, inv_out,
    sib, total, peer, slots, sends, recvs,
):
    links = Links(sends, recvs)
    scatter = Scatter(links, part, 0, sib, total, peer)
    small = SmallSum(links, squares, slots)
    gather = Gather(links, normed_out, EDGE)
    edge = EdgeForward(links, gather)
    links.start_barrier(plane=True, edge=1)
    scatter.start()
    small.start()
    scatter.reduce()
    inv = lax.rsqrt(small.total() * (1.0 / inner_all) + EPS)
    inv_out[...] = inv
    column = inv.T[:, 0:1]
    for start, size in row_chunks():
        at = slice(start, start + size)
        mixed = scatter.own(start, size)
        mixed_out[at] = mixed
        fresh = resid[at] + column[at] * mixed
        resid_out[at] = fresh
        normed_out[gather.own(start, size), :] = (fresh * rms_of(fresh) * gain[...]).astype(BF16)
    gather.start()
    edge.start()
    gather.pass_on()
    scatter.finish()
    small.finish()
    gather.finish()
    edge.finish()


def turn_kernel(
    inner_all, part, squares, resid, cot, block_out, scalars_out,
    sib, total, peer, slots, sends, recvs,
):
    links = Links(sends, recvs)
    scatter = Scatter(links, part, 0, sib, total, peer)
    small = SmallSum(links, squares, slots)
    spread = SmallGather(links, scalars_out)
    rows = pl.ds(pl.multiple_of(links.c * HALF, HALF), HALF)
    share = links.copy(block_out.at[rows, :], block_out.at[rows, :], links.at(0, 1))
    links.start_barrier(plane=True)
    scatter.start()
    small.start()
    scatter.reduce()
    inv = lax.rsqrt(small.total() * (1.0 / inner_all) + EPS)
    column = inv.T[:, 0:1]
    dots = []
    for start, size in row_chunks():
        at = slice(start, start + size)
        mixed = scatter.own(start, size)
        dots.append(jnp.sum(cot[at] * mixed, axis=-1, keepdims=True))
        block_out[pl.ds(pl.multiple_of(links.c * HALF + start, EDGE), size), :] = (
            resid[at] + column[at] * mixed
        ).astype(BF16)
    scalars_out[:, spread.lanes] = as_tile([column, jnp.concatenate(dots)])
    spread.start()
    share.start()
    scatter.finish()
    small.finish()
    spread.finish()
    share.wait()


def grad_rows(links, scatter, edge_slots, grad, resid, gain, gain_out, start, size):
    at = slice(start, start + size)
    d_normed = scatter.own(start, size)
    if start + size == HALF:
        extra = edge_slots[0].astype(F32)
        for i in range(1, 2 * GROUP):
            extra = extra + edge_slots[i].astype(F32)
        used = jnp.logical_and(links.last_of_plane(), links.z < links.groups - 1)
        extra = jnp.where(used, extra, 0.0)
        d_normed = d_normed + jnp.concatenate([jnp.zeros((size - EDGE, extra.shape[1]), F32), extra])
    rows = resid[at]
    inv_rms = rms_of(rows)
    gain_sum = jnp.sum(d_normed * rows * inv_rms, axis=0, keepdims=True)
    gain_out[0:1] = gain_sum if start == 0 else gain_out[0:1] + gain_sum
    d_hidden = d_normed * gain[...]
    return (
        grad[at]
        + inv_rms * d_hidden
        - rows * (inv_rms * inv_rms * inv_rms * jnp.mean(d_hidden * rows, axis=-1, keepdims=True))
    )


class EdgeBackward:
    def __init__(self, links, part, slots):
        self.links = links
        first = links.used
        links.used += 2 * GROUP + 1
        me = links.p * 2 + links.c
        self.send = pltpu.make_async_remote_copy(
            src_ref=part.at[0:EDGE, :], dst_ref=slots.at[me], send_sem=links.sends.at[first], recv_sem=links.recvs.at[first + me],
            device_id=(links.z - 1, jnp.int32(GROUP - 1), jnp.int32(1)), device_id_type=MESH,
        )
        self.recvs = [
            pltpu.make_async_remote_copy(
                src_ref=part.at[0:EDGE, :], dst_ref=slots.at[i], send_sem=links.sends.at[first], recv_sem=links.recvs.at[first + i],
                device_id=(links.z, links.p, 1 - links.c), device_id_type=MESH,
            )
            for i in range(2 * GROUP)
        ]
        self.receiving = jnp.logical_and(links.last_of_plane(), links.z < links.groups - 1)

    def start(self):
        pl.when(self.links.z > 0)(self.send.start)

    def receive(self):
        @pl.when(self.receiving)
        def _():
            for copy in self.recvs:
                copy.wait_recv()

    def finish(self):
        pl.when(self.links.z > 0)(self.send.wait_send)


def layer_below_kernel(
    part, grad, resid, gain, mixed, inv, dmix_out, scalars_out, grad_out, gain_out,
    sib, total, peer, edge_slots, sends, recvs,
):
    links = Links(sends, recvs)
    scatter = Scatter(links, part, EDGE, sib, total, peer)
    edge = EdgeBackward(links, part, edge_slots)
    gather = Gather(links, dmix_out, 0)
    spread = SmallGather(links, scalars_out)
    edge_slots[...] = jnp.zeros_like(edge_slots)
    links.start_barrier(plane=True, edge=-1)
    edge.start()
    scatter.start()
    scatter.reduce()
    edge.receive()
    gain_out[...] = jnp.zeros_like(gain_out)
    dots = []
    for start, size in row_chunks():
        at = slice(start, start + size)
        fresh = grad_rows(links, scatter, edge_slots, grad, resid, gain, gain_out, start, size)
        grad_out[at] = fresh
        low = fresh.astype(BF16)
        dmix_out[gather.own(start, size), :] = low
        dots.append(jnp.sum(low.astype(F32) * mixed[at], axis=-1, keepdims=True))
    scalars_out[:, spread.lanes] = as_tile([inv[...].T[:, 0:1], jnp.concatenate(dots)])
    gather.start()
    spread.start()
    gather.pass_on()
    scatter.finish()
    edge.finish()
    gather.finish()
    spread.finish()


def last_grad_kernel(part, grad, resid, gain, out, gain_out, sib, total, peer, edge_slots, sends, recvs):
    links = Links(sends, recvs)
    scatter = Scatter(links, part, EDGE, sib, total, peer)
    edge = EdgeBackward(links, part, edge_slots)
    rows = pl.ds(pl.multiple_of(links.c * HALF, HALF), HALF)
    share = links.copy(out.at[rows, :], out.at[rows, :], links.at(0, 1))
    edge_slots[...] = jnp.zeros_like(edge_slots)
    links.start_barrier(plane=True, edge=-1)
    edge.start()
    scatter.start()
    scatter.reduce()
    edge.receive()
    gain_out[...] = jnp.zeros_like(gain_out)
    for start, size in row_chunks():
        fresh = grad_rows(links, scatter, edge_slots, grad, resid, gain, gain_out, start, size)
        out[pl.ds(pl.multiple_of(links.c * HALF + start, EDGE), size), :] = fresh.astype(BF16)
    share.start()
    scatter.finish()
    edge.finish()
    share.wait()


def call(body, outs, *args, scratch=(), collective=None, copies=0):
    vmem = pl.BlockSpec(memory_space=pltpu.VMEM)
    scratch = [pltpu.VMEM(shape, kind) for shape, kind in scratch]
    if collective is not None:
        scratch += [pltpu.SemaphoreType.DMA((copies,)), pltpu.SemaphoreType.DMA((copies,))]
    return pl.pallas_call(
        body,
        out_shape=tuple(jax.ShapeDtypeStruct(shape, kind) for shape, kind in outs),
        in_specs=[vmem] * len(args),
        out_specs=tuple([vmem] * len(outs)),
        scratch_shapes=scratch,
        compiler_params=pltpu.CompilerParams(
            vmem_limit_bytes=VMEM_BYTES, collective_id=collective, has_side_effects=collective is not None
        ),
    )(*args)


def on_device(resid_in, cotangent, norm_gain, w_zx, w_dt, w_bc, conv_x, conv_bc, head_params, gated_gain, w_out):
    layers, model = norm_gain.shape
    groups = lax.axis_size("z")
    level, place, core = lax.axis_index("z"), lax.axis_index("p"), lax.axis_index("head")
    shard = w_dt.shape[1]
    inner_core = conv_x.shape[2]
    inner = inner_core // GROUP
    heads_core = head_params.shape[2]
    heads = heads_core // GROUP
    inner_all = inner_core * lax.axis_size("head")
    length = resid_in.shape[1]
    tokens = GROUP * length
    spans = tokens // SPAN
    sources = groups * GROUP
    dt_rows = -(-shard * heads_core // STATE)
    bd_rows = -(-(shard + dt_rows) // EDGE) * EDGE

    def my_part(array, size):
        return lax.dynamic_slice_in_dim(array, place * size, size, array.ndim - 1)

    row_all, bc_all, head_all = [], [], []
    conv_mine = my_part(conv_x, inner).astype(F32)
    gain_mine = my_part(gated_gain, inner).astype(F32)
    head_mine = my_part(head_params, heads)
    gains = [norm_gain[layer].astype(F32)[None] for layer in range(layers)]
    for layer in range(layers):
        skip = jnp.repeat(head_mine[layer, 2], HEADDIM)
        row_all.append(
            jnp.concatenate([conv_mine[layer], gain_mine[layer][None], skip[None], jnp.zeros((1, inner), F32)])
        )
        bc_all.append(jnp.pad(conv_bc[layer].astype(F32), ((0, 3), (0, 0))))
        head_all.append(jnp.pad(head_mine[layer], ((0, 5), (0, 128 - heads))))

    def shards_of(layer):
        flat = w_dt[layer].reshape(-1)
        flat = jnp.pad(flat, (0, (bd_rows - shard) * STATE - flat.shape[0])).reshape(bd_rows - shard, STATE)
        half = lax.dynamic_slice_in_dim(w_bc[layer], core * STATE, STATE, 1)
        return w_zx[layer, 1], w_zx[layer, 0], w_out[layer].T, jnp.concatenate([half, flat])

    def weights_of(wx, wz, wo, wbd):
        wbc = jnp.concatenate([wbd[0, :, :shard], wbd[1, :, :shard]], axis=-1).reshape(model, 2 * STATE)
        own = lax.dynamic_index_in_dim(wbd, core, 0, False)[:, shard:].reshape(sources, -1)
        wdt = own[:, : shard * heads_core].reshape(model, heads_core)
        wdt = jnp.pad(my_part(wdt, heads), ((0, 0), (0, 128 - heads)))
        return wx.reshape(model, inner), wz.reshape(model, inner), wo.reshape(model, inner), wbc, wdt

    def pass_plane(pieces):
        own = jax.tree.map(lambda a: lax.dynamic_index_in_dim(a, place, 0), pieces)
        out = jax.tree.map(lambda a, o: lax.dynamic_update_slice_in_dim(jnp.zeros_like(a), o, place, 0), pieces, own)
        for k in range(1, GROUP):
            there = lax.bitwise_xor(place, jnp.int32(k))
            sent = jax.tree.map(lambda a: lax.dynamic_index_in_dim(a, there, 0), pieces)
            got = jax.tree.map(lambda a: lax.ppermute(a, "p", [(i, i ^ k) for i in range(GROUP)]), sent)
            out = jax.tree.map(lambda o, a: lax.dynamic_update_slice_in_dim(o, a, there, 0), out, got)
        return out

    def pass_groups(pieces):
        out = jax.tree.map(
            lambda a: lax.dynamic_update_slice_in_dim(jnp.zeros((groups, *a.shape), a.dtype), a[None], level, 0), pieces
        )
        for k in range(1, groups):
            got = jax.tree.map(lambda a: lax.ppermute(a, "z", [(i, (i + k) % groups) for i in range(groups)]), pieces)
            source = lax.rem(level + groups - k, groups)
            out = jax.tree.map(lambda o, a: lax.dynamic_update_slice_in_dim(o, a[None], source, 0), out, got)
        return out

    def later_weights(layer):
        wx, wz, wo, wbd = shards_of(layer)
        wide = [jnp.swapaxes(w.reshape(shard, GROUP, inner), 0, 1) for w in (wx, wz, wo)]
        pieces = pass_plane(wide + [jnp.broadcast_to(wbd, (GROUP, *wbd.shape))])
        wx, wz, wo, wbd = [a.reshape(sources, *a.shape[2:]) for a in pass_groups(pieces)]
        other = lax.ppermute(wbd, "head", [(0, 1), (1, 0)])
        wbd = jnp.where(core == 0, jnp.stack([wbd, other]), jnp.stack([other, wbd]))
        return weights_of(wx, wz, wo, wbd)

    half_scratch = [
        ((GROUP, HALF, model), BF16),
        ((GROUP - 1, HALF, model), BF16),
        ((GROUP - 1, HALF, model), BF16),
    ]
    slots = ((2 * GROUP - 1, 8, HALF), F32)
    edges = ((2 * GROUP, EDGE, model), BF16)
    own_rows = ((HALF, model), F32)

    first_shards = shards_of(0)
    normed, last_dmix, wx, wz, wo, wbd, resid, grad = call(
        begin_kernel,
        [
            ((tokens + EDGE, model), BF16),
            ((tokens, model), BF16),
            ((sources, shard, inner), BF16),
            ((sources, shard, inner), BF16),
            ((sources, shard, inner), BF16),
            ((2, sources, bd_rows, STATE), BF16),
            own_rows,
            own_rows,
        ],
        resid_in[0], cotangent[0], gains[0], *first_shards,
        collective=0, copies=44 + 8 * (groups - 1),
    )
    weights = [weights_of(wx, wz, wo, wbd)] + [later_weights(layer) for layer in range(1, layers)]

    def exchanged(state, decay, backward):
        return call(
            functools.partial(exchange_kernel, backward),
            [((groups, STATE, inner), BF16), ((groups, 8, inner), F32)],
            state, decay,
            collective=2 if backward else 1, copies=2 * groups,
        )

    saved = []
    for layer in range(layers):
        wx, wz, wo, wbc, wdt = weights[layer]
        rowp, bcp, headp = row_all[layer], bc_all[layer], head_all[layer]
        z, xin, bcin, x, bc, dtraw, dt, s, y_local, local, decay, sums, decay_all = call(
            forward_local,
            [
                ((tokens, inner), BF16),
                ((tokens + EDGE, inner), BF16),
                ((tokens + EDGE, 2 * STATE), BF16),
                ((tokens, inner), BF16),
                ((tokens, 2 * STATE), BF16),
                ((tokens, 128), BF16),
                ((tokens, 128), F32),
                ((tokens, 128), F32),
                ((tokens, inner), F32),
                ((spans, STATE, inner), F32),
                ((spans, 8, inner), F32),
                ((STATE, inner), BF16),
                ((8, inner), F32),
            ],
            normed, wx, wz, wbc, wdt, rowp, bcp, headp,
            scratch=[((tokens + EDGE, inner + 2 * STATE), F32)],
        )
        all_sums, all_decays = exchanged(sums, decay_all, False)
        y, states, part, squares = call(
            functools.partial(forward_carried, groups),
            [
                ((tokens, inner), F32),
                ((spans, STATE, inner), F32),
                ((tokens, model), BF16),
                ((8, tokens), F32),
            ],
            all_sums, all_decays, local, decay, y_local, x, bc, z, s, wo, rowp,
        )
        kept = (resid, normed, z, xin, bcin, x, bc, dtraw, dt, s, y, states, decay)
        if layer < layers - 1:
            normed, resid, mixed, inv = call(
                functools.partial(next_layer_kernel, inner_all),
                [((tokens + EDGE, model), BF16), own_rows, own_rows, ((8, HALF), F32)],
                part, squares, resid, gains[layer + 1],
                scratch=half_scratch + [slots], collective=3, copies=40,
            )
            saved.append((*kept, mixed, inv))
        else:
            block_out, token_scalars = call(
                functools.partial(turn_kernel, inner_all),
                [((length, model), BF16), ((8, tokens), F32)],
                part, squares, resid, grad,
                scratch=half_scratch + [slots], collective=4, copies=40,
            )
            saved.append((*kept, None, None))

    d_mix = last_dmix
    big, kinds, gain_rows = [None] * layers, [None] * layers, [None] * layers
    for layer in reversed(range(layers)):
        wx, wz, wo, wbc, wdt = weights[layer]
        rowp, bcp, headp = row_all[layer], bc_all[layer], head_all[layer]
        resid, normed, z, xin, bcin, x, bc, dtraw, dt, s, y, states, decay, _, _ = saved[layer]
        dz, dy, gwo, prior, sums, decay_all, gate_small = call(
            functools.partial(backward_gate, inner_all),
            [
                ((tokens, inner), BF16),
                ((tokens, inner), BF16),
                ((model, inner), BF16),
                ((spans, STATE, inner), F32),
                ((STATE, inner), BF16),
                ((8, inner), F32),
                ((8, inner), F32),
            ],
            d_mix, wo, y, z, x, bc, s, decay, token_scalars, rowp,
            scratch=[((tokens, inner), BF16)],
        )
        all_sums, all_decays = exchanged(sums, decay_all, True)
        dcat, row_small, bc_small, head_small = call(
            functools.partial(backward_ssd, groups),
            [
                ((tokens + EDGE, inner + 2 * STATE + 128), BF16),
                ((8, inner), F32),
                ((8, 2 * STATE), F32),
                ((8, 128), F32),
            ],
            all_sums, all_decays, prior, decay, states, dy, x, bc, s, dt, dtraw, xin, bcin, rowp, bcp, headp,
            scratch=[
                ((tokens + 2 * EDGE, inner + 2 * STATE), F32),
                ((spans, STATE, inner), F32),
            ],
        )
        part, gx, gz, gbc, gdt = call(
            backward_project,
            [
                ((tokens + EDGE, model), BF16),
                ((model, inner), BF16),
                ((model, inner), BF16),
                ((model, 2 * STATE), BF16),
                ((EDGE, model), BF16),
            ],
            dcat, dz, normed, wx, wz, wbc, wdt,
        )
        if layer > 0:
            d_mix, token_scalars, grad, gain_rows[layer] = call(
                layer_below_kernel,
                [((tokens, model), BF16), ((8, tokens), F32), own_rows, ((8, model), F32)],
                part, grad, resid, gains[layer], *saved[layer - 1][-2:],
                scratch=half_scratch + [edges], collective=5, copies=60,
            )
        else:
            grad_input, gain_rows[layer] = call(
                last_grad_kernel,
                [((length, model), BF16), ((8, model), F32)],
                part, grad, resid, gains[layer],
                scratch=half_scratch + [edges], collective=6, copies=60,
            )
        big[layer] = [g.reshape(sources, shard, inner) for g in (gx, gz, gwo)]
        tall = jnp.pad(head_small[:2], ((0, 0), (0, inner - 128)))
        wide = jnp.concatenate([row_small[: CONV + 1], gate_small[:2], tall])
        kinds[layer] = (gbc, gdt, jnp.pad(wide, ((0, 7), (0, 0))), bc_small[: CONV + 1])

    def later_grads(layer):
        sent = [g.reshape(groups, GROUP, shard, inner) for g in big[layer]]
        total = [lax.dynamic_index_in_dim(g, level, 0, False).astype(F32) for g in sent]
        for k in range(1, groups):
            there = lax.rem(level + k, groups)
            route = [(i, (i + k) % groups) for i in range(groups)]
            for i in range(3):
                got = lax.ppermute(lax.dynamic_index_in_dim(sent[i], there, 0, False), "z", route)
                total[i] = total[i] + got.astype(F32)
        total = pass_plane([t.astype(BF16) for t in total])
        return [jnp.swapaxes(t, 0, 1).reshape(shard, inner_core) for t in total]

    later = {layer: later_grads(layer) for layer in range(1, layers)}
    vec = jnp.concatenate(
        [gain_rows[layer][0] for layer in range(layers)] + [kinds[layer][3].reshape(-1) for layer in range(layers)]
    )
    vec = jnp.pad(vec, (0, 2 * GROUP * 1024 - vec.shape[0])).reshape(2 * GROUP, 8, 128)
    bc_grads = jnp.stack([kinds[layer][0].reshape(groups, GROUP, shard, 2 * STATE) for layer in range(layers)])
    dt_grads = jnp.concatenate([kinds[layer][1] for layer in range(layers)])
    dt_grads = jnp.swapaxes(dt_grads.reshape(layers * EDGE, groups, GROUP * shard), 0, 1)
    wide = jnp.concatenate([kinds[layer][2] for layer in range(layers)])
    wide_shape, dt_shape, far = wide.shape, dt_grads.shape[1:], groups - 1
    gx, gz, go, g_bc, vec, g_dt, wide = call(
        grads_kernel,
        [
            ((shard, inner_core), BF16),
            ((shard, inner_core), BF16),
            ((shard, inner_core), BF16),
            ((layers, shard, 2 * STATE), BF16),
            (vec.shape, F32),
            ((GROUP, *dt_shape), BF16),
            ((GROUP, *wide_shape), F32),
        ],
        *big[0], bc_grads, vec, dt_grads, wide,
        scratch=[
            ((far, 3, GROUP, shard, inner), BF16),
            ((far, 3, GROUP, shard, inner), BF16),
            ((GROUP, shard, inner), F32),
            ((3, GROUP, shard, inner), BF16),
            ((layers, 2 * GROUP - 1, groups, shard, STATE), BF16),
            ((layers, groups, shard, STATE), BF16),
            ((layers, far, shard, STATE), BF16),
            ((2 * GROUP, 8, 128), F32),
            ((far, 8, 128), F32),
            ((far, *dt_shape), BF16),
            ((far, *wide_shape), F32),
        ],
        collective=7, copies=60 + 12 * groups,
    )
    later[0] = [gx, gz, go]
    vec = vec.reshape(-1)
    grad_gain = vec[: layers * model].reshape(layers, model)
    grad_conv_bc = vec[layers * model :][: layers * (CONV + 1) * 2 * STATE].reshape(layers, CONV + 1, 2 * STATE)
    wide = wide.reshape(GROUP, layers, 16, inner)
    whole = jnp.moveaxis(wide, 0, 2).reshape(layers, 16, inner_core)
    skip_grad = jnp.sum(whole[:, CONV + 2].reshape(layers, heads_core, HEADDIM), axis=-1)
    tall = jnp.moveaxis(wide[:, :, CONV + 3 : CONV + 5, :heads], 0, 2).reshape(layers, 2, heads_core)
    grad_heads = jnp.concatenate([tall, skip_grad[:, None]], axis=1)
    g_dt = lax.dynamic_slice_in_dim(g_dt.reshape(GROUP, layers, EDGE, GROUP, shard), place, 1, 3)[:, :, :heads, 0]
    grad_dt = jnp.transpose(g_dt, (1, 3, 0, 2)).reshape(layers, shard, heads_core)
    low = lambda a: a.astype(BF16)
    return (
        block_out[None],
        grad_input[None],
        low(grad_gain),
        jnp.stack([jnp.stack([later[layer][1], later[layer][0]]) for layer in range(layers)]),
        grad_dt,
        g_bc,
        low(whole[:, : CONV + 1]),
        low(grad_conv_bc),
        low(grad_heads),
        low(whole[:, CONV + 1]),
        jnp.stack([later[layer][2].T for layer in range(layers)]),
    )


def solution(mesh):
    seq, head = mesh.shape["seq"], mesh.shape["head"]
    split = Mesh(mesh.devices.reshape(seq // GROUP, GROUP, head), ("z", "p", "head"))
    seq_axes = ("z", "p")
    specs = (
        P(None, seq_axes, None),
        P(None, seq_axes, None),
        P(),
        P(None, None, seq_axes, "head"),
        P(None, seq_axes, "head"),
        P(None, seq_axes, None),
        P(None, None, "head"),
        P(),
        P(None, None, "head"),
        P(None, "head"),
        P(None, "head", seq_axes),
    )
    return jax.shard_map(on_device, mesh=split, in_specs=specs, out_specs=specs, check_vma=False)
```

```python
import functools

import jax
import jax.numpy as jnp
from jax import lax
from jax.experimental import pallas as pl
from jax.experimental.pallas import tpu as pltpu
from jax.sharding import Mesh, PartitionSpec as P

HEADDIM = 64
STATE = 128
CONV = 4
SPAN = 256
GROUP = 4
EDGE = 16
EPS = 1e-05
HIGH = lax.Precision.HIGHEST
F32, BF16 = jnp.float32, jnp.bfloat16
NN = (((1,), (0,)), ((), ()))
NT = (((1,), (1,)), ((), ()))
TN = (((0,), (0,)), ((), ()))
VMEM_BYTES = 58 << 20


def dot(a, b, dims=NN):
    return lax.dot_general(a, b, dims, preferred_element_type=F32)


def dot_exact(a, b, dims=NN):
    return lax.dot_general(a, b, dims, precision=HIGH, preferred_element_type=F32)


def dot_split(a, b, dims=NN):
    high = a.astype(BF16)
    rest = (a - high.astype(F32)).astype(BF16)
    return dot(high, b, dims) + dot(rest, b, dims)


def sigmoid(v):
    return 1.0 / (1.0 + jnp.exp(-v))


def softplus(v):
    return jnp.maximum(v, 0.0) + jnp.log1p(jnp.exp(-jnp.abs(v)))


def silu_slope(v):
    sig = sigmoid(v)
    return sig * (1.0 + v * (1.0 - sig))


def iota(shape, dim):
    return lax.broadcasted_iota(jnp.int32, shape, dim)


def head_spread(inner):
    return (iota((128, inner), 0) == lax.shift_right_logical(iota((128, inner), 1), 6)).astype(BF16)


def triangle(lower):
    rows, cols = iota((SPAN, SPAN), 0), iota((SPAN, SPAN), 1)
    return ((cols <= rows) if lower else (cols >= rows)).astype(F32)


def half_masks():
    lane = iota((SPAN, 128), 1)
    return (lane < HEADDIM).astype(BF16), (lane >= HEADDIM).astype(BF16)


def conv_taps(window, taps):
    total = jnp.broadcast_to(taps[CONV : CONV + 1], (SPAN, window.shape[1]))
    for j in range(CONV):
        total = total + taps[j : j + 1] * window[EDGE - 3 + j : EDGE - 3 + j + SPAN]
    return total


def head_pick(place, heads):
    row, col = iota((128, 128), 0), iota((128, 128), 1)
    return jnp.logical_and(row == place * heads + col, col < heads).astype(BF16)


def project_and_convolve(
    place, normed, wx, wz, wbc, wdt, rowp, bcp, headp,
    z_out, xin_out, bcin_out, x_out, bc_out, dtraw_out, dt_out, s_out, decay_out,
    ext, local,
):
    inner = x_out.shape[1]
    spans = x_out.shape[0] // SPAN

    def bc_of(rows):
        return jnp.concatenate([dot(rows, wbc[0]), dot(rows, wbc[1])], axis=1).astype(BF16)

    edge = normed[0:EDGE]
    edge_x = dot(edge, wx[...]).astype(BF16)
    edge_bc = bc_of(edge)
    xin_out[0:EDGE] = edge_x
    bcin_out[0:EDGE] = edge_bc
    ext[0:EDGE, 0:inner] = edge_x.astype(F32)
    ext[0:EDGE, inner:] = edge_bc.astype(F32)
    spread = head_spread(inner)
    pick = head_pick(place, inner // HEADDIM)
    low_tri = triangle(True)
    rate = -jnp.exp(headp[0:1])
    bias = headp[1:2]

    def block(q, carry):
        state_sum, decay_all = carry
        at = pl.multiple_of(q * SPAN, SPAN)
        tok = pl.ds(at, SPAN)
        after = pl.ds(pl.multiple_of(at + EDGE, EDGE), SPAN)
        rows = normed[after, :]
        z_out[tok, :] = dot(rows, wz[...]).astype(BF16)
        xin = dot(rows, wx[...]).astype(BF16)
        bcin = bc_of(rows)
        dtraw = dot(dot(rows, wdt[...]).astype(BF16), pick).astype(BF16)
        xin_out[after, :] = xin
        bcin_out[after, :] = bcin
        dtraw_out[tok, :] = dtraw
        ext[after, 0:inner] = xin.astype(F32)
        ext[after, inner:] = bcin.astype(F32)
        window = pl.ds(at, SPAN + EDGE)
        pre_x = conv_taps(ext[window, 0:inner], rowp)
        x = (pre_x * sigmoid(pre_x)).astype(BF16)
        x_out[tok, :] = x
        pre_bc = conv_taps(ext[window, inner:], bcp)
        bc = (pre_bc * sigmoid(pre_bc)).astype(BF16)
        bc_out[tok, :] = bc
        dt = softplus(dtraw.astype(F32) + bias)
        s = dot_exact(low_tri, dt * rate)
        dt_out[tok, :] = dt
        s_out[tok, :] = s
        to_end = jnp.exp(s[SPAN - 1 : SPAN] - s) * dt
        weighted = (x.astype(F32) * dot_split(to_end, spread)).astype(BF16)
        fresh = dot(bc[:, :STATE], weighted, TN)
        decay = dot_split(jnp.exp(s[SPAN - 8 : SPAN]), spread)[7:8]
        local[q] = fresh
        decay_out[q] = jnp.broadcast_to(decay, (8, inner))
        return state_sum * decay + fresh, decay_all * decay

    return lax.fori_loop(0, spans, block, (jnp.zeros((STATE, inner), F32), jnp.ones((1, inner), F32)))


def mix_within_spans(x_in, bc_in, s_in, dt_in, y_out):
    inner = x_in.shape[1]

    def block(q, _):
        tok = pl.ds(pl.multiple_of(q * SPAN, SPAN), SPAN)
        x, bc, s = x_in[tok, :], bc_in[tok, :], s_in[tok, :]
        s_row, dt_row = s.T, dt_in[tok, :].T
        cb = dot(bc[:, STATE:], bc[:, :STATE], NT)
        causal = iota((SPAN, SPAN), 1) <= iota((SPAN, SPAN), 0)
        masks = half_masks()
        for pair in range(inner // 128):
            lanes = slice(pair * 128, pair * 128 + 128)
            x_pair = x[:, lanes]
            total = None
            for e in range(2):
                h = pair * 2 + e
                gap = jnp.where(causal, s[:, h : h + 1] - s_row[h : h + 1, :], -1e30)
                scores = (cb * (jnp.exp(gap) * dt_row[h : h + 1, :])).astype(BF16)
                term = dot(scores, x_pair * masks[e])
                total = term if total is None else total + term
            y_out[tok, lanes] = total
        return 0

    lax.fori_loop(0, x_in.shape[0] // SPAN, block, 0)


def entering_state(place, count, sums, decays, backward):
    inner = sums.shape[2]
    state = jnp.zeros((STATE, inner), F32)
    for turn in range(count):
        other = count - 1 - turn if backward else turn
        ahead = (place < other) if backward else (other < place)
        state = jnp.where(ahead, decays[other, 0:1] * state + sums[other].astype(F32), state)
    return state


def mix_out(state, local, decay, x, bc, z, s, wo, rowp, y_out, states_out, part_out, sq_out):
    inner = x.shape[1]
    spread = head_spread(inner)
    gain, skip = rowp[5:6], rowp[6:7]
    ones = jnp.ones((8, inner), F32)

    def block(q, state):
        tok = pl.ds(pl.multiple_of(q * SPAN, SPAN), SPAN)
        states_out[q] = state
        c = bc[tok, STATE:]
        carried = dot_split(jnp.exp(s[tok, :]), spread) * dot(c, state.astype(BF16))
        y = y_out[tok, :] + carried + skip * x[tok, :].astype(F32)
        y_out[tok, :] = y
        zf = z[tok, :].astype(F32)
        gated = y * (zf * sigmoid(zf))
        sq_out[:, tok] = dot_exact(ones, gated * gated, NT)
        part_out[tok, :] = dot((gated * gain).astype(BF16), wo[...], NT).astype(BF16)
        return decay[q, 0:1] * state + local[q]

    lax.fori_loop(0, x.shape[0] // SPAN, block, state)


def back_through_gate(
    inner_all, dmix, wo, y_in, z, x, bc, s, decay, token_scalars, rowp, dz_out, small_out, dy_out, prior, normed_out
):
    inner = x.shape[1]
    spans = x.shape[0] // SPAN
    spread = head_spread(inner)
    gain = rowp[5:6]

    def block(i, carry):
        grad_sum, gain_sum, skip_sum = carry
        q = spans - 1 - i
        tok = pl.ds(pl.multiple_of(q * SPAN, SPAN), SPAN)
        columns = token_scalars[:, tok].T
        inv, total_dot = columns[:, 0:1], columns[:, 1:2]
        zf = z[tok, :].astype(F32)
        sig = sigmoid(zf)
        act = zf * sig
        y = y_in[tok, :]
        gated = y * act
        d_no = dot(dmix[tok, :], wo[...])
        scaled = gated * inv
        normed_out[tok, :] = (scaled * gain).astype(BF16)
        gain_sum = gain_sum + jnp.sum(d_no * scaled, axis=0, keepdims=True)
        d_gated = inv * (d_no * gain) - gated * (inv * inv * inv * total_dot * (1.0 / inner_all))
        dz_out[tok, :] = (d_gated * y * (sig * (1.0 + zf * (1.0 - sig)))).astype(BF16)
        dy = d_gated * act
        xf = x[tok, :].astype(F32)
        skip_sum = skip_sum + jnp.sum(dy * xf, axis=0, keepdims=True)
        dy_low = dy.astype(BF16)
        dy_out[tok, :] = dy_low
        scaled_dy = (dy_low.astype(F32) * dot_split(jnp.exp(s[tok, :]), spread)).astype(BF16)
        fresh = dot(bc[tok, STATE:], scaled_dy, TN)
        prior[q] = fresh
        return fresh + decay[q, 0:1] * grad_sum, gain_sum, skip_sum

    zero = jnp.zeros((1, inner), F32)
    grad_sum, gain_sum, skip_sum = lax.fori_loop(
        0, spans, block, (jnp.zeros((STATE, inner), F32), zero, zero)
    )
    decay_all = decay[0, 0:1]
    for q in range(1, spans):
        decay_all = decay_all * decay[q, 0:1]
    small_out[0:1] = gain_sum
    small_out[1:2] = skip_sum
    small_out[2:8] = jnp.zeros((6, inner), F32)
    return grad_sum, decay_all


def out_gradient(dmix, normed_out, gwo_out):
    def rows_of(i, _):
        rows = pl.ds(pl.multiple_of(i * SPAN, SPAN), SPAN)
        gwo_out[rows, :] = dot(dmix[:, rows], normed_out[...], TN).astype(BF16)
        return 0

    lax.fori_loop(0, dmix.shape[1] // SPAN, rows_of, 0)


def back_within_spans(dy_in, x_in, bc_in, s_in, dt_in, dpre, flow_out, sum_out):
    inner = x_in.shape[1]

    def block(q, _):
        at = pl.multiple_of(q * SPAN, SPAN)
        tok = pl.ds(at, SPAN)
        after = pl.ds(pl.multiple_of(at + EDGE, EDGE), SPAN)
        x_low, dy = x_in[tok, :], dy_in[tok, :]
        b, c = bc_in[tok, :STATE], bc_in[tok, STATE:]
        s, dt = s_in[tok, :], dt_in[tok, :]
        s_row = s.T
        cb = dot(b, c, NT)
        seen = iota((SPAN, SPAN), 0) <= iota((SPAN, SPAN), 1)
        masks = half_masks()
        d_cb = jnp.zeros((SPAN, SPAN), F32)
        lane = iota((SPAN, 128), 1)
        row_id = iota((128, SPAN), 0)
        sum_k = jnp.zeros((128, SPAN), F32)
        sum_t = jnp.zeros((SPAN, 128), F32)
        for pair in range(inner // 128):
            lanes = slice(pair * 128, pair * 128 + 128)
            x_pair, dy_pair = x_low[:, lanes], dy[:, lanes]
            total = None
            for e in range(2):
                h = pair * 2 + e
                d_scores = dot(x_pair * masks[e], dy_pair, NT)
                fade = jnp.exp(jnp.where(seen, s_row[h : h + 1, :] - s[:, h : h + 1], -1e30))
                dt_h = dt[:, h : h + 1]
                fade_cb = cb * fade
                term = dot((fade_cb * dt_h).astype(BF16), dy_pair * masks[e])
                total = term if total is None else total + term
                d_cb = d_cb + d_scores * (fade * dt_h)
                flow = d_scores * fade_cb
                sum_t = jnp.where(lane == h, jnp.sum(flow, axis=1, keepdims=True), sum_t)
                sum_k = jnp.where(row_id == h, jnp.sum(flow * dt_h, axis=0, keepdims=True), sum_k)
            dpre[after, lanes] = total
        d_cb_low = d_cb.astype(BF16)
        dpre[after, inner : inner + STATE] = dot(d_cb_low, c)
        dpre[after, inner + STATE :] = dot(d_cb_low, b, TN)
        flow_out[tok, :] = sum_k.T - sum_t * dt
        sum_out[tok, :] = sum_t
        return 0

    lax.fori_loop(0, x_in.shape[0] // SPAN, block, 0)


def back_through_states(
    grad, prior, decay, states, dy_in, x, bc, s_in, dt_in, dtraw, xin, bcin, rowp, bcp, headp, flow_in, sum_in,
    dcat_out, row_out, bcrow_out, head_out,
    dpre, dend,
):
    inner = x.shape[1]
    spans = x.shape[0] // SPAN
    spread = head_spread(inner)
    up_tri = triangle(False)
    skip = rowp[6:7]
    rate = -jnp.exp(headp[0:1])
    bias = headp[1:2]
    width = inner + 2 * STATE

    def chain(i, grad):
        q = spans - 1 - i
        dend[q] = grad
        return prior[q] + decay[q, 0:1] * grad

    lax.fori_loop(0, spans, chain, grad)
    dpre[0:EDGE] = jnp.zeros((EDGE, width), F32)
    dpre[EDGE + spans * SPAN :] = jnp.zeros((EDGE, width), F32)
    row_out[...] = jnp.zeros_like(row_out)
    bcrow_out[...] = jnp.zeros_like(bcrow_out)
    head_out[...] = jnp.zeros_like(head_out)
    dcat_out[0:EDGE, width:] = jnp.zeros((EDGE, 128), BF16)

    def block(q, _):
        at = pl.multiple_of(q * SPAN, SPAN)
        tok = pl.ds(at, SPAN)
        after = pl.ds(pl.multiple_of(at + EDGE, EDGE), SPAN)
        window = pl.ds(at, SPAN + EDGE)
        x_low, dy = x[tok, :], dy_in[tok, :]
        xf, dyf = x_low.astype(F32), dy.astype(F32)
        b, c = bc[tok, :STATE], bc[tok, STATE:]
        s, dt = s_in[tok, :], dt_in[tok, :]
        exp_s = jnp.exp(s)
        to_end = jnp.exp(s[SPAN - 1 : SPAN] - s)
        w = to_end * dt
        w_all, s_all = dot_split(w, spread), dot_split(exp_s, spread)
        state, grad = states[q], dend[q]
        state_low, grad_low = state.astype(BF16), grad.astype(BF16)
        carried = s_all * dot(c, state_low)
        ds = dot_split(dyf * carried, spread, NT)
        d_c = dot((dyf * s_all).astype(BF16), state_low, NT)
        d_w = dot(b, grad_low)
        d_b = dot((xf * w_all).astype(BF16), grad_low, NT)
        dx = dpre[after, 0:inner] + dyf * skip + d_w * w_all
        dsw = dot_split(d_w * xf, spread, NT)
        end = dsw * w
        ds = ds + flow_in[tok, :] - end
        held = dot_split(jnp.broadcast_to(jnp.sum(grad * state, axis=0, keepdims=True), (8, inner)), spread, NT)[0:1]
        last = jnp.sum(end, axis=0, keepdims=True) + held * exp_s[SPAN - 1 : SPAN]
        ds = ds + jnp.where(iota((SPAN, 128), 0) == SPAN - 1, last, 0.0)
        da = dot_exact(up_tri, ds)
        d_dt = sum_in[tok, :] + dsw * to_end + da * rate
        d_raw = d_dt * sigmoid(dtraw[tok, :].astype(F32) + bias)
        d_raw = jnp.where(iota((SPAN, 128), 1) < inner // HEADDIM, d_raw, 0.0)
        head_out[0:1] += jnp.sum(da * (dt * rate), axis=0, keepdims=True)
        head_out[1:2] += jnp.sum(d_raw, axis=0, keepdims=True)
        dcat_out[after, width:] = d_raw.astype(BF16)

        win_x = xin[window, :].astype(F32)
        d_x = dx * silu_slope(conv_taps(win_x, rowp))
        dpre[after, 0:inner] = d_x
        for j in range(CONV):
            row_out[j : j + 1] += jnp.sum(d_x * win_x[EDGE - 3 + j : EDGE - 3 + j + SPAN], axis=0, keepdims=True)
        row_out[CONV : CONV + 1] += jnp.sum(d_x, axis=0, keepdims=True)
        win_bc = bcin[window, :].astype(F32)
        d_bc = dpre[after, inner:] + jnp.concatenate([d_b, d_c], axis=1)
        d_bc = d_bc * silu_slope(conv_taps(win_bc, bcp))
        dpre[after, inner:] = d_bc
        for j in range(CONV):
            bcrow_out[j : j + 1] += jnp.sum(d_bc * win_bc[EDGE - 3 + j : EDGE - 3 + j + SPAN], axis=0, keepdims=True)
        bcrow_out[CONV : CONV + 1] += jnp.sum(d_bc, axis=0, keepdims=True)
        return 0

    lax.fori_loop(0, spans, block, 0)

    def back(window, taps, rows):
        total = None
        for j in range(CONV):
            term = taps[j : j + 1] * window[CONV - 1 - j : CONV - 1 - j + rows]
            total = term if total is None else total + term
        return total.astype(BF16)

    dcat_out[0:EDGE, 0:inner] = back(dpre[0 : 2 * EDGE, 0:inner], rowp, EDGE)
    dcat_out[0:EDGE, inner:width] = back(dpre[0 : 2 * EDGE, inner:], bcp, EDGE)

    def conv_block(q, _):
        after = pl.ds(pl.multiple_of(q * SPAN + EDGE, EDGE), SPAN)
        window = pl.ds(pl.multiple_of(q * SPAN + EDGE, EDGE), SPAN + EDGE)
        dcat_out[after, 0:inner] = back(dpre[window, 0:inner], rowp, SPAN)
        dcat_out[after, inner:width] = back(dpre[window, inner:], bcp, SPAN)
        return 0

    lax.fori_loop(0, spans, conv_block, 0)


def backward_project(dcat, dz, normed, wx, wz, wbc, wdt, dn_out, gx_out, gz_out, gbc_out, gdt_out):
    inner = dz.shape[1]
    width = inner + 2 * STATE
    spans = dz.shape[0] // SPAN
    d_edge = dcat[0:EDGE]
    pick = head_pick(lax.axis_index("p"), inner // HEADDIM)
    dn_out[0:EDGE] = (
        dot(d_edge[:, 0:inner], wx[...], NT)
        + dot(d_edge[:, inner : inner + STATE], wbc[0], NT)
        + dot(d_edge[:, inner + STATE : width], wbc[1], NT)
    ).astype(BF16)

    def rows_of(q, _):
        at = pl.multiple_of(q * SPAN, SPAN)
        tok = pl.ds(at, SPAN)
        after = pl.ds(pl.multiple_of(at + EDGE, EDGE), SPAN)
        dn_out[after, :] = (
            dot(dz[tok, :], wz[...], NT)
            + dot(dcat[after, 0:inner], wx[...], NT)
            + dot(dcat[after, inner : inner + STATE], wbc[0], NT)
            + dot(dcat[after, inner + STATE : width], wbc[1], NT)
            + dot(dot(dcat[after, width:], pick, NT).astype(BF16), wdt[...], NT)
        ).astype(BF16)
        return 0

    lax.fori_loop(0, spans, rows_of, 0)

    def grads_of(i, _):
        cols = pl.ds(pl.multiple_of(i * SPAN, SPAN), SPAN)
        part = normed[:, cols]
        both = dot(part, dcat[:, 0:width], TN).astype(BF16)
        gx_out[cols, :] = both[:, 0:inner]
        gbc_out[cols, :] = both[:, inner:]
        gdt_out[:, cols] = dot(dcat[:, width:], part, TN)[0:EDGE].astype(BF16)
        gz_out[cols, :] = dot(part[EDGE:], dz[...], TN).astype(BF16)
        return 0

    lax.fori_loop(0, normed.shape[1] // SPAN, grads_of, 0)


HALF = 128
MESH = pl.DeviceIdType.MESH


class Links:
    def __init__(self, sends, recvs):
        self.z, self.p, self.c = lax.axis_index("z"), lax.axis_index("p"), lax.axis_index("head")
        self.groups = lax.axis_size("z")
        self.sends, self.recvs, self.used = sends, recvs, 0

    def copy(self, src, dst, device):
        i = self.used
        self.used += 1
        return pltpu.make_async_remote_copy(
            src_ref=src, dst_ref=dst, send_sem=self.sends.at[i], recv_sem=self.recvs.at[i],
            device_id=device, device_id_type=MESH,
        )

    def local(self, src, dst):
        i = self.used
        self.used += 1
        return pltpu.make_async_copy(src, dst, self.sends.at[i])

    def at(self, k, e):
        return (self.z, lax.bitwise_xor(self.p, jnp.int32(k)), lax.bitwise_xor(self.c, jnp.int32(e)))

    def last_of_plane(self):
        return jnp.logical_and(self.p == GROUP - 1, self.c == 1)

    def greet(self, plane=False, sibling=False, groups=False, edge=0):
        barrier = pltpu.get_barrier_semaphore()
        z, count = self.z, self.groups
        above = z < count - 1

        def signal(device):
            pl.semaphore_signal(barrier, 1, device_id=device, device_id_type=MESH)

        self.expected = jnp.int32(0)
        for k in range(GROUP):
            for e in range(2):
                if (k or e) if plane else (sibling and e and not k):
                    signal(self.at(k, e))
                    self.expected = self.expected + 1
        if groups:
            for k in range(1, count):
                signal((lax.rem(z + k, count), self.p, self.c))
            self.expected = self.expected + (count - 1)
        sending = jnp.logical_and(self.last_of_plane(), above)
        if edge == 1:
            pl.when(z > 0)(lambda: signal((z - 1, jnp.int32(GROUP - 1), jnp.int32(1))))
            self.expected = self.expected + 2 * GROUP * sending.astype(jnp.int32)
        if edge == -1:

            @pl.when(sending)
            def _():
                for p in range(GROUP):
                    for c in range(2):
                        signal((z + 1, jnp.int32(p), jnp.int32(c)))

            self.expected = self.expected + (z > 0).astype(jnp.int32)

    def meet(self):
        pl.semaphore_wait(pltpu.get_barrier_semaphore(), self.expected)

    def start_barrier(self, **who):
        self.greet(**who)
        self.meet()


class Spread:
    def __init__(self, links, own, out):
        rows = own.shape[0]
        there = out.at[pl.ds(pl.multiple_of(links.z * rows, EDGE), rows)]
        self.keep = links.local(own, there)
        self.copies = [
            links.copy(own, there, (lax.rem(links.z + k, links.groups), links.p, links.c)) for k in range(1, links.groups)
        ]

    def start(self):
        self.keep.start()
        for copy in self.copies:
            copy.start()

    def arrive(self):
        self.keep.wait()
        for copy in self.copies:
            copy.wait_recv()

    def finish(self):
        for copy in self.copies:
            copy.wait_send()


class Collect:
    def __init__(self, links, grad, out):
        rows = grad.shape[0] // links.groups
        z, groups = links.z, links.groups

        def block(index):
            return grad.at[pl.ds(pl.multiple_of(index * rows, EDGE), rows)]

        self.keep = links.local(block(z), out.at[0])
        self.copies = []
        for k in range(1, groups):
            to = lax.rem(z + k, groups)
            self.copies.append(links.copy(block(to), out.at[k], (to, links.p, links.c)))

    def start(self):
        self.keep.start()
        for copy in self.copies:
            copy.start()

    def arrive(self):
        self.keep.wait()
        for copy in self.copies:
            copy.wait_recv()

    def finish(self):
        for copy in self.copies:
            copy.wait_send()


class Deliver:
    def __init__(self, links, parts, final, out):
        self.links, self.parts, self.final, self.out = links, parts, final, out
        inner = parts.shape[2]
        self.mine = pl.ds(pl.multiple_of(links.p * inner, 128), inner)
        self.copies = [
            links.copy(final.at[lax.bitwise_xor(links.p, jnp.int32(k))], out.at[:, self.mine], links.at(k, 0))
            for k in (3, 1, 2)
        ]

    def start(self):
        total = self.parts[0].astype(F32)
        for k in range(1, self.parts.shape[0]):
            total = total + self.parts[k].astype(F32)
        shard = self.final.shape[1]
        for j in range(GROUP):
            self.final[j] = total[j * shard : (j + 1) * shard].astype(BF16)
        for copy in self.copies:
            copy.start()
        self.out[:, self.mine] = self.final[self.links.p]

    def finish(self):
        for copy in self.copies:
            copy.wait()


class States:
    def __init__(self, links, backward, state, decay, states, decays):
        z, groups = links.z, links.groups
        self.links, self.refs = links, (state, decay, states, decays)
        self.found = []
        for k in range(1, groups):
            to, source = (z - k, z + k) if backward else (z + k, z - k)
            sending, receiving = (to >= 0, source < groups) if backward else (to < groups, source >= 0)
            device = (jnp.clip(to, 0, groups - 1), links.p, links.c)
            pair = [links.copy(state, states.at[z], device), links.copy(decay, decays.at[z], device)]
            self.found.append((sending, receiving, pair))

    def start(self):
        for sending, _, pair in self.found:

            @pl.when(sending)
            def _(pair=pair):
                for copy in pair:
                    copy.start()

    def arrive(self):
        for _, receiving, pair in self.found:

            @pl.when(receiving)
            def _(pair=pair):
                for copy in pair:
                    copy.wait_recv()

    def finish(self):
        for sending, _, pair in self.found:

            @pl.when(sending)
            def _(pair=pair):
                for copy in pair:
                    copy.wait_send()


class Gather:
    def __init__(self, links, out, base):
        self.links, self.out, self.base = links, out, base

        def place(k, c):
            row = base + lax.bitwise_xor(links.p, jnp.int32(k)) * (2 * HALF) + c * HALF
            return out.at[pl.ds(pl.multiple_of(row, EDGE), HALF), :]

        own = place(0, links.c)
        self.out_copies = [links.copy(own, own, links.at(k, 0)) for k in (3, 1, 2)]
        self.shared = [links.copy(own, own, links.at(0, 1))]
        self.shared += [links.copy(place(k, links.c), place(k, links.c), links.at(0, 1)) for k in (1, 2, 3)]
        self.arrivals = [self.out_copies[1], self.out_copies[2], self.out_copies[0]]

    def own(self, start, size):
        row = self.base + self.links.p * (2 * HALF) + self.links.c * HALF + start
        return pl.ds(pl.multiple_of(row, EDGE), size)

    def start(self):
        for copy in self.out_copies:
            copy.start()
        self.shared[0].start()

    def pass_on(self):
        for k in range(3):
            self.arrivals[k].wait_recv()
            self.shared[k + 1].start()

    def finish(self):
        for copy in self.shared:
            copy.wait_recv()
        for copy in self.shared + self.out_copies:
            copy.wait_send()


class EdgeForward:
    def __init__(self, links, gather):
        self.links = links
        tail = gather.out.at[gather.own(HALF - EDGE, EDGE), :]
        first = links.used
        links.used += 2 * GROUP + 1
        recv = links.recvs.at[first + 2 * GROUP]
        self.out = gather.out
        self.copies = [
            pltpu.make_async_remote_copy(
                src_ref=tail, dst_ref=gather.out.at[0:EDGE, :], send_sem=links.sends.at[first + p * 2 + c], recv_sem=recv,
                device_id=(links.z + 1, jnp.int32(p), jnp.int32(c)), device_id_type=MESH,
            )
            for p in range(GROUP)
            for c in range(2)
        ]
        self.sending = jnp.logical_and(links.last_of_plane(), links.z < links.groups - 1)

    def start(self):
        @pl.when(self.sending)
        def _():
            for copy in self.copies:
                copy.start()

        @pl.when(self.links.z == 0)
        def _():
            self.out[0:EDGE, :] = jnp.zeros((EDGE, self.out.shape[1]), self.out.dtype)

    def finish(self):
        pl.when(self.links.z > 0)(self.copies[0].wait_recv)

        @pl.when(self.sending)
        def _():
            for copy in self.copies:
                copy.wait_send()


class Scatter:
    def __init__(self, links, part, base, sib, total, peer):
        self.links, self.part, self.base = links, part, base
        self.sib, self.total, self.peer = sib, total, peer
        other = 1 - links.c
        self.to_sibling = {
            k: links.copy(part.at[self.rows(k, other, 0, HALF), :], sib.at[k], links.at(0, 1)) for k in (3, 1, 2, 0)
        }
        self.to_peer = {k: links.copy(total.at[k - 1], peer.at[k - 1], links.at(k, 0)) for k in (3, 1, 2)}

    def rows(self, k, c, start, size):
        row = self.base + lax.bitwise_xor(self.links.p, jnp.int32(k)) * (2 * HALF) + c * HALF + start
        return pl.ds(pl.multiple_of(row, EDGE), size)

    def start(self):
        for copy in self.to_sibling.values():
            copy.start()

    def reduce(self):
        for k in (3, 1, 2):
            self.to_sibling[k].wait_recv()

            def add(i, _, k=k):
                at = pl.ds(pl.multiple_of(i * 32, 32), 32)
                mine = self.part[self.rows(k, self.links.c, i * 32, 32), :].astype(F32)
                self.total[k - 1, at, :] = (mine + self.sib[k, at, :].astype(F32)).astype(BF16)
                return 0

            lax.fori_loop(0, HALF // 32, add, 0)
            self.to_peer[k].start()
        self.to_sibling[0].wait_recv()
        for copy in self.to_peer.values():
            copy.wait_recv()

    def own(self, start, size):
        at = pl.ds(start, size)
        total = self.part[self.rows(0, self.links.c, start, size), :].astype(F32) + self.sib[0, at, :].astype(F32)
        for k in range(3):
            total = total + self.peer[k, at, :].astype(F32)
        return total

    def finish(self):
        for copy in list(self.to_sibling.values()) + list(self.to_peer.values()):
            copy.wait_send()


class SmallSum:
    def __init__(self, links, squares, slots):
        self.links, self.squares, self.slots = links, squares, slots
        self.copies = [
            links.copy(squares.at[:, self.lanes(k, e)], slots.at[2 * k + e - 1], links.at(k, e))
            for k in range(GROUP)
            for e in range(2)
            if k or e
        ]

    def lanes(self, k, e):
        links = self.links
        column = lax.bitwise_xor(links.p, jnp.int32(k)) * (2 * HALF) + lax.bitwise_xor(links.c, jnp.int32(e)) * HALF
        return pl.ds(pl.multiple_of(column, HALF), HALF)

    def start(self):
        for copy in self.copies:
            copy.start()

    def total(self):
        for copy in self.copies:
            copy.wait_recv()
        total = self.squares[:, self.lanes(0, 0)]
        for i in range(len(self.copies)):
            total = total + self.slots[i]
        return total

    def finish(self):
        for copy in self.copies:
            copy.wait_send()


class SmallGather:
    def __init__(self, links, out):
        self.out = out
        self.lanes = pl.ds(pl.multiple_of(links.p * (2 * HALF) + links.c * HALF, HALF), HALF)
        self.copies = [
            links.copy(out.at[:, self.lanes], out.at[:, self.lanes], links.at(k, e))
            for k in range(GROUP)
            for e in range(2)
            if k or e
        ]

    def start(self):
        for copy in self.copies:
            copy.start()

    def finish(self):
        for copy in self.copies:
            copy.wait()


def row_chunks(size=32):
    return [(start, size) for start in range(0, HALF, size)]


def rms_of(rows):
    return lax.rsqrt(jnp.mean(rows * rows, axis=-1, keepdims=True) + EPS)


def as_tile(columns):
    lane = iota((HALF, HALF), 1)
    wide = jnp.zeros((HALF, HALF), F32)
    for i, column in enumerate(columns):
        wide = jnp.where(lane == i, column, wide)
    return wide.T[0:8]


def begin_kernel(count, late, *refs):
    resid, cot, gain = refs[:3]
    shards, rest = refs[3 : 3 + count + late], refs[3 + count + late :]
    normed_out, dmix_out, resid_out, cot_out = rest[:4]
    outs = rest[4 : 4 + count + late]
    sends, recvs = rest[4 + count + late :]
    links = Links(sends, recvs)
    z, p, c, groups = links.z, links.p, links.c, links.groups
    inner = outs[0].shape[-1]
    mine = z * GROUP + p

    def source(i, k):
        if shards[i].shape[1] == STATE:
            return shards[i]
        to = lax.bitwise_xor(p, jnp.int32(k))
        return shards[i].at[:, pl.ds(pl.multiple_of(to * inner, 128), inner)]

    def block(i, at):
        return outs[i].at[c, at] if len(outs[i].shape) == 4 else outs[i].at[at]

    swaps, keeps = [], []
    for i in range(count + late):
        target = block(i, mine if i < count else p)
        swaps.append([links.copy(source(i, k), target, links.at(k, 0)) for k in (3, 1, 2)])
        keeps.append(links.local(source(i, 0), target))
    for copy in keeps:
        copy.start()

    gather = Gather(links, normed_out, EDGE)
    other = Gather(links, dmix_out, 0)
    edge = EdgeForward(links, gather)
    links.greet(plane=True, groups=True, edge=1)
    for start, size in row_chunks():
        rows = pl.ds(pl.multiple_of(c * HALF + start, EDGE), size)
        part = resid[rows, :].astype(F32)
        resid_out[start : start + size] = part
        normed_out[gather.own(start, size), :] = (part * rms_of(part) * gain[...]).astype(BF16)
        part = cot[rows, :]
        cot_out[start : start + size] = part.astype(F32)
        dmix_out[other.own(start, size), :] = part
    links.meet()
    for group in swaps[:count]:
        for copy in group:
            copy.start()

    def lines(step):
        found = []
        up, down = z - step + 1, z + step - 1
        for i in range(count):
            piece = block(i, pl.ds(jnp.maximum(up, 0) * GROUP, GROUP))
            sending = jnp.logical_and(up >= 0, z < groups - 1)
            found.append((sending, z - step >= 0, links.copy(piece, piece, (z + 1, p, c))))
            piece = block(i, pl.ds(jnp.minimum(down, groups - 1) * GROUP, GROUP))
            sending = jnp.logical_and(down < groups, z > 0)
            found.append((sending, z + step < groups, links.copy(piece, piece, (z - 1, p, c))))
        return found

    steps = [lines(step) for step in range(1, groups)]
    for i in range(count):
        keeps[i].wait()
        for copy in swaps[i]:
            copy.wait_recv()
        for can_send, _, copy in steps[0][2 * i : 2 * i + 2]:
            pl.when(can_send)(copy.start)
    gather.start()
    edge.start()
    gather.pass_on()
    other.start()
    for step in range(1, len(steps)):
        for i in range(2 * count):
            pl.when(steps[step - 1][i][1])(steps[step - 1][i][2].wait_recv)
            pl.when(steps[step][i][0])(steps[step][i][2].start)
        if step == 1:
            other.pass_on()
            for group in swaps[count:]:
                for copy in group:
                    copy.start()
    share = []
    for i in range(2 * count):
        pl.when(steps[-1][i][1])(steps[-1][i][2].wait_recv)
        if i % 2 and len(outs[i // 2].shape) == 4:
            whole = outs[i // 2].at[c]
            share.append(links.copy(whole, whole, links.at(0, 1)))
            share[-1].start()
    gather.finish()
    other.finish()
    edge.finish()
    for i in range(count, count + late):
        keeps[i].wait()
        for copy in swaps[i]:
            copy.wait_recv()
    for group in swaps:
        for copy in group:
            copy.wait_send()
    for found in steps:
        for can_send, _, copy in found:
            pl.when(can_send)(copy.wait_send)
    for copy in share:
        copy.wait()


def forward_kernel(last, *refs):
    normed, wx, wz, wbc, wdt, wo, rowp, bcp, headp = refs[:9]
    more = 0 if last else 2
    later, outs = refs[9 : 9 + more], refs[9 + more :]
    (z, xin, bcin, x, bc, dtraw, dt, s, y, states, decay, part, squares, wo_all) = outs[:14]
    later_out = outs[14 : 14 + more]
    ext, local, state_low, decay_row, states_in, decays_in, sends, recvs = outs[14 + more :]
    links = Links(sends, recvs)
    spread = Spread(links, wo, wo_all)
    passing = []
    if not last:
        passing = [Spread(links, later[0], later_out[0].at[links.c]), Spread(links, later[1], later_out[1])]
        whole = later_out[0].at[links.c]
        share = links.copy(whole, whole, links.at(0, 1))
    carried = States(links, False, state_low, decay_row, states_in, decays_in)
    links.start_barrier(sibling=not last, groups=True)
    spread.start()
    state_sum, decay_all = project_and_convolve(
        links.p, normed, wx, wz, wbc, wdt, rowp, bcp, headp,
        z, xin, bcin, x, bc, dtraw, dt, s, decay, ext, local,
    )
    state_low[...] = state_sum.astype(BF16)
    decay_row[...] = jnp.broadcast_to(decay_all, decay_row.shape)
    carried.start()
    for other in passing:
        other.start()
    mix_within_spans(x, bc, s, dt, y)
    carried.arrive()
    state = entering_state(links.z, links.groups, states_in, decays_in, False)
    spread.arrive()
    mix_out(state, local, decay, x, bc, z, s, wo_all, rowp, y, states, part, squares)
    for other in passing:
        other.arrive()
    if not last:
        share.start()
    carried.finish()
    for other in [spread] + passing:
        other.finish()
    if not last:
        share.wait()


def backward_kernel(inner_all, done, *refs):
    (dmix, wo, y, z, x, bc, s, dt, dtraw, xin, bcin, states, decay, token_scalars, rowp, bcp, headp) = refs[:17]
    parts, outs = refs[17 : 17 + done], refs[17 + done :]
    dz, dcat, go_parts, gate_small, row_small, bc_small, head_small = outs[:7]
    delivered = outs[7 : 7 + done]
    (
        dy, gwo, normed_out, prior, dend, dpre, flow, sums, final, state_low, decay_row, states_in, decays_in, sends, recvs
    ) = outs[7 + done :]
    links = Links(sends, recvs)
    carried = States(links, True, state_low, decay_row, states_in, decays_in)
    collect = Collect(links, gwo, go_parts)
    delivers = [Deliver(links, parts[i], final.at[i], delivered[i]) for i in range(done)]
    links.greet(plane=done > 0, groups=True)
    grad_sum, decay_all = back_through_gate(
        inner_all, dmix, wo, y, z, x, bc, s, decay, token_scalars, rowp, dz, gate_small, dy, prior, normed_out
    )
    state_low[...] = grad_sum.astype(BF16)
    decay_row[...] = jnp.broadcast_to(decay_all, decay_row.shape)
    links.meet()
    carried.start()
    out_gradient(dmix, normed_out, gwo)
    collect.start()
    for deliver in delivers:
        deliver.start()
    back_within_spans(dy, x, bc, s, dt, dpre, flow, sums)
    carried.arrive()
    grad = entering_state(links.z, links.groups, states_in, decays_in, True)
    back_through_states(
        grad, prior, decay, states, dy, x, bc, s, dt, dtraw, xin, bcin, rowp, bcp, headp, flow, sums,
        dcat, row_small, bc_small, head_small, dpre, dend,
    )
    carried.finish()
    collect.arrive()
    collect.finish()
    for deliver in delivers:
        deliver.finish()


def next_layer_kernel(
    inner_all, part, squares, resid, gain, wx, wz, normed_out, resid_out, mixed_out, inv_out, wx_out, wz_out,
    sib, total, peer, slots, sends, recvs,
):
    links = Links(sends, recvs)
    scatter = Scatter(links, part, 0, sib, total, peer)
    small = SmallSum(links, squares, slots)
    gather = Gather(links, normed_out, EDGE)
    edge = EdgeForward(links, gather)
    spreads = [Spread(links, wx, wx_out), Spread(links, wz, wz_out)]
    links.start_barrier(plane=True, groups=True, edge=1)
    scatter.start()
    small.start()
    for spread in spreads:
        spread.start()
    scatter.reduce()
    inv = lax.rsqrt(small.total() * (1.0 / inner_all) + EPS)
    inv_out[...] = inv
    column = inv.T[:, 0:1]
    for start, size in row_chunks():
        at = slice(start, start + size)
        mixed = scatter.own(start, size)
        mixed_out[at] = mixed
        fresh = resid[at] + column[at] * mixed
        resid_out[at] = fresh
        normed_out[gather.own(start, size), :] = (fresh * rms_of(fresh) * gain[...]).astype(BF16)
    gather.start()
    edge.start()
    gather.pass_on()
    scatter.finish()
    small.finish()
    gather.finish()
    edge.finish()
    for spread in spreads:
        spread.arrive()
        spread.finish()


def turn_kernel(
    inner_all, part, squares, resid, cot, block_out, scalars_out,
    sib, total, peer, slots, sends, recvs,
):
    links = Links(sends, recvs)
    scatter = Scatter(links, part, 0, sib, total, peer)
    small = SmallSum(links, squares, slots)
    spread = SmallGather(links, scalars_out)
    rows = pl.ds(pl.multiple_of(links.c * HALF, HALF), HALF)
    share = links.copy(block_out.at[rows, :], block_out.at[rows, :], links.at(0, 1))
    links.start_barrier(plane=True)
    scatter.start()
    small.start()
    scatter.reduce()
    inv = lax.rsqrt(small.total() * (1.0 / inner_all) + EPS)
    column = inv.T[:, 0:1]
    dots = []
    for start, size in row_chunks():
        at = slice(start, start + size)
        mixed = scatter.own(start, size)
        dots.append(jnp.sum(cot[at] * mixed, axis=-1, keepdims=True))
        block_out[pl.ds(pl.multiple_of(links.c * HALF + start, EDGE), size), :] = (
            resid[at] + column[at] * mixed
        ).astype(BF16)
    scalars_out[:, spread.lanes] = as_tile([column, jnp.concatenate(dots)])
    spread.start()
    share.start()
    scatter.finish()
    small.finish()
    spread.finish()
    share.wait()


def grad_rows(links, scatter, edge_slots, grad, resid, gain, gain_out, start, size):
    at = slice(start, start + size)
    d_normed = scatter.own(start, size)
    if start + size == HALF:
        extra = edge_slots[0].astype(F32)
        for i in range(1, 2 * GROUP):
            extra = extra + edge_slots[i].astype(F32)
        used = jnp.logical_and(links.last_of_plane(), links.z < links.groups - 1)
        extra = jnp.where(used, extra, 0.0)
        d_normed = d_normed + jnp.concatenate([jnp.zeros((size - EDGE, extra.shape[1]), F32), extra])
    rows = resid[at]
    inv_rms = rms_of(rows)
    gain_sum = jnp.sum(d_normed * rows * inv_rms, axis=0, keepdims=True)
    gain_out[0:1] = gain_sum if start == 0 else gain_out[0:1] + gain_sum
    d_hidden = d_normed * gain[...]
    return (
        grad[at]
        + inv_rms * d_hidden
        - rows * (inv_rms * inv_rms * inv_rms * jnp.mean(d_hidden * rows, axis=-1, keepdims=True))
    )


class EdgeBackward:
    def __init__(self, links, part, slots):
        self.links = links
        first = links.used
        links.used += 2 * GROUP + 1
        me = links.p * 2 + links.c
        self.send = pltpu.make_async_remote_copy(
            src_ref=part.at[0:EDGE, :], dst_ref=slots.at[me], send_sem=links.sends.at[first], recv_sem=links.recvs.at[first + me],
            device_id=(links.z - 1, jnp.int32(GROUP - 1), jnp.int32(1)), device_id_type=MESH,
        )
        self.recvs = [
            pltpu.make_async_remote_copy(
                src_ref=part.at[0:EDGE, :], dst_ref=slots.at[i], send_sem=links.sends.at[first], recv_sem=links.recvs.at[first + i],
                device_id=(links.z, links.p, 1 - links.c), device_id_type=MESH,
            )
            for i in range(2 * GROUP)
        ]
        self.receiving = jnp.logical_and(links.last_of_plane(), links.z < links.groups - 1)

    def start(self):
        pl.when(self.links.z > 0)(self.send.start)

    def receive(self):
        @pl.when(self.receiving)
        def _():
            for copy in self.recvs:
                copy.wait_recv()

    def finish(self):
        pl.when(self.links.z > 0)(self.send.wait_send)


def layer_below_kernel(
    part, grad, resid, gain, mixed, inv, gx, gz, dmix_out, scalars_out, grad_out, gain_out, gx_out, gz_out,
    sib, total, peer, edge_slots, sends, recvs,
):
    links = Links(sends, recvs)
    scatter = Scatter(links, part, EDGE, sib, total, peer)
    edge = EdgeBackward(links, part, edge_slots)
    gather = Gather(links, dmix_out, 0)
    spread = SmallGather(links, scalars_out)
    edge_slots[...] = jnp.zeros_like(edge_slots)
    collects = [Collect(links, gx, gx_out), Collect(links, gz, gz_out)]
    links.start_barrier(plane=True, groups=True, edge=-1)
    edge.start()
    scatter.start()
    for collect in collects:
        collect.start()
    scatter.reduce()
    edge.receive()
    gain_out[...] = jnp.zeros_like(gain_out)
    dots = []
    for start, size in row_chunks():
        at = slice(start, start + size)
        fresh = grad_rows(links, scatter, edge_slots, grad, resid, gain, gain_out, start, size)
        grad_out[at] = fresh
        low = fresh.astype(BF16)
        dmix_out[gather.own(start, size), :] = low
        dots.append(jnp.sum(low.astype(F32) * mixed[at], axis=-1, keepdims=True))
    scalars_out[:, spread.lanes] = as_tile([inv[...].T[:, 0:1], jnp.concatenate(dots)])
    gather.start()
    spread.start()
    gather.pass_on()
    scatter.finish()
    edge.finish()
    gather.finish()
    spread.finish()
    for collect in collects:
        collect.arrive()
        collect.finish()


class SmallSums:
    def __init__(self, links, bc, vec, dt, wide, bc_out, vec_out, dt_out, wide_out, bufs):
        self.links = links
        self.bc, self.vec, self.dt, self.wide = bc, vec, dt, wide
        self.bc_out, self.vec_out, self.dt_out, self.wide_out = bc_out, vec_out, dt_out, wide_out
        self.bc_in, self.bc_sum, self.bc_far, self.vec_in, self.vec_far, self.dt_far, self.wide_far = bufs
        z, p, c, groups = links.z, links.p, links.c, links.groups
        self.first, self.vec_first, self.second, self.third = [], [], [], []
        for k in range(GROUP):
            for e in range(2):
                if not (k or e):
                    continue
                slot = 2 * k + e
                to_p, to_c = lax.bitwise_xor(p, jnp.int32(k)), lax.bitwise_xor(c, jnp.int32(e))
                device = links.at(k, e)
                for layer in range(bc.shape[0]):
                    src = bc.at[layer, :, to_p, :, pl.ds(pl.multiple_of(to_c * STATE, STATE), STATE)]
                    self.first.append(links.copy(src, self.bc_in.at[layer, slot - 1], device))
                self.vec_first.append(links.copy(vec.at[to_p * 2 + to_c], self.vec_in.at[slot - 1], device))
                self.third.append(links.copy(vec_out.at[p * 2 + c], vec_out.at[p * 2 + c], device))
        for k in range(1, groups):
            to = lax.rem(z + k, groups)
            device = (to, p, c)
            for layer in range(bc.shape[0]):
                self.second.append(links.copy(self.bc_sum.at[layer, to], self.bc_far.at[layer, k - 1], device))
            self.second.append(links.copy(self.vec_in.at[7], self.vec_far.at[k - 1], device))
            self.second.append(links.copy(dt.at[to], self.dt_far.at[k - 1], device))
            self.second.append(links.copy(wide, self.wide_far.at[k - 1], device))
        for k in range(1, GROUP):
            device = links.at(k, 0)
            self.third.append(links.copy(dt_out.at[p], dt_out.at[p], device))
            self.third.append(links.copy(wide_out.at[p], wide_out.at[p], device))
        lanes = pl.ds(pl.multiple_of(c * STATE, STATE), STATE)
        self.third.append(links.copy(bc_out.at[:, :, lanes], bc_out.at[:, :, lanes], links.at(0, 1)))

    def round_one(self):
        for copy in self.vec_first + self.first:
            copy.start()

    def round_two(self):
        links = self.links
        for copy in self.vec_first + self.first:
            copy.wait_recv()
        own_lanes = pl.ds(pl.multiple_of(links.c * STATE, STATE), STATE)
        for layer in range(self.bc.shape[0]):

            def add(i, _, layer=layer):
                total = self.bc[layer, i, links.p, :, own_lanes].astype(F32)
                for slot in range(2 * GROUP - 1):
                    total = total + self.bc_in[layer, slot, i].astype(F32)
                self.bc_sum[layer, i] = total.astype(BF16)
                return 0

            lax.fori_loop(0, links.groups, add, 0)
        total = self.vec[links.p * 2 + links.c]
        for slot in range(2 * GROUP - 1):
            total = total + self.vec_in[slot]
        self.vec_in[7] = total
        for copy in self.second:
            copy.start()

    def round_three(self):
        links = self.links
        z, p, c = links.z, links.p, links.c
        for copy in self.second:
            copy.wait_recv()
        far = links.groups - 1
        lanes = pl.ds(pl.multiple_of(c * STATE, STATE), STATE)
        for layer in range(self.bc.shape[0]):
            total = self.bc_sum[layer, z].astype(F32)
            for k in range(far):
                total = total + self.bc_far[layer, k].astype(F32)
            self.bc_out[layer, :, lanes] = total.astype(BF16)
        total = self.vec_in[7]
        dt_total = self.dt[z].astype(F32)
        wide_total = self.wide[...]
        for k in range(far):
            total = total + self.vec_far[k]
            dt_total = dt_total + self.dt_far[k].astype(F32)
            wide_total = wide_total + self.wide_far[k]
        self.vec_out[p * 2 + c] = total
        self.dt_out[p] = dt_total.astype(BF16)
        self.wide_out[p] = wide_total
        for copy in self.third:
            copy.start()

    def finish(self):
        for copy in self.third:
            copy.wait_recv()
        for copy in self.vec_first + self.first + self.second + self.third:
            copy.wait_send()


def final_kernel(
    part, grad, resid, gain, gx, gz, go_parts, bc, vec, dt, wide,
    out, gx_out, gz_out, go_out, bc_out, vec_out, dt_out, wide_out,
    sib, total, peer, edge_slots, gain_row, vec_own, gx_parts, gz_parts, final,
    bc_in, bc_sum, bc_far, vec_in, vec_far, dt_far, wide_far, sends, recvs,
):
    links = Links(sends, recvs)
    scatter = Scatter(links, part, EDGE, sib, total, peer)
    edge = EdgeBackward(links, part, edge_slots)
    rows = pl.ds(pl.multiple_of(links.c * HALF, HALF), HALF)
    share = links.copy(out.at[rows, :], out.at[rows, :], links.at(0, 1))
    collects = [Collect(links, gx, gx_parts), Collect(links, gz, gz_parts)]
    small = SmallSums(
        links, bc, vec_own, dt, wide, bc_out, vec_out, dt_out, wide_out,
        (bc_in, bc_sum, bc_far, vec_in, vec_far, dt_far, wide_far),
    )
    delivers = [
        Deliver(links, parts, final.at[i], place)
        for i, (parts, place) in enumerate(((go_parts, go_out), (gx_parts, gx_out), (gz_parts, gz_out)))
    ]
    edge_slots[...] = jnp.zeros_like(edge_slots)
    links.start_barrier(plane=True, groups=True, edge=-1)
    edge.start()
    scatter.start()
    for collect in collects:
        collect.start()
    scatter.reduce()
    edge.receive()
    gain_row[...] = jnp.zeros_like(gain_row)
    for start, size in row_chunks():
        fresh = grad_rows(links, scatter, edge_slots, grad, resid, gain, gain_row, start, size)
        out[pl.ds(pl.multiple_of(links.c * HALF + start, EDGE), size), :] = fresh.astype(BF16)
    share.start()
    vec_own[...] = vec[...]
    for r in range(gain_row.shape[1] // 128):
        vec_own[r // 8, r % 8 : r % 8 + 1, :] = gain_row[0:1, r * 128 : r * 128 + 128]
    small.round_one()
    delivers[0].start()
    small.round_two()
    small.round_three()
    for i in range(2):
        collects[i].arrive()
        delivers[i + 1].start()
    small.finish()
    scatter.finish()
    edge.finish()
    share.wait()
    for collect in collects:
        collect.finish()
    for deliver in delivers:
        deliver.finish()


def call(body, outs, *args, scratch=(), collective=None, copies=0):
    vmem = pl.BlockSpec(memory_space=pltpu.VMEM)
    scratch = [pltpu.VMEM(shape, kind) for shape, kind in scratch]
    if collective is not None:
        scratch += [pltpu.SemaphoreType.DMA((copies,)), pltpu.SemaphoreType.DMA((copies,))]
    return pl.pallas_call(
        body,
        out_shape=tuple(jax.ShapeDtypeStruct(shape, kind) for shape, kind in outs),
        in_specs=[vmem] * len(args),
        out_specs=tuple([vmem] * len(outs)),
        scratch_shapes=scratch,
        compiler_params=pltpu.CompilerParams(
            vmem_limit_bytes=VMEM_BYTES, collective_id=collective, has_side_effects=collective is not None
        ),
    )(*args)


def on_device(resid_in, cotangent, norm_gain, w_zx, w_dt, w_bc, conv_x, conv_bc, head_params, gated_gain, w_out):
    layers, model = norm_gain.shape
    groups = lax.axis_size("z")
    place, core = lax.axis_index("p"), lax.axis_index("head")
    shard = w_dt.shape[1]
    inner_core = conv_x.shape[2]
    inner = inner_core // GROUP
    heads_core = head_params.shape[2]
    heads = heads_core // GROUP
    inner_all = inner_core * lax.axis_size("head")
    length = resid_in.shape[1]
    tokens = GROUP * length
    spans = tokens // SPAN
    sources = groups * GROUP
    rows = GROUP * shard

    def my_part(array, size):
        return lax.dynamic_slice_in_dim(array, place * size, size, array.ndim - 1)

    row_all, bc_all, head_all = [], [], []
    conv_mine = my_part(conv_x, inner).astype(F32)
    gain_mine = my_part(gated_gain, inner).astype(F32)
    head_mine = my_part(head_params, heads)
    gains = [norm_gain[layer].astype(F32)[None] for layer in range(layers)]
    for layer in range(layers):
        skip = jnp.repeat(head_mine[layer, 2], HEADDIM)
        row_all.append(
            jnp.concatenate([conv_mine[layer], gain_mine[layer][None], skip[None], jnp.zeros((1, inner), F32)])
        )
        bc_all.append(jnp.pad(conv_bc[layer].astype(F32), ((0, 3), (0, 0))))
        head_all.append(jnp.pad(head_mine[layer], ((0, 5), (0, 128 - heads))))

    def shards_of(layer):
        half = lax.dynamic_slice_in_dim(w_bc[layer], core * STATE, STATE, 1)
        steps = jnp.pad(w_dt[layer], ((0, 0), (0, STATE - heads_core)))
        return w_zx[layer, 1], w_zx[layer, 0], half, steps, w_out[layer].T

    half_scratch = [
        ((GROUP, HALF, model), BF16),
        ((GROUP - 1, HALF, model), BF16),
        ((GROUP - 1, HALF, model), BF16),
    ]
    slots = ((2 * GROUP - 1, 8, HALF), F32)
    edges = ((2 * GROUP, EDGE, model), BF16)
    own_rows = ((HALF, model), F32)

    shards = [shards_of(layer) for layer in range(layers)]
    early = list(shards[0][:4])
    late = [shards[0][4]] + [piece for layer in range(1, layers) for piece in shards[layer]]
    wide_piece, thin_piece = (sources, shard, inner), (sources, shard, STATE)
    late_shapes = [(GROUP, shard, a.shape[1] // (GROUP if a.shape[1] > STATE else 1)) for a in late]
    gathered = call(
        functools.partial(begin_kernel, len(early), len(late)),
        [
            ((tokens + EDGE, model), BF16),
            ((tokens, model), BF16),
            own_rows,
            own_rows,
            (wide_piece, BF16),
            (wide_piece, BF16),
            ((2, *thin_piece), BF16),
            (thin_piece, BF16),
        ]
        + [(shape, BF16) for shape in late_shapes],
        resid_in[0], cotangent[0], gains[0], *early, *late,
        collective=0, copies=30 + 4 * (len(early) + len(late)) + 2 * len(early) * (groups - 1),
    )
    normed, last_dmix, resid, grad, wx, wz, wbc, wdt = gathered[:8]
    wx, wz, wdt = [a.reshape(model, -1) for a in (wx, wz, wdt)]
    wbc = wbc.reshape(2, model, STATE)
    own = [a.reshape(rows, -1) for a in gathered[8:]]
    own = [(None, None, None, None, own[0])] + [own[1 + 5 * i : 6 + 5 * i] for i in range(layers - 1)]
    whole = ((model, inner), BF16)

    state_scratch = [
        ((STATE, inner), BF16),
        ((8, inner), F32),
        ((groups, STATE, inner), BF16),
        ((groups, 8, inner), F32),
    ]
    saved, weights = [], []
    for layer in range(layers):
        rowp, bcp, headp = row_all[layer], bc_all[layer], head_all[layer]
        last = layer == layers - 1
        passing = [] if last else [own[layer + 1][2], own[layer + 1][3]]
        results = call(
            functools.partial(forward_kernel, last),
            [
                ((tokens, inner), BF16),
                ((tokens + EDGE, inner), BF16),
                ((tokens + EDGE, 2 * STATE), BF16),
                ((tokens, inner), BF16),
                ((tokens, 2 * STATE), BF16),
                ((tokens, 128), BF16),
                ((tokens, 128), F32),
                ((tokens, 128), F32),
                ((tokens, inner), F32),
                ((spans, STATE, inner), F32),
                ((spans, 8, inner), F32),
                ((tokens, model), BF16),
                ((8, tokens), F32),
                whole,
            ]
            + ([] if last else [((2, model, STATE), BF16), ((model, STATE), BF16)]),
            normed, wx, wz, wbc, wdt, own[layer][4], rowp, bcp, headp, *passing,
            scratch=[((tokens + EDGE, inner + 2 * STATE), F32), ((spans, STATE, inner), F32)] + state_scratch,
            collective=2 if last else 1, copies=8 + 5 * groups,
        )
        z, xin, bcin, x, bc, dtraw, dt, s, y, states, decay, part, squares, wo = results[:14]
        weights.append((wx, wz, wbc, wdt, wo))
        kept = (resid, normed, (y, z, x, bc, s, dt, dtraw, xin, bcin, states, decay))
        if not last:
            wbc, wdt = results[14:]
            normed, resid, mixed, inv, wx, wz = call(
                functools.partial(next_layer_kernel, inner_all),
                [((tokens + EDGE, model), BF16), own_rows, own_rows, ((8, HALF), F32), whole, whole],
                part, squares, resid, gains[layer + 1], own[layer + 1][0], own[layer + 1][1],
                scratch=half_scratch + [slots], collective=3, copies=40 + 2 * groups,
            )
            saved.append((*kept, (mixed, inv)))
        else:
            block_out, token_scalars = call(
                functools.partial(turn_kernel, inner_all),
                [((length, model), BF16), ((8, tokens), F32)],
                part, squares, resid, grad,
                scratch=half_scratch + [slots], collective=4, copies=40,
            )
            saved.append((*kept, None))

    d_mix, ready, delivered = last_dmix, [], {}
    kinds, gain_rows = [None] * layers, [None] * layers
    grad_parts = ((groups, rows, inner), BF16)
    for layer in reversed(range(layers)):
        wx, wz, wbc, wdt, wo = weights[layer]
        rowp, bcp, headp = row_all[layer], bc_all[layer], head_all[layer]
        resid, normed, kept, _ = saved[layer]
        results = call(
            functools.partial(backward_kernel, inner_all, len(ready)),
            [
                ((tokens, inner), BF16),
                ((tokens + EDGE, inner + 2 * STATE + 128), BF16),
                grad_parts,
                ((8, inner), F32),
                ((8, inner), F32),
                ((8, 2 * STATE), F32),
                ((8, 128), F32),
            ]
            + [((shard, inner_core), BF16)] * len(ready),
            d_mix, wo, *kept, token_scalars, rowp, bcp, headp, *ready,
            scratch=[
                ((tokens, inner), BF16),
                whole,
                ((tokens, inner), BF16),
                ((spans, STATE, inner), F32),
                ((spans, STATE, inner), F32),
                ((tokens + 2 * EDGE, inner + 2 * STATE), F32),
                ((tokens, 128), F32),
                ((tokens, 128), F32),
                ((3, GROUP, shard, inner), BF16),
            ]
            + state_scratch,
            collective=5 if ready else 6, copies=20 + 3 * groups,
        )
        dz, dcat, go_parts, gate_small, row_small, bc_small, head_small = results[:7]
        if ready:
            delivered[layer + 1] = results[7:]
        part, gx, gz, gbc, gdt = call(
            backward_project,
            [((tokens + EDGE, model), BF16), whole, whole, ((model, 2 * STATE), BF16), ((EDGE, model), BF16)],
            dcat, dz, normed, wx, wz, wbc, wdt,
        )
        tall = jnp.pad(head_small[:2], ((0, 0), (0, inner - 128)))
        wide = jnp.concatenate([row_small[: CONV + 1], gate_small[:2], tall])
        kinds[layer] = (gbc, gdt, jnp.pad(wide, ((0, 7), (0, 0))), bc_small[: CONV + 1])
        if layer > 0:
            d_mix, token_scalars, grad, gain_rows[layer], gx_parts, gz_parts = call(
                layer_below_kernel,
                [((tokens, model), BF16), ((8, tokens), F32), own_rows, ((8, model), F32), grad_parts, grad_parts],
                part, grad, resid, gains[layer], *saved[layer - 1][3], gx, gz,
                scratch=half_scratch + [edges], collective=7, copies=60 + 2 * groups,
            )
            ready = [gx_parts, gz_parts, go_parts]

    vec = jnp.concatenate(
        [jnp.zeros((model,), F32)]
        + [gain_rows[layer][0] for layer in range(1, layers)]
        + [kinds[layer][3].reshape(-1) for layer in range(layers)]
    )
    vec = jnp.pad(vec, (0, 2 * GROUP * 1024 - vec.shape[0])).reshape(2 * GROUP, 8, 128)
    bc_grads = jnp.stack([kinds[layer][0].reshape(groups, GROUP, shard, 2 * STATE) for layer in range(layers)])
    dt_grads = jnp.concatenate([kinds[layer][1] for layer in range(layers)])
    dt_grads = jnp.swapaxes(dt_grads.reshape(layers * EDGE, groups, rows), 0, 1)
    wide = jnp.concatenate([kinds[layer][2] for layer in range(layers)])
    wide_shape, dt_shape, far = wide.shape, dt_grads.shape[1:], groups - 1
    grad_input, gx, gz, go, g_bc, vec, g_dt, wide = call(
        final_kernel,
        [
            ((length, model), BF16),
            ((shard, inner_core), BF16),
            ((shard, inner_core), BF16),
            ((shard, inner_core), BF16),
            ((layers, shard, 2 * STATE), BF16),
            (vec.shape, F32),
            ((GROUP, *dt_shape), BF16),
            ((GROUP, *wide_shape), F32),
        ],
        part, grad, resid, gains[0], gx, gz, go_parts, bc_grads, vec, dt_grads, wide,
        scratch=half_scratch + [
            edges,
            ((8, model), F32),
            (vec.shape, F32),
            grad_parts,
            grad_parts,
            ((3, GROUP, shard, inner), BF16),
            ((layers, 2 * GROUP - 1, groups, shard, STATE), BF16),
            ((layers, groups, shard, STATE), BF16),
            ((layers, far, shard, STATE), BF16),
            ((2 * GROUP, 8, 128), F32),
            ((far, 8, 128), F32),
            ((far, *dt_shape), BF16),
            ((far, *wide_shape), F32),
        ],
        collective=8, copies=100 + 8 * groups,
    )
    delivered[0] = (gx, gz, go)
    vec = vec.reshape(-1)
    grad_gain = vec[: layers * model].reshape(layers, model)
    grad_conv_bc = vec[layers * model :][: layers * (CONV + 1) * 2 * STATE].reshape(layers, CONV + 1, 2 * STATE)
    wide = wide.reshape(GROUP, layers, 16, inner)
    whole = jnp.moveaxis(wide, 0, 2).reshape(layers, 16, inner_core)
    skip_grad = jnp.sum(whole[:, CONV + 2].reshape(layers, heads_core, HEADDIM), axis=-1)
    tall = jnp.moveaxis(wide[:, :, CONV + 3 : CONV + 5, :heads], 0, 2).reshape(layers, 2, heads_core)
    grad_heads = jnp.concatenate([tall, skip_grad[:, None]], axis=1)
    g_dt = lax.dynamic_slice_in_dim(g_dt.reshape(GROUP, layers, EDGE, GROUP, shard), place, 1, 3)[:, :, :heads, 0]
    grad_dt = jnp.transpose(g_dt, (1, 3, 0, 2)).reshape(layers, shard, heads_core)
    low = lambda a: a.astype(BF16)
    return (
        block_out[None],
        grad_input[None],
        low(grad_gain),
        jnp.stack([jnp.stack([delivered[layer][1], delivered[layer][0]]) for layer in range(layers)]),
        grad_dt,
        g_bc,
        low(whole[:, : CONV + 1]),
        low(grad_conv_bc),
        low(grad_heads),
        low(whole[:, CONV + 1]),
        jnp.stack([delivered[layer][2].T for layer in range(layers)]),
    )


def solution(mesh):
    seq, head = mesh.shape["seq"], mesh.shape["head"]
    split = Mesh(mesh.devices.reshape(seq // GROUP, GROUP, head), ("z", "p", "head"))
    seq_axes = ("z", "p")
    specs = (
        P(None, seq_axes, None),
        P(None, seq_axes, None),
        P(),
        P(None, None, seq_axes, "head"),
        P(None, seq_axes, "head"),
        P(None, seq_axes, None),
        P(None, None, "head"),
        P(),
        P(None, None, "head"),
        P(None, "head"),
        P(None, "head", seq_axes),
    )
    return jax.shard_map(on_device, mesh=split, in_specs=specs, out_specs=specs, check_vma=False)
```

```python
import functools
import typing

import jax
import jax.numpy as jnp
from jax import lax
from jax.experimental import pallas as pl
from jax.experimental.pallas import tpu as pltpu
from jax.sharding import Mesh, PartitionSpec as P

HEADDIM = 64
STATE = 128
CONV = 4
SPAN = 256
GROUP = 4
EDGE = 16
EPS = 1e-05
HIGH = lax.Precision.HIGHEST
F32, BF16 = jnp.float32, jnp.bfloat16
NN = (((1,), (0,)), ((), ()))
NT = (((1,), (1,)), ((), ()))
TN = (((0,), (0,)), ((), ()))
VMEM_BYTES = 58 << 20


def dot(a, b, dims=NN):
    return lax.dot_general(a, b, dims, preferred_element_type=F32)


def dot_exact(a, b, dims=NN):
    return lax.dot_general(a, b, dims, precision=HIGH, preferred_element_type=F32)


def dot_split(a, b, dims=NN):
    high = a.astype(BF16)
    rest = (a - high.astype(F32)).astype(BF16)
    return dot(high, b, dims) + dot(rest, b, dims)


def sigmoid(v):
    return 1.0 / (1.0 + jnp.exp(-v))


def softplus(v):
    return jnp.maximum(v, 0.0) + jnp.log1p(jnp.exp(-jnp.abs(v)))


def silu_slope(v):
    sig = sigmoid(v)
    return sig * (1.0 + v * (1.0 - sig))


def iota(shape, dim):
    return lax.broadcasted_iota(jnp.int32, shape, dim)


def head_spread(inner):
    return (iota((128, inner), 0) == lax.shift_right_logical(iota((128, inner), 1), 6)).astype(BF16)


def triangle(lower):
    rows, cols = iota((SPAN, SPAN), 0), iota((SPAN, SPAN), 1)
    return ((cols <= rows) if lower else (cols >= rows)).astype(F32)


def half_masks():
    lane = iota((SPAN, 128), 1)
    return (lane < HEADDIM).astype(BF16), (lane >= HEADDIM).astype(BF16)


def conv_taps(window, taps):
    total = jnp.broadcast_to(taps[CONV : CONV + 1], (SPAN, window.shape[1]))
    for j in range(CONV):
        total = total + taps[j : j + 1] * window[EDGE - 3 + j : EDGE - 3 + j + SPAN]
    return total


def head_pick(place, heads):
    row, col = iota((128, 128), 0), iota((128, 128), 1)
    return jnp.logical_and(row == place * heads + col, col < heads).astype(BF16)


class Columns(typing.NamedTuple):
    x: slice
    z: slice
    dt: slice
    bc: slice
    size: int


def columns_of(inner):
    first = 2 * inner + 128
    return Columns(
        slice(0, inner), slice(inner, 2 * inner), slice(2 * inner, first), slice(first, first + 2 * STATE), first + 2 * STATE
    )


def project_and_convolve(
    place, normed, w, rowp, bcp, headp,
    z_out, xin_out, bcin_out, x_out, bc_out, dtraw_out, dt_out, s_out, decay_out,
    ext, local,
):
    inner = x_out.shape[1]
    spans = x_out.shape[0] // SPAN

    cols = columns_of(inner)
    edge = normed[0:EDGE]
    edge_x = dot(edge, w[:, cols.x]).astype(BF16)
    edge_bc = dot(edge, w[:, cols.bc]).astype(BF16)
    xin_out[0:EDGE] = edge_x
    bcin_out[0:EDGE] = edge_bc
    ext[0:EDGE, 0:inner] = edge_x.astype(F32)
    ext[0:EDGE, inner:] = edge_bc.astype(F32)
    spread = head_spread(inner)
    pick = head_pick(place, inner // HEADDIM)
    low_tri = triangle(True)
    rate = -jnp.exp(headp[0:1])
    bias = headp[1:2]

    def block(q, carry):
        state_sum, decay_all = carry
        at = pl.multiple_of(q * SPAN, SPAN)
        tok = pl.ds(at, SPAN)
        after = pl.ds(pl.multiple_of(at + EDGE, EDGE), SPAN)
        product = dot(normed[after, :], w[...]).astype(BF16)
        z_out[tok, :] = product[:, cols.z]
        xin, bcin = product[:, cols.x], product[:, cols.bc]
        dtraw = dot(product[:, cols.dt], pick).astype(BF16)
        xin_out[after, :] = xin
        bcin_out[after, :] = bcin
        dtraw_out[tok, :] = dtraw
        ext[after, 0:inner] = xin.astype(F32)
        ext[after, inner:] = bcin.astype(F32)
        window = pl.ds(at, SPAN + EDGE)
        pre_x = conv_taps(ext[window, 0:inner], rowp)
        x = (pre_x * sigmoid(pre_x)).astype(BF16)
        x_out[tok, :] = x
        pre_bc = conv_taps(ext[window, inner:], bcp)
        bc = (pre_bc * sigmoid(pre_bc)).astype(BF16)
        bc_out[tok, :] = bc
        dt = softplus(dtraw.astype(F32) + bias)
        s = dot_exact(low_tri, dt * rate)
        dt_out[tok, :] = dt
        s_out[tok, :] = s
        to_end = jnp.exp(s[SPAN - 1 : SPAN] - s) * dt
        weighted = (x.astype(F32) * dot_split(to_end, spread)).astype(BF16)
        fresh = dot(bc[:, :STATE], weighted, TN)
        decay = dot_split(jnp.exp(s[SPAN - 8 : SPAN]), spread)[7:8]
        local[q] = fresh
        decay_out[q] = jnp.broadcast_to(decay, (8, inner))
        return state_sum * decay + fresh, decay_all * decay

    return lax.fori_loop(0, spans, block, (jnp.zeros((STATE, inner), F32), jnp.ones((1, inner), F32)))


def mix_within_spans(x_in, bc_in, s_in, dt_in, y_out):
    inner = x_in.shape[1]

    def block(q, _):
        tok = pl.ds(pl.multiple_of(q * SPAN, SPAN), SPAN)
        x, bc, s = x_in[tok, :], bc_in[tok, :], s_in[tok, :]
        s_row, dt_row = s.T, dt_in[tok, :].T
        cb = dot(bc[:, STATE:], bc[:, :STATE], NT)
        causal = iota((SPAN, SPAN), 1) <= iota((SPAN, SPAN), 0)
        masks = half_masks()
        for pair in range(inner // 128):
            lanes = slice(pair * 128, pair * 128 + 128)
            x_pair = x[:, lanes]
            total = None
            for e in range(2):
                h = pair * 2 + e
                gap = jnp.where(causal, s[:, h : h + 1] - s_row[h : h + 1, :], -1e30)
                scores = (cb * (jnp.exp(gap) * dt_row[h : h + 1, :])).astype(BF16)
                term = dot(scores, x_pair * masks[e])
                total = term if total is None else total + term
            y_out[tok, lanes] = total
        return 0

    lax.fori_loop(0, x_in.shape[0] // SPAN, block, 0)


def entering_state(place, count, sums, decays, backward):
    inner = sums.shape[2]
    state = jnp.zeros((STATE, inner), F32)
    for turn in range(count):
        other = count - 1 - turn if backward else turn
        ahead = (place < other) if backward else (other < place)
        state = jnp.where(ahead, decays[other, 0:1] * state + sums[other].astype(F32), state)
    return state


def mix_out(state, local, decay, x, bc, z, s, wo, rowp, y_out, states_out, part_out, sq_out):
    inner = x.shape[1]
    spread = head_spread(inner)
    gain, skip = rowp[5:6], rowp[6:7]
    ones = jnp.ones((8, inner), F32)

    def block(q, state):
        tok = pl.ds(pl.multiple_of(q * SPAN, SPAN), SPAN)
        states_out[q] = state
        c = bc[tok, STATE:]
        carried = dot_split(jnp.exp(s[tok, :]), spread) * dot(c, state.astype(BF16))
        y = y_out[tok, :] + carried + skip * x[tok, :].astype(F32)
        y_out[tok, :] = y
        zf = z[tok, :].astype(F32)
        gated = y * (zf * sigmoid(zf))
        sq_out[:, tok] = dot_exact(ones, gated * gated, NT)
        part_out[tok, :] = dot((gated * gain).astype(BF16), wo[...], NT).astype(BF16)
        return decay[q, 0:1] * state + local[q]

    lax.fori_loop(0, x.shape[0] // SPAN, block, state)


def back_through_gate(
    inner_all, dmix, wo, y_in, z, x, bc, s, decay, token_scalars, rowp, cat_out, wide, dy_out, prior, normed_out
):
    inner = x.shape[1]
    spans = x.shape[0] // SPAN
    spread = head_spread(inner)
    gain = rowp[5:6]
    cols = columns_of(inner)

    def block(i, carry):
        grad_sum, gain_sum, skip_sum = carry
        q = spans - 1 - i
        tok = pl.ds(pl.multiple_of(q * SPAN, SPAN), SPAN)
        columns = token_scalars[:, tok].T
        inv, total_dot = columns[:, 0:1], columns[:, 1:2]
        zf = z[tok, :].astype(F32)
        sig = sigmoid(zf)
        act = zf * sig
        y = y_in[tok, :]
        gated = y * act
        d_no = dot(dmix[tok, :], wo[...])
        scaled = gated * inv
        normed_out[tok, :] = (scaled * gain).astype(BF16)
        gain_sum = gain_sum + jnp.sum(d_no * scaled, axis=0, keepdims=True)
        d_gated = inv * (d_no * gain) - gated * (inv * inv * inv * total_dot * (1.0 / inner_all))
        after = pl.ds(pl.multiple_of(q * SPAN + EDGE, EDGE), SPAN)
        cat_out[after, cols.z] = (d_gated * y * (sig * (1.0 + zf * (1.0 - sig)))).astype(BF16)
        dy = d_gated * act
        xf = x[tok, :].astype(F32)
        skip_sum = skip_sum + jnp.sum(dy * xf, axis=0, keepdims=True)
        dy_low = dy.astype(BF16)
        dy_out[tok, :] = dy_low
        scaled_dy = (dy_low.astype(F32) * dot_split(jnp.exp(s[tok, :]), spread)).astype(BF16)
        fresh = dot(bc[tok, STATE:], scaled_dy, TN)
        prior[q] = fresh
        return fresh + decay[q, 0:1] * grad_sum, gain_sum, skip_sum

    zero = jnp.zeros((1, inner), F32)
    grad_sum, gain_sum, skip_sum = lax.fori_loop(
        0, spans, block, (jnp.zeros((STATE, inner), F32), zero, zero)
    )
    decay_all = decay[0, 0:1]
    for q in range(1, spans):
        decay_all = decay_all * decay[q, 0:1]
    wide[...] = jnp.zeros_like(wide)
    wide[5:6] = gain_sum
    wide[6:7] = skip_sum
    return grad_sum, decay_all


def out_gradient(dmix, normed_out, gwo_out):
    def rows_of(i, _):
        rows = pl.ds(pl.multiple_of(i * SPAN, SPAN), SPAN)
        gwo_out[rows, :] = dot(dmix[:, rows], normed_out[...], TN).astype(BF16)
        return 0

    lax.fori_loop(0, dmix.shape[1] // SPAN, rows_of, 0)


def back_within_spans(dy_in, x_in, bc_in, s_in, dt_in, dpre, flow_out, sum_out):
    inner = x_in.shape[1]

    def block(q, _):
        at = pl.multiple_of(q * SPAN, SPAN)
        tok = pl.ds(at, SPAN)
        after = pl.ds(pl.multiple_of(at + EDGE, EDGE), SPAN)
        x_low, dy = x_in[tok, :], dy_in[tok, :]
        b, c = bc_in[tok, :STATE], bc_in[tok, STATE:]
        s, dt = s_in[tok, :], dt_in[tok, :]
        s_row = s.T
        cb = dot(b, c, NT)
        seen = iota((SPAN, SPAN), 0) <= iota((SPAN, SPAN), 1)
        masks = half_masks()
        d_cb = jnp.zeros((SPAN, SPAN), F32)
        lane = iota((SPAN, 128), 1)
        row_id = iota((128, SPAN), 0)
        sum_k = jnp.zeros((128, SPAN), F32)
        sum_t = jnp.zeros((SPAN, 128), F32)
        for pair in range(inner // 128):
            lanes = slice(pair * 128, pair * 128 + 128)
            x_pair, dy_pair = x_low[:, lanes], dy[:, lanes]
            total = None
            for e in range(2):
                h = pair * 2 + e
                d_scores = dot(x_pair * masks[e], dy_pair, NT)
                fade = jnp.exp(jnp.where(seen, s_row[h : h + 1, :] - s[:, h : h + 1], -1e30))
                dt_h = dt[:, h : h + 1]
                fade_cb = cb * fade
                term = dot((fade_cb * dt_h).astype(BF16), dy_pair * masks[e])
                total = term if total is None else total + term
                d_cb = d_cb + d_scores * (fade * dt_h)
                flow = d_scores * fade_cb
                sum_t = jnp.where(lane == h, jnp.sum(flow, axis=1, keepdims=True), sum_t)
                sum_k = jnp.where(row_id == h, jnp.sum(flow * dt_h, axis=0, keepdims=True), sum_k)
            dpre[after, lanes] = total
        d_cb_low = d_cb.astype(BF16)
        dpre[after, inner : inner + STATE] = dot(d_cb_low, c)
        dpre[after, inner + STATE :] = dot(d_cb_low, b, TN)
        flow_out[tok, :] = sum_k.T - sum_t * dt
        sum_out[tok, :] = sum_t
        return 0

    lax.fori_loop(0, x_in.shape[0] // SPAN, block, 0)


def back_through_states(
    grad, prior, decay, states, dy_in, x, bc, s_in, dt_in, dtraw, xin, bcin, rowp, bcp, headp, flow_in, sum_in,
    place, cat_out, step_out, row_out, bcrow_out,
    dpre, dend,
):
    inner = x.shape[1]
    spans = x.shape[0] // SPAN
    spread = head_spread(inner)
    up_tri = triangle(False)
    skip = rowp[6:7]
    rate = -jnp.exp(headp[0:1])
    bias = headp[1:2]
    width = inner + 2 * STATE

    def chain(i, grad):
        q = spans - 1 - i
        dend[q] = grad
        return prior[q] + decay[q, 0:1] * grad

    lax.fori_loop(0, spans, chain, grad)
    dpre[0:EDGE] = jnp.zeros((EDGE, width), F32)
    dpre[EDGE + spans * SPAN :] = jnp.zeros((EDGE, width), F32)
    bcrow_out[...] = jnp.zeros_like(bcrow_out)
    cols = columns_of(inner)
    pick = head_pick(place, inner // HEADDIM)
    cat_out[0:EDGE, cols.z] = jnp.zeros((EDGE, inner), BF16)
    cat_out[0:EDGE, cols.dt] = jnp.zeros((EDGE, 128), BF16)

    def block(q, _):
        at = pl.multiple_of(q * SPAN, SPAN)
        tok = pl.ds(at, SPAN)
        after = pl.ds(pl.multiple_of(at + EDGE, EDGE), SPAN)
        window = pl.ds(at, SPAN + EDGE)
        x_low, dy = x[tok, :], dy_in[tok, :]
        xf, dyf = x_low.astype(F32), dy.astype(F32)
        b, c = bc[tok, :STATE], bc[tok, STATE:]
        s, dt = s_in[tok, :], dt_in[tok, :]
        exp_s = jnp.exp(s)
        to_end = jnp.exp(s[SPAN - 1 : SPAN] - s)
        w = to_end * dt
        w_all, s_all = dot_split(w, spread), dot_split(exp_s, spread)
        state, grad = states[q], dend[q]
        state_low, grad_low = state.astype(BF16), grad.astype(BF16)
        carried = s_all * dot(c, state_low)
        ds = dot_split(dyf * carried, spread, NT)
        d_c = dot((dyf * s_all).astype(BF16), state_low, NT)
        d_w = dot(b, grad_low)
        d_b = dot((xf * w_all).astype(BF16), grad_low, NT)
        dx = dpre[after, 0:inner] + dyf * skip + d_w * w_all
        dsw = dot_split(d_w * xf, spread, NT)
        end = dsw * w
        ds = ds + flow_in[tok, :] - end
        held = dot_split(jnp.broadcast_to(jnp.sum(grad * state, axis=0, keepdims=True), (8, inner)), spread, NT)[0:1]
        last = jnp.sum(end, axis=0, keepdims=True) + held * exp_s[SPAN - 1 : SPAN]
        ds = ds + jnp.where(iota((SPAN, 128), 0) == SPAN - 1, last, 0.0)
        da = dot_exact(up_tri, ds)
        d_dt = sum_in[tok, :] + dsw * to_end + da * rate
        d_raw = d_dt * sigmoid(dtraw[tok, :].astype(F32) + bias)
        d_raw = jnp.where(iota((SPAN, 128), 1) < inner // HEADDIM, d_raw, 0.0)
        row_out[7:8, 0:128] += jnp.sum(da * (dt * rate), axis=0, keepdims=True)
        row_out[8:9, 0:128] += jnp.sum(d_raw, axis=0, keepdims=True)
        d_low = d_raw.astype(BF16)
        step_out[tok, :] = d_low
        cat_out[after, cols.dt] = dot(d_low, pick, NT).astype(BF16)

        win_x = xin[window, :].astype(F32)
        d_x = dx * silu_slope(conv_taps(win_x, rowp))
        dpre[after, 0:inner] = d_x
        for j in range(CONV):
            row_out[j : j + 1] += jnp.sum(d_x * win_x[EDGE - 3 + j : EDGE - 3 + j + SPAN], axis=0, keepdims=True)
        row_out[CONV : CONV + 1] += jnp.sum(d_x, axis=0, keepdims=True)
        win_bc = bcin[window, :].astype(F32)
        d_bc = dpre[after, inner:] + jnp.concatenate([d_b, d_c], axis=1)
        d_bc = d_bc * silu_slope(conv_taps(win_bc, bcp))
        dpre[after, inner:] = d_bc
        for j in range(CONV):
            bcrow_out[j : j + 1] += jnp.sum(d_bc * win_bc[EDGE - 3 + j : EDGE - 3 + j + SPAN], axis=0, keepdims=True)
        bcrow_out[CONV : CONV + 1] += jnp.sum(d_bc, axis=0, keepdims=True)
        return 0

    lax.fori_loop(0, spans, block, 0)

    def back(window, taps, rows):
        total = None
        for j in range(CONV):
            term = taps[j : j + 1] * window[CONV - 1 - j : CONV - 1 - j + rows]
            total = term if total is None else total + term
        return total.astype(BF16)

    cat_out[0:EDGE, cols.x] = back(dpre[0 : 2 * EDGE, 0:inner], rowp, EDGE)
    cat_out[0:EDGE, cols.bc] = back(dpre[0 : 2 * EDGE, inner:], bcp, EDGE)

    def conv_block(q, _):
        after = pl.ds(pl.multiple_of(q * SPAN + EDGE, EDGE), SPAN)
        window = pl.ds(pl.multiple_of(q * SPAN + EDGE, EDGE), SPAN + EDGE)
        cat_out[after, cols.x] = back(dpre[window, 0:inner], rowp, SPAN)
        cat_out[after, cols.bc] = back(dpre[window, inner:], bcp, SPAN)
        return 0

    lax.fori_loop(0, spans, conv_block, 0)


def project_back(cat, w, dn_out):
    cols = columns_of((w.shape[1] - 3 * STATE) // 2)
    dn_out[0:EDGE] = (
        dot(cat[0:EDGE, cols.x], w[:, cols.x], NT) + dot(cat[0:EDGE, cols.bc], w[:, cols.bc], NT)
    ).astype(BF16)

    def rows_of(q, _):
        after = pl.ds(pl.multiple_of(q * SPAN + EDGE, EDGE), SPAN)
        dn_out[after, :] = dot(cat[after, :], w[...], NT).astype(BF16)
        return 0

    lax.fori_loop(0, (cat.shape[0] - EDGE) // SPAN, rows_of, 0)


def weight_gradients(cat, steps, normed, gx_out, gz_out, gbc_out, gdt_out):
    inner = gx_out.shape[1]
    groups, parts, shard, _ = gbc_out.shape
    rows = parts * shard
    cols = columns_of(inner)

    def rows_of(g, _):
        at = pl.ds(pl.multiple_of(g * rows, 128), rows) if rows % 128 == 0 else pl.ds(g * rows, rows)
        edge, tokens = normed[0:EDGE, at], normed[EDGE:, at]
        both = dot(tokens, cat[EDGE:, 0 : 2 * inner], TN)
        gx_out[at, :] = (both[:, 0:inner] + dot(edge, cat[0:EDGE, cols.x], TN)).astype(BF16)
        gz_out[at, :] = both[:, inner:].astype(BF16)
        bc = dot(tokens, cat[EDGE:, cols.bc], TN) + dot(edge, cat[0:EDGE, cols.bc], TN)
        gbc_out[g] = bc.reshape(parts, shard, 2 * STATE).astype(BF16)
        gdt_out[g] = dot(steps[...], tokens, TN)[0:EDGE].astype(BF16)
        return 0

    if rows % 128 == 0:
        lax.fori_loop(0, groups, rows_of, 0)
    else:
        for g in range(groups):
            rows_of(g, 0)


HALF = 128
MESH = pl.DeviceIdType.MESH


class Links:
    def __init__(self, sends, recvs):
        self.z, self.p, self.c = lax.axis_index("z"), lax.axis_index("p"), lax.axis_index("head")
        self.groups = lax.axis_size("z")
        self.sends, self.recvs, self.used = sends, recvs, 0

    def copy(self, src, dst, device):
        i = self.used
        self.used += 1
        return pltpu.make_async_remote_copy(
            src_ref=src, dst_ref=dst, send_sem=self.sends.at[i], recv_sem=self.recvs.at[i],
            device_id=device, device_id_type=MESH,
        )

    def local(self, src, dst):
        i = self.used
        self.used += 1
        return pltpu.make_async_copy(src, dst, self.sends.at[i])

    def at(self, k, e):
        return (self.z, lax.bitwise_xor(self.p, jnp.int32(k)), lax.bitwise_xor(self.c, jnp.int32(e)))

    def last_of_plane(self):
        return jnp.logical_and(self.p == GROUP - 1, self.c == 1)

    def greet(self, plane=False, sibling=False, groups=False, edge=0):
        barrier = pltpu.get_barrier_semaphore()
        z, count = self.z, self.groups
        above = z < count - 1

        def signal(device):
            pl.semaphore_signal(barrier, 1, device_id=device, device_id_type=MESH)

        self.expected = jnp.int32(0)
        for k in range(GROUP):
            for e in range(2):
                if (k or e) if plane else (sibling and e and not k):
                    signal(self.at(k, e))
                    self.expected = self.expected + 1
        if groups:
            for k in range(1, count):
                signal((lax.rem(z + k, count), self.p, self.c))
            self.expected = self.expected + (count - 1)
        sending = jnp.logical_and(self.last_of_plane(), above)
        if edge == 1:
            pl.when(z > 0)(lambda: signal((z - 1, jnp.int32(GROUP - 1), jnp.int32(1))))
            self.expected = self.expected + 2 * GROUP * sending.astype(jnp.int32)
        if edge == -1:

            @pl.when(sending)
            def _():
                for p in range(GROUP):
                    for c in range(2):
                        signal((z + 1, jnp.int32(p), jnp.int32(c)))

            self.expected = self.expected + (z > 0).astype(jnp.int32)

    def meet(self):
        pl.semaphore_wait(pltpu.get_barrier_semaphore(), self.expected)

    def start_barrier(self, **who):
        self.greet(**who)
        self.meet()


class Chain:
    def __init__(self, links, pieces):
        z, p, c, groups = links.z, links.p, links.c, links.groups
        self.steps, self.now = [], 0
        for step in range(1, groups):
            found = []
            up, down = z - step + 1, z + step - 1
            for piece in pieces:
                block = piece(jnp.maximum(up, 0))
                sending = jnp.logical_and(up >= 0, z < groups - 1)
                found.append((sending, z - step >= 0, links.copy(block, block, (z + 1, p, c))))
                block = piece(jnp.minimum(down, groups - 1))
                sending = jnp.logical_and(down < groups, z > 0)
                found.append((sending, z + step < groups, links.copy(block, block, (z - 1, p, c))))
            self.steps.append(found)

    def begin(self):
        for sending, _, copy in self.steps[0]:
            pl.when(sending)(copy.start)

    def advance(self):
        if self.now + 1 < len(self.steps):
            for (_, receiving, copy), (sending, _, later) in zip(self.steps[self.now], self.steps[self.now + 1]):
                pl.when(receiving)(copy.wait_recv)
                pl.when(sending)(later.start)
            self.now += 1

    def complete(self):
        while self.now + 1 < len(self.steps):
            self.advance()
        for _, receiving, copy in self.steps[-1]:
            pl.when(receiving)(copy.wait_recv)

    def finish(self):
        for found in self.steps:
            for sending, _, copy in found:
                pl.when(sending)(copy.wait_send)


class Swap:
    def __init__(self, links, shard, staging, out, lanes, width):
        self.links, self.staging, self.out, self.lanes = links, staging, out, lanes

        def source(k):
            if shard.shape[1] == width:
                return shard
            to = lax.bitwise_xor(links.p, jnp.int32(k))
            return shard.at[:, pl.ds(pl.multiple_of(to * width, 128), width)]

        self.copies = [links.copy(source(k), staging.at[links.p], links.at(k, 0)) for k in (3, 1, 2)]
        self.keep = links.local(source(0), staging.at[links.p])

    def start(self):
        for copy in self.copies:
            copy.start()

    def settle(self):
        self.keep.wait()
        for copy in self.copies:
            copy.wait_recv()
        parts, shard, width = self.staging.shape
        rows = parts * shard
        first = self.links.z * rows
        if shard % EDGE == 0:
            for j in range(parts):
                self.out[pl.ds(pl.multiple_of(first + j * shard, EDGE), shard), self.lanes] = self.staging[j]
        else:
            block = self.staging[...].astype(F32).reshape(rows, width).astype(BF16)
            self.out[pl.ds(pl.multiple_of(first, EDGE), rows), self.lanes] = block

    def finish(self):
        for copy in self.copies:
            copy.wait_send()


class Collect:
    def __init__(self, links, grad, out):
        rows = grad.shape[0] // links.groups
        z, groups = links.z, links.groups

        def block(index):
            return grad.at[pl.ds(pl.multiple_of(index * rows, EDGE), rows)]

        self.keep = links.local(block(z), out.at[0])
        self.copies = []
        for k in range(1, groups):
            to = lax.rem(z + k, groups)
            self.copies.append(links.copy(block(to), out.at[k], (to, links.p, links.c)))

    def start(self):
        self.keep.start()
        for copy in self.copies:
            copy.start()

    def arrive(self):
        self.keep.wait()
        for copy in self.copies:
            copy.wait_recv()

    def finish(self):
        for copy in self.copies:
            copy.wait_send()


class Deliver:
    def __init__(self, links, parts, final, out):
        self.links, self.parts, self.final, self.out = links, parts, final, out
        inner = parts.shape[2]
        self.mine = pl.ds(pl.multiple_of(links.p * inner, 128), inner)
        self.copies = [
            links.copy(final.at[lax.bitwise_xor(links.p, jnp.int32(k))], out.at[:, self.mine], links.at(k, 0))
            for k in (3, 1, 2)
        ]

    def start(self):
        total = self.parts[0].astype(F32)
        for k in range(1, self.parts.shape[0]):
            total = total + self.parts[k].astype(F32)
        shard = self.final.shape[1]
        for j in range(GROUP):
            self.final[j] = total[j * shard : (j + 1) * shard].astype(BF16)
        for copy in self.copies:
            copy.start()
        self.out[:, self.mine] = self.final[self.links.p]

    def finish(self):
        for copy in self.copies:
            copy.wait()


class States:
    def __init__(self, links, backward, state, decay, states, decays):
        z, groups = links.z, links.groups
        self.links, self.refs = links, (state, decay, states, decays)
        self.found = []
        for k in range(1, groups):
            to, source = (z - k, z + k) if backward else (z + k, z - k)
            sending, receiving = (to >= 0, source < groups) if backward else (to < groups, source >= 0)
            device = (jnp.clip(to, 0, groups - 1), links.p, links.c)
            pair = [links.copy(state, states.at[z], device), links.copy(decay, decays.at[z], device)]
            self.found.append((sending, receiving, pair))

    def start(self):
        for sending, _, pair in self.found:

            @pl.when(sending)
            def _(pair=pair):
                for copy in pair:
                    copy.start()

    def arrive(self):
        for _, receiving, pair in self.found:

            @pl.when(receiving)
            def _(pair=pair):
                for copy in pair:
                    copy.wait_recv()

    def finish(self):
        for sending, _, pair in self.found:

            @pl.when(sending)
            def _(pair=pair):
                for copy in pair:
                    copy.wait_send()


class Gather:
    def __init__(self, links, out, base):
        self.links, self.out, self.base = links, out, base

        def place(k, c):
            row = base + lax.bitwise_xor(links.p, jnp.int32(k)) * (2 * HALF) + c * HALF
            return out.at[pl.ds(pl.multiple_of(row, EDGE), HALF), :]

        own = place(0, links.c)
        self.out_copies = [links.copy(own, own, links.at(k, 0)) for k in (3, 1, 2)]
        self.shared = [links.copy(own, own, links.at(0, 1))]
        self.shared += [links.copy(place(k, links.c), place(k, links.c), links.at(0, 1)) for k in (1, 2, 3)]
        self.arrivals = [self.out_copies[1], self.out_copies[2], self.out_copies[0]]

    def own(self, start, size):
        row = self.base + self.links.p * (2 * HALF) + self.links.c * HALF + start
        return pl.ds(pl.multiple_of(row, EDGE), size)

    def start(self):
        for copy in self.out_copies:
            copy.start()
        self.shared[0].start()

    def pass_on(self):
        for k in range(3):
            self.arrivals[k].wait_recv()
            self.shared[k + 1].start()

    def finish(self):
        for copy in self.shared:
            copy.wait_recv()
        for copy in self.shared + self.out_copies:
            copy.wait_send()


class EdgeForward:
    def __init__(self, links, gather):
        self.links = links
        tail = gather.out.at[gather.own(HALF - EDGE, EDGE), :]
        first = links.used
        links.used += 2 * GROUP + 1
        recv = links.recvs.at[first + 2 * GROUP]
        self.out = gather.out
        self.copies = [
            pltpu.make_async_remote_copy(
                src_ref=tail, dst_ref=gather.out.at[0:EDGE, :], send_sem=links.sends.at[first + p * 2 + c], recv_sem=recv,
                device_id=(links.z + 1, jnp.int32(p), jnp.int32(c)), device_id_type=MESH,
            )
            for p in range(GROUP)
            for c in range(2)
        ]
        self.sending = jnp.logical_and(links.last_of_plane(), links.z < links.groups - 1)

    def start(self):
        @pl.when(self.sending)
        def _():
            for copy in self.copies:
                copy.start()

        @pl.when(self.links.z == 0)
        def _():
            self.out[0:EDGE, :] = jnp.zeros((EDGE, self.out.shape[1]), self.out.dtype)

    def finish(self):
        pl.when(self.links.z > 0)(self.copies[0].wait_recv)

        @pl.when(self.sending)
        def _():
            for copy in self.copies:
                copy.wait_send()


class Scatter:
    def __init__(self, links, part, base, sib, total, peer):
        self.links, self.part, self.base = links, part, base
        self.sib, self.total, self.peer = sib, total, peer
        other = 1 - links.c
        self.to_sibling = {
            k: links.copy(part.at[self.rows(k, other, 0, HALF), :], sib.at[k], links.at(0, 1)) for k in (3, 1, 2, 0)
        }
        self.to_peer = {k: links.copy(total.at[k - 1], peer.at[k - 1], links.at(k, 0)) for k in (3, 1, 2)}

    def rows(self, k, c, start, size):
        row = self.base + lax.bitwise_xor(self.links.p, jnp.int32(k)) * (2 * HALF) + c * HALF + start
        return pl.ds(pl.multiple_of(row, EDGE), size)

    def start(self):
        for copy in self.to_sibling.values():
            copy.start()

    def reduce(self):
        for k in (3, 1, 2):
            self.to_sibling[k].wait_recv()

            def add(i, _, k=k):
                at = pl.ds(pl.multiple_of(i * 32, 32), 32)
                mine = self.part[self.rows(k, self.links.c, i * 32, 32), :].astype(F32)
                self.total[k - 1, at, :] = (mine + self.sib[k, at, :].astype(F32)).astype(BF16)
                return 0

            lax.fori_loop(0, HALF // 32, add, 0)
            self.to_peer[k].start()

    def arrive(self):
        self.to_sibling[0].wait_recv()
        for copy in self.to_peer.values():
            copy.wait_recv()

    def own(self, start, size):
        at = pl.ds(start, size)
        total = self.part[self.rows(0, self.links.c, start, size), :].astype(F32) + self.sib[0, at, :].astype(F32)
        for k in range(3):
            total = total + self.peer[k, at, :].astype(F32)
        return total

    def finish(self):
        for copy in list(self.to_sibling.values()) + list(self.to_peer.values()):
            copy.wait_send()


class SmallSum:
    def __init__(self, links, squares, slots):
        self.links, self.squares, self.slots = links, squares, slots
        self.copies = [
            links.copy(squares.at[:, self.lanes(k, e)], slots.at[2 * k + e - 1], links.at(k, e))
            for k in range(GROUP)
            for e in range(2)
            if k or e
        ]

    def lanes(self, k, e):
        links = self.links
        column = lax.bitwise_xor(links.p, jnp.int32(k)) * (2 * HALF) + lax.bitwise_xor(links.c, jnp.int32(e)) * HALF
        return pl.ds(pl.multiple_of(column, HALF), HALF)

    def start(self):
        for copy in self.copies:
            copy.start()

    def total(self):
        for copy in self.copies:
            copy.wait_recv()
        total = self.squares[:, self.lanes(0, 0)]
        for i in range(len(self.copies)):
            total = total + self.slots[i]
        return total

    def finish(self):
        for copy in self.copies:
            copy.wait_send()


class SmallGather:
    def __init__(self, links, out):
        self.out = out
        self.lanes = pl.ds(pl.multiple_of(links.p * (2 * HALF) + links.c * HALF, HALF), HALF)
        self.copies = [
            links.copy(out.at[:, self.lanes], out.at[:, self.lanes], links.at(k, e))
            for k in range(GROUP)
            for e in range(2)
            if k or e
        ]

    def start(self):
        for copy in self.copies:
            copy.start()

    def finish(self):
        for copy in self.copies:
            copy.wait()


def row_chunks(size=32):
    return [(start, size) for start in range(0, HALF, size)]


def rms_of(rows):
    return lax.rsqrt(jnp.mean(rows * rows, axis=-1, keepdims=True) + EPS)


def as_tile(columns):
    lane = iota((HALF, HALF), 1)
    wide = jnp.zeros((HALF, HALF), F32)
    for i, column in enumerate(columns):
        wide = jnp.where(lane == i, column, wide)
    return wide.T[0:8]


def grad_rows(links, scatter, edge_slots, grad, resid, gain, gain_out, start, size):
    at = slice(start, start + size)
    d_normed = scatter.own(start, size)
    if start + size == HALF:
        extra = edge_slots[0].astype(F32)
        for i in range(1, 2 * GROUP):
            extra = extra + edge_slots[i].astype(F32)
        used = jnp.logical_and(links.last_of_plane(), links.z < links.groups - 1)
        extra = jnp.where(used, extra, 0.0)
        d_normed = d_normed + jnp.concatenate([jnp.zeros((size - EDGE, extra.shape[1]), F32), extra])
    rows = resid[at]
    inv_rms = rms_of(rows)
    gain_sum = jnp.sum(d_normed * rows * inv_rms, axis=0, keepdims=True)
    gain_out[0:1] = gain_sum if start == 0 else gain_out[0:1] + gain_sum
    d_hidden = d_normed * gain[...]
    return (
        grad[at]
        + inv_rms * d_hidden
        - rows * (inv_rms * inv_rms * inv_rms * jnp.mean(d_hidden * rows, axis=-1, keepdims=True))
    )


class EdgeBackward:
    def __init__(self, links, part, slots):
        self.links = links
        first = links.used
        links.used += 2 * GROUP + 1
        me = links.p * 2 + links.c
        self.send = pltpu.make_async_remote_copy(
            src_ref=part.at[0:EDGE, :], dst_ref=slots.at[me], send_sem=links.sends.at[first], recv_sem=links.recvs.at[first + me],
            device_id=(links.z - 1, jnp.int32(GROUP - 1), jnp.int32(1)), device_id_type=MESH,
        )
        self.recvs = [
            pltpu.make_async_remote_copy(
                src_ref=part.at[0:EDGE, :], dst_ref=slots.at[i], send_sem=links.sends.at[first], recv_sem=links.recvs.at[first + i],
                device_id=(links.z, links.p, 1 - links.c), device_id_type=MESH,
            )
            for i in range(2 * GROUP)
        ]
        self.receiving = jnp.logical_and(links.last_of_plane(), links.z < links.groups - 1)

    def start(self):
        pl.when(self.links.z > 0)(self.send.start)

    def receive(self):
        @pl.when(self.receiving)
        def _():
            for copy in self.recvs:
                copy.wait_recv()

    def finish(self):
        pl.when(self.links.z > 0)(self.send.wait_send)


class SmallSums:
    def __init__(self, links, bc, vec, dt, wide, bc_out, vec_out, dt_out, wide_out, bufs):
        self.links = links
        self.bc, self.vec, self.dt, self.wide = bc, vec, dt, wide
        self.bc_out, self.vec_out, self.dt_out, self.wide_out = bc_out, vec_out, dt_out, wide_out
        self.bc_in, self.bc_sum, self.bc_far, self.vec_in, self.vec_far, self.dt_far, self.wide_far = bufs
        z, p, c, groups = links.z, links.p, links.c, links.groups
        self.first, self.vec_first, self.second, self.third = [], [], [], []
        for k in range(GROUP):
            for e in range(2):
                if not (k or e):
                    continue
                slot = 2 * k + e
                to_p, to_c = lax.bitwise_xor(p, jnp.int32(k)), lax.bitwise_xor(c, jnp.int32(e))
                device = links.at(k, e)
                for layer in range(len(bc)):
                    src = bc[layer].at[:, to_p, :, pl.ds(pl.multiple_of(to_c * STATE, STATE), STATE)]
                    self.first.append(links.copy(src, self.bc_in.at[layer, slot - 1], device))
                self.vec_first.append(links.copy(vec.at[to_p * 2 + to_c], self.vec_in.at[slot - 1], device))
                self.third.append(links.copy(vec_out.at[p * 2 + c], vec_out.at[p * 2 + c], device))
        for k in range(1, groups):
            to = lax.rem(z + k, groups)
            device = (to, p, c)
            for layer in range(len(bc)):
                self.second.append(links.copy(self.bc_sum.at[layer, to], self.bc_far.at[layer, k - 1], device))
            self.second.append(links.copy(self.vec_in.at[7], self.vec_far.at[k - 1], device))
            self.second.append(links.copy(dt.at[to], self.dt_far.at[k - 1], device))
            self.second.append(links.copy(wide, self.wide_far.at[k - 1], device))
        for k in range(1, GROUP):
            device = links.at(k, 0)
            self.third.append(links.copy(dt_out.at[p], dt_out.at[p], device))
            self.third.append(links.copy(wide_out.at[p], wide_out.at[p], device))
        lanes = pl.ds(pl.multiple_of(c * STATE, STATE), STATE)
        self.third.append(links.copy(bc_out.at[:, :, lanes], bc_out.at[:, :, lanes], links.at(0, 1)))

    def round_one(self):
        for copy in self.vec_first + self.first:
            copy.start()

    def round_two(self):
        links = self.links
        for copy in self.vec_first + self.first:
            copy.wait_recv()
        own_lanes = pl.ds(pl.multiple_of(links.c * STATE, STATE), STATE)
        for layer in range(len(self.bc)):

            def add(i, _, layer=layer):
                total = self.bc[layer][i, links.p, :, own_lanes].astype(F32)
                for slot in range(2 * GROUP - 1):
                    total = total + self.bc_in[layer, slot, i].astype(F32)
                self.bc_sum[layer, i] = total.astype(BF16)
                return 0

            lax.fori_loop(0, links.groups, add, 0)
        total = self.vec[links.p * 2 + links.c]
        for slot in range(2 * GROUP - 1):
            total = total + self.vec_in[slot]
        self.vec_in[7] = total
        for copy in self.second:
            copy.start()

    def round_three(self):
        links = self.links
        z, p, c = links.z, links.p, links.c
        for copy in self.second:
            copy.wait_recv()
        far = links.groups - 1
        lanes = pl.ds(pl.multiple_of(c * STATE, STATE), STATE)
        for layer in range(len(self.bc)):
            total = self.bc_sum[layer, z].astype(F32)
            for k in range(far):
                total = total + self.bc_far[layer, k].astype(F32)
            self.bc_out[layer, :, lanes] = total.astype(BF16)
        total = self.vec_in[7]
        dt_total = self.dt[z].astype(F32)
        wide_total = self.wide[...]
        for k in range(far):
            total = total + self.vec_far[k]
            dt_total = dt_total + self.dt_far[k].astype(F32)
            wide_total = wide_total + self.wide_far[k]
        self.vec_out[p * 2 + c] = total
        self.dt_out[p] = dt_total.astype(BF16)
        self.wide_out[p] = wide_total
        for copy in self.third:
            copy.start()

    def finish(self):
        for copy in self.third:
            copy.wait_recv()
        for copy in self.vec_first + self.first + self.second + self.third:
            copy.wait_send()


def weight_chain(links, w, inner):
    rows = w.shape[0] // links.groups
    first = columns_of(inner).bc.start
    half = pl.ds(pl.multiple_of(first + links.c * STATE, STATE), STATE)

    def at(index):
        return pl.ds(pl.multiple_of(index * rows, EDGE), rows)

    chain = Chain(links, [lambda i: w.at[at(i), 0:first], lambda i: w.at[at(i), half]])
    return chain, links.copy(w.at[:, half], w.at[:, half], links.at(0, 1))


def out_chain(links, wo):
    rows = wo.shape[0] // links.groups
    return Chain(links, [lambda i: wo.at[pl.ds(pl.multiple_of(i * rows, EDGE), rows), :]])


def weight_swaps(links, shards, stagings, w, inner):
    cols = columns_of(inner)
    half = pl.ds(pl.multiple_of(cols.bc.start + links.c * STATE, STATE), STATE)
    places = ((cols.x, inner), (cols.z, inner), (cols.dt, STATE), (half, STATE))
    return [Swap(links, shards[i], stagings[i], w, *places[i]) for i in range(4)]


def forward_layer(links, normed, w, wo, wo_chain, params, saved, part, squares, work):
    rowp, bcp, headp = params
    y, z, x, bc, s, dt, dtraw, xin, bcin, states, decay = saved
    ext, local, state_low, decay_row, states_in, decays_in = work
    carried = States(links, False, state_low, decay_row, states_in, decays_in)
    state_sum, decay_all = project_and_convolve(
        links.p, normed, w, rowp, bcp, headp, z, xin, bcin, x, bc, dtraw, dt, s, decay, ext, local
    )
    state_low[...] = state_sum.astype(BF16)
    decay_row[...] = jnp.broadcast_to(decay_all, decay_row.shape)
    carried.start()
    wo_chain.advance()
    mix_within_spans(x, bc, s, dt, y)
    wo_chain.complete()
    carried.arrive()
    state = entering_state(links.z, links.groups, states_in, decays_in, False)
    return carried, lambda: mix_out(state, local, decay, x, bc, z, s, wo, rowp, y, states, part, squares)


def first_kernel(inner_all, *refs):
    resid, cot, gain, next_gain, rowp, bcp, headp = refs[:7]
    shards, refs = (refs[7:12], refs[12:17]), refs[17:]
    normed, dmix, w, wo, next_w, next_wo = refs[:6]
    saved, refs = refs[6:17], refs[17:]
    resid_out, cot_out, mixed_out, inv_out, normed_out, fresh_out, part, squares = refs[:8]
    stagings, refs = (refs[8:13], refs[13:18]), refs[18:]
    work, (sib, total, peer, slots, sends, recvs) = refs[:6], refs[6:]
    links = Links(sends, recvs)
    z, p, c = links.z, links.p, links.c
    inner = wo.shape[1]
    rows = wo.shape[0] // links.groups

    swaps = weight_swaps(links, shards[0], stagings[0], w, inner)
    swap_o = Swap(links, shards[0][4], stagings[0][4], wo, slice(0, inner), inner)
    next_swaps = weight_swaps(links, shards[1], stagings[1], next_w, inner)
    next_o = Swap(links, shards[1][4], stagings[1][4], next_wo, slice(0, inner), inner)
    all_swaps = swaps + [swap_o] + next_swaps + [next_o]
    gather, other = Gather(links, normed, EDGE), Gather(links, dmix, 0)
    edge = EdgeForward(links, gather)
    chain, share = weight_chain(links, w, inner)
    chain_o = out_chain(links, wo)
    next_chain, next_share = weight_chain(links, next_w, inner)
    scatter = Scatter(links, part, 0, sib, total, peer)
    small = SmallSum(links, squares, slots)
    next_gather = Gather(links, normed_out, EDGE)
    next_edge = EdgeForward(links, next_gather)

    links.greet(plane=True, groups=True, edge=1)
    for swap in all_swaps:
        swap.keep.start()
    for start, size in row_chunks():
        at = pl.ds(pl.multiple_of(c * HALF + start, EDGE), size)
        rows_in = resid[at, :].astype(F32)
        resid_out[start : start + size] = rows_in
        normed[gather.own(start, size), :] = (rows_in * rms_of(rows_in) * gain[...]).astype(BF16)
        rows_in = cot[at, :]
        cot_out[start : start + size] = rows_in.astype(F32)
        dmix[other.own(start, size), :] = rows_in
    links.meet()
    for swap in swaps:
        swap.start()
    for swap in swaps:
        swap.settle()
    chain.begin()
    gather.start()
    edge.start()
    swap_o.start()
    gather.pass_on()
    for swap in next_swaps + [next_o]:
        swap.start()
    other.start()
    chain.advance()
    other.pass_on()
    chain.advance()
    gather.finish()
    edge.finish()
    for swap in [swap_o] + next_swaps + [next_o]:
        swap.settle()
    chain.complete()
    share.start()
    chain_o.begin()
    share.wait()
    carried, mix = forward_layer(
        links, normed, w, wo, chain_o, (rowp, bcp, headp), saved, part, squares, work
    )
    next_chain.begin()
    mix()
    scatter.start()
    small.start()
    scatter.reduce()
    next_chain.advance()
    scatter.arrive()
    inv = lax.rsqrt(small.total() * (1.0 / inner_all) + EPS)
    inv_out[...] = inv
    column = inv.T[:, 0:1]
    for start, size in row_chunks():
        at = slice(start, start + size)
        mixed = scatter.own(start, size)
        mixed_out[at] = mixed
        fresh = resid_out[at] + column[at] * mixed
        fresh_out[at] = fresh
        normed_out[next_gather.own(start, size), :] = (fresh * rms_of(fresh) * next_gain[...]).astype(BF16)
    next_gather.start()
    next_edge.start()
    next_chain.advance()
    next_gather.pass_on()
    next_chain.complete()
    next_share.start()
    other.finish()
    scatter.finish()
    small.finish()
    next_gather.finish()
    next_edge.finish()
    carried.finish()
    for swap in all_swaps:
        swap.finish()
    for one in (chain, chain_o, next_chain):
        one.finish()
    next_share.wait()


def second_kernel(inner_all, *refs):
    normed, w, wo_own, rowp, bcp, headp, resid, cot = refs[:8]
    wo, refs = refs[8], refs[9:]
    saved, refs = refs[:11], refs[11:]
    block_out, scalars_out, part, squares = refs[:4]
    work, (sib, total, peer, slots, sends, recvs) = refs[4:10], refs[10:]
    links = Links(sends, recvs)
    rows = wo_own.shape[0]
    keep = links.local(wo_own, wo.at[pl.ds(pl.multiple_of(links.z * rows, EDGE), rows), :])
    chain_o = out_chain(links, wo)
    scatter = Scatter(links, part, 0, sib, total, peer)
    small = SmallSum(links, squares, slots)
    spread = SmallGather(links, scalars_out)
    at = pl.ds(pl.multiple_of(links.c * HALF, HALF), HALF)
    share = links.copy(block_out.at[at, :], block_out.at[at, :], links.at(0, 1))
    keep.start()
    links.greet(plane=True, groups=True)
    keep.wait()
    links.meet()
    chain_o.begin()
    carried, mix = forward_layer(
        links, normed, w, wo, chain_o, (rowp, bcp, headp), saved, part, squares, work
    )
    mix()
    scatter.start()
    small.start()
    scatter.reduce()
    scatter.arrive()
    inv = lax.rsqrt(small.total() * (1.0 / inner_all) + EPS)
    column = inv.T[:, 0:1]
    dots = []
    for start, size in row_chunks():
        at = slice(start, start + size)
        mixed = scatter.own(start, size)
        dots.append(jnp.sum(cot[at] * mixed, axis=-1, keepdims=True))
        block_out[pl.ds(pl.multiple_of(links.c * HALF + start, EDGE), size), :] = (
            resid[at] + column[at] * mixed
        ).astype(BF16)
    scalars_out[:, spread.lanes] = as_tile([column, jnp.concatenate(dots)])
    spread.start()
    share.start()
    scatter.finish()
    small.finish()
    carried.finish()
    chain_o.finish()
    spread.finish()
    share.wait()


def backward_layer(links, inner_all, dmix, scalars, wo, params, saved, outs, work, delivers):
    rowp, bcp, headp = params
    y, z, x, bc, s, dt, dtraw, xin, bcin, states, decay = saved
    cat, steps, go_parts, wide, bc_rows = outs
    dy, gwo, normed_out, prior, dend, dpre, flow, sums, state_low, decay_row, states_in, decays_in = work
    carried = States(links, True, state_low, decay_row, states_in, decays_in)
    collect = Collect(links, gwo, go_parts)
    grad_sum, decay_all = back_through_gate(
        inner_all, dmix, wo, y, z, x, bc, s, decay, scalars, rowp, cat, wide, dy, prior, normed_out
    )
    state_low[...] = grad_sum.astype(BF16)
    decay_row[...] = jnp.broadcast_to(decay_all, decay_row.shape)
    links.meet()
    carried.start()
    for deliver in delivers:
        deliver.start()
    out_gradient(dmix, normed_out, gwo)
    back_within_spans(dy, x, bc, s, dt, dpre, flow, sums)
    carried.arrive()
    collect.start()
    grad = entering_state(links.z, links.groups, states_in, decays_in, True)
    back_through_states(
        grad, prior, decay, states, dy, x, bc, s, dt, dtraw, xin, bcin, rowp, bcp, headp, flow, sums,
        links.p, cat, steps, wide, bc_rows, dpre, dend,
    )
    return carried, collect


def put_vector(vec, row, values):
    for i in range(values.shape[0]):
        for j in range(values.shape[1] // 128):
            vec[row // 8, row % 8 : row % 8 + 1, :] = values[i : i + 1, j * 128 : j * 128 + 128]
            row += 1


def third_kernel(inner_all, *refs):
    dmix, scalars, wo, w, normed, rowp, bcp, headp, grad, resid, gain, mixed, inv = refs[:13]
    saved, refs = refs[13:24], refs[24:]
    dmix_out, scalars_out, grad_out, go_parts, gx_parts, gz_parts, gbc, gdt, wide, vec = refs[:10]
    work, refs = refs[10:22], refs[22:]
    cat, steps, bc_rows, part, gx, gz, gain_row, sib, total, peer, edge_slots, sends, recvs = refs
    links = Links(sends, recvs)
    scatter = Scatter(links, part, EDGE, sib, total, peer)
    edge = EdgeBackward(links, part, edge_slots)
    gather = Gather(links, dmix_out, 0)
    spread = SmallGather(links, scalars_out)
    collects = [Collect(links, gx, gx_parts), Collect(links, gz, gz_parts)]
    edge_slots[...] = jnp.zeros_like(edge_slots)
    links.greet(plane=True, groups=True, edge=-1)
    carried, collect = backward_layer(
        links, inner_all, dmix, scalars, wo, (rowp, bcp, headp), saved, (cat, steps, go_parts, wide, bc_rows), work, []
    )
    project_back(cat, w, part)
    edge.start()
    scatter.start()
    scatter.reduce()
    weight_gradients(cat, steps, normed, gx, gz, gbc, gdt)
    for one in collects:
        one.start()
    scatter.arrive()
    edge.receive()
    gain_row[...] = jnp.zeros_like(gain_row)
    dots = []
    for start, size in row_chunks():
        at = slice(start, start + size)
        fresh = grad_rows(links, scatter, edge_slots, grad, resid, gain, gain_row, start, size)
        grad_out[at] = fresh
        low = fresh.astype(BF16)
        dmix_out[gather.own(start, size), :] = low
        dots.append(jnp.sum(low.astype(F32) * mixed[at], axis=-1, keepdims=True))
    scalars_out[:, spread.lanes] = as_tile([inv[...].T[:, 0:1], jnp.concatenate(dots)])
    gather.start()
    spread.start()
    vec[...] = jnp.zeros_like(vec)
    model = gain_row.shape[1]
    put_vector(vec, model // 128, gain_row[0:1])
    put_vector(vec, 2 * (model // 128) + 2 * (CONV + 1), bc_rows[0 : CONV + 1])
    gather.pass_on()
    scatter.finish()
    edge.finish()
    gather.finish()
    spread.finish()
    carried.finish()
    for one in [collect] + collects:
        one.arrive()
        one.finish()


def fourth_kernel(inner_all, *refs):
    dmix, scalars, wo, w, normed, rowp, bcp, headp, grad, resid, gain = refs[:11]
    saved, refs = refs[11:22], refs[22:]
    above, refs = refs[:3], refs[3:]
    above_bc, above_dt, above_wide, above_vec = refs[:4]
    out, gx_out, gz_out, go_out = refs[4:8]
    above_out, refs = refs[8:11], refs[11:]
    bc_out, vec_out, dt_out, wide_out = refs[:4]
    work, refs = refs[4:16], refs[16:]
    cat, steps, bc_rows, part, gx, gz, gain_row, sib, total, peer, edge_slots = refs[:11]
    go_parts, gx_parts, gz_parts, final, gbc, gdt, wide, vec, steps_all, wide_all = refs[11:21]
    bufs, (sends, recvs) = refs[21:28], refs[28:]
    links = Links(sends, recvs)
    scatter = Scatter(links, part, EDGE, sib, total, peer)
    edge = EdgeBackward(links, part, edge_slots)
    at = pl.ds(pl.multiple_of(links.c * HALF, HALF), HALF)
    share = links.copy(out.at[at, :], out.at[at, :], links.at(0, 1))
    collects = [Collect(links, gx, gx_parts), Collect(links, gz, gz_parts)]
    delivers = [Deliver(links, above[i], final.at[i], above_out[i]) for i in range(3)]
    own_delivers = [
        Deliver(links, parts, final.at[3 + i], place)
        for i, (parts, place) in enumerate(((go_parts, go_out), (gx_parts, gx_out), (gz_parts, gz_out)))
    ]
    small = SmallSums(
        links, (gbc, above_bc), vec, steps_all, wide_all, bc_out, vec_out, dt_out, wide_out, bufs
    )
    edge_slots[...] = jnp.zeros_like(edge_slots)
    links.greet(plane=True, groups=True, edge=-1)
    carried, collect = backward_layer(
        links, inner_all, dmix, scalars, wo, (rowp, bcp, headp), saved, (cat, steps, go_parts, wide, bc_rows), work,
        delivers,
    )
    weight_gradients(cat, steps, normed, gx, gz, gbc, gdt)
    for one in collects:
        one.start()
    project_back(cat, w, part)
    edge.start()
    scatter.start()
    scatter.reduce()
    steps_all[:, 0:EDGE, :] = gdt[...]
    steps_all[:, EDGE:, :] = above_dt[...]
    wide_all[0:16] = wide[...]
    wide_all[16:32] = above_wide[...]
    scatter.arrive()
    edge.receive()
    gain_row[...] = jnp.zeros_like(gain_row)
    for start, size in row_chunks():
        fresh = grad_rows(links, scatter, edge_slots, grad, resid, gain, gain_row, start, size)
        out[pl.ds(pl.multiple_of(links.c * HALF + start, EDGE), size), :] = fresh.astype(BF16)
    share.start()
    vec[...] = above_vec[...]
    put_vector(vec, 0, gain_row[0:1])
    put_vector(vec, 2 * (gain_row.shape[1] // 128), bc_rows[0 : CONV + 1])
    small.round_one()
    collect.arrive()
    own_delivers[0].start()
    small.round_two()
    small.round_three()
    for i in range(2):
        collects[i].arrive()
        own_delivers[i + 1].start()
    small.finish()
    scatter.finish()
    edge.finish()
    share.wait()
    carried.finish()
    for one in [collect] + collects:
        one.finish()
    for deliver in delivers + own_delivers:
        deliver.finish()


def call(body, outs, *args, scratch=(), collective=None, copies=0):
    vmem = pl.BlockSpec(memory_space=pltpu.VMEM)
    scratch = [pltpu.VMEM(shape, kind) for shape, kind in scratch]
    if collective is not None:
        scratch += [pltpu.SemaphoreType.DMA((copies,)), pltpu.SemaphoreType.DMA((copies,))]
    return pl.pallas_call(
        body,
        out_shape=tuple(jax.ShapeDtypeStruct(shape, kind) for shape, kind in outs),
        in_specs=[vmem] * len(args),
        out_specs=tuple([vmem] * len(outs)),
        scratch_shapes=scratch,
        compiler_params=pltpu.CompilerParams(
            vmem_limit_bytes=VMEM_BYTES, collective_id=collective, has_side_effects=collective is not None
        ),
    )(*args)


def on_device(resid_in, cotangent, norm_gain, w_zx, w_dt, w_bc, conv_x, conv_bc, head_params, gated_gain, w_out):
    layers, model = norm_gain.shape
    groups = lax.axis_size("z")
    level, place, core = lax.axis_index("z"), lax.axis_index("p"), lax.axis_index("head")
    shard = w_dt.shape[1]
    inner_core = conv_x.shape[2]
    inner = inner_core // GROUP
    heads_core = head_params.shape[2]
    heads = heads_core // GROUP
    inner_all = inner_core * lax.axis_size("head")
    length = resid_in.shape[1]
    tokens = GROUP * length
    spans = tokens // SPAN
    rows = GROUP * shard

    def my_part(array, size):
        return lax.dynamic_slice_in_dim(array, place * size, size, array.ndim - 1)

    row_all, bc_all, head_all = [], [], []
    conv_mine = my_part(conv_x, inner).astype(F32)
    gain_mine = my_part(gated_gain, inner).astype(F32)
    head_mine = my_part(head_params, heads)
    gains = [norm_gain[layer].astype(F32)[None] for layer in range(layers)]
    for layer in range(layers):
        skip = jnp.repeat(head_mine[layer, 2], HEADDIM)
        row_all.append(
            jnp.concatenate([conv_mine[layer], gain_mine[layer][None], skip[None], jnp.zeros((1, inner), F32)])
        )
        bc_all.append(jnp.pad(conv_bc[layer].astype(F32), ((0, 3), (0, 0))))
        head_all.append(jnp.pad(head_mine[layer], ((0, 5), (0, 128 - heads))))

    def shards_of(layer):
        half = lax.dynamic_slice_in_dim(w_bc[layer], core * STATE, STATE, 1)
        steps = jnp.pad(w_dt[layer], ((0, 0), (0, STATE - heads_core)))
        return w_zx[layer, 1], w_zx[layer, 0], steps, half, w_out[layer].T

    half_scratch = [
        ((GROUP, HALF, model), BF16),
        ((GROUP - 1, HALF, model), BF16),
        ((GROUP - 1, HALF, model), BF16),
    ]
    slots = ((2 * GROUP - 1, 8, HALF), F32)
    edges = ((2 * GROUP, EDGE, model), BF16)
    own_rows = ((HALF, model), F32)
    all_rows, edged_rows = ((tokens, model), BF16), ((tokens + EDGE, model), BF16)
    columns = columns_of(inner).size
    w_shape, wo_shape = ((model, columns), BF16), ((model, inner), BF16)
    tile = ((8, HALF), F32)
    scalars = ((8, tokens), F32)
    state_shape = ((spans, STATE, inner), F32)
    state_scratch = [
        ((STATE, inner), BF16),
        ((8, inner), F32),
        ((groups, STATE, inner), BF16),
        ((groups, 8, inner), F32),
    ]
    saved_shapes = [
        ((tokens, inner), F32),
        ((tokens, inner), BF16),
        ((tokens, inner), BF16),
        ((tokens, 2 * STATE), BF16),
        ((tokens, 128), F32),
        ((tokens, 128), F32),
        ((tokens, 128), BF16),
        ((tokens + EDGE, inner), BF16),
        ((tokens + EDGE, 2 * STATE), BF16),
        state_shape,
        ((spans, 8, inner), F32),
    ]
    forward_scratch = [((tokens + EDGE, inner + 2 * STATE), F32), state_shape] + state_scratch

    def params(layer):
        return row_all[layer], bc_all[layer], head_all[layer]

    stagings = [((GROUP, shard, width), BF16) for width in (inner, inner, STATE, STATE, inner)]
    results = call(
        functools.partial(first_kernel, inner_all),
        [edged_rows, all_rows, w_shape, wo_shape, w_shape, wo_shape]
        + saved_shapes
        + [own_rows, own_rows, own_rows, tile, edged_rows, own_rows],
        resid_in[0], cotangent[0], gains[0], gains[1], *params(0), *shards_of(0), *shards_of(1),
        scratch=[all_rows, scalars] + stagings + stagings + forward_scratch + half_scratch + [slots],
        collective=0, copies=160 + 10 * (groups - 1) + 2 * groups,
    )
    normed0, d_mix, w0, wo0, w1, wo1 = results[:6]
    saved0 = results[6:17]
    resid0, grad, mixed, inv, normed1, resid1 = results[17:]
    wo_own = lax.dynamic_slice_in_dim(wo1, level * rows, rows, 0)
    results = call(
        functools.partial(second_kernel, inner_all),
        [wo_shape] + saved_shapes + [((length, model), BF16), scalars],
        normed1, w1, wo_own, *params(1), resid1, grad,
        scratch=[all_rows, scalars] + forward_scratch + half_scratch + [slots],
        collective=1, copies=60 + 4 * groups,
    )
    wo1, saved1, (block_out, token_scalars) = results[0], results[1:12], results[12:]

    grad_parts = ((groups, rows, inner), BF16)
    back_scratch = [
        ((tokens, inner), BF16),
        wo_shape,
        ((tokens, inner), BF16),
        state_shape,
        state_shape,
        ((tokens + 2 * EDGE, inner + 2 * STATE), F32),
        ((tokens, 128), F32),
        ((tokens, 128), F32),
    ] + state_scratch
    more_scratch = [
        ((tokens + EDGE, columns), BF16),
        ((tokens, 128), BF16),
        ((8, 2 * STATE), F32),
        edged_rows,
        wo_shape,
        wo_shape,
        ((8, model), F32),
    ]
    bc_grad = ((groups, GROUP, shard, 2 * STATE), BF16)
    dt_grad = ((groups, EDGE, rows), BF16)
    wide_grad = ((16, inner), F32)
    vec_shape = ((2 * GROUP, 8, 128), F32)
    d_mix, token_scalars, grad, go_parts, gx_parts, gz_parts, gbc, gdt, wide, vec = call(
        functools.partial(third_kernel, inner_all),
        [all_rows, scalars, own_rows, grad_parts, grad_parts, grad_parts, bc_grad, dt_grad, wide_grad, vec_shape],
        d_mix, token_scalars, wo1, w1, normed1, *params(1), grad, resid1, gains[1], mixed, inv, *saved1,
        scratch=back_scratch + more_scratch + half_scratch + [edges],
        collective=2, copies=60 + 6 * groups,
    )
    far = groups - 1
    rows_shape = ((shard, inner_core), BF16)
    dt_shape, wide_shape = (layers * EDGE, rows), (layers * 16, inner)
    grad_input, gx0, gz0, go0, gx1, gz1, go1, g_bc, vec, g_dt, wide = call(
        functools.partial(fourth_kernel, inner_all),
        [((length, model), BF16)]
        + [rows_shape] * 6
        + [
            ((layers, shard, 2 * STATE), BF16),
            vec_shape,
            ((GROUP, *dt_shape), BF16),
            ((GROUP, *wide_shape), F32),
        ],
        d_mix, token_scalars, wo0, w0, normed0, *params(0), grad, resid0, gains[0], *saved0,
        gx_parts, gz_parts, go_parts, gbc, gdt, wide, vec,
        scratch=back_scratch + more_scratch + half_scratch + [
            edges,
            grad_parts,
            grad_parts,
            grad_parts,
            ((6, GROUP, shard, inner), BF16),
            bc_grad,
            dt_grad,
            wide_grad,
            vec_shape,
            ((groups, *dt_shape), BF16),
            (wide_shape, F32),
            ((layers, 2 * GROUP - 1, groups, shard, STATE), BF16),
            ((layers, groups, shard, STATE), BF16),
            ((layers, far, shard, STATE), BF16),
            ((2 * GROUP, 8, 128), F32),
            ((far, 8, 128), F32),
            ((far, *dt_shape), BF16),
            ((far, *wide_shape), F32),
        ],
        collective=3, copies=120 + 12 * groups,
    )
    delivered = ((gx0, gz0, go0), (gx1, gz1, go1))
    vec = vec.reshape(-1)
    grad_gain = vec[: layers * model].reshape(layers, model)
    grad_conv_bc = vec[layers * model :][: layers * (CONV + 1) * 2 * STATE].reshape(layers, CONV + 1, 2 * STATE)
    wide = wide.reshape(GROUP, layers, 16, inner)
    whole = jnp.moveaxis(wide, 0, 2).reshape(layers, 16, inner_core)
    skip_grad = jnp.sum(whole[:, CONV + 2].reshape(layers, heads_core, HEADDIM), axis=-1)
    tall = jnp.moveaxis(wide[:, :, CONV + 3 : CONV + 5, :heads], 0, 2).reshape(layers, 2, heads_core)
    grad_heads = jnp.concatenate([tall, skip_grad[:, None]], axis=1)
    g_dt = lax.dynamic_slice_in_dim(g_dt.reshape(GROUP, layers, EDGE, GROUP, shard), place, 1, 3)[:, :, :heads, 0]
    grad_dt = jnp.transpose(g_dt, (1, 3, 0, 2)).reshape(layers, shard, heads_core)
    low = lambda a: a.astype(BF16)
    return (
        block_out[None],
        grad_input[None],
        low(grad_gain),
        jnp.stack([jnp.stack([delivered[layer][1], delivered[layer][0]]) for layer in range(layers)]),
        grad_dt,
        g_bc,
        low(whole[:, : CONV + 1]),
        low(grad_conv_bc),
        low(grad_heads),
        low(whole[:, CONV + 1]),
        jnp.stack([delivered[layer][2].T for layer in range(layers)]),
    )


def solution(mesh):
    seq, head = mesh.shape["seq"], mesh.shape["head"]
    split = Mesh(mesh.devices.reshape(seq // GROUP, GROUP, head), ("z", "p", "head"))
    seq_axes = ("z", "p")
    specs = (
        P(None, seq_axes, None),
        P(None, seq_axes, None),
        P(),
        P(None, None, seq_axes, "head"),
        P(None, seq_axes, "head"),
        P(None, seq_axes, None),
        P(None, None, "head"),
        P(),
        P(None, None, "head"),
        P(None, "head"),
        P(None, "head", seq_axes),
    )
    return jax.shard_map(on_device, mesh=split, in_specs=specs, out_specs=specs, check_vma=False)
```

```python
import functools
import types
import typing

import jax
import jax.numpy as jnp
from jax import lax
from jax.experimental import pallas as pl
from jax.experimental.pallas import tpu as pltpu
from jax.sharding import Mesh, PartitionSpec as P

HEADDIM = 64
STATE = 128
CONV = 4
SPAN = 256
GROUP = 4
EDGE = 16
EPS = 1e-05
HIGH = lax.Precision.HIGHEST
F32, BF16 = jnp.float32, jnp.bfloat16
NN = (((1,), (0,)), ((), ()))
NT = (((1,), (1,)), ((), ()))
TN = (((0,), (0,)), ((), ()))
VMEM_BYTES = 58 << 20


def dot(a, b, dims=NN):
    return lax.dot_general(a, b, dims, preferred_element_type=F32)


def dot_exact(a, b, dims=NN):
    return lax.dot_general(a, b, dims, precision=HIGH, preferred_element_type=F32)


def dot_split(a, b, dims=NN):
    high = a.astype(BF16)
    rest = (a - high.astype(F32)).astype(BF16)
    return dot(high, b, dims) + dot(rest, b, dims)


def sigmoid(v):
    return 1.0 / (1.0 + jnp.exp(-v))


def softplus(v):
    return jnp.maximum(v, 0.0) + jnp.log1p(jnp.exp(-jnp.abs(v)))


def silu_slope(v):
    sig = sigmoid(v)
    return sig * (1.0 + v * (1.0 - sig))


def iota(shape, dim):
    return lax.broadcasted_iota(jnp.int32, shape, dim)


def head_spread(inner):
    return (iota((128, inner), 0) == lax.shift_right_logical(iota((128, inner), 1), 6)).astype(BF16)


def triangle(lower):
    rows, cols = iota((SPAN, SPAN), 0), iota((SPAN, SPAN), 1)
    return ((cols <= rows) if lower else (cols >= rows)).astype(F32)


def half_masks():
    lane = iota((SPAN, 128), 1)
    return (lane < HEADDIM).astype(BF16), (lane >= HEADDIM).astype(BF16)


def conv_taps(window, taps):
    total = jnp.broadcast_to(taps[CONV : CONV + 1], (SPAN, window.shape[1]))
    for j in range(CONV):
        total = total + taps[j : j + 1] * window[EDGE - 3 + j : EDGE - 3 + j + SPAN]
    return total


def head_pick(place, heads):
    row, col = iota((128, 128), 0), iota((128, 128), 1)
    return jnp.logical_and(row == place * heads + col, col < heads).astype(BF16)


class Columns(typing.NamedTuple):
    x: slice
    z: slice
    dt: slice
    bc: slice
    size: int


def columns_of(inner):
    first = 2 * inner + 128
    return Columns(
        slice(0, inner), slice(inner, 2 * inner), slice(2 * inner, first), slice(first, first + 2 * STATE), first + 2 * STATE
    )


def project_and_convolve(
    place, normed, w, rowp, bcp, headp,
    z_out, xin_out, bcin_out, x_out, bc_out, dtraw_out, dt_out, s_out, decay_out,
    ext, local, at_block,
):
    inner = x_out.shape[1]
    spans = x_out.shape[0] // SPAN

    cols = columns_of(inner)
    edge = normed[0:EDGE]
    edge_x = dot(edge, w[:, cols.x]).astype(BF16)
    edge_bc = dot(edge, w[:, cols.bc]).astype(BF16)
    xin_out[0:EDGE] = edge_x
    bcin_out[0:EDGE] = edge_bc
    ext[0:EDGE, 0:inner] = edge_x.astype(F32)
    ext[0:EDGE, inner:] = edge_bc.astype(F32)
    spread = head_spread(inner)
    pick = head_pick(place, inner // HEADDIM)
    low_tri = triangle(True)
    rate = -jnp.exp(headp[0:1])
    bias = headp[1:2]

    def block(q, carry):
        state_sum, decay_all = carry
        at = pl.multiple_of(q * SPAN, SPAN)
        tok = pl.ds(at, SPAN)
        after = pl.ds(pl.multiple_of(at + EDGE, EDGE), SPAN)
        at_block(q)
        product = dot(normed[after, :], w[...]).astype(BF16)
        z_out[tok, :] = product[:, cols.z]
        xin, bcin = product[:, cols.x], product[:, cols.bc]
        dtraw = dot(product[:, cols.dt], pick).astype(BF16)
        xin_out[after, :] = xin
        bcin_out[after, :] = bcin
        dtraw_out[tok, :] = dtraw
        ext[after, 0:inner] = xin.astype(F32)
        ext[after, inner:] = bcin.astype(F32)
        window = pl.ds(at, SPAN + EDGE)
        pre_x = conv_taps(ext[window, 0:inner], rowp)
        x = (pre_x * sigmoid(pre_x)).astype(BF16)
        x_out[tok, :] = x
        pre_bc = conv_taps(ext[window, inner:], bcp)
        bc = (pre_bc * sigmoid(pre_bc)).astype(BF16)
        bc_out[tok, :] = bc
        dt = softplus(dtraw.astype(F32) + bias)
        s = dot_exact(low_tri, dt * rate)
        dt_out[tok, :] = dt
        s_out[tok, :] = s
        to_end = jnp.exp(s[SPAN - 1 : SPAN] - s) * dt
        weighted = (x.astype(F32) * dot_split(to_end, spread)).astype(BF16)
        fresh = dot(bc[:, :STATE], weighted, TN)
        decay = dot_split(jnp.exp(s[SPAN - 8 : SPAN]), spread)[7:8]
        local[q] = fresh
        decay_out[q] = jnp.broadcast_to(decay, (8, inner))
        return state_sum * decay + fresh, decay_all * decay

    return lax.fori_loop(0, spans, block, (jnp.zeros((STATE, inner), F32), jnp.ones((1, inner), F32)))


def mix_within_spans(x_in, bc_in, s_in, dt_in, y_out):
    inner = x_in.shape[1]

    def block(q, _):
        tok = pl.ds(pl.multiple_of(q * SPAN, SPAN), SPAN)
        x, bc, s = x_in[tok, :], bc_in[tok, :], s_in[tok, :]
        s_row, dt_row = s.T, dt_in[tok, :].T
        cb = dot(bc[:, STATE:], bc[:, :STATE], NT)
        causal = iota((SPAN, SPAN), 1) <= iota((SPAN, SPAN), 0)
        masks = half_masks()
        for pair in range(inner // 128):
            lanes = slice(pair * 128, pair * 128 + 128)
            x_pair = x[:, lanes]
            total = None
            for e in range(2):
                h = pair * 2 + e
                gap = jnp.where(causal, s[:, h : h + 1] - s_row[h : h + 1, :], -1e30)
                scores = (cb * (jnp.exp(gap) * dt_row[h : h + 1, :])).astype(BF16)
                term = dot(scores, x_pair * masks[e])
                total = term if total is None else total + term
            y_out[tok, lanes] = total
        return 0

    lax.fori_loop(0, x_in.shape[0] // SPAN, block, 0)


def entering_state(place, count, sums, decays, backward):
    inner = sums.shape[2]
    state = jnp.zeros((STATE, inner), F32)
    for turn in range(count):
        other = count - 1 - turn if backward else turn
        ahead = (place < other) if backward else (other < place)
        state = jnp.where(ahead, decays[other, 0:1] * state + sums[other].astype(F32), state)
    return state


def chain_states(state, local, decay, states_out):
    def block(q, state):
        states_out[q] = state
        return decay[q, 0:1] * state + local[q]

    lax.fori_loop(0, local.shape[0], block, state)


def mix_out(q, states, x, bc, z, s, wo, rowp, y_out, part_out, sq_out):
    inner = x.shape[1]
    tok = pl.ds(pl.multiple_of(q * SPAN, SPAN), SPAN)
    carried = dot_split(jnp.exp(s[tok, :]), head_spread(inner)) * dot(bc[tok, STATE:], states[q].astype(BF16))
    y = y_out[tok, :] + carried + rowp[6:7] * x[tok, :].astype(F32)
    y_out[tok, :] = y
    zf = z[tok, :].astype(F32)
    gated = y * (zf * sigmoid(zf))
    sq_out[:, tok] = dot_exact(jnp.ones((8, inner), F32), gated * gated, NT)
    part_out[tok, :] = dot((gated * rowp[5:6]).astype(BF16), wo[...], NT).astype(BF16)


def back_through_gate(
    inner_all, dmix, wo, y_in, z, x, bc, s, decay, token_scalars, rowp, cat_out, wide, dy_out, prior, normed_out
):
    inner = x.shape[1]
    spans = x.shape[0] // SPAN
    spread = head_spread(inner)
    gain = rowp[5:6]
    cols = columns_of(inner)

    def block(i, carry):
        grad_sum, gain_sum, skip_sum = carry
        q = spans - 1 - i
        tok = pl.ds(pl.multiple_of(q * SPAN, SPAN), SPAN)
        columns = token_scalars[:, tok].T
        inv, total_dot = columns[:, 0:1], columns[:, 1:2]
        zf = z[tok, :].astype(F32)
        sig = sigmoid(zf)
        act = zf * sig
        y = y_in[tok, :]
        gated = y * act
        d_no = dot(dmix[tok, :], wo[...])
        scaled = gated * inv
        normed_out[tok, :] = (scaled * gain).astype(BF16)
        gain_sum = gain_sum + jnp.sum(d_no * scaled, axis=0, keepdims=True)
        d_gated = inv * (d_no * gain) - gated * (inv * inv * inv * total_dot * (1.0 / inner_all))
        after = pl.ds(pl.multiple_of(q * SPAN + EDGE, EDGE), SPAN)
        cat_out[after, cols.z] = (d_gated * y * (sig * (1.0 + zf * (1.0 - sig)))).astype(BF16)
        dy = d_gated * act
        xf = x[tok, :].astype(F32)
        skip_sum = skip_sum + jnp.sum(dy * xf, axis=0, keepdims=True)
        dy_low = dy.astype(BF16)
        dy_out[tok, :] = dy_low
        scaled_dy = (dy_low.astype(F32) * dot_split(jnp.exp(s[tok, :]), spread)).astype(BF16)
        fresh = dot(bc[tok, STATE:], scaled_dy, TN)
        prior[q] = fresh
        return fresh + decay[q, 0:1] * grad_sum, gain_sum, skip_sum

    zero = jnp.zeros((1, inner), F32)
    grad_sum, gain_sum, skip_sum = lax.fori_loop(
        0, spans, block, (jnp.zeros((STATE, inner), F32), zero, zero)
    )
    decay_all = decay[0, 0:1]
    for q in range(1, spans):
        decay_all = decay_all * decay[q, 0:1]
    wide[...] = jnp.zeros_like(wide)
    wide[5:6] = gain_sum
    wide[6:7] = skip_sum
    return grad_sum, decay_all


def out_gradient(dmix, normed_out, gwo_out):
    def rows_of(i, _):
        rows = pl.ds(pl.multiple_of(i * SPAN, SPAN), SPAN)
        gwo_out[rows, :] = dot(dmix[:, rows], normed_out[...], TN).astype(BF16)
        return 0

    lax.fori_loop(0, dmix.shape[1] // SPAN, rows_of, 0)


def back_within_spans(dy_in, x_in, bc_in, s_in, dt_in, dpre, flow_out, sum_out):
    inner = x_in.shape[1]

    def block(q, _):
        at = pl.multiple_of(q * SPAN, SPAN)
        tok = pl.ds(at, SPAN)
        after = pl.ds(pl.multiple_of(at + EDGE, EDGE), SPAN)
        x_low, dy = x_in[tok, :], dy_in[tok, :]
        b, c = bc_in[tok, :STATE], bc_in[tok, STATE:]
        s, dt = s_in[tok, :], dt_in[tok, :]
        s_row = s.T
        cb = dot(b, c, NT)
        seen = iota((SPAN, SPAN), 0) <= iota((SPAN, SPAN), 1)
        masks = half_masks()
        d_cb = jnp.zeros((SPAN, SPAN), F32)
        lane = iota((SPAN, 128), 1)
        row_id = iota((128, SPAN), 0)
        sum_k = jnp.zeros((128, SPAN), F32)
        sum_t = jnp.zeros((SPAN, 128), F32)
        for pair in range(inner // 128):
            lanes = slice(pair * 128, pair * 128 + 128)
            x_pair, dy_pair = x_low[:, lanes], dy[:, lanes]
            total = None
            for e in range(2):
                h = pair * 2 + e
                d_scores = dot(x_pair * masks[e], dy_pair, NT)
                fade = jnp.exp(jnp.where(seen, s_row[h : h + 1, :] - s[:, h : h + 1], -1e30))
                dt_h = dt[:, h : h + 1]
                fade_cb = cb * fade
                term = dot((fade_cb * dt_h).astype(BF16), dy_pair * masks[e])
                total = term if total is None else total + term
                d_cb = d_cb + d_scores * (fade * dt_h)
                flow = d_scores * fade_cb
                sum_t = jnp.where(lane == h, jnp.sum(flow, axis=1, keepdims=True), sum_t)
                sum_k = jnp.where(row_id == h, jnp.sum(flow * dt_h, axis=0, keepdims=True), sum_k)
            dpre[after, lanes] = total
        d_cb_low = d_cb.astype(BF16)
        dpre[after, inner : inner + STATE] = dot(d_cb_low, c)
        dpre[after, inner + STATE :] = dot(d_cb_low, b, TN)
        flow_out[tok, :] = sum_k.T - sum_t * dt
        sum_out[tok, :] = sum_t
        return 0

    lax.fori_loop(0, x_in.shape[0] // SPAN, block, 0)


def back_through_states(
    grad, prior, decay, states, dy_in, x, bc, s_in, dt_in, dtraw, xin, bcin, rowp, bcp, headp, flow_in, sum_in,
    place, cat_out, step_out, row_out, bcrow_out,
    dpre, dend,
):
    inner = x.shape[1]
    spans = x.shape[0] // SPAN
    spread = head_spread(inner)
    up_tri = triangle(False)
    skip = rowp[6:7]
    rate = -jnp.exp(headp[0:1])
    bias = headp[1:2]
    width = inner + 2 * STATE

    def chain(i, grad):
        q = spans - 1 - i
        before = prior[q] + decay[q, 0:1] * grad
        dend[q] = grad
        return before

    lax.fori_loop(0, spans, chain, grad)
    dpre[0:EDGE] = jnp.zeros((EDGE, width), F32)
    dpre[EDGE + spans * SPAN :] = jnp.zeros((EDGE, width), F32)
    bcrow_out[...] = jnp.zeros_like(bcrow_out)
    cols = columns_of(inner)
    pick = head_pick(place, inner // HEADDIM)
    cat_out[0:EDGE, cols.z] = jnp.zeros((EDGE, inner), BF16)
    cat_out[0:EDGE, cols.dt] = jnp.zeros((EDGE, 128), BF16)

    def block(q, _):
        at = pl.multiple_of(q * SPAN, SPAN)
        tok = pl.ds(at, SPAN)
        after = pl.ds(pl.multiple_of(at + EDGE, EDGE), SPAN)
        window = pl.ds(at, SPAN + EDGE)
        x_low, dy = x[tok, :], dy_in[tok, :]
        xf, dyf = x_low.astype(F32), dy.astype(F32)
        b, c = bc[tok, :STATE], bc[tok, STATE:]
        s, dt = s_in[tok, :], dt_in[tok, :]
        exp_s = jnp.exp(s)
        to_end = jnp.exp(s[SPAN - 1 : SPAN] - s)
        w = to_end * dt
        w_all, s_all = dot_split(w, spread), dot_split(exp_s, spread)
        state, grad = states[q], dend[q]
        state_low, grad_low = state.astype(BF16), grad.astype(BF16)
        carried = s_all * dot(c, state_low)
        ds = dot_split(dyf * carried, spread, NT)
        d_c = dot((dyf * s_all).astype(BF16), state_low, NT)
        d_w = dot(b, grad_low)
        d_b = dot((xf * w_all).astype(BF16), grad_low, NT)
        dx = dpre[after, 0:inner] + dyf * skip + d_w * w_all
        dsw = dot_split(d_w * xf, spread, NT)
        end = dsw * w
        ds = ds + flow_in[tok, :] - end
        held = dot_split(jnp.broadcast_to(jnp.sum(grad * state, axis=0, keepdims=True), (8, inner)), spread, NT)[0:1]
        last = jnp.sum(end, axis=0, keepdims=True) + held * exp_s[SPAN - 1 : SPAN]
        ds = ds + jnp.where(iota((SPAN, 128), 0) == SPAN - 1, last, 0.0)
        da = dot_exact(up_tri, ds)
        d_dt = sum_in[tok, :] + dsw * to_end + da * rate
        d_raw = d_dt * sigmoid(dtraw[tok, :].astype(F32) + bias)
        d_raw = jnp.where(iota((SPAN, 128), 1) < inner // HEADDIM, d_raw, 0.0)
        row_out[7:8, 0:128] += jnp.sum(da * (dt * rate), axis=0, keepdims=True)
        row_out[8:9, 0:128] += jnp.sum(d_raw, axis=0, keepdims=True)
        d_low = d_raw.astype(BF16)
        step_out[tok, :] = d_low
        cat_out[after, cols.dt] = dot(d_low, pick, NT).astype(BF16)

        win_x = xin[window, :].astype(F32)
        d_x = dx * silu_slope(conv_taps(win_x, rowp))
        dpre[after, 0:inner] = d_x
        for j in range(CONV):
            row_out[j : j + 1] += jnp.sum(d_x * win_x[EDGE - 3 + j : EDGE - 3 + j + SPAN], axis=0, keepdims=True)
        row_out[CONV : CONV + 1] += jnp.sum(d_x, axis=0, keepdims=True)
        win_bc = bcin[window, :].astype(F32)
        d_bc = dpre[after, inner:] + jnp.concatenate([d_b, d_c], axis=1)
        d_bc = d_bc * silu_slope(conv_taps(win_bc, bcp))
        dpre[after, inner:] = d_bc
        for j in range(CONV):
            bcrow_out[j : j + 1] += jnp.sum(d_bc * win_bc[EDGE - 3 + j : EDGE - 3 + j + SPAN], axis=0, keepdims=True)
        bcrow_out[CONV : CONV + 1] += jnp.sum(d_bc, axis=0, keepdims=True)
        return 0

    lax.fori_loop(0, spans, block, 0)

    def back(window, taps, rows):
        total = None
        for j in range(CONV):
            term = taps[j : j + 1] * window[CONV - 1 - j : CONV - 1 - j + rows]
            total = term if total is None else total + term
        return total.astype(BF16)

    cat_out[0:EDGE, cols.x] = back(dpre[0 : 2 * EDGE, 0:inner], rowp, EDGE)
    cat_out[0:EDGE, cols.bc] = back(dpre[0 : 2 * EDGE, inner:], bcp, EDGE)

    def conv_block(q, _):
        after = pl.ds(pl.multiple_of(q * SPAN + EDGE, EDGE), SPAN)
        window = pl.ds(pl.multiple_of(q * SPAN + EDGE, EDGE), SPAN + EDGE)
        cat_out[after, cols.x] = back(dpre[window, 0:inner], rowp, SPAN)
        cat_out[after, cols.bc] = back(dpre[window, inner:], bcp, SPAN)
        return 0

    lax.fori_loop(0, spans, conv_block, 0)


def project_back_edge(cat, w, dn_out):
    cols = columns_of((w.shape[1] - 3 * STATE) // 2)
    dn_out[0:EDGE] = (
        dot(cat[0:EDGE, cols.x], w[:, cols.x], NT) + dot(cat[0:EDGE, cols.bc], w[:, cols.bc], NT)
    ).astype(BF16)


def project_back(q, cat, w, dn_out):
    after = pl.ds(pl.multiple_of(q * SPAN + EDGE, EDGE), SPAN)
    dn_out[after, :] = dot(cat[after, :], w[...], NT).astype(BF16)


def for_row_blocks(grad, body):
    groups, rows = grad

    def one(g, _):
        body(pl.ds(pl.multiple_of(g * rows, 128), rows) if rows % 128 == 0 else pl.ds(g * rows, rows), g)
        return 0

    if rows % 128 == 0:
        lax.fori_loop(0, groups, one, 0)
    else:
        for g in range(groups):
            one(g, 0)


def x_gradient(cat, normed, gx_out):
    cols = columns_of(gx_out.shape[1])

    def body(at, _):
        total = dot(normed[EDGE:, at], cat[EDGE:, cols.x], TN) + dot(normed[0:EDGE, at], cat[0:EDGE, cols.x], TN)
        gx_out[at, :] = total.astype(BF16)

    for_row_blocks((normed.shape[1] // SPAN, SPAN), body)


def z_gradient(cat, normed, gz_out):
    cols = columns_of(gz_out.shape[1])

    def body(at, _):
        gz_out[at, :] = dot(normed[EDGE:, at], cat[EDGE:, cols.z], TN).astype(BF16)

    for_row_blocks((normed.shape[1] // SPAN, SPAN), body)


def small_gradients(cat, steps, normed, gbc_out, gdt_out):
    groups, parts, shard, _ = gbc_out.shape
    cols = columns_of((cat.shape[1] - 3 * STATE) // 2)

    def body(at, g):
        edge, tokens = normed[0:EDGE, at], normed[EDGE:, at]
        bc = dot(tokens, cat[EDGE:, cols.bc], TN) + dot(edge, cat[0:EDGE, cols.bc], TN)
        gbc_out[g] = bc.reshape(parts, shard, 2 * STATE).astype(BF16)
        gdt_out[g] = dot(steps[...], tokens, TN)[0:EDGE].astype(BF16)

    for_row_blocks((groups, parts * shard), body)


HALF = 128
MESH = pl.DeviceIdType.MESH


class Links:
    def __init__(self, sends, recvs):
        self.z, self.p, self.c = lax.axis_index("z"), lax.axis_index("p"), lax.axis_index("head")
        self.groups = lax.axis_size("z")
        self.sends, self.recvs, self.used = sends, recvs, 0

    def copy(self, src, dst, device):
        i = self.used
        self.used += 1
        return pltpu.make_async_remote_copy(
            src_ref=src, dst_ref=dst, send_sem=self.sends.at[i], recv_sem=self.recvs.at[i],
            device_id=device, device_id_type=MESH,
        )

    def local(self, src, dst):
        i = self.used
        self.used += 1
        return pltpu.make_async_copy(src, dst, self.sends.at[i])

    def at(self, k, e):
        return (self.z, lax.bitwise_xor(self.p, jnp.int32(k)), lax.bitwise_xor(self.c, jnp.int32(e)))

    def last_of_plane(self):
        return jnp.logical_and(self.p == GROUP - 1, self.c == 1)

    def greet(self, plane=False, sibling=False, groups=False, edge=0):
        barrier = pltpu.get_barrier_semaphore()
        z, count = self.z, self.groups
        above = z < count - 1

        def signal(device):
            pl.semaphore_signal(barrier, 1, device_id=device, device_id_type=MESH)

        self.expected = jnp.int32(0)
        for k in range(GROUP):
            for e in range(2):
                if (k or e) if plane else (sibling and e and not k):
                    signal(self.at(k, e))
                    self.expected = self.expected + 1
        if groups:
            for k in range(1, count):
                signal((lax.rem(z + k, count), self.p, self.c))
            self.expected = self.expected + (count - 1)
        sending = jnp.logical_and(self.last_of_plane(), above)
        if edge == 1:
            pl.when(z > 0)(lambda: signal((z - 1, jnp.int32(GROUP - 1), jnp.int32(1))))
            self.expected = self.expected + 2 * GROUP * sending.astype(jnp.int32)
        if edge == -1:

            @pl.when(sending)
            def _():
                for p in range(GROUP):
                    for c in range(2):
                        signal((z + 1, jnp.int32(p), jnp.int32(c)))

            self.expected = self.expected + (z > 0).astype(jnp.int32)

    def meet(self):
        pl.semaphore_wait(pltpu.get_barrier_semaphore(), self.expected)

    def start_barrier(self, **who):
        self.greet(**who)
        self.meet()


class Chain:
    def __init__(self, links, pieces):
        z, p, c, groups = links.z, links.p, links.c, links.groups
        self.steps, self.now = [], 0
        for step in range(1, groups):
            found = []
            up, down = z - step + 1, z + step - 1
            for piece in pieces:
                block = piece(jnp.maximum(up, 0))
                sending = jnp.logical_and(up >= 0, z < groups - 1)
                found.append((sending, z - step >= 0, links.copy(block, block, (z + 1, p, c))))
                block = piece(jnp.minimum(down, groups - 1))
                sending = jnp.logical_and(down < groups, z > 0)
                found.append((sending, z + step < groups, links.copy(block, block, (z - 1, p, c))))
            self.steps.append(found)

    def begin(self):
        for sending, _, copy in self.steps[0]:
            pl.when(sending)(copy.start)

    def advance(self):
        if self.now + 1 < len(self.steps):
            for (_, receiving, copy), (sending, _, later) in zip(self.steps[self.now], self.steps[self.now + 1]):
                pl.when(receiving)(copy.wait_recv)
                pl.when(sending)(later.start)
            self.now += 1

    def complete(self):
        while self.now + 1 < len(self.steps):
            self.advance()
        for _, receiving, copy in self.steps[-1]:
            pl.when(receiving)(copy.wait_recv)

    def finish(self):
        for found in self.steps:
            for sending, _, copy in found:
                pl.when(sending)(copy.wait_send)


class Swap:
    def __init__(self, links, shard, staging, out, lanes, width):
        self.links, self.staging, self.out, self.lanes = links, staging, out, lanes

        def source(k):
            if shard.shape[1] == width:
                return shard
            to = lax.bitwise_xor(links.p, jnp.int32(k))
            return shard.at[:, pl.ds(pl.multiple_of(to * width, 128), width)]

        self.copies = [links.copy(source(k), staging.at[links.p], links.at(k, 0)) for k in (3, 1, 2)]
        self.keep = links.local(source(0), staging.at[links.p])

    def start(self):
        for copy in self.copies:
            copy.start()

    def settle(self):
        self.keep.wait()
        for copy in self.copies:
            copy.wait_recv()
        parts, shard, width = self.staging.shape
        rows = parts * shard
        first = self.links.z * rows
        if shard % EDGE == 0:
            for j in range(parts):
                self.out[pl.ds(pl.multiple_of(first + j * shard, EDGE), shard), self.lanes] = self.staging[j]
        else:
            block = self.staging[...].astype(F32).reshape(rows, width).astype(BF16)
            self.out[pl.ds(pl.multiple_of(first, EDGE), rows), self.lanes] = block

    def finish(self):
        for copy in self.copies:
            copy.wait_send()


class Collect:
    def __init__(self, links, grad, out):
        rows = grad.shape[0] // links.groups
        z, groups = links.z, links.groups

        def block(index):
            return grad.at[pl.ds(pl.multiple_of(index * rows, EDGE), rows)]

        self.keep = links.local(block(z), out.at[0])
        self.copies = []
        for k in range(1, groups):
            to = lax.rem(z + k, groups)
            self.copies.append(links.copy(block(to), out.at[k], (to, links.p, links.c)))

    def start(self):
        self.keep.start()
        for copy in self.copies:
            copy.start()

    def arrive(self):
        self.keep.wait()
        for copy in self.copies:
            copy.wait_recv()

    def finish(self):
        for copy in self.copies:
            copy.wait_send()


class Deliver:
    def __init__(self, links, parts, final, out):
        self.links, self.parts, self.final, self.out = links, parts, final, out
        inner = parts.shape[2]
        self.mine = pl.ds(pl.multiple_of(links.p * inner, 128), inner)
        self.copies = [
            links.copy(final.at[lax.bitwise_xor(links.p, jnp.int32(k))], out.at[:, self.mine], links.at(k, 0))
            for k in (3, 1, 2)
        ]

    def start(self):
        total = self.parts[0].astype(F32)
        for k in range(1, self.parts.shape[0]):
            total = total + self.parts[k].astype(F32)
        shard = self.final.shape[1]
        for j in range(GROUP):
            self.final[j] = total[j * shard : (j + 1) * shard].astype(BF16)
        for copy in self.copies:
            copy.start()
        self.out[:, self.mine] = self.final[self.links.p]

    def finish(self):
        for copy in self.copies:
            copy.wait()


class States:
    def __init__(self, links, backward, state, decay, states, decays):
        z, groups = links.z, links.groups
        self.links, self.refs = links, (state, decay, states, decays)
        self.found = []
        for k in range(1, groups):
            to, source = (z - k, z + k) if backward else (z + k, z - k)
            sending, receiving = (to >= 0, source < groups) if backward else (to < groups, source >= 0)
            device = (jnp.clip(to, 0, groups - 1), links.p, links.c)
            pair = [links.copy(state, states.at[z], device), links.copy(decay, decays.at[z], device)]
            self.found.append((sending, receiving, pair))

    def start(self):
        for sending, _, pair in self.found:

            @pl.when(sending)
            def _(pair=pair):
                for copy in pair:
                    copy.start()

    def arrive(self):
        for _, receiving, pair in self.found:

            @pl.when(receiving)
            def _(pair=pair):
                for copy in pair:
                    copy.wait_recv()

    def finish(self):
        for sending, _, pair in self.found:

            @pl.when(sending)
            def _(pair=pair):
                for copy in pair:
                    copy.wait_send()


class Gather:
    def __init__(self, links, out, base):
        self.links, self.out, self.base = links, out, base

        def place(k, c):
            row = base + lax.bitwise_xor(links.p, jnp.int32(k)) * (2 * HALF) + c * HALF
            return out.at[pl.ds(pl.multiple_of(row, EDGE), HALF), :]

        own = place(0, links.c)
        self.out_copies = [links.copy(own, own, links.at(k, 0)) for k in (3, 1, 2)]
        self.shared = [links.copy(own, own, links.at(0, 1))]
        self.shared += [links.copy(place(k, links.c), place(k, links.c), links.at(0, 1)) for k in (1, 2, 3)]
        self.arrivals = [self.out_copies[1], self.out_copies[2], self.out_copies[0]]

    def own(self, start, size):
        row = self.base + self.links.p * (2 * HALF) + self.links.c * HALF + start
        return pl.ds(pl.multiple_of(row, EDGE), size)

    def start(self):
        for copy in self.out_copies:
            copy.start()
        self.shared[0].start()

    def pass_on(self):
        for k in range(3):
            self.arrivals[k].wait_recv()
            self.shared[k + 1].start()

    def finish(self):
        for copy in self.shared:
            copy.wait_recv()
        for copy in self.shared + self.out_copies:
            copy.wait_send()


class EdgeForward:
    def __init__(self, links, gather):
        self.links = links
        tail = gather.out.at[gather.own(HALF - EDGE, EDGE), :]
        first = links.used
        links.used += 2 * GROUP + 1
        recv = links.recvs.at[first + 2 * GROUP]
        self.out = gather.out
        self.copies = [
            pltpu.make_async_remote_copy(
                src_ref=tail, dst_ref=gather.out.at[0:EDGE, :], send_sem=links.sends.at[first + p * 2 + c], recv_sem=recv,
                device_id=(links.z + 1, jnp.int32(p), jnp.int32(c)), device_id_type=MESH,
            )
            for p in range(GROUP)
            for c in range(2)
        ]
        self.sending = jnp.logical_and(links.last_of_plane(), links.z < links.groups - 1)

    def start(self):
        @pl.when(self.sending)
        def _():
            for copy in self.copies:
                copy.start()

        @pl.when(self.links.z == 0)
        def _():
            self.out[0:EDGE, :] = jnp.zeros((EDGE, self.out.shape[1]), self.out.dtype)

    def finish(self):
        pl.when(self.links.z > 0)(self.copies[0].wait_recv)

        @pl.when(self.sending)
        def _():
            for copy in self.copies:
                copy.wait_send()


class Scatter:
    def __init__(self, links, part, base, sib, total, peer):
        self.links, self.part, self.base = links, part, base
        self.sib, self.total, self.peer = sib, total, peer
        other = 1 - links.c
        self.to_sibling = {
            k: links.copy(part.at[self.rows(k, other, 0, HALF), :], sib.at[k], links.at(0, 1)) for k in (3, 1, 2, 0)
        }
        self.to_peer = {k: links.copy(total.at[k - 1], peer.at[k - 1], links.at(k, 0)) for k in (3, 1, 2)}

    def rows(self, k, c, start, size):
        row = self.base + lax.bitwise_xor(self.links.p, jnp.int32(k)) * (2 * HALF) + c * HALF + start
        return pl.ds(pl.multiple_of(row, EDGE), size)

    def pass_on(self, k):
        self.to_sibling[k].wait_recv()
        if k == 0:
            return

        def add(i, _):
            at = pl.ds(pl.multiple_of(i * 32, 32), 32)
            mine = self.part[self.rows(k, self.links.c, i * 32, 32), :].astype(F32)
            self.total[k - 1, at, :] = (mine + self.sib[k, at, :].astype(F32)).astype(BF16)
            return 0

        lax.fori_loop(0, HALF // 32, add, 0)
        self.to_peer[k].start()

    def arrive(self):
        for copy in self.to_peer.values():
            copy.wait_recv()

    def own(self, start, size):
        at = pl.ds(start, size)
        total = self.part[self.rows(0, self.links.c, start, size), :].astype(F32) + self.sib[0, at, :].astype(F32)
        for k in range(3):
            total = total + self.peer[k, at, :].astype(F32)
        return total

    def finish(self):
        for copy in list(self.to_sibling.values()) + list(self.to_peer.values()):
            copy.wait_send()


class SmallSum:
    def __init__(self, links, squares, slots):
        self.links, self.squares, self.slots = links, squares, slots
        self.copies = [
            links.copy(squares.at[:, self.lanes(k, e)], slots.at[2 * k + e - 1], links.at(k, e))
            for k in range(GROUP)
            for e in range(2)
            if k or e
        ]

    def lanes(self, k, e):
        links = self.links
        column = lax.bitwise_xor(links.p, jnp.int32(k)) * (2 * HALF) + lax.bitwise_xor(links.c, jnp.int32(e)) * HALF
        return pl.ds(pl.multiple_of(column, HALF), HALF)

    def start(self):
        for copy in self.copies:
            copy.start()

    def total(self):
        for copy in self.copies:
            copy.wait_recv()
        total = self.squares[:, self.lanes(0, 0)]
        for i in range(len(self.copies)):
            total = total + self.slots[i]
        return total

    def finish(self):
        for copy in self.copies:
            copy.wait_send()


class SmallGather:
    def __init__(self, links, out):
        self.out = out
        self.lanes = pl.ds(pl.multiple_of(links.p * (2 * HALF) + links.c * HALF, HALF), HALF)
        self.copies = [
            links.copy(out.at[:, self.lanes], out.at[:, self.lanes], links.at(k, e))
            for k in range(GROUP)
            for e in range(2)
            if k or e
        ]

    def start(self):
        for copy in self.copies:
            copy.start()

    def finish(self):
        for copy in self.copies:
            copy.wait()


def row_chunks(size=32):
    return [(start, size) for start in range(0, HALF, size)]


def rms_of(rows):
    return lax.rsqrt(jnp.mean(rows * rows, axis=-1, keepdims=True) + EPS)


def as_tile(columns):
    lane = iota((HALF, HALF), 1)
    wide = jnp.zeros((HALF, HALF), F32)
    for i, column in enumerate(columns):
        wide = jnp.where(lane == i, column, wide)
    return wide.T[0:8]


def grad_rows(links, scatter, edge_slots, grad, resid, gain, gain_out, start, size):
    at = slice(start, start + size)
    d_normed = scatter.own(start, size)
    if start + size == HALF:
        extra = edge_slots[0].astype(F32)
        for i in range(1, 2 * GROUP):
            extra = extra + edge_slots[i].astype(F32)
        used = jnp.logical_and(links.last_of_plane(), links.z < links.groups - 1)
        extra = jnp.where(used, extra, 0.0)
        d_normed = d_normed + jnp.concatenate([jnp.zeros((size - EDGE, extra.shape[1]), F32), extra])
    rows = resid[at]
    inv_rms = rms_of(rows)
    gain_sum = jnp.sum(d_normed * rows * inv_rms, axis=0, keepdims=True)
    gain_out[0:1] = gain_sum if start == 0 else gain_out[0:1] + gain_sum
    d_hidden = d_normed * gain[...]
    return (
        grad[at]
        + inv_rms * d_hidden
        - rows * (inv_rms * inv_rms * inv_rms * jnp.mean(d_hidden * rows, axis=-1, keepdims=True))
    )


class EdgeBackward:
    def __init__(self, links, part, slots):
        self.links = links
        first = links.used
        links.used += 2 * GROUP + 1
        me = links.p * 2 + links.c
        self.send = pltpu.make_async_remote_copy(
            src_ref=part.at[0:EDGE, :], dst_ref=slots.at[me], send_sem=links.sends.at[first], recv_sem=links.recvs.at[first + me],
            device_id=(links.z - 1, jnp.int32(GROUP - 1), jnp.int32(1)), device_id_type=MESH,
        )
        self.recvs = [
            pltpu.make_async_remote_copy(
                src_ref=part.at[0:EDGE, :], dst_ref=slots.at[i], send_sem=links.sends.at[first], recv_sem=links.recvs.at[first + i],
                device_id=(links.z, links.p, 1 - links.c), device_id_type=MESH,
            )
            for i in range(2 * GROUP)
        ]
        self.receiving = jnp.logical_and(links.last_of_plane(), links.z < links.groups - 1)

    def start(self):
        pl.when(self.links.z > 0)(self.send.start)

    def receive(self):
        @pl.when(self.receiving)
        def _():
            for copy in self.recvs:
                copy.wait_recv()

    def finish(self):
        pl.when(self.links.z > 0)(self.send.wait_send)


class BcSum:
    def __init__(self, links, bc, out, bufs):
        self.links, self.bc, self.out = links, bc, out
        self.sib, self.chip, self.peer, self.total, self.far = bufs
        p, c, groups = links.p, links.c, links.groups
        self.own = pl.ds(pl.multiple_of(c * STATE, STATE), STATE)
        other = pl.ds(pl.multiple_of((1 - c) * STATE, STATE), STATE)
        self.first = [links.copy(bc.at[:, :, :, other], self.sib, links.at(0, 1))]
        self.second = [
            links.copy(self.chip.at[:, lax.bitwise_xor(p, jnp.int32(k))], self.peer.at[k - 1], links.at(k, 0))
            for k in (3, 1, 2)
        ]
        self.third = []
        for k in range(1, groups):
            to = lax.rem(links.z + k, groups)
            self.third.append(links.copy(self.total.at[to], self.far.at[k - 1], (to, p, c)))
        self.fourth = [links.copy(out.at[:, self.own], out.at[:, self.own], links.at(0, 1))]

    @staticmethod
    def begin(copies):
        for copy in copies:
            copy.start()

    @staticmethod
    def arrive(copies):
        for copy in copies:
            copy.wait_recv()

    def cores(self):
        self.begin(self.first)

    def plane(self):
        self.arrive(self.first)

        def add(i, _):
            for q in range(GROUP):
                mine = self.bc[i, q, :, self.own].astype(F32)
                self.chip[i, q] = (mine + self.sib[i, q].astype(F32)).astype(BF16)
            return 0

        lax.fori_loop(0, self.links.groups, add, 0)
        self.begin(self.second)

    def groups(self):
        self.arrive(self.second)

        def add(i, _):
            total = self.chip[i, self.links.p].astype(F32)
            for k in range(GROUP - 1):
                total = total + self.peer[k, i].astype(F32)
            self.total[i] = total.astype(BF16)
            return 0

        lax.fori_loop(0, self.links.groups, add, 0)
        self.begin(self.third)

    def share(self):
        self.arrive(self.third)
        total = self.total[self.links.z].astype(F32)
        for k in range(self.links.groups - 1):
            total = total + self.far[k].astype(F32)
        self.out[:, self.own] = total.astype(BF16)
        self.begin(self.fourth)

    def finish(self):
        self.arrive(self.fourth)
        for copy in self.first + self.second + self.third + self.fourth:
            copy.wait_send()


class LaidOut:
    def __init__(self, links, dt, wide, dt_out, wide_out, dt_far, wide_far):
        self.links, self.refs = links, (dt, wide, dt_out, wide_out, dt_far, wide_far)
        z, p, c, groups = links.z, links.p, links.c, links.groups
        self.first, self.second = [], []
        for k in range(1, groups):
            to = lax.rem(z + k, groups)
            self.first.append(links.copy(dt.at[to], dt_far.at[k - 1], (to, p, c)))
            self.first.append(links.copy(wide, wide_far.at[k - 1], (to, p, c)))
        for k in range(1, GROUP):
            self.second.append(links.copy(dt_out.at[p], dt_out.at[p], links.at(k, 0)))
            self.second.append(links.copy(wide_out.at[p], wide_out.at[p], links.at(k, 0)))

    def groups(self):
        BcSum.begin(self.first)

    def plane(self):
        BcSum.arrive(self.first)
        dt, wide, dt_out, wide_out, dt_far, wide_far = self.refs
        dt_total, wide_total = dt[self.links.z].astype(F32), wide[...]
        for k in range(self.links.groups - 1):
            dt_total = dt_total + dt_far[k].astype(F32)
            wide_total = wide_total + wide_far[k]
        dt_out[self.links.p] = dt_total.astype(BF16)
        wide_out[self.links.p] = wide_total
        BcSum.begin(self.second)

    def finish(self):
        BcSum.arrive(self.second)
        for copy in self.first + self.second:
            copy.wait_send()


class VecSum:
    def __init__(self, links, vec, out, near, far):
        self.links, self.refs = links, (vec, out, near, far)
        z, p, c, groups = links.z, links.p, links.c, links.groups
        self.first, self.second, self.third = [], [], []
        for k in range(GROUP):
            for e in range(2):
                if k or e:
                    to = lax.bitwise_xor(p, jnp.int32(k)) * 2 + lax.bitwise_xor(c, jnp.int32(e))
                    self.first.append(links.copy(vec.at[to], near.at[2 * k + e - 1], links.at(k, e)))
                    self.third.append(links.copy(out.at[p * 2 + c], out.at[p * 2 + c], links.at(k, e)))
        for k in range(1, groups):
            self.second.append(links.copy(near.at[7], far.at[k - 1], (lax.rem(z + k, groups), p, c)))

    def plane(self):
        BcSum.begin(self.first)

    def groups(self):
        BcSum.arrive(self.first)
        vec, _, near, _ = self.refs
        total = vec[self.links.p * 2 + self.links.c]
        for slot in range(2 * GROUP - 1):
            total = total + near[slot]
        near[7] = total
        BcSum.begin(self.second)

    def back(self):
        BcSum.arrive(self.second)
        _, out, near, far = self.refs
        total = near[7]
        for k in range(self.links.groups - 1):
            total = total + far[k]
        out[self.links.p * 2 + self.links.c] = total
        BcSum.begin(self.third)

    def finish(self):
        BcSum.arrive(self.third)
        for copy in self.first + self.second + self.third:
            copy.wait_send()


class Refs:
    def __init__(self, refs, twins, sems):
        self.__dict__.update(refs)
        self.twins = {id(near): (far, near, sems.at[i]) for i, (far, near) in enumerate(twins)}
        self.waits = []

    def fetch(self, *refs):
        for ref in refs:
            far, near, sem = self.twins[id(ref)]
            pltpu.make_async_copy(far, near, sem).start()

    def need(self, *refs):
        for ref in refs:
            pltpu.make_async_copy(*self.twins[id(ref)]).wait()

    def flush(self, *refs):
        for ref in refs:
            far, near, sem = self.twins[id(ref)]
            self.waits.append(pltpu.make_async_copy(near, far, sem))
            self.waits[-1].start()

    def done(self):
        for copy in self.waits:
            copy.wait()


def weight_chain(links, w, inner):
    rows = w.shape[0] // links.groups
    cols = columns_of(inner)
    half = pl.ds(pl.multiple_of(cols.bc.start + links.c * STATE, STATE), STATE)

    def at(index):
        return pl.ds(pl.multiple_of(index * rows, EDGE), rows)

    pieces = [
        lambda i: w.at[at(i), cols.x],
        lambda i: w.at[at(i), cols.z.start : cols.dt.stop],
        lambda i: w.at[at(i), half],
    ]
    return Chain(links, pieces), links.copy(w.at[:, half], w.at[:, half], links.at(0, 1))


def out_chain(links, wo):
    rows = wo.shape[0] // links.groups
    return Chain(links, [lambda i: wo.at[pl.ds(pl.multiple_of(i * rows, EDGE), rows), :]])


def weight_swaps(links, shards, stagings, w, wo, inner):
    cols = columns_of(inner)
    half = pl.ds(pl.multiple_of(cols.bc.start + links.c * STATE, STATE), STATE)
    places = ((cols.x, inner), (cols.z, inner), (cols.dt, STATE), (half, STATE))
    swaps = [Swap(links, shards[i], stagings[i], w, *places[i]) for i in range(4)]
    return swaps, Swap(links, shards[4], stagings[4], wo, slice(0, inner), inner)


def scatter_blocks(scatter, compute):
    before = None
    for k in (3, 1, 2, 0):
        compute(lax.bitwise_xor(scatter.links.p, jnp.int32(k)))
        scatter.to_sibling[k].start()
        if before is not None:
            scatter.pass_on(before)
        before = k


def forward_layer(links, r, normed, w, wo, wo_chain, scatter, meanwhile):
    carried = States(links, False, r.state_low, r.decay_row, r.states_in, r.decays_in)
    state_sum, decay_all = project_and_convolve(
        links.p, normed, w, r.rowp, r.bcp, r.headp, r.z, r.xin, r.bcin, r.x, r.bc, r.dtraw, r.dt, r.s, r.decay, r.ext, r.local,
        lambda q: pl.when(q == 3)(wo_chain.advance),
    )
    r.state_low[...] = state_sum.astype(BF16)
    r.decay_row[...] = jnp.broadcast_to(decay_all, r.decay_row.shape)
    carried.start()
    r.flush(r.z, r.xin, r.bcin, r.x, r.bc, r.dtraw, r.dt, r.s, r.decay)
    wo_chain.advance()
    mix_within_spans(r.x, r.bc, r.s, r.dt, r.y)
    wo_chain.complete()
    meanwhile()
    carried.arrive()
    chain_states(entering_state(links.z, links.groups, r.states_in, r.decays_in, False), r.local, r.decay, r.states)
    scatter_blocks(
        scatter, lambda q: mix_out(q, r.states, r.x, r.bc, r.z, r.s, wo, r.rowp, r.y, r.part, r.squares)
    )
    r.flush(r.y, r.states)
    return carried


def first_kernel(inner_all, r):
    links = Links(r.sends, r.recvs)
    c = links.c
    inner = r.wo.shape[1]
    swaps, swap_o = weight_swaps(links, r.shards[0], r.stagings[0], r.w, r.wo, inner)
    next_swaps, next_o = weight_swaps(links, r.shards[1], r.stagings[1], r.next_w, r.next_wo, inner)
    all_swaps = swaps + [swap_o] + next_swaps + [next_o]
    gather, other = Gather(links, r.normed, EDGE), Gather(links, r.dmix, 0)
    edge = EdgeForward(links, gather)
    chain, share = weight_chain(links, r.w, inner)
    chain_o = out_chain(links, r.wo)
    next_chain, next_share = weight_chain(links, r.next_w, inner)
    scatter = Scatter(links, r.part, 0, r.sib, r.total, r.peer)
    small = SmallSum(links, r.squares, r.slots)
    next_gather = Gather(links, r.next_normed, EDGE)
    next_edge = EdgeForward(links, next_gather)

    links.greet(plane=True, groups=True, edge=1)
    for swap in all_swaps:
        swap.keep.start()
    for start, size in row_chunks():
        at = pl.ds(pl.multiple_of(c * HALF + start, EDGE), size)
        rows_in = r.resid[at, :].astype(F32)
        r.resid_out[start : start + size] = rows_in
        r.normed[gather.own(start, size), :] = (rows_in * rms_of(rows_in) * r.gain[...]).astype(BF16)
        rows_in = r.cot[at, :]
        r.cot_out[start : start + size] = rows_in.astype(F32)
        r.dmix[other.own(start, size), :] = rows_in
    links.meet()
    for swap in swaps:
        swap.start()
    for swap in swaps:
        swap.settle()
    chain.begin()
    gather.start()
    edge.start()
    swap_o.start()
    chain.advance()
    gather.pass_on()
    for swap in next_swaps + [next_o]:
        swap.start()
    chain.advance()
    swap_o.settle()
    gather.finish()
    edge.finish()
    chain.complete()
    share.start()
    chain_o.begin()
    other.start()
    r.flush(r.normed)
    share.wait()
    r.flush(r.w)

    def meanwhile():
        for swap in next_swaps + [next_o]:
            swap.settle()
        next_chain.begin()
        other.pass_on()
        r.flush(r.wo)

    carried = forward_layer(links, r, r.normed, r.w, r.wo, chain_o, scatter, meanwhile)
    small.start()
    next_chain.advance()
    scatter.pass_on(0)
    scatter.arrive()
    inv = lax.rsqrt(small.total() * (1.0 / inner_all) + EPS)
    r.inv_out[...] = inv
    column = inv.T[:, 0:1]
    for start, size in row_chunks():
        at = slice(start, start + size)
        mixed = scatter.own(start, size)
        r.mixed_out[at] = mixed
        fresh = r.resid_out[at] + column[at] * mixed
        r.fresh_out[at] = fresh
        r.next_normed[next_gather.own(start, size), :] = (fresh * rms_of(fresh) * r.next_gain[...]).astype(BF16)
    next_gather.start()
    next_edge.start()
    other.finish()
    r.flush(r.dmix)
    next_chain.advance()
    next_gather.pass_on()
    next_chain.complete()
    next_share.start()
    scatter.finish()
    small.finish()
    next_gather.finish()
    next_edge.finish()
    carried.finish()
    for swap in all_swaps:
        swap.finish()
    for one in (chain, chain_o, next_chain):
        one.finish()
    next_share.wait()
    r.done()


def second_kernel(inner_all, r):
    links = Links(r.sends, r.recvs)
    rows = r.wo_own.shape[0]
    keep = links.local(r.wo_own, r.wo.at[pl.ds(pl.multiple_of(links.z * rows, EDGE), rows), :])
    chain_o = out_chain(links, r.wo)
    scatter = Scatter(links, r.part, 0, r.sib, r.total, r.peer)
    small = SmallSum(links, r.squares, r.slots)
    spread = SmallGather(links, r.scalars_out)
    at = pl.ds(pl.multiple_of(links.c * HALF, HALF), HALF)
    share = links.copy(r.block_out.at[at, :], r.block_out.at[at, :], links.at(0, 1))
    keep.start()
    links.greet(plane=True, groups=True)
    keep.wait()
    links.meet()
    chain_o.begin()
    carried = forward_layer(links, r, r.normed, r.w, r.wo, chain_o, scatter, lambda: r.flush(r.wo))
    small.start()
    scatter.pass_on(0)
    scatter.arrive()
    inv = lax.rsqrt(small.total() * (1.0 / inner_all) + EPS)
    column = inv.T[:, 0:1]
    dots = []
    for start, size in row_chunks():
        at = slice(start, start + size)
        mixed = scatter.own(start, size)
        dots.append(jnp.sum(r.cot[at] * mixed, axis=-1, keepdims=True))
        r.block_out[pl.ds(pl.multiple_of(links.c * HALF + start, EDGE), size), :] = (
            r.resid[at] + column[at] * mixed
        ).astype(BF16)
    r.scalars_out[:, spread.lanes] = as_tile([column, jnp.concatenate(dots)])
    spread.start()
    share.start()
    scatter.finish()
    small.finish()
    carried.finish()
    chain_o.finish()
    spread.finish()
    share.wait()
    r.done()


def backward_layer(links, inner_all, r, at_start, before_collect, at_middle):
    carried = States(links, True, r.state_low, r.decay_row, r.states_in, r.decays_in)
    collect = Collect(links, r.gwo, r.go_parts)
    grad_sum, decay_all = back_through_gate(
        inner_all, r.dmix, r.wo, r.y, r.z, r.x, r.bc, r.s, r.decay, r.scalars, r.rowp,
        r.cat, r.wide, r.dy, r.prior, r.normed_out,
    )
    r.state_low[...] = grad_sum.astype(BF16)
    r.decay_row[...] = jnp.broadcast_to(decay_all, r.decay_row.shape)
    links.meet()
    carried.start()
    at_start()
    out_gradient(r.dmix, r.normed_out, r.gwo)
    before_collect()
    collect.start()
    r.need(r.dt)
    back_within_spans(r.dy, r.x, r.bc, r.s, r.dt, r.dpre, r.flow, r.sums)
    at_middle()
    carried.arrive()
    grad = entering_state(links.z, links.groups, r.states_in, r.decays_in, True)
    r.need(r.states, r.dtraw, r.xin, r.bcin)
    back_through_states(
        grad, r.prior, r.decay, r.states, r.dy, r.x, r.bc, r.s, r.dt, r.dtraw, r.xin, r.bcin, r.rowp, r.bcp, r.headp,
        r.flow, r.sums, links.p, r.cat, r.steps, r.wide, r.bc_rows, r.dpre, r.prior,
    )
    return carried, collect


def put_vector(vec, row, values):
    for i in range(values.shape[0]):
        for j in range(values.shape[1] // 128):
            vec[row // 8, row % 8 : row % 8 + 1, :] = values[i : i + 1, j * 128 : j * 128 + 128]
            row += 1


def third_kernel(inner_all, r):
    links = Links(r.sends, r.recvs)
    r.fetch(r.dt, r.states, r.dtraw, r.xin, r.bcin, r.w, r.normed, r.grad, r.resid, r.mixed)
    scatter = Scatter(links, r.part, EDGE, r.sib, r.total, r.peer)
    edge = EdgeBackward(links, r.part, r.edge_slots)
    gather = Gather(links, r.dmix_out, 0)
    spread = SmallGather(links, r.scalars_out)
    collects = [Collect(links, r.gx, r.gx_parts), Collect(links, r.gz, r.gz_parts)]
    r.edge_slots[...] = jnp.zeros_like(r.edge_slots)
    links.greet(plane=True, groups=True, edge=-1)
    carried, collect = backward_layer(links, inner_all, r, lambda: None, lambda: None, lambda: None)
    r.need(r.w, r.normed)
    x_gradient(r.cat, r.normed, r.gx)
    collects[0].start()
    project_back_edge(r.cat, r.w, r.part)
    edge.start()
    scatter_blocks(scatter, lambda q: project_back(q, r.cat, r.w, r.part))
    scatter.pass_on(0)
    z_gradient(r.cat, r.normed, r.gz)
    collects[1].start()
    small_gradients(r.cat, r.steps, r.normed, r.gbc, r.gdt)
    scatter.arrive()
    edge.receive()
    r.need(r.grad, r.resid, r.mixed)
    r.gain_row[...] = jnp.zeros_like(r.gain_row)
    dots = []
    for start, size in row_chunks():
        at = slice(start, start + size)
        fresh = grad_rows(links, scatter, r.edge_slots, r.grad, r.resid, r.gain, r.gain_row, start, size)
        r.grad_out[at] = fresh
        low = fresh.astype(BF16)
        r.dmix_out[gather.own(start, size), :] = low
        dots.append(jnp.sum(low.astype(F32) * r.mixed[at], axis=-1, keepdims=True))
    r.scalars_out[:, spread.lanes] = as_tile([r.inv[...].T[:, 0:1], jnp.concatenate(dots)])
    gather.start()
    spread.start()
    r.vec[...] = jnp.zeros_like(r.vec)
    model = r.gain_row.shape[1]
    put_vector(r.vec, model // 128, r.gain_row[0:1])
    put_vector(r.vec, 2 * (model // 128) + 2 * (CONV + 1), r.bc_rows[0 : CONV + 1])
    gather.pass_on()
    scatter.finish()
    edge.finish()
    gather.finish()
    spread.finish()
    carried.finish()
    for one in [collect] + collects:
        one.arrive()
        one.finish()


def fourth_kernel(inner_all, r):
    links = Links(r.sends, r.recvs)
    r.fetch(r.dt, r.states, r.dtraw, r.xin, r.bcin, r.above_bc, r.above_x, r.above_z, r.above_o, r.normed, r.w, r.grad, r.resid)
    scatter = Scatter(links, r.part, EDGE, r.sib, r.total, r.peer)
    edge = EdgeBackward(links, r.part, r.edge_slots)
    at = pl.ds(pl.multiple_of(links.c * HALF, HALF), HALF)
    share = links.copy(r.out.at[at, :], r.out.at[at, :], links.at(0, 1))
    collects = [Collect(links, r.gx, r.gx_parts), Collect(links, r.gz, r.gz_parts)]
    above = zip((r.above_x, r.above_z, r.above_o), r.big_out[1])
    own = ((r.go_parts, r.big_out[0][2]), (r.gx_parts, r.big_out[0][0]), (r.gz_parts, r.big_out[0][1]))
    delivers = [Deliver(links, parts, r.final.at[i], out) for i, (parts, out) in enumerate(above)]
    own_delivers = [Deliver(links, parts, r.final.at[3 + i], out) for i, (parts, out) in enumerate(own)]
    bc_sums = [
        BcSum(links, bc, r.bc_out.at[i], r.bc_bufs[i])
        for i, bc in enumerate((r.gbc, r.above_bc))
    ]
    laid = LaidOut(links, r.steps_all, r.wide_all, r.dt_out, r.wide_out, r.dt_far, r.wide_far)
    vec_sum = VecSum(links, r.vec, r.vec_out, r.vec_near, r.vec_far)
    r.edge_slots[...] = jnp.zeros_like(r.edge_slots)
    links.greet(plane=True, groups=True, edge=-1)

    def at_start():
        r.need(r.above_bc)
        bc_sums[1].cores()

    def at_middle():
        bc_sums[1].groups()
        r.need(r.above_x, r.above_z, r.above_o)
        for deliver in delivers:
            deliver.start()

    carried, collect = backward_layer(links, inner_all, r, at_start, bc_sums[1].plane, at_middle)
    r.need(r.normed)
    small_gradients(r.cat, r.steps, r.normed, r.gbc, r.gdt)
    bc_sums[0].cores()
    r.steps_all[:, 0:EDGE, :] = r.gdt[...]
    r.steps_all[:, EDGE:, :] = r.above_dt[...]
    r.wide_all[0:16] = r.wide[...]
    r.wide_all[16:32] = r.above_wide[...]
    laid.groups()
    x_gradient(r.cat, r.normed, r.gx)
    collects[0].start()
    bc_sums[0].plane()
    r.need(r.w)
    project_back_edge(r.cat, r.w, r.part)
    edge.start()
    scatter_blocks(scatter, lambda q: project_back(q, r.cat, r.w, r.part))
    scatter.pass_on(0)
    bc_sums[0].groups()
    z_gradient(r.cat, r.normed, r.gz)
    scatter.arrive()
    edge.receive()
    r.need(r.grad, r.resid)
    r.gain_row[...] = jnp.zeros_like(r.gain_row)
    for start, size in row_chunks():
        fresh = grad_rows(links, scatter, r.edge_slots, r.grad, r.resid, r.gain, r.gain_row, start, size)
        r.out[pl.ds(pl.multiple_of(links.c * HALF + start, EDGE), size), :] = fresh.astype(BF16)
    share.start()
    r.vec[...] = r.above_vec[...]
    put_vector(r.vec, 0, r.gain_row[0:1])
    put_vector(r.vec, 2 * (r.gain_row.shape[1] // 128), r.bc_rows[0 : CONV + 1])
    vec_sum.plane()
    vec_sum.groups()
    collects[1].start()
    collect.arrive()
    own_delivers[0].start()
    bc_sums[1].share()
    laid.plane()
    collects[0].arrive()
    own_delivers[1].start()
    bc_sums[0].share()
    vec_sum.back()
    collects[1].arrive()
    own_delivers[2].start()
    for one in bc_sums + [laid, vec_sum, scatter, edge, carried, collect] + collects:
        one.finish()
    share.wait()
    for deliver in delivers + own_delivers:
        deliver.finish()


def flat(value):
    return [a for member in value for a in flat(member)] if isinstance(value, list) else [value]


def shaped(value, leaves):
    return [shaped(member, leaves) for member in value] if isinstance(value, list) else leaves.pop(0)


def call(body, collective, copies, outs, hbm_outs, ins, hbm_ins, scratch):
    vmem, hbm = pl.BlockSpec(memory_space=pltpu.VMEM), pl.BlockSpec(memory_space=pl.ANY)
    twins = {**{name: (a.shape, a.dtype) for name, a in hbm_ins.items()}, **hbm_outs}
    sides = [list(ins.values()), list(hbm_ins.values()), list(outs.values()), list(hbm_outs.values())]
    counts = [len(flat(side)) for side in sides]
    buffers = flat([list(scratch.values()), list(twins.values())])

    def kernel(*refs):
        refs = list(refs)
        groups = [shaped(side, refs) for side in sides]
        inner = shaped([list(scratch.values()), list(twins.values())], refs)
        sends, recvs, sems = refs
        near = dict(zip(twins, inner[1]))
        named = {**dict(zip(ins, groups[0])), **dict(zip(outs, groups[2])), **dict(zip(scratch, inner[0])), **near}
        body(Refs(dict(named, sends=sends, recvs=recvs), list(zip(groups[1] + groups[3], inner[1])), sems))

    results = pl.pallas_call(
        kernel,
        out_shape=tuple(jax.ShapeDtypeStruct(*a) for a in flat(sides[2:])),
        in_specs=[vmem] * counts[0] + [hbm] * counts[1],
        out_specs=tuple([vmem] * counts[2] + [hbm] * counts[3]),
        scratch_shapes=[pltpu.VMEM(*a) for a in buffers]
        + [pltpu.SemaphoreType.DMA((n,)) for n in (copies, copies, max(1, len(twins)))],
        compiler_params=pltpu.CompilerParams(
            vmem_limit_bytes=VMEM_BYTES, collective_id=collective, has_side_effects=True
        ),
    )(*flat(sides[:2]))
    found = shaped(sides[2:], list(results))
    return types.SimpleNamespace(**dict(zip(outs, found[0])), **dict(zip(hbm_outs, found[1])))


def on_device(resid_in, cotangent, norm_gain, w_zx, w_dt, w_bc, conv_x, conv_bc, head_params, gated_gain, w_out):
    layers, model = norm_gain.shape
    groups = lax.axis_size("z")
    level, place, core = lax.axis_index("z"), lax.axis_index("p"), lax.axis_index("head")
    shard = w_dt.shape[1]
    inner_core = conv_x.shape[2]
    inner = inner_core // GROUP
    heads_core = head_params.shape[2]
    heads = heads_core // GROUP
    inner_all = inner_core * lax.axis_size("head")
    length = resid_in.shape[1]
    tokens = GROUP * length
    spans = tokens // SPAN
    rows = GROUP * shard

    def my_part(array, size):
        return lax.dynamic_slice_in_dim(array, place * size, size, array.ndim - 1)

    row_all, bc_all, head_all = [], [], []
    conv_mine = my_part(conv_x, inner).astype(F32)
    gain_mine = my_part(gated_gain, inner).astype(F32)
    head_mine = my_part(head_params, heads)
    gains = [norm_gain[layer].astype(F32)[None] for layer in range(layers)]
    for layer in range(layers):
        skip = jnp.repeat(head_mine[layer, 2], HEADDIM)
        row_all.append(
            jnp.concatenate([conv_mine[layer], gain_mine[layer][None], skip[None], jnp.zeros((1, inner), F32)])
        )
        bc_all.append(jnp.pad(conv_bc[layer].astype(F32), ((0, 3), (0, 0))))
        head_all.append(jnp.pad(head_mine[layer], ((0, 5), (0, 128 - heads))))

    def shards_of(layer):
        half = lax.dynamic_slice_in_dim(w_bc[layer], core * STATE, STATE, 1)
        steps = jnp.pad(w_dt[layer], ((0, 0), (0, STATE - heads_core)))
        return w_zx[layer, 1], w_zx[layer, 0], steps, half, w_out[layer].T

    own_rows = ((HALF, model), F32)
    all_rows, edged_rows = ((tokens, model), BF16), ((tokens + EDGE, model), BF16)
    columns = columns_of(inner).size
    w_shape, wo_shape = ((model, columns), BF16), ((model, inner), BF16)
    scalars = ((8, tokens), F32)
    state_shape = ((spans, STATE, inner), F32)
    low_rows, steps_shape = ((tokens, inner), BF16), ((tokens, 128), F32)
    scatter_scratch = dict(
        sib=((GROUP, HALF, model), BF16),
        total=((GROUP - 1, HALF, model), BF16),
        peer=((GROUP - 1, HALF, model), BF16),
    )
    state_scratch = dict(
        state_low=((STATE, inner), BF16),
        decay_row=((8, inner), F32),
        states_in=((groups, STATE, inner), BF16),
        decays_in=((groups, 8, inner), F32),
    )
    saved_shapes = dict(
        y=((tokens, inner), F32),
        z=low_rows,
        x=low_rows,
        bc=((tokens, 2 * STATE), BF16),
        s=steps_shape,
        dt=steps_shape,
        dtraw=((tokens, 128), BF16),
        xin=((tokens + EDGE, inner), BF16),
        bcin=((tokens + EDGE, 2 * STATE), BF16),
        states=state_shape,
        decay=((spans, 8, inner), F32),
    )
    forward_scratch = dict(
        ext=((tokens + EDGE, inner + 2 * STATE), F32),
        local=state_shape,
        part=all_rows,
        squares=scalars,
        slots=((2 * GROUP - 1, 8, HALF), F32),
        **state_scratch,
        **scatter_scratch,
    )

    def params(layer):
        return dict(rowp=row_all[layer], bcp=bc_all[layer], headp=head_all[layer])

    stagings = [((GROUP, shard, width), BF16) for width in (inner, inner, STATE, STATE, inner)]
    first = call(
        functools.partial(first_kernel, inner_all),
        0,
        160 + 14 * (groups - 1) + 2 * groups,
        dict(
            next_w=w_shape,
            next_wo=wo_shape,
            next_normed=edged_rows,
            resid_out=own_rows,
            cot_out=own_rows,
            mixed_out=own_rows,
            fresh_out=own_rows,
            inv_out=((8, HALF), F32),
        ),
        dict(normed=edged_rows, dmix=all_rows, w=w_shape, wo=wo_shape, **saved_shapes),
        dict(
            resid=resid_in[0],
            cot=cotangent[0],
            gain=gains[0],
            next_gain=gains[1],
            **params(0),
            shards=[list(shards_of(0)), list(shards_of(1))],
        ),
        dict(),
        dict(**forward_scratch, stagings=[stagings, stagings]),
    )
    second = call(
        functools.partial(second_kernel, inner_all),
        1,
        60 + 4 * groups,
        dict(block_out=((length, model), BF16), scalars_out=scalars),
        dict(wo=wo_shape, **saved_shapes),
        dict(
            normed=first.next_normed,
            w=first.next_w,
            wo_own=lax.dynamic_slice_in_dim(first.next_wo, level * rows, rows, 0),
            **params(1),
            resid=first.fresh_out,
            cot=first.cot_out,
        ),
        dict(),
        forward_scratch,
    )
    grad_parts = ((groups, rows, inner), BF16)
    bc_grad = ((groups, GROUP, shard, 2 * STATE), BF16)
    dt_grad = ((groups, EDGE, rows), BF16)
    wide_grad = ((16, inner), F32)
    vec_shape = ((2 * GROUP, 8, 128), F32)
    back_scratch = dict(
        dy=low_rows,
        gwo=wo_shape,
        normed_out=low_rows,
        prior=state_shape,
        dpre=((tokens + 2 * EDGE, inner + 2 * STATE), F32),
        flow=steps_shape,
        sums=steps_shape,
        cat=((tokens + EDGE, columns), BF16),
        steps=((tokens, 128), BF16),
        bc_rows=((8, 2 * STATE), F32),
        part=edged_rows,
        gx=wo_shape,
        gz=wo_shape,
        gain_row=((8, model), F32),
        edge_slots=((2 * GROUP, EDGE, model), BF16),
        **state_scratch,
        **scatter_scratch,
    )
    def at_once(run):
        return dict(y=run.y, z=run.z, x=run.x, bc=run.bc, s=run.s, decay=run.decay)

    def later(run):
        return dict(dt=run.dt, states=run.states, dtraw=run.dtraw, xin=run.xin, bcin=run.bcin)

    third = call(
        functools.partial(third_kernel, inner_all),
        2,
        60 + 6 * groups,
        dict(
            dmix_out=all_rows,
            scalars_out=scalars,
            grad_out=own_rows,
            go_parts=grad_parts,
            gx_parts=grad_parts,
            gz_parts=grad_parts,
            gbc=bc_grad,
            gdt=dt_grad,
            wide=wide_grad,
            vec=vec_shape,
        ),
        dict(),
        dict(
            dmix=first.dmix,
            scalars=second.scalars_out,
            wo=second.wo,
            **params(1),
            gain=gains[1],
            inv=first.inv_out,
            **at_once(second),
        ),
        dict(
            w=first.next_w,
            normed=first.next_normed,
            grad=first.cot_out,
            resid=first.fresh_out,
            mixed=first.mixed_out,
            **later(second),
        ),
        back_scratch,
    )
    far = groups - 1
    rows_shape = ((shard, inner_core), BF16)
    dt_shape, wide_shape = (layers * EDGE, rows), (layers * 16, inner)
    half_bc = (groups, GROUP, shard, STATE)
    bc_bufs = [
        (half_bc, BF16),
        (half_bc, BF16),
        ((GROUP - 1, groups, shard, STATE), BF16),
        ((groups, shard, STATE), BF16),
        ((far, shard, STATE), BF16),
    ]
    fourth = call(
        functools.partial(fourth_kernel, inner_all),
        3,
        130 + 14 * groups,
        dict(
            out=((length, model), BF16),
            big_out=[[rows_shape] * 3] * layers,
            bc_out=((layers, shard, 2 * STATE), BF16),
            vec_out=vec_shape,
            dt_out=((GROUP, *dt_shape), BF16),
            wide_out=((GROUP, *wide_shape), F32),
        ),
        dict(),
        dict(
            dmix=third.dmix_out,
            scalars=third.scalars_out,
            wo=first.wo,
            **params(0),
            gain=gains[0],
            above_dt=third.gdt,
            above_wide=third.wide,
            above_vec=third.vec,
            **at_once(first),
        ),
        dict(
            w=first.w,
            normed=first.normed,
            grad=third.grad_out,
            resid=first.resid_out,
            above_x=third.gx_parts,
            above_z=third.gz_parts,
            above_o=third.go_parts,
            above_bc=third.gbc,
            **later(first),
        ),
        dict(
            **back_scratch,
            go_parts=grad_parts,
            gx_parts=grad_parts,
            gz_parts=grad_parts,
            final=((6, GROUP, shard, inner), BF16),
            gbc=bc_grad,
            gdt=dt_grad,
            wide=wide_grad,
            vec=vec_shape,
            steps_all=((groups, *dt_shape), BF16),
            wide_all=(wide_shape, F32),
            bc_bufs=[bc_bufs, bc_bufs],
            vec_near=vec_shape,
            vec_far=((far, 8, 128), F32),
            dt_far=((far, *dt_shape), BF16),
            wide_far=((far, *wide_shape), F32),
        ),
    )
    block_out, grad_input, g_bc = second.block_out, fourth.out, fourth.bc_out
    vec, g_dt, wide = fourth.vec_out, fourth.dt_out, fourth.wide_out
    delivered = fourth.big_out
    vec = vec.reshape(-1)
    grad_gain = vec[: layers * model].reshape(layers, model)
    grad_conv_bc = vec[layers * model :][: layers * (CONV + 1) * 2 * STATE].reshape(layers, CONV + 1, 2 * STATE)
    wide = wide.reshape(GROUP, layers, 16, inner)
    whole = jnp.moveaxis(wide, 0, 2).reshape(layers, 16, inner_core)
    skip_grad = jnp.sum(whole[:, CONV + 2].reshape(layers, heads_core, HEADDIM), axis=-1)
    tall = jnp.moveaxis(wide[:, :, CONV + 3 : CONV + 5, :heads], 0, 2).reshape(layers, 2, heads_core)
    grad_heads = jnp.concatenate([tall, skip_grad[:, None]], axis=1)
    g_dt = lax.dynamic_slice_in_dim(g_dt.reshape(GROUP, layers, EDGE, GROUP, shard), place, 1, 3)[:, :, :heads, 0]
    grad_dt = jnp.transpose(g_dt, (1, 3, 0, 2)).reshape(layers, shard, heads_core)
    low = lambda a: a.astype(BF16)
    return (
        block_out[None],
        grad_input[None],
        low(grad_gain),
        jnp.stack([jnp.stack([delivered[layer][1], delivered[layer][0]]) for layer in range(layers)]),
        grad_dt,
        g_bc,
        low(whole[:, : CONV + 1]),
        low(grad_conv_bc),
        low(grad_heads),
        low(whole[:, CONV + 1]),
        jnp.stack([delivered[layer][2].T for layer in range(layers)]),
    )


def solution(mesh):
    seq, head = mesh.shape["seq"], mesh.shape["head"]
    split = Mesh(mesh.devices.reshape(seq // GROUP, GROUP, head), ("z", "p", "head"))
    seq_axes = ("z", "p")
    specs = (
        P(None, seq_axes, None),
        P(None, seq_axes, None),
        P(),
        P(None, None, seq_axes, "head"),
        P(None, seq_axes, "head"),
        P(None, seq_axes, None),
        P(None, None, "head"),
        P(),
        P(None, None, "head"),
        P(None, "head"),
        P(None, "head", seq_axes),
    )
    return jax.shard_map(on_device, mesh=split, in_specs=specs, out_specs=specs, check_vma=False)
```

```python
import functools
import types
import typing

import jax
import jax.numpy as jnp
from jax import lax
from jax.experimental import pallas as pl
from jax.experimental.pallas import tpu as pltpu
from jax.sharding import Mesh, PartitionSpec as P

HEADDIM = 64
STATE = 128
CONV = 4
SPAN = 256
GROUP = 4
EDGE = 16
EPS = 1e-05
HIGH = lax.Precision.HIGHEST
F32, BF16 = jnp.float32, jnp.bfloat16
NN = (((1,), (0,)), ((), ()))
NT = (((1,), (1,)), ((), ()))
TN = (((0,), (0,)), ((), ()))
VMEM_BYTES = 58 << 20


def dot(a, b, dims=NN):
    return lax.dot_general(a, b, dims, preferred_element_type=F32)


def dot_exact(a, b, dims=NN):
    return lax.dot_general(a, b, dims, precision=HIGH, preferred_element_type=F32)


def dot_split(a, b, dims=NN):
    high = a.astype(BF16)
    rest = (a - high.astype(F32)).astype(BF16)
    return dot(high, b, dims) + dot(rest, b, dims)


def sigmoid(v):
    return 1.0 / (1.0 + jnp.exp(-v))


def softplus(v):
    return jnp.maximum(v, 0.0) + jnp.log1p(jnp.exp(-jnp.abs(v)))


def silu_slope(v):
    sig = sigmoid(v)
    return sig * (1.0 + v * (1.0 - sig))


def iota(shape, dim):
    return lax.broadcasted_iota(jnp.int32, shape, dim)


def head_spread(inner):
    return (iota((128, inner), 0) == lax.shift_right_logical(iota((128, inner), 1), 6)).astype(BF16)


def triangle(lower):
    rows, cols = iota((SPAN, SPAN), 0), iota((SPAN, SPAN), 1)
    return ((cols <= rows) if lower else (cols >= rows)).astype(F32)


def half_masks():
    lane = iota((SPAN, 128), 1)
    return (lane < HEADDIM).astype(BF16), (lane >= HEADDIM).astype(BF16)


def conv_taps(window, taps):
    total = jnp.broadcast_to(taps[CONV : CONV + 1], (SPAN, window.shape[1]))
    for j in range(CONV):
        total = total + taps[j : j + 1] * window[EDGE - 3 + j : EDGE - 3 + j + SPAN]
    return total


def head_pick(place, heads):
    row, col = iota((128, 128), 0), iota((128, 128), 1)
    return jnp.logical_and(row == place * heads + col, col < heads).astype(BF16)


class Columns(typing.NamedTuple):
    x: slice
    z: slice
    dt: slice
    bc: slice
    size: int


def columns_of(inner):
    first = 2 * inner + 128
    return Columns(
        slice(0, inner), slice(inner, 2 * inner), slice(2 * inner, first), slice(first, first + 2 * STATE), first + 2 * STATE
    )


def project_and_convolve(
    normed, w, rowp, bcp, headp,
    z_out, xin_out, bcin_out, x_out, bc_out, dtraw_out, dt_out, s_out, decay_out,
    ext, local, at_block,
):
    inner = x_out.shape[1]
    spans = x_out.shape[0] // SPAN

    cols = columns_of(inner)
    edge = normed[0:EDGE]
    edge_x = dot(edge, w[:, cols.x]).astype(BF16)
    edge_bc = dot(edge, w[:, cols.bc]).astype(BF16)
    xin_out[0:EDGE] = edge_x
    bcin_out[0:EDGE] = edge_bc
    ext[0:EDGE, 0:inner] = edge_x.astype(F32)
    ext[0:EDGE, inner:] = edge_bc.astype(F32)
    spread = head_spread(inner)
    low_tri = triangle(True)
    rate = -jnp.exp(headp[0:1])
    bias = headp[1:2]

    def block(q, carry):
        state_sum, decay_all = carry
        at = pl.multiple_of(q * SPAN, SPAN)
        tok = pl.ds(at, SPAN)
        after = pl.ds(pl.multiple_of(at + EDGE, EDGE), SPAN)
        at_block(q)
        product = dot(normed[after, :], w[...]).astype(BF16)
        z_out[tok, :] = product[:, cols.z]
        xin, bcin = product[:, cols.x], product[:, cols.bc]
        dtraw = product[:, cols.dt]
        xin_out[after, :] = xin
        bcin_out[after, :] = bcin
        dtraw_out[tok, :] = dtraw
        ext[after, 0:inner] = xin.astype(F32)
        ext[after, inner:] = bcin.astype(F32)
        window = pl.ds(at, SPAN + EDGE)
        pre_x = conv_taps(ext[window, 0:inner], rowp)
        x = (pre_x * sigmoid(pre_x)).astype(BF16)
        x_out[tok, :] = x
        pre_bc = conv_taps(ext[window, inner:], bcp)
        bc = (pre_bc * sigmoid(pre_bc)).astype(BF16)
        bc_out[tok, :] = bc
        dt = softplus(dtraw.astype(F32) + bias)
        s = dot_exact(low_tri, dt * rate)
        dt_out[tok, :] = dt
        s_out[tok, :] = s
        to_end = jnp.exp(s[SPAN - 1 : SPAN] - s) * dt
        weighted = (x.astype(F32) * dot_split(to_end, spread)).astype(BF16)
        fresh = dot(bc[:, :STATE], weighted, TN)
        decay = dot_split(jnp.exp(s[SPAN - 8 : SPAN]), spread)[7:8]
        local[q] = fresh
        decay_out[q] = jnp.broadcast_to(decay, (8, inner))
        return state_sum * decay + fresh, decay_all * decay

    return lax.fori_loop(0, spans, block, (jnp.zeros((STATE, inner), F32), jnp.ones((1, inner), F32)))


def mix_within_spans(x_in, bc_in, s_in, dt_in, y_out):
    inner = x_in.shape[1]

    def block(q, _):
        tok = pl.ds(pl.multiple_of(q * SPAN, SPAN), SPAN)
        x, bc, s = x_in[tok, :], bc_in[tok, :], s_in[tok, :]
        s_row, dt_row = s.T, dt_in[tok, :].T
        cb = dot(bc[:, STATE:], bc[:, :STATE], NT)
        causal = iota((SPAN, SPAN), 1) <= iota((SPAN, SPAN), 0)
        masks = half_masks()
        for pair in range(inner // 128):
            lanes = slice(pair * 128, pair * 128 + 128)
            x_pair = x[:, lanes]
            total = None
            for e in range(2):
                h = pair * 2 + e
                gap = jnp.where(causal, s[:, h : h + 1] - s_row[h : h + 1, :], -1e30)
                scores = (cb * (jnp.exp(gap) * dt_row[h : h + 1, :])).astype(BF16)
                term = dot(scores, x_pair * masks[e])
                total = term if total is None else total + term
            y_out[tok, lanes] = total
        return 0

    lax.fori_loop(0, x_in.shape[0] // SPAN, block, 0)


def entering_state(place, count, sums, decays, backward):
    inner = sums.shape[2]
    state = jnp.zeros((STATE, inner), F32)
    for turn in range(count):
        other = count - 1 - turn if backward else turn
        ahead = (place < other) if backward else (other < place)
        state = jnp.where(ahead, decays[other, 0:1] * state + sums[other].astype(F32), state)
    return state


def chain_states(state, local, decay, states_out):
    def block(q, state):
        states_out[q] = state
        return decay[q, 0:1] * state + local[q]

    lax.fori_loop(0, local.shape[0], block, state)


def mix_out(q, states, x, bc, z, s, wo, rowp, y_out, part_out, sq_out):
    inner = x.shape[1]
    tok = pl.ds(pl.multiple_of(q * SPAN, SPAN), SPAN)
    carried = dot_split(jnp.exp(s[tok, :]), head_spread(inner)) * dot(bc[tok, STATE:], states[q].astype(BF16))
    y = y_out[tok, :] + carried + rowp[6:7] * x[tok, :].astype(F32)
    y_out[tok, :] = y
    zf = z[tok, :].astype(F32)
    gated = y * (zf * sigmoid(zf))
    sq_out[:, tok] = dot_exact(jnp.ones((8, inner), F32), gated * gated, NT)
    part_out[tok, :] = dot((gated * rowp[5:6]).astype(BF16), wo[...], NT).astype(BF16)


def back_through_gate(
    inner_all, dmix, wo, y_in, z, x, bc, s, decay, token_scalars, rowp, cat_out, wide, dy_out, prior, normed_out
):
    inner = x.shape[1]
    spans = x.shape[0] // SPAN
    spread = head_spread(inner)
    gain = rowp[5:6]
    cols = columns_of(inner)

    def block(i, carry):
        grad_sum, gain_sum, skip_sum = carry
        q = spans - 1 - i
        tok = pl.ds(pl.multiple_of(q * SPAN, SPAN), SPAN)
        columns = token_scalars[:, tok].T
        inv, total_dot = columns[:, 0:1], columns[:, 1:2]
        zf = z[tok, :].astype(F32)
        sig = sigmoid(zf)
        act = zf * sig
        y = y_in[tok, :]
        gated = y * act
        d_no = dot(dmix[tok, :], wo[...])
        scaled = gated * inv
        normed_out[tok, :] = (scaled * gain).astype(BF16)
        gain_sum = gain_sum + jnp.sum(d_no * scaled, axis=0, keepdims=True)
        d_gated = inv * (d_no * gain) - gated * (inv * inv * inv * total_dot * (1.0 / inner_all))
        after = pl.ds(pl.multiple_of(q * SPAN + EDGE, EDGE), SPAN)
        cat_out[after, cols.z] = (d_gated * y * (sig * (1.0 + zf * (1.0 - sig)))).astype(BF16)
        dy = d_gated * act
        xf = x[tok, :].astype(F32)
        skip_sum = skip_sum + jnp.sum(dy * xf, axis=0, keepdims=True)
        dy_low = dy.astype(BF16)
        dy_out[tok, :] = dy_low
        scaled_dy = (dy_low.astype(F32) * dot_split(jnp.exp(s[tok, :]), spread)).astype(BF16)
        fresh = dot(bc[tok, STATE:], scaled_dy, TN)
        prior[q] = fresh
        return fresh + decay[q, 0:1] * grad_sum, gain_sum, skip_sum

    zero = jnp.zeros((1, inner), F32)
    grad_sum, gain_sum, skip_sum = lax.fori_loop(
        0, spans, block, (jnp.zeros((STATE, inner), F32), zero, zero)
    )
    decay_all = decay[0, 0:1]
    for q in range(1, spans):
        decay_all = decay_all * decay[q, 0:1]
    wide[...] = jnp.zeros_like(wide)
    wide[5:6] = gain_sum
    wide[6:7] = skip_sum
    return grad_sum, decay_all


def out_gradient(dmix, normed_out, gwo_out):
    def rows_of(i, _):
        rows = pl.ds(pl.multiple_of(i * SPAN, SPAN), SPAN)
        gwo_out[rows, :] = dot(dmix[:, rows], normed_out[...], TN).astype(BF16)
        return 0

    lax.fori_loop(0, dmix.shape[1] // SPAN, rows_of, 0)


def back_within_spans(dy_in, x_in, bc_in, s_in, dt_in, dpre, flow_out, sum_out):
    inner = x_in.shape[1]

    def block(q, _):
        at = pl.multiple_of(q * SPAN, SPAN)
        tok = pl.ds(at, SPAN)
        after = pl.ds(pl.multiple_of(at + EDGE, EDGE), SPAN)
        x_low, dy = x_in[tok, :], dy_in[tok, :]
        b, c = bc_in[tok, :STATE], bc_in[tok, STATE:]
        s, dt = s_in[tok, :], dt_in[tok, :]
        s_row = s.T
        cb = dot(b, c, NT)
        seen = iota((SPAN, SPAN), 0) <= iota((SPAN, SPAN), 1)
        masks = half_masks()
        d_cb = jnp.zeros((SPAN, SPAN), F32)
        lane = iota((SPAN, 128), 1)
        row_id = iota((128, SPAN), 0)
        sum_k = jnp.zeros((128, SPAN), F32)
        sum_t = jnp.zeros((SPAN, 128), F32)
        for pair in range(inner // 128):
            lanes = slice(pair * 128, pair * 128 + 128)
            x_pair, dy_pair = x_low[:, lanes], dy[:, lanes]
            total = None
            for e in range(2):
                h = pair * 2 + e
                d_scores = dot(x_pair * masks[e], dy_pair, NT)
                fade = jnp.exp(jnp.where(seen, s_row[h : h + 1, :] - s[:, h : h + 1], -1e30))
                dt_h = dt[:, h : h + 1]
                fade_cb = cb * fade
                term = dot((fade_cb * dt_h).astype(BF16), dy_pair * masks[e])
                total = term if total is None else total + term
                d_cb = d_cb + d_scores * (fade * dt_h)
                flow = d_scores * fade_cb
                sum_t = jnp.where(lane == h, jnp.sum(flow, axis=1, keepdims=True), sum_t)
                sum_k = jnp.where(row_id == h, jnp.sum(flow * dt_h, axis=0, keepdims=True), sum_k)
            dpre[after, lanes] = total
        d_cb_low = d_cb.astype(BF16)
        dpre[after, inner : inner + STATE] = dot(d_cb_low, c)
        dpre[after, inner + STATE :] = dot(d_cb_low, b, TN)
        flow_out[tok, :] = sum_k.T - sum_t * dt
        sum_out[tok, :] = sum_t
        return 0

    lax.fori_loop(0, x_in.shape[0] // SPAN, block, 0)


def back_through_states(
    grad, prior, decay, states, dy_in, x, bc, s_in, dt_in, dtraw, xin, bcin, rowp, bcp, headp, flow_in, sum_in,
    cat_out, row_out, bcrow_out,
    dpre, dend,
):
    inner = x.shape[1]
    spans = x.shape[0] // SPAN
    spread = head_spread(inner)
    up_tri = triangle(False)
    skip = rowp[6:7]
    rate = -jnp.exp(headp[0:1])
    bias = headp[1:2]
    width = inner + 2 * STATE

    def chain(i, grad):
        q = spans - 1 - i
        before = prior[q] + decay[q, 0:1] * grad
        dend[q] = grad
        return before

    lax.fori_loop(0, spans, chain, grad)
    dpre[0:EDGE] = jnp.zeros((EDGE, width), F32)
    dpre[EDGE + spans * SPAN :] = jnp.zeros((EDGE, width), F32)
    bcrow_out[...] = jnp.zeros_like(bcrow_out)
    cols = columns_of(inner)
    cat_out[0:EDGE, cols.z] = jnp.zeros((EDGE, inner), BF16)
    cat_out[0:EDGE, cols.dt] = jnp.zeros((EDGE, 128), BF16)

    def block(q, _):
        at = pl.multiple_of(q * SPAN, SPAN)
        tok = pl.ds(at, SPAN)
        after = pl.ds(pl.multiple_of(at + EDGE, EDGE), SPAN)
        window = pl.ds(at, SPAN + EDGE)
        x_low, dy = x[tok, :], dy_in[tok, :]
        xf, dyf = x_low.astype(F32), dy.astype(F32)
        b, c = bc[tok, :STATE], bc[tok, STATE:]
        s, dt = s_in[tok, :], dt_in[tok, :]
        exp_s = jnp.exp(s)
        to_end = jnp.exp(s[SPAN - 1 : SPAN] - s)
        w = to_end * dt
        w_all, s_all = dot_split(w, spread), dot_split(exp_s, spread)
        state, grad = states[q], dend[q]
        state_low, grad_low = state.astype(BF16), grad.astype(BF16)
        carried = s_all * dot(c, state_low)
        ds = dot_split(dyf * carried, spread, NT)
        d_c = dot((dyf * s_all).astype(BF16), state_low, NT)
        d_w = dot(b, grad_low)
        d_b = dot((xf * w_all).astype(BF16), grad_low, NT)
        dx = dpre[after, 0:inner] + dyf * skip + d_w * w_all
        dsw = dot_split(d_w * xf, spread, NT)
        end = dsw * w
        ds = ds + flow_in[tok, :] - end
        held = dot_split(jnp.broadcast_to(jnp.sum(grad * state, axis=0, keepdims=True), (8, inner)), spread, NT)[0:1]
        last = jnp.sum(end, axis=0, keepdims=True) + held * exp_s[SPAN - 1 : SPAN]
        ds = ds + jnp.where(iota((SPAN, 128), 0) == SPAN - 1, last, 0.0)
        da = dot_exact(up_tri, ds)
        d_dt = sum_in[tok, :] + dsw * to_end + da * rate
        d_raw = d_dt * sigmoid(dtraw[tok, :].astype(F32) + bias)
        d_raw = jnp.where(iota((SPAN, 128), 1) < inner // HEADDIM, d_raw, 0.0)
        row_out[7:8, 0:128] += jnp.sum(da * (dt * rate), axis=0, keepdims=True)
        row_out[8:9, 0:128] += jnp.sum(d_raw, axis=0, keepdims=True)
        d_low = d_raw.astype(BF16)
        cat_out[after, cols.dt] = d_low

        win_x = xin[window, :].astype(F32)
        d_x = dx * silu_slope(conv_taps(win_x, rowp))
        dpre[after, 0:inner] = d_x
        for j in range(CONV):
            row_out[j : j + 1] += jnp.sum(d_x * win_x[EDGE - 3 + j : EDGE - 3 + j + SPAN], axis=0, keepdims=True)
        row_out[CONV : CONV + 1] += jnp.sum(d_x, axis=0, keepdims=True)
        win_bc = bcin[window, :].astype(F32)
        d_bc = dpre[after, inner:] + jnp.concatenate([d_b, d_c], axis=1)
        d_bc = d_bc * silu_slope(conv_taps(win_bc, bcp))
        dpre[after, inner:] = d_bc
        for j in range(CONV):
            bcrow_out[j : j + 1] += jnp.sum(d_bc * win_bc[EDGE - 3 + j : EDGE - 3 + j + SPAN], axis=0, keepdims=True)
        bcrow_out[CONV : CONV + 1] += jnp.sum(d_bc, axis=0, keepdims=True)
        return 0

    lax.fori_loop(0, spans, block, 0)

    def back(window, taps, rows):
        total = None
        for j in range(CONV):
            term = taps[j : j + 1] * window[CONV - 1 - j : CONV - 1 - j + rows]
            total = term if total is None else total + term
        return total.astype(BF16)

    cat_out[0:EDGE, cols.x] = back(dpre[0 : 2 * EDGE, 0:inner], rowp, EDGE)
    cat_out[0:EDGE, cols.bc] = back(dpre[0 : 2 * EDGE, inner:], bcp, EDGE)

    def conv_block(q, _):
        after = pl.ds(pl.multiple_of(q * SPAN + EDGE, EDGE), SPAN)
        window = pl.ds(pl.multiple_of(q * SPAN + EDGE, EDGE), SPAN + EDGE)
        cat_out[after, cols.x] = back(dpre[window, 0:inner], rowp, SPAN)
        cat_out[after, cols.bc] = back(dpre[window, inner:], bcp, SPAN)
        return 0

    lax.fori_loop(0, spans, conv_block, 0)


def project_back_edge(cat, w, dn_out):
    cols = columns_of((w.shape[1] - 3 * STATE) // 2)
    dn_out[0:EDGE] = (
        dot(cat[0:EDGE, cols.x], w[:, cols.x], NT) + dot(cat[0:EDGE, cols.bc], w[:, cols.bc], NT)
    ).astype(BF16)


def project_back(q, cat, w, dn_out):
    after = pl.ds(pl.multiple_of(q * SPAN + EDGE, EDGE), SPAN)
    dn_out[after, :] = dot(cat[after, :], w[...], NT).astype(BF16)


def for_row_blocks(grad, body):
    groups, rows = grad

    def one(g, _):
        body(pl.ds(pl.multiple_of(g * rows, 128), rows) if rows % 128 == 0 else pl.ds(g * rows, rows), g)
        return 0

    if rows % 128 == 0:
        lax.fori_loop(0, groups, one, 0)
    else:
        for g in range(groups):
            one(g, 0)


def x_gradient(cat, normed, gx_out):
    cols = columns_of(gx_out.shape[1])

    def body(at, _):
        total = dot(normed[EDGE:, at], cat[EDGE:, cols.x], TN) + dot(normed[0:EDGE, at], cat[0:EDGE, cols.x], TN)
        gx_out[at, :] = total.astype(BF16)

    for_row_blocks((normed.shape[1] // SPAN, SPAN), body)


def z_gradient(cat, normed, gz_out):
    cols = columns_of(gz_out.shape[1])

    def body(at, _):
        gz_out[at, :] = dot(normed[EDGE:, at], cat[EDGE:, cols.z], TN).astype(BF16)

    for_row_blocks((normed.shape[1] // SPAN, SPAN), body)


def small_gradients(cat, normed, gbc_out, gdt_out):
    groups, parts, shard, _ = gbc_out.shape
    cols = columns_of((cat.shape[1] - 3 * STATE) // 2)

    def body(at, g):
        edge, tokens = normed[0:EDGE, at], normed[EDGE:, at]
        bc = dot(tokens, cat[EDGE:, cols.bc], TN) + dot(edge, cat[0:EDGE, cols.bc], TN)
        gbc_out[g] = bc.reshape(parts, shard, 2 * STATE).astype(BF16)
        gdt_out[g] = dot(cat[EDGE:, cols.dt], tokens, TN)[0:EDGE].astype(BF16)

    for_row_blocks((groups, parts * shard), body)


HALF = 128
MESH = pl.DeviceIdType.MESH


class Links:
    def __init__(self, sends, recvs):
        self.z, self.p, self.c = lax.axis_index("z"), lax.axis_index("p"), lax.axis_index("head")
        self.groups = lax.axis_size("z")
        self.sends, self.recvs, self.used = sends, recvs, 0

    def copy(self, src, dst, device):
        i = self.used
        self.used += 1
        return pltpu.make_async_remote_copy(
            src_ref=src, dst_ref=dst, send_sem=self.sends.at[i], recv_sem=self.recvs.at[i],
            device_id=device, device_id_type=MESH,
        )

    def local(self, src, dst):
        i = self.used
        self.used += 1
        return pltpu.make_async_copy(src, dst, self.sends.at[i])

    def at(self, k, e):
        return (self.z, lax.bitwise_xor(self.p, jnp.int32(k)), lax.bitwise_xor(self.c, jnp.int32(e)))

    def last_of_plane(self):
        return jnp.logical_and(self.p == GROUP - 1, self.c == 1)

    def greet(self, plane=False, sibling=False, groups=False, edge=0):
        barrier = pltpu.get_barrier_semaphore()
        z, count = self.z, self.groups
        above = z < count - 1

        def signal(device):
            pl.semaphore_signal(barrier, 1, device_id=device, device_id_type=MESH)

        self.expected = jnp.int32(0)
        for k in range(GROUP):
            for e in range(2):
                if (k or e) if plane else (sibling and e and not k):
                    signal(self.at(k, e))
                    self.expected = self.expected + 1
        if groups:
            for k in range(1, count):
                signal((lax.rem(z + k, count), self.p, self.c))
            self.expected = self.expected + (count - 1)
        sending = jnp.logical_and(self.last_of_plane(), above)
        if edge == 1:
            pl.when(z > 0)(lambda: signal((z - 1, jnp.int32(GROUP - 1), jnp.int32(1))))
            self.expected = self.expected + 2 * GROUP * sending.astype(jnp.int32)
        if edge == -1:

            @pl.when(sending)
            def _():
                for p in range(GROUP):
                    for c in range(2):
                        signal((z + 1, jnp.int32(p), jnp.int32(c)))

            self.expected = self.expected + (z > 0).astype(jnp.int32)

    def meet(self):
        pl.semaphore_wait(pltpu.get_barrier_semaphore(), self.expected)

    def start_barrier(self, **who):
        self.greet(**who)
        self.meet()


class Chain:
    def __init__(self, links, pieces):
        z, p, c, groups = links.z, links.p, links.c, links.groups
        self.steps, self.now = [], 0
        for step in range(1, groups):
            found = []
            up, down = z - step + 1, z + step - 1
            for piece in pieces:
                block = piece(jnp.maximum(up, 0))
                sending = jnp.logical_and(up >= 0, z < groups - 1)
                found.append((sending, z - step >= 0, links.copy(block, block, (z + 1, p, c))))
                block = piece(jnp.minimum(down, groups - 1))
                sending = jnp.logical_and(down < groups, z > 0)
                found.append((sending, z + step < groups, links.copy(block, block, (z - 1, p, c))))
            self.steps.append(found)

    def begin(self):
        for sending, _, copy in self.steps[0]:
            pl.when(sending)(copy.start)

    def advance(self):
        if self.now + 1 < len(self.steps):
            for (_, receiving, copy), (sending, _, later) in zip(self.steps[self.now], self.steps[self.now + 1]):
                pl.when(receiving)(copy.wait_recv)
                pl.when(sending)(later.start)
            self.now += 1

    def complete(self):
        while self.now + 1 < len(self.steps):
            self.advance()
        for _, receiving, copy in self.steps[-1]:
            pl.when(receiving)(copy.wait_recv)

    def finish(self):
        for found in self.steps:
            for sending, _, copy in found:
                pl.when(sending)(copy.wait_send)


class Swap:
    def __init__(self, links, shard, staging, out, lanes, width):
        self.links, self.staging, self.out, self.lanes = links, staging, out, lanes

        def source(k):
            to = lax.bitwise_xor(links.p, jnp.int32(k))
            if len(shard.shape) == 3:
                return shard.at[to]
            if shard.shape[1] == width:
                return shard
            return shard.at[:, pl.ds(pl.multiple_of(to * width, 128), width)]

        self.copies = [links.copy(source(k), staging.at[links.p], links.at(k, 0)) for k in (3, 1, 2)]
        self.keep = links.local(source(0), staging.at[links.p])

    def start(self):
        for copy in self.copies:
            copy.start()

    def settle(self):
        self.keep.wait()
        for copy in self.copies:
            copy.wait_recv()
        parts, shard, width = self.staging.shape
        rows = parts * shard
        first = self.links.z * rows if self.out.shape[0] > rows else 0
        if shard % EDGE == 0:
            for j in range(parts):
                self.out[pl.ds(pl.multiple_of(first + j * shard, EDGE), shard), self.lanes] = self.staging[j]
        else:
            block = self.staging[...].astype(F32).reshape(rows, width).astype(BF16)
            self.out[pl.ds(pl.multiple_of(first, EDGE), rows), self.lanes] = block

    def finish(self):
        for copy in self.copies:
            copy.wait_send()


class Collect:
    def __init__(self, links, grad, out):
        rows = grad.shape[0] // links.groups
        z, groups = links.z, links.groups

        def block(index):
            return grad.at[pl.ds(pl.multiple_of(index * rows, EDGE), rows)]

        self.keep = links.local(block(z), out.at[0])
        self.kept = False
        self.copies = []
        for k in range(1, groups):
            to = lax.rem(z + k, groups)
            self.copies.append(links.copy(block(to), out.at[k], (to, links.p, links.c)))

    def start(self):
        self.keep.start()
        for copy in self.copies:
            copy.start()

    def keep_own(self):
        if not self.kept:
            self.keep.wait()
        self.kept = True

    def arrive(self):
        self.keep_own()
        for copy in self.copies:
            copy.wait_recv()

    def finish(self):
        self.keep_own()
        for copy in self.copies:
            copy.wait_send()


class Deliver:
    def __init__(self, links, parts, final, out):
        self.links, self.parts, self.final, self.out = links, parts, final, out
        inner = parts.shape[2]
        self.mine = pl.ds(pl.multiple_of(links.p * inner, 128), inner)
        self.copies = [
            links.copy(final.at[lax.bitwise_xor(links.p, jnp.int32(k))], out.at[:, self.mine], links.at(k, 0))
            for k in (3, 1, 2)
        ]

    def start(self):
        total = self.parts[0].astype(F32)
        for k in range(1, self.parts.shape[0]):
            total = total + self.parts[k].astype(F32)
        shard = self.final.shape[1]
        for j in range(GROUP):
            self.final[j] = total[j * shard : (j + 1) * shard].astype(BF16)
        for copy in self.copies:
            copy.start()
        self.out[:, self.mine] = self.final[self.links.p]

    def arrive(self):
        for copy in self.copies:
            copy.wait_recv()

    def finish(self):
        for copy in self.copies:
            copy.wait_send()


class States:
    def __init__(self, links, backward, state, decay, states, decays):
        z, groups = links.z, links.groups
        self.links, self.refs = links, (state, decay, states, decays)
        self.found = []
        for k in range(1, groups):
            to, source = (z - k, z + k) if backward else (z + k, z - k)
            sending, receiving = (to >= 0, source < groups) if backward else (to < groups, source >= 0)
            device = (jnp.clip(to, 0, groups - 1), links.p, links.c)
            pair = [links.copy(state, states.at[z], device), links.copy(decay, decays.at[z], device)]
            self.found.append((sending, receiving, pair))

    def start(self):
        for sending, _, pair in self.found:

            @pl.when(sending)
            def _(pair=pair):
                for copy in pair:
                    copy.start()

    def arrive(self):
        for _, receiving, pair in self.found:

            @pl.when(receiving)
            def _(pair=pair):
                for copy in pair:
                    copy.wait_recv()

    def finish(self):
        for sending, _, pair in self.found:

            @pl.when(sending)
            def _(pair=pair):
                for copy in pair:
                    copy.wait_send()


class Gather:
    def __init__(self, links, out, base):
        self.links, self.out, self.base = links, out, base

        def place(k, c):
            row = base + lax.bitwise_xor(links.p, jnp.int32(k)) * (2 * HALF) + c * HALF
            return out.at[pl.ds(pl.multiple_of(row, EDGE), HALF), :]

        own = place(0, links.c)
        self.out_copies = [links.copy(own, own, links.at(k, 0)) for k in (3, 1, 2)]
        self.shared = [links.copy(own, own, links.at(0, 1))]
        self.shared += [links.copy(place(k, links.c), place(k, links.c), links.at(0, 1)) for k in (1, 2, 3)]
        self.arrivals = [self.out_copies[1], self.out_copies[2], self.out_copies[0]]

    def own(self, start, size):
        row = self.base + self.links.p * (2 * HALF) + self.links.c * HALF + start
        return pl.ds(pl.multiple_of(row, EDGE), size)

    def start(self):
        for copy in self.out_copies:
            copy.start()
        self.shared[0].start()

    def pass_on(self):
        for k in range(3):
            self.arrivals[k].wait_recv()
            self.shared[k + 1].start()

    def finish(self):
        for copy in self.shared:
            copy.wait_recv()
        for copy in self.shared + self.out_copies:
            copy.wait_send()


class EdgeForward:
    def __init__(self, links, gather):
        self.links = links
        tail = gather.out.at[gather.own(HALF - EDGE, EDGE), :]
        first = links.used
        links.used += 2 * GROUP + 1
        recv = links.recvs.at[first + 2 * GROUP]
        self.out = gather.out
        self.copies = [
            pltpu.make_async_remote_copy(
                src_ref=tail, dst_ref=gather.out.at[0:EDGE, :], send_sem=links.sends.at[first + p * 2 + c], recv_sem=recv,
                device_id=(links.z + 1, jnp.int32(p), jnp.int32(c)), device_id_type=MESH,
            )
            for p in range(GROUP)
            for c in range(2)
        ]
        self.sending = jnp.logical_and(links.last_of_plane(), links.z < links.groups - 1)

    def start(self):
        @pl.when(self.sending)
        def _():
            for copy in self.copies:
                copy.start()

        @pl.when(self.links.z == 0)
        def _():
            self.out[0:EDGE, :] = jnp.zeros((EDGE, self.out.shape[1]), self.out.dtype)

    def finish(self):
        pl.when(self.links.z > 0)(self.copies[0].wait_recv)

        @pl.when(self.sending)
        def _():
            for copy in self.copies:
                copy.wait_send()


class Scatter:
    def __init__(self, links, part, base, sib, total, peer):
        self.links, self.part, self.base = links, part, base
        self.sib, self.total, self.peer = sib, total, peer
        other = 1 - links.c
        self.to_sibling = {
            k: links.copy(part.at[self.rows(k, other, 0, HALF), :], sib.at[k], links.at(0, 1)) for k in (3, 1, 2, 0)
        }
        self.to_peer = {k: links.copy(total.at[k - 1], peer.at[k - 1], links.at(k, 0)) for k in (3, 1, 2)}

    def rows(self, k, c, start, size):
        row = self.base + lax.bitwise_xor(self.links.p, jnp.int32(k)) * (2 * HALF) + c * HALF + start
        return pl.ds(pl.multiple_of(row, EDGE), size)

    def pass_on(self, k):
        self.to_sibling[k].wait_recv()
        if k == 0:
            return

        def add(i, _):
            at = pl.ds(pl.multiple_of(i * 32, 32), 32)
            mine = self.part[self.rows(k, self.links.c, i * 32, 32), :].astype(F32)
            self.total[k - 1, at, :] = (mine + self.sib[k, at, :].astype(F32)).astype(BF16)
            return 0

        lax.fori_loop(0, HALF // 32, add, 0)
        self.to_peer[k].start()

    def arrive(self):
        for copy in self.to_peer.values():
            copy.wait_recv()

    def own(self, start, size):
        at = pl.ds(start, size)
        total = self.part[self.rows(0, self.links.c, start, size), :].astype(F32) + self.sib[0, at, :].astype(F32)
        for k in range(3):
            total = total + self.peer[k, at, :].astype(F32)
        return total

    def finish(self):
        for copy in list(self.to_sibling.values()) + list(self.to_peer.values()):
            copy.wait_send()


class SmallSum:
    def __init__(self, links, squares, slots):
        self.links, self.squares, self.slots = links, squares, slots
        self.copies = [
            links.copy(squares.at[:, self.lanes(k, e)], slots.at[2 * k + e - 1], links.at(k, e))
            for k in range(GROUP)
            for e in range(2)
            if k or e
        ]

    def lanes(self, k, e):
        links = self.links
        column = lax.bitwise_xor(links.p, jnp.int32(k)) * (2 * HALF) + lax.bitwise_xor(links.c, jnp.int32(e)) * HALF
        return pl.ds(pl.multiple_of(column, HALF), HALF)

    def start(self):
        for copy in self.copies:
            copy.start()

    def total(self):
        for copy in self.copies:
            copy.wait_recv()
        total = self.squares[:, self.lanes(0, 0)]
        for i in range(len(self.copies)):
            total = total + self.slots[i]
        return total

    def finish(self):
        for copy in self.copies:
            copy.wait_send()


class SmallGather:
    def __init__(self, links, out):
        self.out = out
        self.lanes = pl.ds(pl.multiple_of(links.p * (2 * HALF) + links.c * HALF, HALF), HALF)
        self.copies = [
            links.copy(out.at[:, self.lanes], out.at[:, self.lanes], links.at(k, e))
            for k in range(GROUP)
            for e in range(2)
            if k or e
        ]

    def start(self):
        for copy in self.copies:
            copy.start()

    def finish(self):
        for copy in self.copies:
            copy.wait()


def row_chunks(size=32):
    return [(start, size) for start in range(0, HALF, size)]


def rms_of(rows):
    return lax.rsqrt(jnp.mean(rows * rows, axis=-1, keepdims=True) + EPS)


def as_tile(columns):
    lane = iota((HALF, HALF), 1)
    wide = jnp.zeros((HALF, HALF), F32)
    for i, column in enumerate(columns):
        wide = jnp.where(lane == i, column, wide)
    return wide.T[0:8]


def grad_rows(links, scatter, edge_slots, grad, resid, gain, gain_out, start, size):
    at = slice(start, start + size)
    d_normed = scatter.own(start, size)
    if start + size == HALF:
        extra = edge_slots[0].astype(F32)
        for i in range(1, 2 * GROUP):
            extra = extra + edge_slots[i].astype(F32)
        used = jnp.logical_and(links.last_of_plane(), links.z < links.groups - 1)
        extra = jnp.where(used, extra, 0.0)
        d_normed = d_normed + jnp.concatenate([jnp.zeros((size - EDGE, extra.shape[1]), F32), extra])
    rows = resid[at]
    inv_rms = rms_of(rows)
    gain_sum = jnp.sum(d_normed * rows * inv_rms, axis=0, keepdims=True)
    gain_out[0:1] = gain_sum if start == 0 else gain_out[0:1] + gain_sum
    d_hidden = d_normed * gain[...]
    return (
        grad[at]
        + inv_rms * d_hidden
        - rows * (inv_rms * inv_rms * inv_rms * jnp.mean(d_hidden * rows, axis=-1, keepdims=True))
    )


class EdgeBackward:
    def __init__(self, links, part, slots):
        self.links = links
        first = links.used
        links.used += 2 * GROUP + 1
        me = links.p * 2 + links.c
        self.send = pltpu.make_async_remote_copy(
            src_ref=part.at[0:EDGE, :], dst_ref=slots.at[me], send_sem=links.sends.at[first], recv_sem=links.recvs.at[first + me],
            device_id=(links.z - 1, jnp.int32(GROUP - 1), jnp.int32(1)), device_id_type=MESH,
        )
        self.recvs = [
            pltpu.make_async_remote_copy(
                src_ref=part.at[0:EDGE, :], dst_ref=slots.at[i], send_sem=links.sends.at[first], recv_sem=links.recvs.at[first + i],
                device_id=(links.z, links.p, 1 - links.c), device_id_type=MESH,
            )
            for i in range(2 * GROUP)
        ]
        self.receiving = jnp.logical_and(links.last_of_plane(), links.z < links.groups - 1)

    def start(self):
        pl.when(self.links.z > 0)(self.send.start)

    def receive(self):
        @pl.when(self.receiving)
        def _():
            for copy in self.recvs:
                copy.wait_recv()

    def finish(self):
        pl.when(self.links.z > 0)(self.send.wait_send)


class BcSum:
    def __init__(self, links, bc, out, bufs):
        self.links, self.bc, self.out = links, bc, out
        self.sib, self.chip, self.peer, self.total, self.far = bufs
        p, c, groups = links.p, links.c, links.groups
        self.own = pl.ds(pl.multiple_of(c * STATE, STATE), STATE)
        other = pl.ds(pl.multiple_of((1 - c) * STATE, STATE), STATE)
        self.first = [links.copy(bc.at[:, :, :, other], self.sib, links.at(0, 1))]
        self.second = [
            links.copy(self.chip.at[:, lax.bitwise_xor(p, jnp.int32(k))], self.peer.at[k - 1], links.at(k, 0))
            for k in (3, 1, 2)
        ]
        self.third = []
        for k in range(1, groups):
            to = lax.rem(links.z + k, groups)
            self.third.append(links.copy(self.total.at[to], self.far.at[k - 1], (to, p, c)))
        self.fourth = [links.copy(out.at[:, self.own], out.at[:, self.own], links.at(0, 1))]

    @staticmethod
    def begin(copies):
        for copy in copies:
            copy.start()

    @staticmethod
    def arrive(copies):
        for copy in copies:
            copy.wait_recv()

    def cores(self):
        self.begin(self.first)

    def plane(self):
        self.arrive(self.first)

        def add(i, _):
            for q in range(GROUP):
                mine = self.bc[i, q, :, self.own].astype(F32)
                self.chip[i, q] = (mine + self.sib[i, q].astype(F32)).astype(BF16)
            return 0

        lax.fori_loop(0, self.links.groups, add, 0)
        self.begin(self.second)

    def groups(self):
        self.arrive(self.second)

        def add(i, _):
            total = self.chip[i, self.links.p].astype(F32)
            for k in range(GROUP - 1):
                total = total + self.peer[k, i].astype(F32)
            self.total[i] = total.astype(BF16)
            return 0

        lax.fori_loop(0, self.links.groups, add, 0)
        self.begin(self.third)

    def share(self):
        self.arrive(self.third)
        total = self.total[self.links.z].astype(F32)
        for k in range(self.links.groups - 1):
            total = total + self.far[k].astype(F32)
        self.out[:, self.own] = total.astype(BF16)
        self.begin(self.fourth)

    def finish(self):
        self.arrive(self.fourth)
        for copy in self.first + self.second + self.third + self.fourth:
            copy.wait_send()


class LaidOut:
    def __init__(self, links, dt, wide, dt_out, wide_out, dt_far, wide_far):
        self.links, self.refs = links, (dt, wide, dt_out, wide_out, dt_far, wide_far)
        z, p, c, groups = links.z, links.p, links.c, links.groups
        self.first, self.second = [], []
        for k in range(1, groups):
            to = lax.rem(z + k, groups)
            self.first.append(links.copy(dt.at[to], dt_far.at[k - 1], (to, p, c)))
            self.first.append(links.copy(wide, wide_far.at[k - 1], (to, p, c)))
        for k in range(1, GROUP):
            self.second.append(links.copy(dt_out.at[p], dt_out.at[p], links.at(k, 0)))
            self.second.append(links.copy(wide_out.at[p], wide_out.at[p], links.at(k, 0)))

    def groups(self):
        BcSum.begin(self.first)

    def plane(self):
        BcSum.arrive(self.first)
        dt, wide, dt_out, wide_out, dt_far, wide_far = self.refs
        dt_total, wide_total = dt[self.links.z].astype(F32), wide[...]
        for k in range(self.links.groups - 1):
            dt_total = dt_total + dt_far[k].astype(F32)
            wide_total = wide_total + wide_far[k]
        dt_out[self.links.p] = dt_total.astype(BF16)
        wide_out[self.links.p] = wide_total
        BcSum.begin(self.second)

    def finish(self):
        BcSum.arrive(self.second)
        for copy in self.first + self.second:
            copy.wait_send()


class VecSum:
    def __init__(self, links, vec, out, near, far):
        self.links, self.refs = links, (vec, out, near, far)
        z, p, c, groups = links.z, links.p, links.c, links.groups
        self.first, self.second, self.third = [], [], []
        for k in range(GROUP):
            for e in range(2):
                if k or e:
                    to = lax.bitwise_xor(p, jnp.int32(k)) * 2 + lax.bitwise_xor(c, jnp.int32(e))
                    self.first.append(links.copy(vec.at[to], near.at[2 * k + e - 1], links.at(k, e)))
                    self.third.append(links.copy(out.at[p * 2 + c], out.at[p * 2 + c], links.at(k, e)))
        for k in range(1, groups):
            self.second.append(links.copy(near.at[7], far.at[k - 1], (lax.rem(z + k, groups), p, c)))

    def plane(self):
        BcSum.begin(self.first)

    def groups(self):
        BcSum.arrive(self.first)
        vec, _, near, _ = self.refs
        total = vec[self.links.p * 2 + self.links.c]
        for slot in range(2 * GROUP - 1):
            total = total + near[slot]
        near[7] = total
        BcSum.begin(self.second)

    def back(self):
        BcSum.arrive(self.second)
        _, out, near, far = self.refs
        total = near[7]
        for k in range(self.links.groups - 1):
            total = total + far[k]
        out[self.links.p * 2 + self.links.c] = total
        BcSum.begin(self.third)

    def finish(self):
        BcSum.arrive(self.third)
        for copy in self.first + self.second + self.third:
            copy.wait_send()


class Refs:
    def __init__(self, refs, twins, sems):
        self.__dict__.update(refs)
        self.twins = {id(near): (far, near, sems.at[i]) for i, (far, near) in enumerate(twins)}
        self.waits = []

    def fetch(self, *refs):
        for ref in refs:
            far, near, sem = self.twins[id(ref)]
            pltpu.make_async_copy(far, near, sem).start()

    def need(self, *refs):
        for ref in refs:
            pltpu.make_async_copy(*self.twins[id(ref)]).wait()

    def flush(self, *refs):
        for ref in refs:
            far, near, sem = self.twins[id(ref)]
            self.waits.append(pltpu.make_async_copy(near, far, sem))
            self.waits[-1].start()

    def done(self):
        for copy in self.waits:
            copy.wait()


def weight_chain(links, w, steps, inner):
    rows, step_rows = w.shape[0] // links.groups, steps.shape[0] // links.groups
    cols = columns_of(inner)
    half = pl.ds(pl.multiple_of(cols.bc.start + links.c * STATE, STATE), STATE)

    def at(index):
        return pl.ds(pl.multiple_of(index * rows, EDGE), rows)

    pieces = [
        lambda i: w.at[at(i), cols.x],
        lambda i: w.at[at(i), cols.z],
        lambda i: w.at[at(i), half],
        lambda i: steps.at[pl.ds(pl.multiple_of(i * step_rows, EDGE), step_rows), :],
    ]
    return Chain(links, pieces), links.copy(w.at[:, half], w.at[:, half], links.at(0, 1))


def pack_steps(w_dt, steps_out, wide):
    heads_core, shard = w_dt.shape
    heads = heads_core // GROUP
    wide[...] = jnp.zeros_like(wide)
    wide[0:heads_core, 0:shard] = w_dt
    row, col = iota((EDGE, 128), 0), iota((EDGE, 128), 1)
    for q in range(GROUP):
        pick = jnp.logical_and(col == q * heads + row, row < heads).astype(BF16)
        steps_out[q] = dot(pick, wide[...]).astype(BF16)


def unpack_steps(steps, w, shard, inner):
    lanes = columns_of(inner).dt
    rows = GROUP * shard
    blank = jnp.zeros((128 - EDGE, 128), F32)

    def block(g, _):
        parts = []
        for j in range(GROUP):
            at = pl.ds(pl.multiple_of(g * (GROUP * EDGE) + j * EDGE, EDGE), EDGE)
            parts.append(jnp.concatenate([steps[at, :].astype(F32), blank]).T[0:shard])
        w[pl.ds(pl.multiple_of(g * rows, EDGE), rows), lanes] = jnp.concatenate(parts).astype(BF16)
        return 0

    lax.fori_loop(0, w.shape[0] // rows, block, 0)


def prepare(links, r, layer):
    inner = r.rowp.shape[1]
    heads_core = r.head_params.shape[2]
    lanes = pl.ds(pl.multiple_of(links.p * inner, 128), inner)
    r.gains[...] = r.norm_gain[...].astype(F32)
    r.headp[...] = jnp.zeros_like(r.headp)
    for i in range(3):
        r.headp[i : i + 1, 0:heads_core] = r.head_params[i, layer : layer + 1, :]
    mine = dot_exact(r.headp[...], head_pick(links.p, inner // HEADDIM).astype(F32))
    r.headp[...] = mine
    r.rowp[...] = jnp.zeros_like(r.rowp)
    r.rowp[0 : CONV + 1] = r.conv_x[:, :, lanes].astype(F32)[:, layer]
    r.rowp[5:6] = r.gated_gain[:, lanes].astype(F32)[layer : layer + 1]
    r.rowp[6:7] = dot_exact(mine, head_spread(inner).astype(F32))[2:3]
    r.bcp[...] = jnp.zeros_like(r.bcp)
    r.bcp[0 : CONV + 1] = r.conv_bc[...].astype(F32)[:, layer]


def out_chain(links, wo):
    rows = wo.shape[0] // links.groups
    return Chain(links, [lambda i: wo.at[pl.ds(pl.multiple_of(i * rows, EDGE), rows), :]])


def weight_swaps(links, r, layer, w, steps, wo):
    inner = wo.shape[1]
    cols = columns_of(inner)
    stagings = r.stagings[layer]
    here = pl.ds(pl.multiple_of(links.c * STATE, STATE), STATE)
    half = pl.ds(pl.multiple_of(cols.bc.start + links.c * STATE, STATE), STATE)
    swaps = [
        Swap(links, r.w_zx.at[layer, 1], stagings[0], w, cols.x, inner),
        Swap(links, r.w_zx.at[layer, 0], stagings[1], w, cols.z, inner),
        Swap(links, r.w_bc.at[layer, :, here], stagings[2], w, half, STATE),
        Swap(links, r.packed_steps.at[layer], stagings[3], steps, slice(0, 128), 128),
    ]
    return swaps, Swap(links, r.w_out.at[layer], stagings[4], wo, slice(0, inner), inner)


def scatter_blocks(scatter, compute):
    before = None
    for k in (3, 1, 2, 0):
        compute(lax.bitwise_xor(scatter.links.p, jnp.int32(k)))
        scatter.to_sibling[k].start()
        if before is not None:
            scatter.pass_on(before)
        before = k


def forward_layer(links, r, normed, w, wo, wo_chain, scatter, meanwhile):
    carried = States(links, False, r.state_low, r.decay_row, r.states_in, r.decays_in)
    state_sum, decay_all = project_and_convolve(
        normed, w, r.rowp, r.bcp, r.headp, r.z, r.xin, r.bcin, r.x, r.bc, r.dtraw, r.dt, r.s, r.decay, r.ext, r.local,
        lambda q: pl.when(q == 3)(wo_chain.advance),
    )
    r.state_low[...] = state_sum.astype(BF16)
    r.decay_row[...] = jnp.broadcast_to(decay_all, r.decay_row.shape)
    carried.start()
    r.flush(r.z, r.xin, r.bcin, r.x, r.bc, r.dtraw, r.dt, r.s, r.decay)
    wo_chain.advance()
    mix_within_spans(r.x, r.bc, r.s, r.dt, r.y)
    wo_chain.complete()
    meanwhile()
    carried.arrive()
    chain_states(entering_state(links.z, links.groups, r.states_in, r.decays_in, False), r.local, r.decay, r.states)
    scatter_blocks(
        scatter, lambda q: mix_out(q, r.states, r.x, r.bc, r.z, r.s, wo, r.rowp, r.y, r.part, r.squares)
    )
    r.flush(r.y, r.states)
    return carried


def first_kernel(inner_all, r):
    links = Links(r.sends, r.recvs)
    c = links.c
    inner = r.wo.shape[1]
    shard = r.w_dt.shape[2]
    links.greet(plane=True, groups=True, edge=1)
    for layer in range(2):
        pack_steps(r.w_dt[layer], r.packed_steps.at[layer], r.wide_steps)
    swaps, swap_o = weight_swaps(links, r, 0, r.w, r.dt_rows, r.wo)
    next_swaps, next_o = weight_swaps(links, r, 1, r.next_w, r.next_dt_rows, r.next_wo)
    all_swaps = swaps + [swap_o] + next_swaps + [next_o]
    gather, other = Gather(links, r.normed, EDGE), Gather(links, r.dmix, 0)
    edge = EdgeForward(links, gather)
    chain, share = weight_chain(links, r.w, r.dt_rows, inner)
    chain_o = out_chain(links, r.wo)
    next_chain, next_share = weight_chain(links, r.next_w, r.next_dt_rows, inner)
    scatter = Scatter(links, r.part, 0, r.sib, r.total, r.peer)
    small = SmallSum(links, r.squares, r.slots)
    next_gather = Gather(links, r.next_normed, EDGE)
    next_edge = EdgeForward(links, next_gather)

    prepare(links, r, 0)
    for swap in all_swaps:
        swap.keep.start()
    for start, size in row_chunks():
        at = pl.ds(pl.multiple_of(c * HALF + start, EDGE), size)
        rows_in = r.resid[at, :].astype(F32)
        r.resid_out[start : start + size] = rows_in
        r.normed[gather.own(start, size), :] = (rows_in * rms_of(rows_in) * r.gains[0:1]).astype(BF16)
        rows_in = r.cot[at, :]
        r.cot_out[start : start + size] = rows_in.astype(F32)
        r.dmix[other.own(start, size), :] = rows_in
    links.meet()
    for swap in swaps:
        swap.start()
    for swap in swaps:
        swap.settle()
    chain.begin()
    gather.start()
    edge.start()
    swap_o.start()
    chain.advance()
    gather.pass_on()
    for swap in next_swaps + [next_o]:
        swap.start()
    chain.advance()
    swap_o.settle()
    gather.finish()
    edge.finish()
    chain.complete()
    share.start()
    chain_o.begin()
    other.start()
    unpack_steps(r.dt_rows, r.w, shard, inner)
    r.flush(r.normed)
    share.wait()
    r.flush(r.w)

    def meanwhile():
        for swap in next_swaps + [next_o]:
            swap.settle()
        next_chain.begin()
        other.pass_on()
        r.flush(r.wo)

    carried = forward_layer(links, r, r.normed, r.w, r.wo, chain_o, scatter, meanwhile)
    small.start()
    next_chain.advance()
    scatter.pass_on(0)
    scatter.arrive()
    inv = lax.rsqrt(small.total() * (1.0 / inner_all) + EPS)
    r.inv_out[...] = inv
    column = inv.T[:, 0:1]
    for start, size in row_chunks():
        at = slice(start, start + size)
        mixed = scatter.own(start, size)
        r.mixed_out[at] = mixed
        fresh = r.resid_out[at] + column[at] * mixed
        r.fresh_out[at] = fresh
        r.next_normed[next_gather.own(start, size), :] = (fresh * rms_of(fresh) * r.gains[1:2]).astype(BF16)
    next_gather.start()
    next_edge.start()
    other.finish()
    r.flush(r.dmix)
    next_chain.advance()
    next_gather.pass_on()
    next_chain.complete()
    next_share.start()
    unpack_steps(r.next_dt_rows, r.next_w, shard, inner)
    scatter.finish()
    small.finish()
    next_gather.finish()
    next_edge.finish()
    carried.finish()
    for swap in all_swaps:
        swap.finish()
    for one in (chain, chain_o, next_chain):
        one.finish()
    next_share.wait()
    r.done()


def second_kernel(inner_all, r):
    links = Links(r.sends, r.recvs)
    rows = r.wo_own.shape[0]
    keep = links.local(r.wo_own, r.wo.at[pl.ds(pl.multiple_of(links.z * rows, EDGE), rows), :])
    chain_o = out_chain(links, r.wo)
    scatter = Scatter(links, r.part, 0, r.sib, r.total, r.peer)
    small = SmallSum(links, r.squares, r.slots)
    spread = SmallGather(links, r.scalars_out)
    at = pl.ds(pl.multiple_of(links.c * HALF, HALF), HALF)
    share = links.copy(r.block_out.at[at, :], r.block_out.at[at, :], links.at(0, 1))
    keep.start()
    links.greet(plane=True, groups=True)
    prepare(links, r, 1)
    keep.wait()
    links.meet()
    chain_o.begin()
    carried = forward_layer(links, r, r.normed, r.w, r.wo, chain_o, scatter, lambda: r.flush(r.wo))
    small.start()
    scatter.pass_on(0)
    scatter.arrive()
    inv = lax.rsqrt(small.total() * (1.0 / inner_all) + EPS)
    column = inv.T[:, 0:1]
    dots = []
    for start, size in row_chunks():
        at = slice(start, start + size)
        mixed = scatter.own(start, size)
        dots.append(jnp.sum(r.cot[at] * mixed, axis=-1, keepdims=True))
        r.block_out[pl.ds(pl.multiple_of(links.c * HALF + start, EDGE), size), :] = (
            r.resid[at] + column[at] * mixed
        ).astype(BF16)
    r.scalars_out[:, spread.lanes] = as_tile([column, jnp.concatenate(dots)])
    spread.start()
    share.start()
    scatter.finish()
    small.finish()
    carried.finish()
    chain_o.finish()
    spread.finish()
    share.wait()
    r.done()


def backward_layer(links, inner_all, r, at_start, before_collect, at_middle):
    carried = States(links, True, r.state_low, r.decay_row, r.states_in, r.decays_in)
    collect = Collect(links, r.gwo, r.go_parts)
    grad_sum, decay_all = back_through_gate(
        inner_all, r.dmix, r.wo, r.y, r.z, r.x, r.bc, r.s, r.decay, r.scalars, r.rowp,
        r.cat, r.wide, r.dy, r.prior, r.normed_out,
    )
    r.state_low[...] = grad_sum.astype(BF16)
    r.decay_row[...] = jnp.broadcast_to(decay_all, r.decay_row.shape)
    links.meet()
    carried.start()
    at_start()
    out_gradient(r.dmix, r.normed_out, r.gwo)
    before_collect()
    collect.start()
    r.need(r.dt)
    back_within_spans(r.dy, r.x, r.bc, r.s, r.dt, r.dpre, r.flow, r.sums)
    at_middle()
    carried.arrive()
    grad = entering_state(links.z, links.groups, r.states_in, r.decays_in, True)
    r.need(r.states, r.dtraw, r.xin, r.bcin)
    back_through_states(
        grad, r.prior, r.decay, r.states, r.dy, r.x, r.bc, r.s, r.dt, r.dtraw, r.xin, r.bcin, r.rowp, r.bcp, r.headp,
        r.flow, r.sums, r.cat, r.wide, r.bc_rows, r.dpre, r.prior,
    )
    return carried, collect


def put_vector(vec, row, values):
    for i in range(values.shape[0]):
        for j in range(values.shape[1] // 128):
            vec[row // 8, row % 8 : row % 8 + 1, :] = values[i : i + 1, j * 128 : j * 128 + 128]
            row += 1


def third_kernel(inner_all, r):
    links = Links(r.sends, r.recvs)
    r.fetch(r.dt, r.states, r.dtraw, r.xin, r.bcin, r.w, r.normed, r.grad, r.resid, r.mixed)
    scatter = Scatter(links, r.part, EDGE, r.sib, r.total, r.peer)
    edge = EdgeBackward(links, r.part, r.edge_slots)
    gather = Gather(links, r.dmix_out, 0)
    spread = SmallGather(links, r.scalars_out)
    collects = [Collect(links, r.gx, r.gx_parts), Collect(links, r.gwo, r.gz_parts)]
    r.edge_slots[...] = jnp.zeros_like(r.edge_slots)
    links.greet(plane=True, groups=True, edge=-1)
    prepare(links, r, 1)
    carried, collect = backward_layer(links, inner_all, r, lambda: None, lambda: None, lambda: None)
    r.need(r.w, r.normed)
    x_gradient(r.cat, r.normed, r.gx)
    collects[0].start()
    project_back_edge(r.cat, r.w, r.part)
    edge.start()
    scatter_blocks(scatter, lambda q: project_back(q, r.cat, r.w, r.part))
    scatter.pass_on(0)
    collect.finish()
    z_gradient(r.cat, r.normed, r.gwo)
    collects[1].start()
    small_gradients(r.cat, r.normed, r.gbc, r.gdt)
    scatter.arrive()
    edge.receive()
    r.need(r.grad, r.resid, r.mixed)
    r.gain_row[...] = jnp.zeros_like(r.gain_row)
    dots = []
    for start, size in row_chunks():
        at = slice(start, start + size)
        fresh = grad_rows(links, scatter, r.edge_slots, r.grad, r.resid, r.gains[1:2], r.gain_row, start, size)
        r.grad_out[at] = fresh
        low = fresh.astype(BF16)
        r.dmix_out[gather.own(start, size), :] = low
        dots.append(jnp.sum(low.astype(F32) * r.mixed[at], axis=-1, keepdims=True))
    r.scalars_out[:, spread.lanes] = as_tile([r.inv[...].T[:, 0:1], jnp.concatenate(dots)])
    gather.start()
    spread.start()
    r.vec[...] = jnp.zeros_like(r.vec)
    model = r.gain_row.shape[1]
    put_vector(r.vec, model // 128, r.gain_row[0:1])
    put_vector(r.vec, 2 * (model // 128) + 2 * (CONV + 1), r.bc_rows[0 : CONV + 1])
    gather.pass_on()
    scatter.finish()
    edge.finish()
    gather.finish()
    spread.finish()
    carried.finish()
    for one in [collect] + collects:
        one.arrive()
    for one in collects:
        one.finish()


def fourth_kernel(inner_all, r):
    links = Links(r.sends, r.recvs)
    r.fetch(r.dt, r.states, r.dtraw, r.xin, r.bcin, r.above_bc, r.above_x, r.above_z, r.above_o, r.normed, r.w, r.grad, r.resid)
    scatter = Scatter(links, r.part, EDGE, r.sib, r.total, r.peer)
    edge = EdgeBackward(links, r.part, r.edge_slots)
    at = pl.ds(pl.multiple_of(links.c * HALF, HALF), HALF)
    share = links.copy(r.out.at[at, :], r.out.at[at, :], links.at(0, 1))
    collects = [Collect(links, r.gx, r.gx_parts), Collect(links, r.gwo, r.gz_parts)]
    above = ((r.above_x, r.g_zx.at[1, 1]), (r.above_z, r.g_zx.at[1, 0]), (r.above_o, r.g_out.at[1]))
    own = ((r.go_parts, r.g_out.at[0]), (r.gx_parts, r.g_zx.at[0, 1]), (r.gz_parts, r.g_zx.at[0, 0]))
    delivers = [Deliver(links, parts, r.final.at[i], out) for i, (parts, out) in enumerate(above)]
    own_delivers = [Deliver(links, parts, r.final.at[3 + i], out) for i, (parts, out) in enumerate(own)]
    bc_sums = [
        BcSum(links, bc, r.bc_out.at[i], r.bc_bufs[i])
        for i, bc in enumerate((r.gbc, r.above_bc))
    ]
    laid = LaidOut(links, r.steps_all, r.wide_all, r.dt_out, r.wide_out, r.dt_far, r.wide_far)
    vec_sum = VecSum(links, r.vec, r.vec_out, r.vec_near, r.vec_far)
    r.edge_slots[...] = jnp.zeros_like(r.edge_slots)
    links.greet(plane=True, groups=True, edge=-1)
    prepare(links, r, 0)

    def at_start():
        r.need(r.above_bc)
        bc_sums[1].cores()

    def at_middle():
        bc_sums[1].groups()
        r.need(r.above_x, r.above_z, r.above_o)
        for deliver in delivers:
            deliver.start()

    carried, collect = backward_layer(links, inner_all, r, at_start, bc_sums[1].plane, at_middle)
    r.need(r.normed)
    small_gradients(r.cat, r.normed, r.gbc, r.gdt)
    bc_sums[0].cores()
    r.steps_all[:, 0:EDGE, :] = r.gdt[...]
    r.steps_all[:, EDGE:, :] = r.above_dt[...]
    r.wide_all[0:16] = r.wide[...]
    r.wide_all[16:32] = r.above_wide[...]
    laid.groups()
    x_gradient(r.cat, r.normed, r.gx)
    collects[0].start()
    bc_sums[0].plane()
    r.need(r.w)
    project_back_edge(r.cat, r.w, r.part)
    edge.start()
    scatter_blocks(scatter, lambda q: project_back(q, r.cat, r.w, r.part))
    scatter.pass_on(0)
    bc_sums[0].groups()
    collect.finish()
    z_gradient(r.cat, r.normed, r.gwo)
    collects[1].start()
    scatter.arrive()
    edge.receive()
    r.need(r.grad, r.resid)
    r.gain_row[...] = jnp.zeros_like(r.gain_row)
    for start, size in row_chunks():
        fresh = grad_rows(links, scatter, r.edge_slots, r.grad, r.resid, r.gains[0:1], r.gain_row, start, size)
        r.out[pl.ds(pl.multiple_of(links.c * HALF + start, EDGE), size), :] = fresh.astype(BF16)
    share.start()
    r.vec[...] = r.above_vec[...]
    put_vector(r.vec, 0, r.gain_row[0:1])
    put_vector(r.vec, 2 * (r.gain_row.shape[1] // 128), r.bc_rows[0 : CONV + 1])
    vec_sum.plane()
    vec_sum.groups()
    collect.arrive()
    own_delivers[0].start()
    bc_sums[1].share()
    laid.plane()
    collects[0].arrive()
    own_delivers[1].start()
    laid.finish()
    lay_out_heads(links, r)
    bc_sums[0].share()
    collects[1].arrive()
    own_delivers[2].start()
    vec_sum.back()
    for one in bc_sums + [scatter, edge, carried] + collects:
        one.finish()
    vec_sum.finish()
    lay_out_vector(r)
    share.wait()
    for deliver in delivers + own_delivers:
        deliver.arrive()
        deliver.finish()


def lay_out_heads(links, r):
    inner = r.wide.shape[1]
    heads = inner // HEADDIM
    heads_core, shard = r.g_dt.shape[1:]
    spread = head_spread(inner).astype(F32)
    row, col = iota((128, 128), 0), iota((128, 128), 1)
    blank = jnp.zeros((128 - 2 * EDGE, r.dt_out.shape[2]), F32)
    steps = [jnp.zeros((shard, 128), F32) for _ in range(2)]
    tall = [jnp.zeros((8, 128), F32) for _ in range(2)]
    for q in range(GROUP):
        lanes = slice(q * inner, q * inner + inner)
        r.step_rows[...] = jnp.concatenate([r.dt_out[q].astype(F32), blank]).T
        mine = r.step_rows[pl.ds(pl.multiple_of(links.p * shard, 8), shard), :]
        gains, taps = [], []
        for layer in range(2):
            first, second = r.wide_out[q, 16 * layer : 16 * layer + 8], r.wide_out[q, 16 * layer + 8 : 16 * layer + 16]
            taps.append(first[0 : CONV + 1])
            gains.append(first[5:6])
            place = jnp.logical_and(row - EDGE * layer == col - q * heads, jnp.logical_and(row >= EDGE * layer, row < EDGE * layer + heads))
            steps[layer] = steps[layer] + dot_exact(mine, place.astype(F32))
            place = jnp.logical_and(row == col - q * heads, row < heads).astype(F32)
            skip = dot_exact(first, spread, NT)[6:7]
            rows = jnp.concatenate([first[7:8, 0:128], second[0:1, 0:128], skip, jnp.zeros((5, 128), F32)])
            tall[layer] = tall[layer] + dot_exact(rows, place)
        for j in range(CONV + 1):
            r.g_conv_x[j, :, lanes] = jnp.concatenate([tap[j : j + 1] for tap in taps]).astype(BF16)
        r.g_gain[:, lanes] = jnp.concatenate(gains).astype(BF16)
    for layer in range(2):
        r.g_dt[layer] = steps[layer].T[0:heads_core].astype(BF16)
    for i in range(3):
        r.g_head[i] = jnp.concatenate([one[i : i + 1, 0:heads_core] for one in tall]).astype(BF16)


def lay_out_vector(r):
    def row(i):
        return r.vec_out[i // 8, i % 8 : i % 8 + 1, :]

    count = r.g_norm.shape[1] // 128
    for i in range(count):
        r.g_norm[:, i * 128 : i * 128 + 128] = jnp.concatenate([row(i), row(count + i)]).astype(BF16)
    for half in range(2):
        for j in range(CONV + 1):
            firsts = [2 * count + layer * 2 * (CONV + 1) + 2 * j + half for layer in range(2)]
            rows = jnp.concatenate([row(first) for first in firsts])
            r.g_conv_bc[j, :, half * 128 : half * 128 + 128] = rows.astype(BF16)


def flat(value):
    return [a for member in value for a in flat(member)] if isinstance(value, list) else [value]


def shaped(value, leaves):
    return [shaped(member, leaves) for member in value] if isinstance(value, list) else leaves.pop(0)


def call(body, collective, copies, outs, hbm_outs, ins, hbm_ins, scratch):
    vmem, hbm = pl.BlockSpec(memory_space=pltpu.VMEM), pl.BlockSpec(memory_space=pl.ANY)
    twins = {**{name: (a.shape, a.dtype) for name, a in hbm_ins.items()}, **hbm_outs}
    sides = [list(ins.values()), list(hbm_ins.values()), list(outs.values()), list(hbm_outs.values())]
    counts = [len(flat(side)) for side in sides]
    buffers = flat([list(scratch.values()), list(twins.values())])

    def kernel(*refs):
        refs = list(refs)
        groups = [shaped(side, refs) for side in sides]
        inner = shaped([list(scratch.values()), list(twins.values())], refs)
        sends, recvs, sems = refs
        near = dict(zip(twins, inner[1]))
        named = {**dict(zip(ins, groups[0])), **dict(zip(outs, groups[2])), **dict(zip(scratch, inner[0])), **near}
        body(Refs(dict(named, sends=sends, recvs=recvs), list(zip(groups[1] + groups[3], inner[1])), sems))

    results = pl.pallas_call(
        kernel,
        out_shape=tuple(jax.ShapeDtypeStruct(*a) for a in flat(sides[2:])),
        in_specs=[vmem] * counts[0] + [hbm] * counts[1],
        out_specs=tuple([vmem] * counts[2] + [hbm] * counts[3]),
        scratch_shapes=[pltpu.VMEM(*a) for a in buffers]
        + [pltpu.SemaphoreType.DMA((n,)) for n in (copies, copies, max(1, len(twins)))],
        compiler_params=pltpu.CompilerParams(
            vmem_limit_bytes=VMEM_BYTES, collective_id=collective, has_side_effects=True
        ),
    )(*flat(sides[:2]))
    found = shaped(sides[2:], list(results))
    return types.SimpleNamespace(**dict(zip(outs, found[0])), **dict(zip(hbm_outs, found[1])))


def on_device(resid_in, cotangent, norm_gain, w_zx, w_dt, w_bc, conv_x, conv_bc, head_params, gated_gain, w_out):
    layers, model = norm_gain.shape
    groups = lax.axis_size("z")
    shard = w_dt.shape[1]
    inner_core = conv_x.shape[2]
    inner = inner_core // GROUP
    heads_core = head_params.shape[2]
    inner_all = inner_core * lax.axis_size("head")
    length = resid_in.shape[1]
    tokens = GROUP * length
    spans = tokens // SPAN
    rows = GROUP * shard

    own_rows = ((HALF, model), F32)
    all_rows, edged_rows = ((tokens, model), BF16), ((tokens + EDGE, model), BF16)
    columns = columns_of(inner).size
    w_shape, wo_shape = ((model, columns), BF16), ((model, inner), BF16)
    scalars = ((8, tokens), F32)
    state_shape = ((spans, STATE, inner), F32)
    low_rows, steps_shape = ((tokens, inner), BF16), ((tokens, 128), F32)
    scatter_scratch = dict(
        sib=((GROUP, HALF, model), BF16),
        total=((GROUP - 1, HALF, model), BF16),
        peer=((GROUP - 1, HALF, model), BF16),
    )
    state_scratch = dict(
        state_low=((STATE, inner), BF16),
        decay_row=((8, inner), F32),
        states_in=((groups, STATE, inner), BF16),
        decays_in=((groups, 8, inner), F32),
    )
    saved_shapes = dict(
        y=((tokens, inner), F32),
        z=low_rows,
        x=low_rows,
        bc=((tokens, 2 * STATE), BF16),
        s=steps_shape,
        dt=steps_shape,
        dtraw=((tokens, 128), BF16),
        xin=((tokens + EDGE, inner), BF16),
        bcin=((tokens + EDGE, 2 * STATE), BF16),
        states=state_shape,
        decay=((spans, 8, inner), F32),
    )
    forward_scratch = dict(
        ext=((tokens + EDGE, inner + 2 * STATE), F32),
        local=state_shape,
        part=all_rows,
        squares=scalars,
        slots=((2 * GROUP - 1, 8, HALF), F32),
        **state_scratch,
        **scatter_scratch,
    )

    conv_x, conv_bc, head_params = [jnp.swapaxes(a, 0, 1) for a in (conv_x, conv_bc, head_params)]
    w_dt, w_out = jnp.swapaxes(w_dt, 1, 2), jnp.swapaxes(w_out, 1, 2)
    params = dict(
        norm_gain=norm_gain, conv_x=conv_x, conv_bc=conv_bc, head_params=head_params, gated_gain=gated_gain
    )
    param_scratch = dict(
        rowp=((8, inner), F32), bcp=((8, 2 * STATE), F32), headp=((8, 128), F32), gains=((layers, model), F32)
    )
    stagings = [((GROUP, rows_in, width), BF16) for rows_in, width in (
        (shard, inner), (shard, inner), (shard, STATE), (EDGE, 128), (shard, inner)
    )]
    step_rows = ((groups * GROUP * EDGE, 128), BF16)
    first = call(
        functools.partial(first_kernel, inner_all),
        0,
        160 + 14 * (groups - 1) + 2 * groups,
        dict(
            next_w=w_shape,
            next_wo=((rows, inner), BF16),
            next_normed=edged_rows,
            resid_out=own_rows,
            cot_out=own_rows,
            mixed_out=own_rows,
            fresh_out=own_rows,
            inv_out=((8, HALF), F32),
        ),
        dict(normed=edged_rows, dmix=all_rows, w=w_shape, wo=wo_shape, **saved_shapes),
        dict(
            resid=resid_in[0],
            cot=cotangent[0],
            w_zx=w_zx,
            w_dt=w_dt,
            w_bc=w_bc,
            w_out=w_out,
            **params,
        ),
        dict(),
        dict(
            **forward_scratch,
            **param_scratch,
            stagings=[stagings, stagings],
            dt_rows=step_rows,
            next_dt_rows=step_rows,
            packed_steps=((layers, GROUP, EDGE, 128), BF16),
            wide_steps=((128, 128), BF16),
        ),
    )
    second = call(
        functools.partial(second_kernel, inner_all),
        1,
        60 + 4 * groups,
        dict(block_out=((length, model), BF16), scalars_out=scalars),
        dict(wo=wo_shape, **saved_shapes),
        dict(
            normed=first.next_normed,
            w=first.next_w,
            wo_own=first.next_wo,
            **params,
            resid=first.fresh_out,
            cot=first.cot_out,
        ),
        dict(),
        dict(**forward_scratch, **param_scratch),
    )
    grad_parts = ((groups, rows, inner), BF16)
    bc_grad = ((groups, GROUP, shard, 2 * STATE), BF16)
    dt_grad = ((groups, EDGE, rows), BF16)
    wide_grad = ((16, inner), F32)
    vec_shape = ((2 * GROUP, 8, 128), F32)
    back_scratch = dict(
        dy=low_rows,
        gwo=wo_shape,
        normed_out=low_rows,
        prior=state_shape,
        dpre=((tokens + 2 * EDGE, inner + 2 * STATE), F32),
        flow=steps_shape,
        sums=steps_shape,
        cat=((tokens + EDGE, columns), BF16),
        bc_rows=((8, 2 * STATE), F32),
        part=edged_rows,
        gx=wo_shape,
        gain_row=((8, model), F32),
        edge_slots=((2 * GROUP, EDGE, model), BF16),
        **state_scratch,
        **param_scratch,
        **scatter_scratch,
    )

    def at_once(run):
        return dict(y=run.y, z=run.z, x=run.x, bc=run.bc, s=run.s, decay=run.decay)

    def later(run):
        return dict(dt=run.dt, states=run.states, dtraw=run.dtraw, xin=run.xin, bcin=run.bcin)

    third = call(
        functools.partial(third_kernel, inner_all),
        2,
        60 + 6 * groups,
        dict(
            dmix_out=all_rows,
            scalars_out=scalars,
            grad_out=own_rows,
            go_parts=grad_parts,
            gx_parts=grad_parts,
            gz_parts=grad_parts,
            gbc=bc_grad,
            gdt=dt_grad,
            wide=wide_grad,
            vec=vec_shape,
        ),
        dict(),
        dict(
            dmix=first.dmix,
            scalars=second.scalars_out,
            wo=second.wo,
            **params,
            inv=first.inv_out,
            **at_once(second),
        ),
        dict(
            w=first.next_w,
            normed=first.next_normed,
            grad=first.cot_out,
            resid=first.fresh_out,
            mixed=first.mixed_out,
            **later(second),
        ),
        back_scratch,
    )
    far = groups - 1
    dt_shape, wide_shape = (layers * EDGE, rows), (layers * 16, inner)
    half_bc = (groups, GROUP, shard, STATE)
    bc_bufs = [
        (half_bc, BF16),
        (half_bc, BF16),
        ((GROUP - 1, groups, shard, STATE), BF16),
        ((groups, shard, STATE), BF16),
        ((far, shard, STATE), BF16),
    ]
    fourth = call(
        functools.partial(fourth_kernel, inner_all),
        3,
        130 + 14 * groups,
        dict(
            out=((length, model), BF16),
            bc_out=((layers, shard, 2 * STATE), BF16),
            g_norm=(norm_gain.shape, BF16),
            g_zx=(w_zx.shape, BF16),
            g_dt=(w_dt.shape, BF16),
            g_conv_x=(conv_x.shape, BF16),
            g_conv_bc=(conv_bc.shape, BF16),
            g_head=(head_params.shape, BF16),
            g_gain=(gated_gain.shape, BF16),
            g_out=(w_out.shape, BF16),
        ),
        dict(),
        dict(
            dmix=third.dmix_out,
            scalars=third.scalars_out,
            wo=first.wo,
            **params,
            above_dt=third.gdt,
            above_wide=third.wide,
            above_vec=third.vec,
            **at_once(first),
        ),
        dict(
            w=first.w,
            normed=first.normed,
            grad=third.grad_out,
            resid=first.resid_out,
            above_x=third.gx_parts,
            above_z=third.gz_parts,
            above_o=third.go_parts,
            above_bc=third.gbc,
            **later(first),
        ),
        dict(
            **back_scratch,
            vec_out=vec_shape,
            dt_out=((GROUP, *dt_shape), BF16),
            wide_out=((GROUP, *wide_shape), F32),
            step_rows=((rows, 128), F32),
            go_parts=grad_parts,
            gx_parts=grad_parts,
            gz_parts=grad_parts,
            final=((6, GROUP, shard, inner), BF16),
            gbc=bc_grad,
            gdt=dt_grad,
            wide=wide_grad,
            vec=vec_shape,
            steps_all=((groups, *dt_shape), BF16),
            wide_all=(wide_shape, F32),
            bc_bufs=[bc_bufs, bc_bufs],
            vec_near=vec_shape,
            vec_far=((far, 8, 128), F32),
            dt_far=((far, *dt_shape), BF16),
            wide_far=((far, *wide_shape), F32),
        ),
    )
    return (
        second.block_out[None],
        fourth.out[None],
        fourth.g_norm,
        fourth.g_zx,
        jnp.swapaxes(fourth.g_dt, 1, 2),
        fourth.bc_out,
        *[jnp.swapaxes(a, 0, 1) for a in (fourth.g_conv_x, fourth.g_conv_bc, fourth.g_head)],
        fourth.g_gain,
        jnp.swapaxes(fourth.g_out, 1, 2),
    )


def solution(mesh):
    seq, head = mesh.shape["seq"], mesh.shape["head"]
    split = Mesh(mesh.devices.reshape(seq // GROUP, GROUP, head), ("z", "p", "head"))
    seq_axes = ("z", "p")
    specs = (
        P(None, seq_axes, None),
        P(None, seq_axes, None),
        P(),
        P(None, None, seq_axes, "head"),
        P(None, seq_axes, "head"),
        P(None, seq_axes, None),
        P(None, None, "head"),
        P(),
        P(None, None, "head"),
        P(None, "head"),
        P(None, "head", seq_axes),
    )
    return jax.shard_map(on_device, mesh=split, in_specs=specs, out_specs=specs, check_vma=False)
```

```python
import functools
import types
import typing

import jax
import jax.numpy as jnp
from jax import lax
from jax.experimental import pallas as pl
from jax.experimental.pallas import tpu as pltpu
from jax.sharding import Mesh, PartitionSpec as P

HEADDIM = 64
STATE = 128
CONV = 4
SPAN = 256
GROUP = 4
EDGE = 16
EPS = 1e-05
HIGH = lax.Precision.HIGHEST
F32, BF16 = jnp.float32, jnp.bfloat16
NN = (((1,), (0,)), ((), ()))
NT = (((1,), (1,)), ((), ()))
TN = (((0,), (0,)), ((), ()))
VMEM_BYTES = 58 << 20


def dot(a, b, dims=NN):
    return lax.dot_general(a, b, dims, preferred_element_type=F32)


def dot_exact(a, b, dims=NN):
    return lax.dot_general(a, b, dims, precision=HIGH, preferred_element_type=F32)


def dot_split(a, b, dims=NN):
    high = a.astype(BF16)
    rest = (a - high.astype(F32)).astype(BF16)
    return dot(high, b, dims) + dot(rest, b, dims)


def sigmoid(v):
    return 1.0 / (1.0 + jnp.exp(-v))


def softplus(v):
    return jnp.maximum(v, 0.0) + jnp.log1p(jnp.exp(-jnp.abs(v)))


def silu_slope(v):
    sig = sigmoid(v)
    return sig * (1.0 + v * (1.0 - sig))


def iota(shape, dim):
    return lax.broadcasted_iota(jnp.int32, shape, dim)


def head_spread(inner):
    return (iota((128, inner), 0) == lax.shift_right_logical(iota((128, inner), 1), 6)).astype(BF16)


def triangle(lower):
    rows, cols = iota((SPAN, SPAN), 0), iota((SPAN, SPAN), 1)
    return ((cols <= rows) if lower else (cols >= rows)).astype(F32)


def half_masks():
    lane = iota((SPAN, 128), 1)
    return (lane < HEADDIM).astype(BF16), (lane >= HEADDIM).astype(BF16)


def conv_taps(window, taps):
    total = jnp.broadcast_to(taps[CONV : CONV + 1], (SPAN, window.shape[1]))
    for j in range(CONV):
        total = total + taps[j : j + 1] * window[EDGE - 3 + j : EDGE - 3 + j + SPAN]
    return total


def head_pick(place, heads):
    row, col = iota((128, 128), 0), iota((128, 128), 1)
    return jnp.logical_and(row == place * heads + col, col < heads).astype(BF16)


class Columns(typing.NamedTuple):
    x: slice
    z: slice
    dt: slice
    bc: slice
    size: int


def columns_of(inner):
    first = 2 * inner + 128
    return Columns(
        slice(0, inner), slice(inner, 2 * inner), slice(2 * inner, first), slice(first, first + 2 * STATE), first + 2 * STATE
    )


def project_and_convolve(
    normed, w, rowp, bcp, headp,
    z_out, xin_out, bcin_out, x_out, bc_out, dtraw_out, dt_out, s_out, decay_out,
    ext, local, at_block,
):
    inner = x_out.shape[1]
    spans = x_out.shape[0] // SPAN

    cols = columns_of(inner)
    edge = normed[0:EDGE]
    edge_x = dot(edge, w[:, cols.x]).astype(BF16)
    edge_bc = dot(edge, w[:, cols.bc]).astype(BF16)
    xin_out[0:EDGE] = edge_x
    bcin_out[0:EDGE] = edge_bc
    ext[0:EDGE, 0:inner] = edge_x.astype(F32)
    ext[0:EDGE, inner:] = edge_bc.astype(F32)
    spread = head_spread(inner)
    low_tri = triangle(True)
    rate = -jnp.exp(headp[0:1])
    bias = headp[1:2]

    def block(q, carry):
        state_sum, decay_all = carry
        at = pl.multiple_of(q * SPAN, SPAN)
        tok = pl.ds(at, SPAN)
        after = pl.ds(pl.multiple_of(at + EDGE, EDGE), SPAN)
        at_block(q)
        product = dot(normed[after, :], w[...]).astype(BF16)
        z_out[tok, :] = product[:, cols.z]
        xin, bcin = product[:, cols.x], product[:, cols.bc]
        dtraw = product[:, cols.dt]
        xin_out[after, :] = xin
        bcin_out[after, :] = bcin
        dtraw_out[tok, :] = dtraw
        ext[after, 0:inner] = xin.astype(F32)
        ext[after, inner:] = bcin.astype(F32)
        window = pl.ds(at, SPAN + EDGE)
        pre_x = conv_taps(ext[window, 0:inner], rowp)
        x = (pre_x * sigmoid(pre_x)).astype(BF16)
        x_out[tok, :] = x
        pre_bc = conv_taps(ext[window, inner:], bcp)
        bc = (pre_bc * sigmoid(pre_bc)).astype(BF16)
        bc_out[tok, :] = bc
        dt = softplus(dtraw.astype(F32) + bias)
        s = dot_exact(low_tri, dt * rate)
        dt_out[tok, :] = dt
        s_out[tok, :] = s
        to_end = jnp.exp(s[SPAN - 1 : SPAN] - s) * dt
        weighted = (x.astype(F32) * dot_split(to_end, spread)).astype(BF16)
        fresh = dot(bc[:, :STATE], weighted, TN)
        decay = dot_split(jnp.exp(s[SPAN - 8 : SPAN]), spread)[7:8]
        local[q] = fresh
        decay_out[q] = jnp.broadcast_to(decay, (8, inner))
        return state_sum * decay + fresh, decay_all * decay

    return lax.fori_loop(0, spans, block, (jnp.zeros((STATE, inner), F32), jnp.ones((1, inner), F32)))


def mix_within_spans(x_in, bc_in, s_in, dt_in, y_out):
    inner = x_in.shape[1]

    def block(q, _):
        tok = pl.ds(pl.multiple_of(q * SPAN, SPAN), SPAN)
        x, bc, s = x_in[tok, :], bc_in[tok, :], s_in[tok, :]
        s_row, dt_row = s.T, dt_in[tok, :].T
        cb = dot(bc[:, STATE:], bc[:, :STATE], NT)
        causal = iota((SPAN, SPAN), 1) <= iota((SPAN, SPAN), 0)
        masks = half_masks()
        for pair in range(inner // 128):
            lanes = slice(pair * 128, pair * 128 + 128)
            x_pair = x[:, lanes]
            total = None
            for e in range(2):
                h = pair * 2 + e
                gap = jnp.where(causal, s[:, h : h + 1] - s_row[h : h + 1, :], -1e30)
                scores = (cb * (jnp.exp(gap) * dt_row[h : h + 1, :])).astype(BF16)
                term = dot(scores, x_pair * masks[e])
                total = term if total is None else total + term
            y_out[tok, lanes] = total
        return 0

    lax.fori_loop(0, x_in.shape[0] // SPAN, block, 0)


def entering_state(place, count, sums, decays, backward):
    inner = sums.shape[2]
    state = jnp.zeros((STATE, inner), F32)
    for turn in range(count):
        other = count - 1 - turn if backward else turn
        ahead = (place < other) if backward else (other < place)
        state = jnp.where(ahead, decays[other, 0:1] * state + sums[other].astype(F32), state)
    return state


def chain_states(state, local, decay, states_out):
    def block(q, state):
        states_out[q] = state
        return decay[q, 0:1] * state + local[q]

    lax.fori_loop(0, local.shape[0], block, state)


def mix_out(q, states, x, bc, z, s, wo, rowp, y_out, part_out, sq_out):
    inner = x.shape[1]
    tok = pl.ds(pl.multiple_of(q * SPAN, SPAN), SPAN)
    carried = dot_split(jnp.exp(s[tok, :]), head_spread(inner)) * dot(bc[tok, STATE:], states[q].astype(BF16))
    y = y_out[tok, :] + carried + rowp[6:7] * x[tok, :].astype(F32)
    y_out[tok, :] = y
    zf = z[tok, :].astype(F32)
    gated = y * (zf * sigmoid(zf))
    sq_out[:, tok] = dot_exact(jnp.ones((8, inner), F32), gated * gated, NT)
    part_out[tok, :] = dot((gated * rowp[5:6]).astype(BF16), wo[...], NT).astype(BF16)


def back_through_gate(
    inner_all, dmix, wo, y_in, z, x, bc, s, decay, token_scalars, rowp, cat_out, wide, dy_out, prior, normed_out
):
    inner = x.shape[1]
    spans = x.shape[0] // SPAN
    spread = head_spread(inner)
    gain = rowp[5:6]
    cols = columns_of(inner)

    def block(i, carry):
        grad_sum, gain_sum, skip_sum = carry
        q = spans - 1 - i
        tok = pl.ds(pl.multiple_of(q * SPAN, SPAN), SPAN)
        columns = token_scalars[:, tok].T
        inv, total_dot = columns[:, 0:1], columns[:, 1:2]
        zf = z[tok, :].astype(F32)
        sig = sigmoid(zf)
        act = zf * sig
        y = y_in[tok, :]
        gated = y * act
        d_no = dot(dmix[tok, :], wo[...])
        scaled = gated * inv
        normed_out[tok, :] = (scaled * gain).astype(BF16)
        gain_sum = gain_sum + jnp.sum(d_no * scaled, axis=0, keepdims=True)
        d_gated = inv * (d_no * gain) - gated * (inv * inv * inv * total_dot * (1.0 / inner_all))
        after = pl.ds(pl.multiple_of(q * SPAN + EDGE, EDGE), SPAN)
        cat_out[after, cols.z] = (d_gated * y * (sig * (1.0 + zf * (1.0 - sig)))).astype(BF16)
        dy = d_gated * act
        xf = x[tok, :].astype(F32)
        skip_sum = skip_sum + jnp.sum(dy * xf, axis=0, keepdims=True)
        dy_low = dy.astype(BF16)
        dy_out[tok, :] = dy_low
        scaled_dy = (dy_low.astype(F32) * dot_split(jnp.exp(s[tok, :]), spread)).astype(BF16)
        fresh = dot(bc[tok, STATE:], scaled_dy, TN)
        prior[q] = fresh
        return fresh + decay[q, 0:1] * grad_sum, gain_sum, skip_sum

    zero = jnp.zeros((1, inner), F32)
    grad_sum, gain_sum, skip_sum = lax.fori_loop(
        0, spans, block, (jnp.zeros((STATE, inner), F32), zero, zero)
    )
    decay_all = decay[0, 0:1]
    for q in range(1, spans):
        decay_all = decay_all * decay[q, 0:1]
    wide[...] = jnp.zeros_like(wide)
    wide[5:6] = gain_sum
    wide[6:7] = skip_sum
    return grad_sum, decay_all


def out_gradient(dmix, normed_out, gwo_out):
    def rows_of(i, _):
        rows = pl.ds(pl.multiple_of(i * SPAN, SPAN), SPAN)
        gwo_out[rows, :] = dot(dmix[:, rows], normed_out[...], TN).astype(BF16)
        return 0

    lax.fori_loop(0, dmix.shape[1] // SPAN, rows_of, 0)


def back_within_spans(dy_in, x_in, bc_in, s_in, dt_in, dpre, flow_out, sum_out):
    inner = x_in.shape[1]

    def block(q, _):
        at = pl.multiple_of(q * SPAN, SPAN)
        tok = pl.ds(at, SPAN)
        after = pl.ds(pl.multiple_of(at + EDGE, EDGE), SPAN)
        x_low, dy = x_in[tok, :], dy_in[tok, :]
        b, c = bc_in[tok, :STATE], bc_in[tok, STATE:]
        s, dt = s_in[tok, :], dt_in[tok, :]
        s_row = s.T
        cb = dot(b, c, NT)
        seen = iota((SPAN, SPAN), 0) <= iota((SPAN, SPAN), 1)
        masks = half_masks()
        d_cb = jnp.zeros((SPAN, SPAN), F32)
        lane = iota((SPAN, 128), 1)
        row_id = iota((128, SPAN), 0)
        sum_k = jnp.zeros((128, SPAN), F32)
        sum_t = jnp.zeros((SPAN, 128), F32)
        for pair in range(inner // 128):
            lanes = slice(pair * 128, pair * 128 + 128)
            x_pair, dy_pair = x_low[:, lanes], dy[:, lanes]
            total = None
            for e in range(2):
                h = pair * 2 + e
                d_scores = dot(x_pair * masks[e], dy_pair, NT)
                fade = jnp.exp(jnp.where(seen, s_row[h : h + 1, :] - s[:, h : h + 1], -1e30))
                dt_h = dt[:, h : h + 1]
                fade_cb = cb * fade
                term = dot((fade_cb * dt_h).astype(BF16), dy_pair * masks[e])
                total = term if total is None else total + term
                d_cb = d_cb + d_scores * (fade * dt_h)
                flow = d_scores * fade_cb
                sum_t = jnp.where(lane == h, jnp.sum(flow, axis=1, keepdims=True), sum_t)
                sum_k = jnp.where(row_id == h, jnp.sum(flow * dt_h, axis=0, keepdims=True), sum_k)
            dpre[after, lanes] = total
        d_cb_low = d_cb.astype(BF16)
        dpre[after, inner : inner + STATE] = dot(d_cb_low, c)
        dpre[after, inner + STATE :] = dot(d_cb_low, b, TN)
        flow_out[tok, :] = sum_k.T - sum_t * dt
        sum_out[tok, :] = sum_t
        return 0

    lax.fori_loop(0, x_in.shape[0] // SPAN, block, 0)


def back_through_states(
    grad, prior, decay, states, dy_in, x, bc, s_in, dt_in, dtraw, xin, bcin, rowp, bcp, headp, flow_in, sum_in,
    cat_out, row_out, bcrow_out,
    dpre, dend, at_block,
):
    inner = x.shape[1]
    spans = x.shape[0] // SPAN
    spread = head_spread(inner)
    up_tri = triangle(False)
    skip = rowp[6:7]
    rate = -jnp.exp(headp[0:1])
    bias = headp[1:2]
    width = inner + 2 * STATE

    def chain(i, grad):
        q = spans - 1 - i
        before = prior[q] + decay[q, 0:1] * grad
        dend[q] = grad
        return before

    lax.fori_loop(0, spans, chain, grad)
    dpre[0:EDGE] = jnp.zeros((EDGE, width), F32)
    dpre[EDGE + spans * SPAN :] = jnp.zeros((EDGE, width), F32)
    bcrow_out[...] = jnp.zeros_like(bcrow_out)
    cols = columns_of(inner)
    cat_out[0:EDGE, cols.z] = jnp.zeros((EDGE, inner), BF16)
    cat_out[0:EDGE, cols.dt] = jnp.zeros((EDGE, 128), BF16)

    def block(q, _):
        at = pl.multiple_of(q * SPAN, SPAN)
        tok = pl.ds(at, SPAN)
        after = pl.ds(pl.multiple_of(at + EDGE, EDGE), SPAN)
        window = pl.ds(at, SPAN + EDGE)
        at_block(q)
        x_low, dy = x[tok, :], dy_in[tok, :]
        xf, dyf = x_low.astype(F32), dy.astype(F32)
        b, c = bc[tok, :STATE], bc[tok, STATE:]
        s, dt = s_in[tok, :], dt_in[tok, :]
        exp_s = jnp.exp(s)
        to_end = jnp.exp(s[SPAN - 1 : SPAN] - s)
        w = to_end * dt
        w_all, s_all = dot_split(w, spread), dot_split(exp_s, spread)
        state, grad = states[q], dend[q]
        state_low, grad_low = state.astype(BF16), grad.astype(BF16)
        carried = s_all * dot(c, state_low)
        ds = dot_split(dyf * carried, spread, NT)
        d_c = dot((dyf * s_all).astype(BF16), state_low, NT)
        d_w = dot(b, grad_low)
        d_b = dot((xf * w_all).astype(BF16), grad_low, NT)
        dx = dpre[after, 0:inner] + dyf * skip + d_w * w_all
        dsw = dot_split(d_w * xf, spread, NT)
        end = dsw * w
        ds = ds + flow_in[tok, :] - end
        held = dot_split(jnp.broadcast_to(jnp.sum(grad * state, axis=0, keepdims=True), (8, inner)), spread, NT)[0:1]
        last = jnp.sum(end, axis=0, keepdims=True) + held * exp_s[SPAN - 1 : SPAN]
        ds = ds + jnp.where(iota((SPAN, 128), 0) == SPAN - 1, last, 0.0)
        da = dot_exact(up_tri, ds)
        d_dt = sum_in[tok, :] + dsw * to_end + da * rate
        d_raw = d_dt * sigmoid(dtraw[tok, :].astype(F32) + bias)
        d_raw = jnp.where(iota((SPAN, 128), 1) < inner // HEADDIM, d_raw, 0.0)
        row_out[7:8, 0:128] += jnp.sum(da * (dt * rate), axis=0, keepdims=True)
        row_out[8:9, 0:128] += jnp.sum(d_raw, axis=0, keepdims=True)
        d_low = d_raw.astype(BF16)
        cat_out[after, cols.dt] = d_low

        win_x = xin[window, :].astype(F32)
        d_x = dx * silu_slope(conv_taps(win_x, rowp))
        dpre[after, 0:inner] = d_x
        for j in range(CONV):
            row_out[j : j + 1] += jnp.sum(d_x * win_x[EDGE - 3 + j : EDGE - 3 + j + SPAN], axis=0, keepdims=True)
        row_out[CONV : CONV + 1] += jnp.sum(d_x, axis=0, keepdims=True)
        win_bc = bcin[window, :].astype(F32)
        d_bc = dpre[after, inner:] + jnp.concatenate([d_b, d_c], axis=1)
        d_bc = d_bc * silu_slope(conv_taps(win_bc, bcp))
        dpre[after, inner:] = d_bc
        for j in range(CONV):
            bcrow_out[j : j + 1] += jnp.sum(d_bc * win_bc[EDGE - 3 + j : EDGE - 3 + j + SPAN], axis=0, keepdims=True)
        bcrow_out[CONV : CONV + 1] += jnp.sum(d_bc, axis=0, keepdims=True)
        return 0

    lax.fori_loop(0, spans, block, 0)

    def back(window, taps, rows):
        total = None
        for j in range(CONV):
            term = taps[j : j + 1] * window[CONV - 1 - j : CONV - 1 - j + rows]
            total = term if total is None else total + term
        return total.astype(BF16)

    cat_out[0:EDGE, cols.x] = back(dpre[0 : 2 * EDGE, 0:inner], rowp, EDGE)
    cat_out[0:EDGE, cols.bc] = back(dpre[0 : 2 * EDGE, inner:], bcp, EDGE)

    def conv_block(q, _):
        after = pl.ds(pl.multiple_of(q * SPAN + EDGE, EDGE), SPAN)
        window = pl.ds(pl.multiple_of(q * SPAN + EDGE, EDGE), SPAN + EDGE)
        cat_out[after, cols.x] = back(dpre[window, 0:inner], rowp, SPAN)
        cat_out[after, cols.bc] = back(dpre[window, inner:], bcp, SPAN)
        return 0

    lax.fori_loop(0, spans, conv_block, 0)


def project_back_edge(cat, w, dn_out):
    cols = columns_of((w.shape[1] - 3 * STATE) // 2)
    dn_out[0:EDGE] = (
        dot(cat[0:EDGE, cols.x], w[:, cols.x], NT) + dot(cat[0:EDGE, cols.bc], w[:, cols.bc], NT)
    ).astype(BF16)


def project_back(q, cat, w, dn_out):
    after = pl.ds(pl.multiple_of(q * SPAN + EDGE, EDGE), SPAN)
    dn_out[after, :] = dot(cat[after, :], w[...], NT).astype(BF16)


def for_row_blocks(grad, body):
    groups, rows = grad

    def one(g, _):
        body(pl.ds(pl.multiple_of(g * rows, 128), rows) if rows % 128 == 0 else pl.ds(g * rows, rows), g)
        return 0

    if rows % 128 == 0:
        lax.fori_loop(0, groups, one, 0)
    else:
        for g in range(groups):
            one(g, 0)


def x_gradient(cat, normed, gx_out):
    cols = columns_of(gx_out.shape[1])

    def body(at, _):
        total = dot(normed[EDGE:, at], cat[EDGE:, cols.x], TN) + dot(normed[0:EDGE, at], cat[0:EDGE, cols.x], TN)
        gx_out[at, :] = total.astype(BF16)

    for_row_blocks((normed.shape[1] // SPAN, SPAN), body)


def z_gradient(cat, normed, gz_out):
    cols = columns_of(gz_out.shape[1])

    def body(at, _):
        gz_out[at, :] = dot(normed[EDGE:, at], cat[EDGE:, cols.z], TN).astype(BF16)

    for_row_blocks((normed.shape[1] // SPAN, SPAN), body)


def small_gradients(cat, normed, gbc_out, gdt_out):
    groups, parts, shard, _ = gbc_out.shape
    cols = columns_of((cat.shape[1] - 3 * STATE) // 2)

    def body(at, g):
        edge, tokens = normed[0:EDGE, at], normed[EDGE:, at]
        bc = dot(tokens, cat[EDGE:, cols.bc], TN) + dot(edge, cat[0:EDGE, cols.bc], TN)
        gbc_out[g] = bc.reshape(parts, shard, 2 * STATE).astype(BF16)
        gdt_out[g] = dot(cat[EDGE:, cols.dt], tokens, TN)[0:EDGE].astype(BF16)

    for_row_blocks((groups, parts * shard), body)


HALF = 128
MESH = pl.DeviceIdType.MESH


class Links:
    def __init__(self, sends, recvs):
        self.z, self.p, self.c = lax.axis_index("z"), lax.axis_index("p"), lax.axis_index("head")
        self.groups = lax.axis_size("z")
        self.sends, self.recvs, self.used = sends, recvs, 0

    def copy(self, src, dst, device):
        i = self.used
        self.used += 1
        return pltpu.make_async_remote_copy(
            src_ref=src, dst_ref=dst, send_sem=self.sends.at[i], recv_sem=self.recvs.at[i],
            device_id=device, device_id_type=MESH,
        )

    def local(self, src, dst):
        i = self.used
        self.used += 1
        return pltpu.make_async_copy(src, dst, self.sends.at[i])

    def at(self, k, e):
        return (self.z, lax.bitwise_xor(self.p, jnp.int32(k)), lax.bitwise_xor(self.c, jnp.int32(e)))

    def last_of_plane(self):
        return jnp.logical_and(self.p == GROUP - 1, self.c == 1)

    def greet(self, plane=False, sibling=False, groups=False, edge=0):
        barrier = pltpu.get_barrier_semaphore()
        z, count = self.z, self.groups
        above = z < count - 1

        def signal(device):
            pl.semaphore_signal(barrier, 1, device_id=device, device_id_type=MESH)

        self.expected = jnp.int32(0)
        for k in range(GROUP):
            for e in range(2):
                if (k or e) if plane else (sibling and e and not k):
                    signal(self.at(k, e))
                    self.expected = self.expected + 1
        if groups:
            for k in range(1, count):
                signal((lax.rem(z + k, count), self.p, self.c))
            self.expected = self.expected + (count - 1)
        sending = jnp.logical_and(self.last_of_plane(), above)
        if edge == 1:
            pl.when(z > 0)(lambda: signal((z - 1, jnp.int32(GROUP - 1), jnp.int32(1))))
            self.expected = self.expected + 2 * GROUP * sending.astype(jnp.int32)
        if edge == -1:

            @pl.when(sending)
            def _():
                for p in range(GROUP):
                    for c in range(2):
                        signal((z + 1, jnp.int32(p), jnp.int32(c)))

            self.expected = self.expected + (z > 0).astype(jnp.int32)

    def meet(self):
        pl.semaphore_wait(pltpu.get_barrier_semaphore(), self.expected)

    def start_barrier(self, **who):
        self.greet(**who)
        self.meet()


class Chain:
    def __init__(self, links, pieces):
        z, p, c, groups = links.z, links.p, links.c, links.groups
        self.steps, self.now = [], 0
        for step in range(1, groups):
            found = []
            up, down = z - step + 1, z + step - 1
            for piece in pieces:
                block = piece(jnp.maximum(up, 0))
                sending = jnp.logical_and(up >= 0, z < groups - 1)
                found.append((sending, z - step >= 0, links.copy(block, block, (z + 1, p, c))))
                block = piece(jnp.minimum(down, groups - 1))
                sending = jnp.logical_and(down < groups, z > 0)
                found.append((sending, z + step < groups, links.copy(block, block, (z - 1, p, c))))
            self.steps.append(found)

    def begin(self):
        for sending, _, copy in self.steps[0]:
            pl.when(sending)(copy.start)

    def advance(self):
        if self.now + 1 < len(self.steps):
            for (_, receiving, copy), (sending, _, later) in zip(self.steps[self.now], self.steps[self.now + 1]):
                pl.when(receiving)(copy.wait_recv)
                pl.when(sending)(later.start)
            self.now += 1

    def complete(self):
        while self.now + 1 < len(self.steps):
            self.advance()
        for _, receiving, copy in self.steps[-1]:
            pl.when(receiving)(copy.wait_recv)

    def finish(self):
        for found in self.steps:
            for sending, _, copy in found:
                pl.when(sending)(copy.wait_send)


class Swap:
    def __init__(self, links, shard, staging, out, lanes, width):
        self.links, self.staging, self.out, self.lanes = links, staging, out, lanes

        def source(k):
            to = lax.bitwise_xor(links.p, jnp.int32(k))
            if len(shard.shape) == 3:
                return shard.at[to]
            if shard.shape[1] == width:
                return shard
            return shard.at[:, pl.ds(pl.multiple_of(to * width, 128), width)]

        self.copies = [links.copy(source(k), staging.at[links.p], links.at(k, 0)) for k in (3, 1, 2)]
        self.keep = links.local(source(0), staging.at[links.p])

    def start(self):
        for copy in self.copies:
            copy.start()

    def settle(self):
        self.keep.wait()
        for copy in self.copies:
            copy.wait_recv()
        parts, shard, width = self.staging.shape
        rows = parts * shard
        first = self.links.z * rows if self.out.shape[0] > rows else 0
        if shard % EDGE == 0:
            for j in range(parts):
                self.out[pl.ds(pl.multiple_of(first + j * shard, EDGE), shard), self.lanes] = self.staging[j]
        else:
            block = self.staging[...].astype(F32).reshape(rows, width).astype(BF16)
            self.out[pl.ds(pl.multiple_of(first, EDGE), rows), self.lanes] = block

    def finish(self):
        for copy in self.copies:
            copy.wait_send()


class Halve:
    def __init__(self, links, grad, arrived, sums):
        self.links, self.grad, self.arrived, self.sums = links, grad, arrived, sums
        z, groups = links.z, links.groups
        self.rows, self.steps, self.now = grad.shape[0] // groups, [], 0
        first, bit = 0, 1
        while bit < groups:
            low = lax.rem(z, bit)
            mine = lax.rem(lax.div(z, bit), 2)
            device = (z + bit - 2 * bit * mine, links.p, links.c)
            found = []
            for j in range(groups // (2 * bit)):
                away = j * 2 * bit + (1 - mine) * bit + low
                kept = j * 2 * bit + mine * bit + low
                copy = links.copy(self.held(away), arrived.at[first + j], device)
                found.append((first + j, self.held(kept), copy))
            self.steps.append(found)
            self.before = (first, 2 * bit)
            first, bit = first + groups // (2 * bit), 2 * bit

    def held(self, target):
        if not self.steps:
            return self.grad.at[pl.ds(pl.multiple_of(target * self.rows, EDGE), self.rows), :]
        first, size = self.before
        return self.arrived.at[first + lax.div(target, size)]

    def begin(self):
        for _, _, copy in self.steps[0]:
            copy.start()

    def advance(self):
        for slot, held, copy in self.steps[self.now]:
            copy.wait_recv()

            def add(i, _, slot=slot, held=held):
                at = pl.ds(pl.multiple_of(i * 32, 32), 32)
                total = self.arrived[slot, at, :].astype(F32) + held[at, :].astype(F32)
                self.arrived[slot, at, :] = total.astype(BF16)
                return 0

            lax.fori_loop(0, self.rows // 32, add, 0)
        self.now += 1
        for _, _, copy in self.steps[self.now]:
            copy.start()

    def complete(self):
        while self.now + 1 < len(self.steps):
            self.advance()
        ((slot, held, copy),) = self.steps[-1]
        copy.wait_recv()
        total = self.arrived[slot].astype(F32) + held[...].astype(F32)
        shard = self.sums.shape[1]
        for j in range(GROUP):
            self.sums[j] = total[j * shard : (j + 1) * shard].astype(BF16)

    def finish(self):
        for found in self.steps:
            for _, _, copy in found:
                copy.wait_send()


class Deliver:
    def __init__(self, links, sums, out):
        self.links, self.sums, self.out = links, sums, out
        inner = sums.shape[2]
        self.mine = pl.ds(pl.multiple_of(links.p * inner, 128), inner)
        self.copies = [
            links.copy(sums.at[lax.bitwise_xor(links.p, jnp.int32(k))], out.at[:, self.mine], links.at(k, 0))
            for k in (3, 1, 2)
        ]

    def start(self):
        for copy in self.copies:
            copy.start()
        self.out[:, self.mine] = self.sums[self.links.p]

    def arrive(self):
        for copy in self.copies:
            copy.wait_recv()

    def finish(self):
        for copy in self.copies:
            copy.wait_send()


class States:
    def __init__(self, links, backward, state, decay, states, decays):
        z, groups = links.z, links.groups
        self.links, self.refs = links, (state, decay, states, decays)
        self.found = []
        for k in range(1, groups):
            to, source = (z - k, z + k) if backward else (z + k, z - k)
            sending, receiving = (to >= 0, source < groups) if backward else (to < groups, source >= 0)
            device = (jnp.clip(to, 0, groups - 1), links.p, links.c)
            pair = [links.copy(state, states.at[z], device), links.copy(decay, decays.at[z], device)]
            self.found.append((sending, receiving, pair))

    def start(self):
        for sending, _, pair in self.found:

            @pl.when(sending)
            def _(pair=pair):
                for copy in pair:
                    copy.start()

    def arrive(self):
        for _, receiving, pair in self.found:

            @pl.when(receiving)
            def _(pair=pair):
                for copy in pair:
                    copy.wait_recv()

    def finish(self):
        for sending, _, pair in self.found:

            @pl.when(sending)
            def _(pair=pair):
                for copy in pair:
                    copy.wait_send()


class Gather:
    def __init__(self, links, out, base):
        self.links, self.out, self.base = links, out, base

        def place(k, c):
            row = base + lax.bitwise_xor(links.p, jnp.int32(k)) * (2 * HALF) + c * HALF
            return out.at[pl.ds(pl.multiple_of(row, EDGE), HALF), :]

        own = place(0, links.c)
        self.out_copies = [links.copy(own, own, links.at(k, 0)) for k in (3, 1, 2)]
        self.shared = [links.copy(own, own, links.at(0, 1))]
        self.shared += [links.copy(place(k, links.c), place(k, links.c), links.at(0, 1)) for k in (1, 2, 3)]
        self.arrivals = [self.out_copies[1], self.out_copies[2], self.out_copies[0]]

    def own(self, start, size):
        row = self.base + self.links.p * (2 * HALF) + self.links.c * HALF + start
        return pl.ds(pl.multiple_of(row, EDGE), size)

    def start(self):
        for copy in self.out_copies:
            copy.start()
        self.shared[0].start()

    def pass_on(self):
        for k in range(3):
            self.arrivals[k].wait_recv()
            self.shared[k + 1].start()

    def finish(self):
        for copy in self.shared:
            copy.wait_recv()
        for copy in self.shared + self.out_copies:
            copy.wait_send()


class EdgeForward:
    def __init__(self, links, gather):
        self.links = links
        tail = gather.out.at[gather.own(HALF - EDGE, EDGE), :]
        first = links.used
        links.used += 2 * GROUP + 1
        recv = links.recvs.at[first + 2 * GROUP]
        self.out = gather.out
        self.copies = [
            pltpu.make_async_remote_copy(
                src_ref=tail, dst_ref=gather.out.at[0:EDGE, :], send_sem=links.sends.at[first + p * 2 + c], recv_sem=recv,
                device_id=(links.z + 1, jnp.int32(p), jnp.int32(c)), device_id_type=MESH,
            )
            for p in range(GROUP)
            for c in range(2)
        ]
        self.sending = jnp.logical_and(links.last_of_plane(), links.z < links.groups - 1)

    def start(self):
        @pl.when(self.sending)
        def _():
            for copy in self.copies:
                copy.start()

        @pl.when(self.links.z == 0)
        def _():
            self.out[0:EDGE, :] = jnp.zeros((EDGE, self.out.shape[1]), self.out.dtype)

    def finish(self):
        pl.when(self.links.z > 0)(self.copies[0].wait_recv)

        @pl.when(self.sending)
        def _():
            for copy in self.copies:
                copy.wait_send()


class Scatter:
    def __init__(self, links, part, base, sib, total, peer):
        self.links, self.part, self.base = links, part, base
        self.sib, self.total, self.peer = sib, total, peer
        other = 1 - links.c
        self.to_sibling = {
            k: links.copy(part.at[self.rows(k, other, 0, HALF), :], sib.at[k], links.at(0, 1)) for k in (3, 1, 2, 0)
        }
        self.to_peer = {k: links.copy(total.at[k - 1], peer.at[k - 1], links.at(k, 0)) for k in (3, 1, 2)}

    def rows(self, k, c, start, size):
        row = self.base + lax.bitwise_xor(self.links.p, jnp.int32(k)) * (2 * HALF) + c * HALF + start
        return pl.ds(pl.multiple_of(row, EDGE), size)

    def pass_on(self, k):
        self.to_sibling[k].wait_recv()
        if k == 0:
            return

        def add(i, _):
            at = pl.ds(pl.multiple_of(i * 32, 32), 32)
            mine = self.part[self.rows(k, self.links.c, i * 32, 32), :].astype(F32)
            self.total[k - 1, at, :] = (mine + self.sib[k, at, :].astype(F32)).astype(BF16)
            return 0

        lax.fori_loop(0, HALF // 32, add, 0)
        self.to_peer[k].start()

    def arrive(self):
        for copy in self.to_peer.values():
            copy.wait_recv()

    def own(self, start, size):
        at = pl.ds(start, size)
        total = self.part[self.rows(0, self.links.c, start, size), :].astype(F32) + self.sib[0, at, :].astype(F32)
        for k in range(3):
            total = total + self.peer[k, at, :].astype(F32)
        return total

    def finish(self):
        for copy in list(self.to_sibling.values()) + list(self.to_peer.values()):
            copy.wait_send()


class SmallSum:
    def __init__(self, links, squares, slots):
        self.links, self.squares, self.slots = links, squares, slots
        self.copies = [
            links.copy(squares.at[:, self.lanes(k, e)], slots.at[2 * k + e - 1], links.at(k, e))
            for k in range(GROUP)
            for e in range(2)
            if k or e
        ]

    def lanes(self, k, e):
        links = self.links
        column = lax.bitwise_xor(links.p, jnp.int32(k)) * (2 * HALF) + lax.bitwise_xor(links.c, jnp.int32(e)) * HALF
        return pl.ds(pl.multiple_of(column, HALF), HALF)

    def start(self):
        for copy in self.copies:
            copy.start()

    def total(self):
        for copy in self.copies:
            copy.wait_recv()
        total = self.squares[:, self.lanes(0, 0)]
        for i in range(len(self.copies)):
            total = total + self.slots[i]
        return total

    def finish(self):
        for copy in self.copies:
            copy.wait_send()


class SmallGather:
    def __init__(self, links, out):
        self.out = out
        self.lanes = pl.ds(pl.multiple_of(links.p * (2 * HALF) + links.c * HALF, HALF), HALF)
        self.copies = [
            links.copy(out.at[:, self.lanes], out.at[:, self.lanes], links.at(k, e))
            for k in range(GROUP)
            for e in range(2)
            if k or e
        ]

    def start(self):
        for copy in self.copies:
            copy.start()

    def finish(self):
        for copy in self.copies:
            copy.wait()


def row_chunks(size=32):
    return [(start, size) for start in range(0, HALF, size)]


def rms_of(rows):
    return lax.rsqrt(jnp.mean(rows * rows, axis=-1, keepdims=True) + EPS)


def as_tile(columns):
    lane = iota((HALF, HALF), 1)
    wide = jnp.zeros((HALF, HALF), F32)
    for i, column in enumerate(columns):
        wide = jnp.where(lane == i, column, wide)
    return wide.T[0:8]


def grad_rows(links, scatter, edge_slots, grad, resid, gain, gain_out, start, size):
    at = slice(start, start + size)
    d_normed = scatter.own(start, size)
    if start + size == HALF:
        extra = edge_slots[0].astype(F32)
        for i in range(1, 2 * GROUP):
            extra = extra + edge_slots[i].astype(F32)
        used = jnp.logical_and(links.last_of_plane(), links.z < links.groups - 1)
        extra = jnp.where(used, extra, 0.0)
        d_normed = d_normed + jnp.concatenate([jnp.zeros((size - EDGE, extra.shape[1]), F32), extra])
    rows = resid[at]
    inv_rms = rms_of(rows)
    gain_sum = jnp.sum(d_normed * rows * inv_rms, axis=0, keepdims=True)
    gain_out[0:1] = gain_sum if start == 0 else gain_out[0:1] + gain_sum
    d_hidden = d_normed * gain[...]
    return (
        grad[at]
        + inv_rms * d_hidden
        - rows * (inv_rms * inv_rms * inv_rms * jnp.mean(d_hidden * rows, axis=-1, keepdims=True))
    )


class EdgeBackward:
    def __init__(self, links, part, slots):
        self.links = links
        first = links.used
        links.used += 2 * GROUP + 1
        me = links.p * 2 + links.c
        self.send = pltpu.make_async_remote_copy(
            src_ref=part.at[0:EDGE, :], dst_ref=slots.at[me], send_sem=links.sends.at[first], recv_sem=links.recvs.at[first + me],
            device_id=(links.z - 1, jnp.int32(GROUP - 1), jnp.int32(1)), device_id_type=MESH,
        )
        self.recvs = [
            pltpu.make_async_remote_copy(
                src_ref=part.at[0:EDGE, :], dst_ref=slots.at[i], send_sem=links.sends.at[first], recv_sem=links.recvs.at[first + i],
                device_id=(links.z, links.p, 1 - links.c), device_id_type=MESH,
            )
            for i in range(2 * GROUP)
        ]
        self.receiving = jnp.logical_and(links.last_of_plane(), links.z < links.groups - 1)

    def start(self):
        pl.when(self.links.z > 0)(self.send.start)

    def receive(self):
        @pl.when(self.receiving)
        def _():
            for copy in self.recvs:
                copy.wait_recv()

    def finish(self):
        pl.when(self.links.z > 0)(self.send.wait_send)


class BcSum:
    def __init__(self, links, bc, out, bufs):
        self.links, self.bc, self.out = links, bc, out
        self.sib, self.chip, self.peer, self.total, self.far = bufs
        p, c, groups = links.p, links.c, links.groups
        self.own = pl.ds(pl.multiple_of(c * STATE, STATE), STATE)
        other = pl.ds(pl.multiple_of((1 - c) * STATE, STATE), STATE)
        self.first = [links.copy(bc.at[:, :, :, other], self.sib, links.at(0, 1))]
        self.second = [
            links.copy(self.chip.at[:, lax.bitwise_xor(p, jnp.int32(k))], self.peer.at[k - 1], links.at(k, 0))
            for k in (3, 1, 2)
        ]
        self.third = []
        for k in range(1, groups):
            to = lax.rem(links.z + k, groups)
            self.third.append(links.copy(self.total.at[to], self.far.at[k - 1], (to, p, c)))
        self.fourth = [links.copy(out.at[:, self.own], out.at[:, self.own], links.at(0, 1))]

    @staticmethod
    def begin(copies):
        for copy in copies:
            copy.start()

    @staticmethod
    def arrive(copies):
        for copy in copies:
            copy.wait_recv()

    def cores(self):
        self.begin(self.first)

    def plane(self):
        self.arrive(self.first)

        def add(i, _):
            for q in range(GROUP):
                mine = self.bc[i, q, :, self.own].astype(F32)
                self.chip[i, q] = (mine + self.sib[i, q].astype(F32)).astype(BF16)
            return 0

        lax.fori_loop(0, self.links.groups, add, 0)
        self.begin(self.second)

    def groups(self):
        self.arrive(self.second)

        def add(i, _):
            total = self.chip[i, self.links.p].astype(F32)
            for k in range(GROUP - 1):
                total = total + self.peer[k, i].astype(F32)
            self.total[i] = total.astype(BF16)
            return 0

        lax.fori_loop(0, self.links.groups, add, 0)
        self.begin(self.third)

    def share(self):
        self.arrive(self.third)
        total = self.total[self.links.z].astype(F32)
        for k in range(self.links.groups - 1):
            total = total + self.far[k].astype(F32)
        self.out[:, self.own] = total.astype(BF16)
        self.begin(self.fourth)

    def finish(self):
        self.arrive(self.fourth)
        for copy in self.first + self.second + self.third + self.fourth:
            copy.wait_send()


class LaidOut:
    def __init__(self, links, dt, wide, dt_out, wide_out, dt_far, wide_far):
        self.links, self.refs = links, (dt, wide, dt_out, wide_out, dt_far, wide_far)
        z, p, c, groups = links.z, links.p, links.c, links.groups
        self.first, self.second = [], []
        for k in range(1, groups):
            to = lax.rem(z + k, groups)
            self.first.append(links.copy(dt.at[to], dt_far.at[k - 1], (to, p, c)))
            self.first.append(links.copy(wide, wide_far.at[k - 1], (to, p, c)))
        for k in range(1, GROUP):
            self.second.append(links.copy(dt_out.at[p], dt_out.at[p], links.at(k, 0)))
            self.second.append(links.copy(wide_out.at[p], wide_out.at[p], links.at(k, 0)))

    def groups(self):
        BcSum.begin(self.first)

    def plane(self):
        BcSum.arrive(self.first)
        dt, wide, dt_out, wide_out, dt_far, wide_far = self.refs
        dt_total, wide_total = dt[self.links.z].astype(F32), wide[...]
        for k in range(self.links.groups - 1):
            dt_total = dt_total + dt_far[k].astype(F32)
            wide_total = wide_total + wide_far[k]
        dt_out[self.links.p] = dt_total.astype(BF16)
        wide_out[self.links.p] = wide_total
        BcSum.begin(self.second)

    def finish(self):
        BcSum.arrive(self.second)
        for copy in self.first + self.second:
            copy.wait_send()


class VecSum:
    def __init__(self, links, vec, out, near, far):
        self.links, self.refs = links, (vec, out, near, far)
        z, p, c, groups = links.z, links.p, links.c, links.groups
        self.first, self.second, self.third = [], [], []
        for k in range(GROUP):
            for e in range(2):
                if k or e:
                    to = lax.bitwise_xor(p, jnp.int32(k)) * 2 + lax.bitwise_xor(c, jnp.int32(e))
                    self.first.append(links.copy(vec.at[to], near.at[2 * k + e - 1], links.at(k, e)))
                    self.third.append(links.copy(out.at[p * 2 + c], out.at[p * 2 + c], links.at(k, e)))
        for k in range(1, groups):
            self.second.append(links.copy(near.at[7], far.at[k - 1], (lax.rem(z + k, groups), p, c)))

    def plane(self):
        BcSum.begin(self.first)

    def groups(self):
        BcSum.arrive(self.first)
        vec, _, near, _ = self.refs
        total = vec[self.links.p * 2 + self.links.c]
        for slot in range(2 * GROUP - 1):
            total = total + near[slot]
        near[7] = total
        BcSum.begin(self.second)

    def back(self):
        BcSum.arrive(self.second)
        _, out, near, far = self.refs
        total = near[7]
        for k in range(self.links.groups - 1):
            total = total + far[k]
        out[self.links.p * 2 + self.links.c] = total
        BcSum.begin(self.third)

    def finish(self):
        BcSum.arrive(self.third)
        for copy in self.first + self.second + self.third:
            copy.wait_send()


class Refs:
    def __init__(self, refs, twins, sems):
        self.__dict__.update(refs)
        self.twins = {id(near): (far, near, sems.at[i]) for i, (far, near) in enumerate(twins)}
        self.waits = []

    def fetch(self, *refs):
        for ref in refs:
            far, near, sem = self.twins[id(ref)]
            pltpu.make_async_copy(far, near, sem).start()

    def need(self, *refs):
        for ref in refs:
            pltpu.make_async_copy(*self.twins[id(ref)]).wait()

    def flush(self, *refs):
        for ref in refs:
            far, near, sem = self.twins[id(ref)]
            self.waits.append(pltpu.make_async_copy(near, far, sem))
            self.waits[-1].start()

    def done(self):
        for copy in self.waits:
            copy.wait()


def weight_chain(links, w, steps, inner):
    rows, step_rows = w.shape[0] // links.groups, steps.shape[0] // links.groups
    cols = columns_of(inner)
    half = pl.ds(pl.multiple_of(cols.bc.start + links.c * STATE, STATE), STATE)

    def at(index):
        return pl.ds(pl.multiple_of(index * rows, EDGE), rows)

    pieces = [
        lambda i: w.at[at(i), cols.x],
        lambda i: w.at[at(i), cols.z],
        lambda i: w.at[at(i), half],
        lambda i: steps.at[pl.ds(pl.multiple_of(i * step_rows, EDGE), step_rows), :],
    ]
    return Chain(links, pieces), links.copy(w.at[:, half], w.at[:, half], links.at(0, 1))


def pack_steps(w_dt, steps_out, wide):
    heads_core, shard = w_dt.shape
    heads = heads_core // GROUP
    wide[...] = jnp.zeros_like(wide)
    wide[0:heads_core, 0:shard] = w_dt
    row, col = iota((EDGE, 128), 0), iota((EDGE, 128), 1)
    for q in range(GROUP):
        pick = jnp.logical_and(col == q * heads + row, row < heads).astype(BF16)
        steps_out[q] = dot(pick, wide[...]).astype(BF16)


def unpack_steps(steps, w, shard, inner):
    lanes = columns_of(inner).dt
    rows = GROUP * shard
    blank = jnp.zeros((128 - EDGE, 128), F32)

    def block(g, _):
        parts = []
        for j in range(GROUP):
            at = pl.ds(pl.multiple_of(g * (GROUP * EDGE) + j * EDGE, EDGE), EDGE)
            parts.append(jnp.concatenate([steps[at, :].astype(F32), blank]).T[0:shard])
        w[pl.ds(pl.multiple_of(g * rows, EDGE), rows), lanes] = jnp.concatenate(parts).astype(BF16)
        return 0

    lax.fori_loop(0, w.shape[0] // rows, block, 0)


def prepare(links, r, layer):
    inner = r.rowp.shape[1]
    heads_core = r.head_params.shape[2]
    lanes = pl.ds(pl.multiple_of(links.p * inner, 128), inner)
    r.gains[...] = r.norm_gain[...].astype(F32)
    r.headp[...] = jnp.zeros_like(r.headp)
    for i in range(3):
        r.headp[i : i + 1, 0:heads_core] = r.head_params[i, layer : layer + 1, :]
    mine = dot_exact(r.headp[...], head_pick(links.p, inner // HEADDIM).astype(F32))
    r.headp[...] = mine
    r.rowp[...] = jnp.zeros_like(r.rowp)
    r.rowp[0 : CONV + 1] = r.conv_x[:, :, lanes].astype(F32)[:, layer]
    r.rowp[5:6] = r.gated_gain[:, lanes].astype(F32)[layer : layer + 1]
    r.rowp[6:7] = dot_exact(mine, head_spread(inner).astype(F32))[2:3]
    r.bcp[...] = jnp.zeros_like(r.bcp)
    r.bcp[0 : CONV + 1] = r.conv_bc[...].astype(F32)[:, layer]


def out_chain(links, wo):
    rows = wo.shape[0] // links.groups
    return Chain(links, [lambda i: wo.at[pl.ds(pl.multiple_of(i * rows, EDGE), rows), :]])


def weight_swaps(links, r, layer, w, steps, wo):
    inner = wo.shape[1]
    cols = columns_of(inner)
    stagings = r.stagings[layer]
    here = pl.ds(pl.multiple_of(links.c * STATE, STATE), STATE)
    half = pl.ds(pl.multiple_of(cols.bc.start + links.c * STATE, STATE), STATE)
    swaps = [
        Swap(links, r.w_zx.at[layer, 1], stagings[0], w, cols.x, inner),
        Swap(links, r.w_zx.at[layer, 0], stagings[1], w, cols.z, inner),
        Swap(links, r.w_bc.at[layer, :, here], stagings[2], w, half, STATE),
        Swap(links, r.packed_steps.at[layer], stagings[3], steps, slice(0, 128), 128),
    ]
    return swaps, Swap(links, r.w_out.at[layer], stagings[4], wo, slice(0, inner), inner)


def scatter_blocks(scatter, compute):
    before = None
    for k in (3, 1, 2, 0):
        compute(lax.bitwise_xor(scatter.links.p, jnp.int32(k)))
        scatter.to_sibling[k].start()
        if before is not None:
            scatter.pass_on(before)
        before = k


def forward_layer(links, r, normed, w, wo, wo_chain, scatter, meanwhile):
    carried = States(links, False, r.state_low, r.decay_row, r.states_in, r.decays_in)
    state_sum, decay_all = project_and_convolve(
        normed, w, r.rowp, r.bcp, r.headp, r.z, r.xin, r.bcin, r.x, r.bc, r.dtraw, r.dt, r.s, r.decay, r.ext, r.local,
        lambda q: pl.when(q == 3)(wo_chain.advance),
    )
    r.state_low[...] = state_sum.astype(BF16)
    r.decay_row[...] = jnp.broadcast_to(decay_all, r.decay_row.shape)
    carried.start()
    r.flush(r.z, r.xin, r.bcin, r.x, r.bc, r.dtraw, r.dt, r.s, r.decay)
    wo_chain.advance()
    mix_within_spans(r.x, r.bc, r.s, r.dt, r.y)
    wo_chain.complete()
    meanwhile()
    carried.arrive()
    chain_states(entering_state(links.z, links.groups, r.states_in, r.decays_in, False), r.local, r.decay, r.states)
    scatter_blocks(
        scatter, lambda q: mix_out(q, r.states, r.x, r.bc, r.z, r.s, wo, r.rowp, r.y, r.part, r.squares)
    )
    r.flush(r.y, r.states)
    return carried


def first_kernel(inner_all, r):
    links = Links(r.sends, r.recvs)
    c = links.c
    inner = r.wo.shape[1]
    shard = r.w_dt.shape[2]
    links.greet(plane=True, groups=True, edge=1)
    for layer in range(2):
        pack_steps(r.w_dt[layer], r.packed_steps.at[layer], r.wide_steps)
    swaps, swap_o = weight_swaps(links, r, 0, r.w, r.dt_rows, r.wo)
    next_swaps, next_o = weight_swaps(links, r, 1, r.next_w, r.next_dt_rows, r.next_wo)
    all_swaps = swaps + [swap_o] + next_swaps + [next_o]
    gather, other = Gather(links, r.normed, EDGE), Gather(links, r.dmix, 0)
    edge = EdgeForward(links, gather)
    chain, share = weight_chain(links, r.w, r.dt_rows, inner)
    chain_o = out_chain(links, r.wo)
    next_chain, next_share = weight_chain(links, r.next_w, r.next_dt_rows, inner)
    scatter = Scatter(links, r.part, 0, r.sib, r.total, r.peer)
    small = SmallSum(links, r.squares, r.slots)
    next_gather = Gather(links, r.next_normed, EDGE)
    next_edge = EdgeForward(links, next_gather)

    prepare(links, r, 0)
    for swap in all_swaps:
        swap.keep.start()
    for start, size in row_chunks():
        at = pl.ds(pl.multiple_of(c * HALF + start, EDGE), size)
        rows_in = r.resid[at, :].astype(F32)
        r.resid_out[start : start + size] = rows_in
        r.normed[gather.own(start, size), :] = (rows_in * rms_of(rows_in) * r.gains[0:1]).astype(BF16)
        rows_in = r.cot[at, :]
        r.cot_out[start : start + size] = rows_in.astype(F32)
        r.dmix[other.own(start, size), :] = rows_in
    links.meet()
    for swap in swaps:
        swap.start()
    for swap in swaps:
        swap.settle()
    chain.begin()
    gather.start()
    edge.start()
    swap_o.start()
    chain.advance()
    gather.pass_on()
    for swap in next_swaps + [next_o]:
        swap.start()
    chain.advance()
    swap_o.settle()
    gather.finish()
    edge.finish()
    chain.complete()
    share.start()
    chain_o.begin()
    other.start()
    unpack_steps(r.dt_rows, r.w, shard, inner)
    r.flush(r.normed)
    share.wait()
    r.flush(r.w)

    def meanwhile():
        for swap in next_swaps + [next_o]:
            swap.settle()
        next_chain.begin()
        other.pass_on()
        r.flush(r.wo)

    carried = forward_layer(links, r, r.normed, r.w, r.wo, chain_o, scatter, meanwhile)
    small.start()
    next_chain.advance()
    scatter.pass_on(0)
    scatter.arrive()
    inv = lax.rsqrt(small.total() * (1.0 / inner_all) + EPS)
    r.inv_out[...] = inv
    column = inv.T[:, 0:1]
    for start, size in row_chunks():
        at = slice(start, start + size)
        mixed = scatter.own(start, size)
        r.mixed_out[at] = mixed
        fresh = r.resid_out[at] + column[at] * mixed
        r.fresh_out[at] = fresh
        r.next_normed[next_gather.own(start, size), :] = (fresh * rms_of(fresh) * r.gains[1:2]).astype(BF16)
    next_gather.start()
    next_edge.start()
    other.finish()
    r.flush(r.dmix)
    next_chain.advance()
    next_gather.pass_on()
    next_chain.complete()
    next_share.start()
    unpack_steps(r.next_dt_rows, r.next_w, shard, inner)
    scatter.finish()
    small.finish()
    next_gather.finish()
    next_edge.finish()
    carried.finish()
    for swap in all_swaps:
        swap.finish()
    for one in (chain, chain_o, next_chain):
        one.finish()
    next_share.wait()
    r.done()


def second_kernel(inner_all, r):
    links = Links(r.sends, r.recvs)
    rows = r.wo_own.shape[0]
    keep = links.local(r.wo_own, r.wo.at[pl.ds(pl.multiple_of(links.z * rows, EDGE), rows), :])
    chain_o = out_chain(links, r.wo)
    scatter = Scatter(links, r.part, 0, r.sib, r.total, r.peer)
    small = SmallSum(links, r.squares, r.slots)
    spread = SmallGather(links, r.scalars_out)
    at = pl.ds(pl.multiple_of(links.c * HALF, HALF), HALF)
    share = links.copy(r.block_out.at[at, :], r.block_out.at[at, :], links.at(0, 1))
    keep.start()
    links.greet(plane=True, groups=True)
    prepare(links, r, 1)
    keep.wait()
    links.meet()
    chain_o.begin()
    carried = forward_layer(links, r, r.normed, r.w, r.wo, chain_o, scatter, lambda: r.flush(r.wo))
    small.start()
    scatter.pass_on(0)
    scatter.arrive()
    inv = lax.rsqrt(small.total() * (1.0 / inner_all) + EPS)
    column = inv.T[:, 0:1]
    dots = []
    for start, size in row_chunks():
        at = slice(start, start + size)
        mixed = scatter.own(start, size)
        dots.append(jnp.sum(r.cot[at] * mixed, axis=-1, keepdims=True))
        r.block_out[pl.ds(pl.multiple_of(links.c * HALF + start, EDGE), size), :] = (
            r.resid[at] + column[at] * mixed
        ).astype(BF16)
    r.scalars_out[:, spread.lanes] = as_tile([column, jnp.concatenate(dots)])
    spread.start()
    share.start()
    scatter.finish()
    small.finish()
    carried.finish()
    chain_o.finish()
    spread.finish()
    share.wait()
    r.done()


def backward_layer(links, inner_all, r, at_start, before_collect, at_middle):
    carried = States(links, True, r.state_low, r.decay_row, r.states_in, r.decays_in)
    collect = Halve(links, r.gwo, r.go_in, r.go_sum)
    grad_sum, decay_all = back_through_gate(
        inner_all, r.dmix, r.wo, r.y, r.z, r.x, r.bc, r.s, r.decay, r.scalars, r.rowp,
        r.cat, r.wide, r.dy, r.prior, r.normed_out,
    )
    r.state_low[...] = grad_sum.astype(BF16)
    r.decay_row[...] = jnp.broadcast_to(decay_all, r.decay_row.shape)
    links.meet()
    carried.start()
    at_start()
    out_gradient(r.dmix, r.normed_out, r.gwo)
    before_collect()
    collect.begin()
    r.need(r.dt)
    back_within_spans(r.dy, r.x, r.bc, r.s, r.dt, r.dpre, r.flow, r.sums)
    at_middle()
    carried.arrive()
    grad = entering_state(links.z, links.groups, r.states_in, r.decays_in, True)
    r.need(r.states, r.dtraw, r.xin, r.bcin)
    back_through_states(
        grad, r.prior, r.decay, r.states, r.dy, r.x, r.bc, r.s, r.dt, r.dtraw, r.xin, r.bcin, r.rowp, r.bcp, r.headp,
        r.flow, r.sums, r.cat, r.wide, r.bc_rows, r.dpre, r.prior,
        lambda q: pl.when(q == 2)(collect.advance),
    )
    return carried, collect


def put_vector(vec, row, values):
    for i in range(values.shape[0]):
        for j in range(values.shape[1] // 128):
            vec[row // 8, row % 8 : row % 8 + 1, :] = values[i : i + 1, j * 128 : j * 128 + 128]
            row += 1


def third_kernel(inner_all, r):
    links = Links(r.sends, r.recvs)
    r.fetch(r.dt, r.states, r.dtraw, r.xin, r.bcin, r.w, r.normed, r.grad, r.resid, r.mixed)
    scatter = Scatter(links, r.part, EDGE, r.sib, r.total, r.peer)
    edge = EdgeBackward(links, r.part, r.edge_slots)
    gather = Gather(links, r.dmix_out, 0)
    spread = SmallGather(links, r.scalars_out)
    collects = [Halve(links, r.gx, r.gx_in, r.gx_sum), Halve(links, r.gwo, r.gz_in, r.gz_sum)]
    r.edge_slots[...] = jnp.zeros_like(r.edge_slots)
    links.greet(plane=True, groups=True, edge=-1)
    prepare(links, r, 1)
    carried, collect = backward_layer(links, inner_all, r, lambda: None, lambda: None, lambda: None)
    r.need(r.w, r.normed)
    x_gradient(r.cat, r.normed, r.gx)
    collects[0].begin()
    project_back_edge(r.cat, r.w, r.part)
    edge.start()
    scatter_blocks(scatter, lambda q: project_back(q, r.cat, r.w, r.part))
    scatter.pass_on(0)
    small_gradients(r.cat, r.normed, r.gbc, r.gdt)
    collect.complete()
    collect.finish()
    z_gradient(r.cat, r.normed, r.gwo)
    collects[1].begin()
    collects[0].advance()
    scatter.arrive()
    edge.receive()
    r.need(r.grad, r.resid, r.mixed)
    r.gain_row[...] = jnp.zeros_like(r.gain_row)
    dots = []
    for start, size in row_chunks():
        at = slice(start, start + size)
        fresh = grad_rows(links, scatter, r.edge_slots, r.grad, r.resid, r.gains[1:2], r.gain_row, start, size)
        r.grad_out[at] = fresh
        low = fresh.astype(BF16)
        r.dmix_out[gather.own(start, size), :] = low
        dots.append(jnp.sum(low.astype(F32) * r.mixed[at], axis=-1, keepdims=True))
    r.scalars_out[:, spread.lanes] = as_tile([r.inv[...].T[:, 0:1], jnp.concatenate(dots)])
    gather.start()
    spread.start()
    r.vec[...] = jnp.zeros_like(r.vec)
    model = r.gain_row.shape[1]
    put_vector(r.vec, model // 128, r.gain_row[0:1])
    put_vector(r.vec, 2 * (model // 128) + 2 * (CONV + 1), r.bc_rows[0 : CONV + 1])
    collects[1].advance()
    gather.pass_on()
    collects[0].complete()
    scatter.finish()
    edge.finish()
    gather.finish()
    spread.finish()
    carried.finish()
    collects[1].complete()
    for one in collects:
        one.finish()


def fourth_kernel(inner_all, r):
    links = Links(r.sends, r.recvs)
    r.fetch(r.dt, r.states, r.dtraw, r.xin, r.bcin, r.above_bc, r.above_x, r.above_z, r.above_o, r.normed, r.w, r.grad, r.resid)
    scatter = Scatter(links, r.part, EDGE, r.sib, r.total, r.peer)
    edge = EdgeBackward(links, r.part, r.edge_slots)
    at = pl.ds(pl.multiple_of(links.c * HALF, HALF), HALF)
    share = links.copy(r.out.at[at, :], r.out.at[at, :], links.at(0, 1))
    collects = [Halve(links, r.gx, r.gx_in, r.gx_sum), Halve(links, r.gwo, r.gz_in, r.gz_sum)]
    above = ((r.above_x, r.g_zx.at[1, 1]), (r.above_z, r.g_zx.at[1, 0]), (r.above_o, r.g_out.at[1]))
    own = ((r.go_sum, r.g_out.at[0]), (r.gx_sum, r.g_zx.at[0, 1]), (r.gz_sum, r.g_zx.at[0, 0]))
    delivers = [Deliver(links, parts, out) for parts, out in above]
    own_delivers = [Deliver(links, parts, out) for parts, out in own]
    bc_sums = [
        BcSum(links, bc, r.bc_out.at[i], r.bc_bufs[i])
        for i, bc in enumerate((r.gbc, r.above_bc))
    ]
    laid = LaidOut(links, r.steps_all, r.wide_all, r.dt_out, r.wide_out, r.dt_far, r.wide_far)
    vec_sum = VecSum(links, r.vec, r.vec_out, r.vec_near, r.vec_far)
    r.edge_slots[...] = jnp.zeros_like(r.edge_slots)
    links.greet(plane=True, groups=True, edge=-1)
    prepare(links, r, 0)

    def at_start():
        r.need(r.above_bc)
        bc_sums[1].cores()

    def at_middle():
        bc_sums[1].groups()
        r.need(r.above_x, r.above_z, r.above_o)
        for deliver in delivers:
            deliver.start()

    carried, collect = backward_layer(links, inner_all, r, at_start, bc_sums[1].plane, at_middle)
    r.need(r.normed)
    small_gradients(r.cat, r.normed, r.gbc, r.gdt)
    bc_sums[0].cores()
    r.steps_all[:, 0:EDGE, :] = r.gdt[...]
    r.steps_all[:, EDGE:, :] = r.above_dt[...]
    r.wide_all[0:16] = r.wide[...]
    r.wide_all[16:32] = r.above_wide[...]
    laid.groups()
    x_gradient(r.cat, r.normed, r.gx)
    collects[0].begin()
    bc_sums[0].plane()
    r.need(r.w)
    project_back_edge(r.cat, r.w, r.part)
    edge.start()
    scatter_blocks(scatter, lambda q: project_back(q, r.cat, r.w, r.part))
    scatter.pass_on(0)
    bc_sums[0].groups()
    collect.complete()
    collect.finish()
    z_gradient(r.cat, r.normed, r.gwo)
    collects[1].begin()
    collects[0].advance()
    own_delivers[0].start()
    scatter.arrive()
    edge.receive()
    r.need(r.grad, r.resid)
    r.gain_row[...] = jnp.zeros_like(r.gain_row)
    for start, size in row_chunks():
        fresh = grad_rows(links, scatter, r.edge_slots, r.grad, r.resid, r.gains[0:1], r.gain_row, start, size)
        r.out[pl.ds(pl.multiple_of(links.c * HALF + start, EDGE), size), :] = fresh.astype(BF16)
    share.start()
    r.vec[...] = r.above_vec[...]
    put_vector(r.vec, 0, r.gain_row[0:1])
    put_vector(r.vec, 2 * (r.gain_row.shape[1] // 128), r.bc_rows[0 : CONV + 1])
    vec_sum.plane()
    vec_sum.groups()
    collects[1].advance()
    bc_sums[1].share()
    laid.plane()
    collects[0].complete()
    own_delivers[1].start()
    laid.finish()
    lay_out_heads(links, r)
    bc_sums[0].share()
    vec_sum.back()
    collects[1].complete()
    own_delivers[2].start()
    for one in bc_sums + [scatter, edge, carried] + collects:
        one.finish()
    vec_sum.finish()
    lay_out_vector(r)
    share.wait()
    for deliver in delivers + own_delivers:
        deliver.arrive()
        deliver.finish()


def lay_out_heads(links, r):
    inner = r.wide.shape[1]
    heads = inner // HEADDIM
    heads_core, shard = r.g_dt.shape[1:]
    spread = head_spread(inner).astype(F32)
    row, col = iota((128, 128), 0), iota((128, 128), 1)
    blank = jnp.zeros((128 - 2 * EDGE, r.dt_out.shape[2]), F32)
    steps = [jnp.zeros((shard, 128), F32) for _ in range(2)]
    tall = [jnp.zeros((8, 128), F32) for _ in range(2)]
    for q in range(GROUP):
        lanes = slice(q * inner, q * inner + inner)
        r.step_rows[...] = jnp.concatenate([r.dt_out[q].astype(F32), blank]).T
        mine = r.step_rows[pl.ds(pl.multiple_of(links.p * shard, 8), shard), :]
        gains, taps = [], []
        for layer in range(2):
            first, second = r.wide_out[q, 16 * layer : 16 * layer + 8], r.wide_out[q, 16 * layer + 8 : 16 * layer + 16]
            taps.append(first[0 : CONV + 1])
            gains.append(first[5:6])
            place = jnp.logical_and(row - EDGE * layer == col - q * heads, jnp.logical_and(row >= EDGE * layer, row < EDGE * layer + heads))
            steps[layer] = steps[layer] + dot_exact(mine, place.astype(F32))
            place = jnp.logical_and(row == col - q * heads, row < heads).astype(F32)
            skip = dot_exact(first, spread, NT)[6:7]
            rows = jnp.concatenate([first[7:8, 0:128], second[0:1, 0:128], skip, jnp.zeros((5, 128), F32)])
            tall[layer] = tall[layer] + dot_exact(rows, place)
        for j in range(CONV + 1):
            r.g_conv_x[j, :, lanes] = jnp.concatenate([tap[j : j + 1] for tap in taps]).astype(BF16)
        r.g_gain[:, lanes] = jnp.concatenate(gains).astype(BF16)
    for layer in range(2):
        r.g_dt[layer] = steps[layer].T[0:heads_core].astype(BF16)
    for i in range(3):
        r.g_head[i] = jnp.concatenate([one[i : i + 1, 0:heads_core] for one in tall]).astype(BF16)


def lay_out_vector(r):
    def row(i):
        return r.vec_out[i // 8, i % 8 : i % 8 + 1, :]

    count = r.g_norm.shape[1] // 128
    for i in range(count):
        r.g_norm[:, i * 128 : i * 128 + 128] = jnp.concatenate([row(i), row(count + i)]).astype(BF16)
    for half in range(2):
        for j in range(CONV + 1):
            firsts = [2 * count + layer * 2 * (CONV + 1) + 2 * j + half for layer in range(2)]
            rows = jnp.concatenate([row(first) for first in firsts])
            r.g_conv_bc[j, :, half * 128 : half * 128 + 128] = rows.astype(BF16)


def flat(value):
    return [a for member in value for a in flat(member)] if isinstance(value, list) else [value]


def shaped(value, leaves):
    return [shaped(member, leaves) for member in value] if isinstance(value, list) else leaves.pop(0)


def call(body, collective, copies, outs, hbm_outs, ins, hbm_ins, scratch):
    vmem, hbm = pl.BlockSpec(memory_space=pltpu.VMEM), pl.BlockSpec(memory_space=pl.ANY)
    twins = {**{name: (a.shape, a.dtype) for name, a in hbm_ins.items()}, **hbm_outs}
    sides = [list(ins.values()), list(hbm_ins.values()), list(outs.values()), list(hbm_outs.values())]
    counts = [len(flat(side)) for side in sides]
    buffers = flat([list(scratch.values()), list(twins.values())])

    def kernel(*refs):
        refs = list(refs)
        groups = [shaped(side, refs) for side in sides]
        inner = shaped([list(scratch.values()), list(twins.values())], refs)
        sends, recvs, sems = refs
        near = dict(zip(twins, inner[1]))
        named = {**dict(zip(ins, groups[0])), **dict(zip(outs, groups[2])), **dict(zip(scratch, inner[0])), **near}
        body(Refs(dict(named, sends=sends, recvs=recvs), list(zip(groups[1] + groups[3], inner[1])), sems))

    results = pl.pallas_call(
        kernel,
        out_shape=tuple(jax.ShapeDtypeStruct(*a) for a in flat(sides[2:])),
        in_specs=[vmem] * counts[0] + [hbm] * counts[1],
        out_specs=tuple([vmem] * counts[2] + [hbm] * counts[3]),
        scratch_shapes=[pltpu.VMEM(*a) for a in buffers]
        + [pltpu.SemaphoreType.DMA((n,)) for n in (copies, copies, max(1, len(twins)))],
        compiler_params=pltpu.CompilerParams(
            vmem_limit_bytes=VMEM_BYTES, collective_id=collective, has_side_effects=True
        ),
    )(*flat(sides[:2]))
    found = shaped(sides[2:], list(results))
    return types.SimpleNamespace(**dict(zip(outs, found[0])), **dict(zip(hbm_outs, found[1])))


def on_device(resid_in, cotangent, norm_gain, w_zx, w_dt, w_bc, conv_x, conv_bc, head_params, gated_gain, w_out):
    layers, model = norm_gain.shape
    groups = lax.axis_size("z")
    shard = w_dt.shape[1]
    inner_core = conv_x.shape[2]
    inner = inner_core // GROUP
    heads_core = head_params.shape[2]
    inner_all = inner_core * lax.axis_size("head")
    length = resid_in.shape[1]
    tokens = GROUP * length
    spans = tokens // SPAN
    rows = GROUP * shard

    own_rows = ((HALF, model), F32)
    all_rows, edged_rows = ((tokens, model), BF16), ((tokens + EDGE, model), BF16)
    columns = columns_of(inner).size
    w_shape, wo_shape = ((model, columns), BF16), ((model, inner), BF16)
    scalars = ((8, tokens), F32)
    state_shape = ((spans, STATE, inner), F32)
    low_rows, steps_shape = ((tokens, inner), BF16), ((tokens, 128), F32)
    scatter_scratch = dict(
        sib=((GROUP, HALF, model), BF16),
        total=((GROUP - 1, HALF, model), BF16),
        peer=((GROUP - 1, HALF, model), BF16),
    )
    state_scratch = dict(
        state_low=((STATE, inner), BF16),
        decay_row=((8, inner), F32),
        states_in=((groups, STATE, inner), BF16),
        decays_in=((groups, 8, inner), F32),
    )
    saved_shapes = dict(
        y=((tokens, inner), F32),
        z=low_rows,
        x=low_rows,
        bc=((tokens, 2 * STATE), BF16),
        s=steps_shape,
        dt=steps_shape,
        dtraw=((tokens, 128), BF16),
        xin=((tokens + EDGE, inner), BF16),
        bcin=((tokens + EDGE, 2 * STATE), BF16),
        states=state_shape,
        decay=((spans, 8, inner), F32),
    )
    forward_scratch = dict(
        ext=((tokens + EDGE, inner + 2 * STATE), F32),
        local=state_shape,
        part=all_rows,
        squares=scalars,
        slots=((2 * GROUP - 1, 8, HALF), F32),
        **state_scratch,
        **scatter_scratch,
    )

    conv_x, conv_bc, head_params = [jnp.swapaxes(a, 0, 1) for a in (conv_x, conv_bc, head_params)]
    w_dt, w_out = jnp.swapaxes(w_dt, 1, 2), jnp.swapaxes(w_out, 1, 2)
    params = dict(
        norm_gain=norm_gain, conv_x=conv_x, conv_bc=conv_bc, head_params=head_params, gated_gain=gated_gain
    )
    param_scratch = dict(
        rowp=((8, inner), F32), bcp=((8, 2 * STATE), F32), headp=((8, 128), F32), gains=((layers, model), F32)
    )
    stagings = [((GROUP, rows_in, width), BF16) for rows_in, width in (
        (shard, inner), (shard, inner), (shard, STATE), (EDGE, 128), (shard, inner)
    )]
    step_rows = ((groups * GROUP * EDGE, 128), BF16)
    first = call(
        functools.partial(first_kernel, inner_all),
        0,
        160 + 14 * (groups - 1) + 2 * groups,
        dict(
            next_w=w_shape,
            next_wo=((rows, inner), BF16),
            next_normed=edged_rows,
            resid_out=own_rows,
            cot_out=own_rows,
            mixed_out=own_rows,
            fresh_out=own_rows,
            inv_out=((8, HALF), F32),
        ),
        dict(normed=edged_rows, dmix=all_rows, w=w_shape, wo=wo_shape, **saved_shapes),
        dict(
            resid=resid_in[0],
            cot=cotangent[0],
            w_zx=w_zx,
            w_dt=w_dt,
            w_bc=w_bc,
            w_out=w_out,
            **params,
        ),
        dict(),
        dict(
            **forward_scratch,
            **param_scratch,
            stagings=[stagings, stagings],
            dt_rows=step_rows,
            next_dt_rows=step_rows,
            packed_steps=((layers, GROUP, EDGE, 128), BF16),
            wide_steps=((128, 128), BF16),
        ),
    )
    second = call(
        functools.partial(second_kernel, inner_all),
        1,
        60 + 4 * groups,
        dict(block_out=((length, model), BF16), scalars_out=scalars),
        dict(wo=wo_shape, **saved_shapes),
        dict(
            normed=first.next_normed,
            w=first.next_w,
            wo_own=first.next_wo,
            **params,
            resid=first.fresh_out,
            cot=first.cot_out,
        ),
        dict(),
        dict(**forward_scratch, **param_scratch),
    )
    grad_in = ((groups - 1, rows, inner), BF16)
    grad_sum = ((GROUP, shard, inner), BF16)
    bc_grad = ((groups, GROUP, shard, 2 * STATE), BF16)
    dt_grad = ((groups, EDGE, rows), BF16)
    wide_grad = ((16, inner), F32)
    vec_shape = ((2 * GROUP, 8, 128), F32)
    back_scratch = dict(
        dy=low_rows,
        gwo=wo_shape,
        normed_out=low_rows,
        prior=state_shape,
        dpre=((tokens + 2 * EDGE, inner + 2 * STATE), F32),
        flow=steps_shape,
        sums=steps_shape,
        cat=((tokens + EDGE, columns), BF16),
        bc_rows=((8, 2 * STATE), F32),
        part=edged_rows,
        gx=wo_shape,
        go_in=grad_in,
        gx_in=grad_in,
        gz_in=grad_in,
        gain_row=((8, model), F32),
        edge_slots=((2 * GROUP, EDGE, model), BF16),
        **state_scratch,
        **param_scratch,
        **scatter_scratch,
    )

    def at_once(run):
        return dict(y=run.y, z=run.z, x=run.x, bc=run.bc, s=run.s, decay=run.decay)

    def later(run):
        return dict(dt=run.dt, states=run.states, dtraw=run.dtraw, xin=run.xin, bcin=run.bcin)

    third = call(
        functools.partial(third_kernel, inner_all),
        2,
        60 + 6 * groups,
        dict(
            dmix_out=all_rows,
            scalars_out=scalars,
            grad_out=own_rows,
            go_sum=grad_sum,
            gx_sum=grad_sum,
            gz_sum=grad_sum,
            gbc=bc_grad,
            gdt=dt_grad,
            wide=wide_grad,
            vec=vec_shape,
        ),
        dict(),
        dict(
            dmix=first.dmix,
            scalars=second.scalars_out,
            wo=second.wo,
            **params,
            inv=first.inv_out,
            **at_once(second),
        ),
        dict(
            w=first.next_w,
            normed=first.next_normed,
            grad=first.cot_out,
            resid=first.fresh_out,
            mixed=first.mixed_out,
            **later(second),
        ),
        back_scratch,
    )
    far = groups - 1
    dt_shape, wide_shape = (layers * EDGE, rows), (layers * 16, inner)
    half_bc = (groups, GROUP, shard, STATE)
    bc_bufs = [
        (half_bc, BF16),
        (half_bc, BF16),
        ((GROUP - 1, groups, shard, STATE), BF16),
        ((groups, shard, STATE), BF16),
        ((far, shard, STATE), BF16),
    ]
    fourth = call(
        functools.partial(fourth_kernel, inner_all),
        3,
        130 + 14 * groups,
        dict(
            out=((length, model), BF16),
            bc_out=((layers, shard, 2 * STATE), BF16),
            g_norm=(norm_gain.shape, BF16),
            g_zx=(w_zx.shape, BF16),
            g_dt=(w_dt.shape, BF16),
            g_conv_x=(conv_x.shape, BF16),
            g_conv_bc=(conv_bc.shape, BF16),
            g_head=(head_params.shape, BF16),
            g_gain=(gated_gain.shape, BF16),
            g_out=(w_out.shape, BF16),
        ),
        dict(),
        dict(
            dmix=third.dmix_out,
            scalars=third.scalars_out,
            wo=first.wo,
            **params,
            above_dt=third.gdt,
            above_wide=third.wide,
            above_vec=third.vec,
            **at_once(first),
        ),
        dict(
            w=first.w,
            normed=first.normed,
            grad=third.grad_out,
            resid=first.resid_out,
            above_x=third.gx_sum,
            above_z=third.gz_sum,
            above_o=third.go_sum,
            above_bc=third.gbc,
            **later(first),
        ),
        dict(
            **back_scratch,
            vec_out=vec_shape,
            dt_out=((GROUP, *dt_shape), BF16),
            wide_out=((GROUP, *wide_shape), F32),
            step_rows=((rows, 128), F32),
            go_sum=grad_sum,
            gx_sum=grad_sum,
            gz_sum=grad_sum,
            gbc=bc_grad,
            gdt=dt_grad,
            wide=wide_grad,
            vec=vec_shape,
            steps_all=((groups, *dt_shape), BF16),
            wide_all=(wide_shape, F32),
            bc_bufs=[bc_bufs, bc_bufs],
            vec_near=vec_shape,
            vec_far=((far, 8, 128), F32),
            dt_far=((far, *dt_shape), BF16),
            wide_far=((far, *wide_shape), F32),
        ),
    )
    return (
        second.block_out[None],
        fourth.out[None],
        fourth.g_norm,
        fourth.g_zx,
        jnp.swapaxes(fourth.g_dt, 1, 2),
        fourth.bc_out,
        *[jnp.swapaxes(a, 0, 1) for a in (fourth.g_conv_x, fourth.g_conv_bc, fourth.g_head)],
        fourth.g_gain,
        jnp.swapaxes(fourth.g_out, 1, 2),
    )


def solution(mesh):
    seq, head = mesh.shape["seq"], mesh.shape["head"]
    split = Mesh(mesh.devices.reshape(seq // GROUP, GROUP, head), ("z", "p", "head"))
    seq_axes = ("z", "p")
    specs = (
        P(None, seq_axes, None),
        P(None, seq_axes, None),
        P(),
        P(None, None, seq_axes, "head"),
        P(None, seq_axes, "head"),
        P(None, seq_axes, None),
        P(None, None, "head"),
        P(),
        P(None, None, "head"),
        P(None, "head"),
        P(None, "head", seq_axes),
    )
    return jax.shard_map(on_device, mesh=split, in_specs=specs, out_specs=specs, check_vma=False)
```

```python
import functools
import types
import typing

import jax
import jax.numpy as jnp
from jax import lax
from jax.experimental import pallas as pl
from jax.experimental.pallas import tpu as pltpu
from jax.sharding import Mesh, PartitionSpec as P

HEADDIM = 64
STATE = 128
CONV = 4
SPAN = 256
GROUP = 4
EDGE = 16
EPS = 1e-05
HIGH = lax.Precision.HIGHEST
F32, BF16 = jnp.float32, jnp.bfloat16
NN = (((1,), (0,)), ((), ()))
NT = (((1,), (1,)), ((), ()))
TN = (((0,), (0,)), ((), ()))
VMEM_BYTES = 58 << 20


def dot(a, b, dims=NN):
    return lax.dot_general(a, b, dims, preferred_element_type=F32)


def dot_exact(a, b, dims=NN):
    return lax.dot_general(a, b, dims, precision=HIGH, preferred_element_type=F32)


def dot_split(a, b, dims=NN):
    high = a.astype(BF16)
    rest = (a - high.astype(F32)).astype(BF16)
    return dot(high, b, dims) + dot(rest, b, dims)


def sigmoid(v):
    return 1.0 / (1.0 + jnp.exp(-v))


def softplus(v):
    return jnp.maximum(v, 0.0) + jnp.log1p(jnp.exp(-jnp.abs(v)))


def silu_slope(v):
    sig = sigmoid(v)
    return sig * (1.0 + v * (1.0 - sig))


def iota(shape, dim):
    return lax.broadcasted_iota(jnp.int32, shape, dim)


def head_spread(inner):
    return (iota((128, inner), 0) == lax.shift_right_logical(iota((128, inner), 1), 6)).astype(BF16)


def triangle(lower):
    rows, cols = iota((SPAN, SPAN), 0), iota((SPAN, SPAN), 1)
    return ((cols <= rows) if lower else (cols >= rows)).astype(F32)


def half_masks():
    lane = iota((SPAN, 128), 1)
    return (lane < HEADDIM).astype(BF16), (lane >= HEADDIM).astype(BF16)


def conv_taps(window, taps):
    total = jnp.broadcast_to(taps[CONV : CONV + 1], (SPAN, window.shape[1]))
    for j in range(CONV):
        total = total + taps[j : j + 1] * window[EDGE - 3 + j : EDGE - 3 + j + SPAN]
    return total


def head_pick(place, heads):
    row, col = iota((128, 128), 0), iota((128, 128), 1)
    return jnp.logical_and(row == place * heads + col, col < heads).astype(BF16)


class Columns(typing.NamedTuple):
    x: slice
    z: slice
    dt: slice
    bc: slice
    size: int


def columns_of(inner):
    first = 2 * inner + 128
    return Columns(
        slice(0, inner), slice(inner, 2 * inner), slice(2 * inner, first), slice(first, first + 2 * STATE), first + 2 * STATE
    )


def project_and_convolve(
    normed, w, rowp, bcp, headp,
    z_out, xin_out, bcin_out, x_out, bc_out, dtraw_out, dt_out, s_out, decay_out,
    ext, local, at_block,
):
    inner = x_out.shape[1]
    spans = x_out.shape[0] // SPAN

    cols = columns_of(inner)
    edge = normed[0:EDGE]
    edge_x = dot(edge, w[:, cols.x]).astype(BF16)
    edge_bc = dot(edge, w[:, cols.bc]).astype(BF16)
    xin_out[0:EDGE] = edge_x
    bcin_out[0:EDGE] = edge_bc
    ext[0:EDGE, 0:inner] = edge_x.astype(F32)
    ext[0:EDGE, inner:] = edge_bc.astype(F32)
    spread = head_spread(inner)
    low_tri = triangle(True)
    rate = -jnp.exp(headp[0:1])
    bias = headp[1:2]

    def block(q, carry):
        state_sum, decay_all = carry
        at = pl.multiple_of(q * SPAN, SPAN)
        tok = pl.ds(at, SPAN)
        after = pl.ds(pl.multiple_of(at + EDGE, EDGE), SPAN)
        at_block(q)
        product = dot(normed[after, :], w[...]).astype(BF16)
        z_out[tok, :] = product[:, cols.z]
        xin, bcin = product[:, cols.x], product[:, cols.bc]
        dtraw = product[:, cols.dt]
        xin_out[after, :] = xin
        bcin_out[after, :] = bcin
        dtraw_out[tok, :] = dtraw
        ext[after, 0:inner] = xin.astype(F32)
        ext[after, inner:] = bcin.astype(F32)
        window = pl.ds(at, SPAN + EDGE)
        pre_x = conv_taps(ext[window, 0:inner], rowp)
        x = (pre_x * sigmoid(pre_x)).astype(BF16)
        x_out[tok, :] = x
        pre_bc = conv_taps(ext[window, inner:], bcp)
        bc = (pre_bc * sigmoid(pre_bc)).astype(BF16)
        bc_out[tok, :] = bc
        dt = softplus(dtraw.astype(F32) + bias)
        s = dot_exact(low_tri, dt * rate)
        dt_out[tok, :] = dt
        s_out[tok, :] = s
        to_end = jnp.exp(s[SPAN - 1 : SPAN] - s) * dt
        weighted = (x.astype(F32) * dot_split(to_end, spread)).astype(BF16)
        fresh = dot(bc[:, :STATE], weighted, TN)
        decay = dot_split(jnp.exp(s[SPAN - 8 : SPAN]), spread)[7:8]
        local[q] = fresh
        decay_out[q] = jnp.broadcast_to(decay, (8, inner))
        return state_sum * decay + fresh, decay_all * decay

    return lax.fori_loop(0, spans, block, (jnp.zeros((STATE, inner), F32), jnp.ones((1, inner), F32)))


def mix_within_spans(x_in, bc_in, s_in, dt_in, y_out):
    inner = x_in.shape[1]

    def block(q, _):
        tok = pl.ds(pl.multiple_of(q * SPAN, SPAN), SPAN)
        x, bc, s = x_in[tok, :], bc_in[tok, :], s_in[tok, :]
        s_row, dt_row = s.T, dt_in[tok, :].T
        cb = dot(bc[:, STATE:], bc[:, :STATE], NT)
        causal = iota((SPAN, SPAN), 1) <= iota((SPAN, SPAN), 0)
        masks = half_masks()
        for pair in range(inner // 128):
            lanes = slice(pair * 128, pair * 128 + 128)
            x_pair = x[:, lanes]
            total = None
            for e in range(2):
                h = pair * 2 + e
                gap = jnp.where(causal, s[:, h : h + 1] - s_row[h : h + 1, :], -1e30)
                scores = (cb * (jnp.exp(gap) * dt_row[h : h + 1, :])).astype(BF16)
                term = dot(scores, x_pair * masks[e])
                total = term if total is None else total + term
            y_out[tok, lanes] = total
        return 0

    lax.fori_loop(0, x_in.shape[0] // SPAN, block, 0)


def entering_state(place, count, sums, decays, backward):
    inner = sums.shape[2]
    state = jnp.zeros((STATE, inner), F32)
    for turn in range(count):
        other = count - 1 - turn if backward else turn
        ahead = (place < other) if backward else (other < place)
        state = jnp.where(ahead, decays[other, 0:1] * state + sums[other].astype(F32), state)
    return state


def chain_states(state, local, decay, states_out):
    def block(q, state):
        states_out[q] = state
        return decay[q, 0:1] * state + local[q]

    lax.fori_loop(0, local.shape[0], block, state)


def mix_out(q, states, x, bc, z, s, wo, rowp, y_out, part_out, sq_out):
    inner = x.shape[1]
    tok = pl.ds(pl.multiple_of(q * SPAN, SPAN), SPAN)
    carried = dot_split(jnp.exp(s[tok, :]), head_spread(inner)) * dot(bc[tok, STATE:], states[q].astype(BF16))
    y = y_out[tok, :] + carried + rowp[6:7] * x[tok, :].astype(F32)
    y_out[tok, :] = y
    zf = z[tok, :].astype(F32)
    gated = y * (zf * sigmoid(zf))
    sq_out[:, tok] = dot_exact(jnp.ones((8, inner), F32), gated * gated, NT)
    part_out[tok, :] = dot((gated * rowp[5:6]).astype(BF16), wo[...], NT).astype(BF16)


def back_through_gate(
    inner_all, dmix, wo, y_in, z, x, bc, s, decay, token_scalars, rowp, cat_out, wide, dy_out, prior, normed_out
):
    inner = x.shape[1]
    spans = x.shape[0] // SPAN
    spread = head_spread(inner)
    gain = rowp[5:6]
    cols = columns_of(inner)

    def block(i, carry):
        grad_sum, gain_sum, skip_sum = carry
        q = spans - 1 - i
        tok = pl.ds(pl.multiple_of(q * SPAN, SPAN), SPAN)
        columns = token_scalars[:, tok].T
        inv, total_dot = columns[:, 0:1], columns[:, 1:2]
        zf = z[tok, :].astype(F32)
        sig = sigmoid(zf)
        act = zf * sig
        y = y_in[tok, :]
        gated = y * act
        d_no = dot(dmix[tok, :], wo[...])
        scaled = gated * inv
        normed_out[tok, :] = (scaled * gain).astype(BF16)
        gain_sum = gain_sum + jnp.sum(d_no * scaled, axis=0, keepdims=True)
        d_gated = inv * (d_no * gain) - gated * (inv * inv * inv * total_dot * (1.0 / inner_all))
        after = pl.ds(pl.multiple_of(q * SPAN + EDGE, EDGE), SPAN)
        cat_out[after, cols.z] = (d_gated * y * (sig * (1.0 + zf * (1.0 - sig)))).astype(BF16)
        dy = d_gated * act
        xf = x[tok, :].astype(F32)
        skip_sum = skip_sum + jnp.sum(dy * xf, axis=0, keepdims=True)
        dy_low = dy.astype(BF16)
        dy_out[tok, :] = dy_low
        scaled_dy = (dy_low.astype(F32) * dot_split(jnp.exp(s[tok, :]), spread)).astype(BF16)
        fresh = dot(bc[tok, STATE:], scaled_dy, TN)
        prior[q] = fresh
        return fresh + decay[q, 0:1] * grad_sum, gain_sum, skip_sum

    zero = jnp.zeros((1, inner), F32)
    grad_sum, gain_sum, skip_sum = lax.fori_loop(
        0, spans, block, (jnp.zeros((STATE, inner), F32), zero, zero)
    )
    decay_all = decay[0, 0:1]
    for q in range(1, spans):
        decay_all = decay_all * decay[q, 0:1]
    wide[...] = jnp.zeros_like(wide)
    wide[5:6] = gain_sum
    wide[6:7] = skip_sum
    return grad_sum, decay_all


def out_gradient(dmix, normed_out, gwo_out):
    def rows_of(i, _):
        rows = pl.ds(pl.multiple_of(i * SPAN, SPAN), SPAN)
        gwo_out[rows, :] = dot(dmix[:, rows], normed_out[...], TN).astype(BF16)
        return 0

    lax.fori_loop(0, dmix.shape[1] // SPAN, rows_of, 0)


def back_within_spans(dy_in, x_in, bc_in, s_in, dt_in, dpre, flow_out, sum_out):
    inner = x_in.shape[1]

    def block(q, _):
        at = pl.multiple_of(q * SPAN, SPAN)
        tok = pl.ds(at, SPAN)
        after = pl.ds(pl.multiple_of(at + EDGE, EDGE), SPAN)
        x_low, dy = x_in[tok, :], dy_in[tok, :]
        b, c = bc_in[tok, :STATE], bc_in[tok, STATE:]
        s, dt = s_in[tok, :], dt_in[tok, :]
        s_row = s.T
        cb = dot(b, c, NT)
        seen = iota((SPAN, SPAN), 0) <= iota((SPAN, SPAN), 1)
        masks = half_masks()
        d_cb = jnp.zeros((SPAN, SPAN), F32)
        lane = iota((SPAN, 128), 1)
        row_id = iota((128, SPAN), 0)
        sum_k = jnp.zeros((128, SPAN), F32)
        sum_t = jnp.zeros((SPAN, 128), F32)
        for pair in range(inner // 128):
            lanes = slice(pair * 128, pair * 128 + 128)
            x_pair, dy_pair = x_low[:, lanes], dy[:, lanes]
            total = None
            for e in range(2):
                h = pair * 2 + e
                d_scores = dot(x_pair * masks[e], dy_pair, NT)
                fade = jnp.exp(jnp.where(seen, s_row[h : h + 1, :] - s[:, h : h + 1], -1e30))
                dt_h = dt[:, h : h + 1]
                fade_cb = cb * fade
                term = dot((fade_cb * dt_h).astype(BF16), dy_pair * masks[e])
                total = term if total is None else total + term
                d_cb = d_cb + d_scores * (fade * dt_h)
                flow = d_scores * fade_cb
                sum_t = jnp.where(lane == h, jnp.sum(flow, axis=1, keepdims=True), sum_t)
                sum_k = jnp.where(row_id == h, jnp.sum(flow * dt_h, axis=0, keepdims=True), sum_k)
            dpre[after, lanes] = total
        d_cb_low = d_cb.astype(BF16)
        dpre[after, inner : inner + STATE] = dot(d_cb_low, c)
        dpre[after, inner + STATE :] = dot(d_cb_low, b, TN)
        flow_out[tok, :] = sum_k.T - sum_t * dt
        sum_out[tok, :] = sum_t
        return 0

    lax.fori_loop(0, x_in.shape[0] // SPAN, block, 0)


def back_through_states(
    grad, prior, decay, states, dy_in, x, bc, s_in, dt_in, dtraw, xin, bcin, rowp, bcp, headp, flow_in, sum_in,
    cat_out, row_out, bcrow_out,
    dpre, dend, at_block,
):
    inner = x.shape[1]
    spans = x.shape[0] // SPAN
    spread = head_spread(inner)
    up_tri = triangle(False)
    skip = rowp[6:7]
    rate = -jnp.exp(headp[0:1])
    bias = headp[1:2]
    width = inner + 2 * STATE

    def chain(i, grad):
        q = spans - 1 - i
        before = prior[q] + decay[q, 0:1] * grad
        dend[q] = grad
        return before

    lax.fori_loop(0, spans, chain, grad)
    dpre[0:EDGE] = jnp.zeros((EDGE, width), F32)
    dpre[EDGE + spans * SPAN :] = jnp.zeros((EDGE, width), F32)
    bcrow_out[...] = jnp.zeros_like(bcrow_out)
    cols = columns_of(inner)
    cat_out[0:EDGE, cols.z] = jnp.zeros((EDGE, inner), BF16)
    cat_out[0:EDGE, cols.dt] = jnp.zeros((EDGE, 128), BF16)

    def block(q, _):
        at = pl.multiple_of(q * SPAN, SPAN)
        tok = pl.ds(at, SPAN)
        after = pl.ds(pl.multiple_of(at + EDGE, EDGE), SPAN)
        window = pl.ds(at, SPAN + EDGE)
        at_block(q)
        x_low, dy = x[tok, :], dy_in[tok, :]
        xf, dyf = x_low.astype(F32), dy.astype(F32)
        b, c = bc[tok, :STATE], bc[tok, STATE:]
        s, dt = s_in[tok, :], dt_in[tok, :]
        exp_s = jnp.exp(s)
        to_end = jnp.exp(s[SPAN - 1 : SPAN] - s)
        w = to_end * dt
        w_all, s_all = dot_split(w, spread), dot_split(exp_s, spread)
        state, grad = states[q], dend[q]
        state_low, grad_low = state.astype(BF16), grad.astype(BF16)
        carried = s_all * dot(c, state_low)
        ds = dot_split(dyf * carried, spread, NT)
        d_c = dot((dyf * s_all).astype(BF16), state_low, NT)
        d_w = dot(b, grad_low)
        d_b = dot((xf * w_all).astype(BF16), grad_low, NT)
        dx = dpre[after, 0:inner] + dyf * skip + d_w * w_all
        dsw = dot_split(d_w * xf, spread, NT)
        end = dsw * w
        ds = ds + flow_in[tok, :] - end
        held = dot_split(jnp.broadcast_to(jnp.sum(grad * state, axis=0, keepdims=True), (8, inner)), spread, NT)[0:1]
        last = jnp.sum(end, axis=0, keepdims=True) + held * exp_s[SPAN - 1 : SPAN]
        ds = ds + jnp.where(iota((SPAN, 128), 0) == SPAN - 1, last, 0.0)
        da = dot_exact(up_tri, ds)
        d_dt = sum_in[tok, :] + dsw * to_end + da * rate
        d_raw = d_dt * sigmoid(dtraw[tok, :].astype(F32) + bias)
        d_raw = jnp.where(iota((SPAN, 128), 1) < inner // HEADDIM, d_raw, 0.0)
        row_out[7:8, 0:128] += jnp.sum(da * (dt * rate), axis=0, keepdims=True)
        row_out[8:9, 0:128] += jnp.sum(d_raw, axis=0, keepdims=True)
        d_low = d_raw.astype(BF16)
        cat_out[after, cols.dt] = d_low

        win_x = xin[window, :].astype(F32)
        d_x = dx * silu_slope(conv_taps(win_x, rowp))
        dpre[after, 0:inner] = d_x
        for j in range(CONV):
            row_out[j : j + 1] += jnp.sum(d_x * win_x[EDGE - 3 + j : EDGE - 3 + j + SPAN], axis=0, keepdims=True)
        row_out[CONV : CONV + 1] += jnp.sum(d_x, axis=0, keepdims=True)
        win_bc = bcin[window, :].astype(F32)
        d_bc = dpre[after, inner:] + jnp.concatenate([d_b, d_c], axis=1)
        d_bc = d_bc * silu_slope(conv_taps(win_bc, bcp))
        dpre[after, inner:] = d_bc
        for j in range(CONV):
            bcrow_out[j : j + 1] += jnp.sum(d_bc * win_bc[EDGE - 3 + j : EDGE - 3 + j + SPAN], axis=0, keepdims=True)
        bcrow_out[CONV : CONV + 1] += jnp.sum(d_bc, axis=0, keepdims=True)
        return 0

    lax.fori_loop(0, spans, block, 0)

    def back(window, taps, rows):
        total = None
        for j in range(CONV):
            term = taps[j : j + 1] * window[CONV - 1 - j : CONV - 1 - j + rows]
            total = term if total is None else total + term
        return total.astype(BF16)

    cat_out[0:EDGE, cols.x] = back(dpre[0 : 2 * EDGE, 0:inner], rowp, EDGE)
    cat_out[0:EDGE, cols.bc] = back(dpre[0 : 2 * EDGE, inner:], bcp, EDGE)

    def conv_block(q, _):
        after = pl.ds(pl.multiple_of(q * SPAN + EDGE, EDGE), SPAN)
        window = pl.ds(pl.multiple_of(q * SPAN + EDGE, EDGE), SPAN + EDGE)
        cat_out[after, cols.x] = back(dpre[window, 0:inner], rowp, SPAN)
        cat_out[after, cols.bc] = back(dpre[window, inner:], bcp, SPAN)
        return 0

    lax.fori_loop(0, spans, conv_block, 0)


def project_back_edge(cat, w, dn_out):
    cols = columns_of((w.shape[1] - 3 * STATE) // 2)
    dn_out[0:EDGE] = (
        dot(cat[0:EDGE, cols.x], w[:, cols.x], NT) + dot(cat[0:EDGE, cols.bc], w[:, cols.bc], NT)
    ).astype(BF16)


def project_back(q, cat, w, dn_out):
    after = pl.ds(pl.multiple_of(q * SPAN + EDGE, EDGE), SPAN)
    dn_out[after, :] = dot(cat[after, :], w[...], NT).astype(BF16)


def for_row_blocks(grad, body):
    groups, rows = grad

    def one(g, _):
        body(pl.ds(pl.multiple_of(g * rows, 128), rows) if rows % 128 == 0 else pl.ds(g * rows, rows), g)
        return 0

    if rows % 128 == 0:
        lax.fori_loop(0, groups, one, 0)
    else:
        for g in range(groups):
            one(g, 0)


def x_gradient(cat, normed, gx_out):
    cols = columns_of(gx_out.shape[1])

    def body(at, _):
        total = dot(normed[EDGE:, at], cat[EDGE:, cols.x], TN) + dot(normed[0:EDGE, at], cat[0:EDGE, cols.x], TN)
        gx_out[at, :] = total.astype(BF16)

    for_row_blocks((normed.shape[1] // SPAN, SPAN), body)


def z_gradient(cat, normed, gz_out):
    cols = columns_of(gz_out.shape[1])

    def body(at, _):
        gz_out[at, :] = dot(normed[EDGE:, at], cat[EDGE:, cols.z], TN).astype(BF16)

    for_row_blocks((normed.shape[1] // SPAN, SPAN), body)


def small_gradients(cat, normed, gbc_out, gdt_out):
    groups, parts, shard, _ = gbc_out.shape
    cols = columns_of((cat.shape[1] - 3 * STATE) // 2)

    def body(at, g):
        edge, tokens = normed[0:EDGE, at], normed[EDGE:, at]
        bc = dot(tokens, cat[EDGE:, cols.bc], TN) + dot(edge, cat[0:EDGE, cols.bc], TN)
        gbc_out[g] = bc.reshape(parts, shard, 2 * STATE).astype(BF16)
        gdt_out[g] = dot(cat[EDGE:, cols.dt], tokens, TN)[0:EDGE].astype(BF16)

    for_row_blocks((groups, parts * shard), body)


HALF = 128
MESH = pl.DeviceIdType.MESH


class Links:
    def __init__(self, sends, recvs):
        self.z, self.p, self.c = lax.axis_index("z"), lax.axis_index("p"), lax.axis_index("head")
        self.groups = lax.axis_size("z")
        self.sends, self.recvs, self.used = sends, recvs, 0

    def copy(self, src, dst, device):
        i = self.used
        self.used += 1
        return pltpu.make_async_remote_copy(
            src_ref=src, dst_ref=dst, send_sem=self.sends.at[i], recv_sem=self.recvs.at[i],
            device_id=device, device_id_type=MESH,
        )

    def local(self, src, dst):
        i = self.used
        self.used += 1
        return pltpu.make_async_copy(src, dst, self.sends.at[i])

    def at(self, k, e):
        return (self.z, lax.bitwise_xor(self.p, jnp.int32(k)), lax.bitwise_xor(self.c, jnp.int32(e)))

    def last_of_plane(self):
        return jnp.logical_and(self.p == GROUP - 1, self.c == 1)

    def greet(self, plane=False, sibling=False, groups=False, edge=0):
        barrier = pltpu.get_barrier_semaphore()
        z, count = self.z, self.groups
        above = z < count - 1

        def signal(device):
            pl.semaphore_signal(barrier, 1, device_id=device, device_id_type=MESH)

        self.expected = jnp.int32(0)
        for k in range(GROUP):
            for e in range(2):
                if (k or e) if plane else (sibling and e and not k):
                    signal(self.at(k, e))
                    self.expected = self.expected + 1
        if groups:
            for k in range(1, count):
                signal((lax.rem(z + k, count), self.p, self.c))
            self.expected = self.expected + (count - 1)
        sending = jnp.logical_and(self.last_of_plane(), above)
        if edge == 1:
            pl.when(z > 0)(lambda: signal((z - 1, jnp.int32(GROUP - 1), jnp.int32(1))))
            self.expected = self.expected + 2 * GROUP * sending.astype(jnp.int32)
        if edge == -1:

            @pl.when(sending)
            def _():
                for p in range(GROUP):
                    for c in range(2):
                        signal((z + 1, jnp.int32(p), jnp.int32(c)))

            self.expected = self.expected + (z > 0).astype(jnp.int32)

    def meet(self):
        pl.semaphore_wait(pltpu.get_barrier_semaphore(), self.expected)

    def start_barrier(self, **who):
        self.greet(**who)
        self.meet()


class Chain:
    def __init__(self, links, pieces):
        z, p, c, groups = links.z, links.p, links.c, links.groups
        self.steps, self.now = [], 0
        for step in range(1, groups):
            found = []
            up, down = z - step + 1, z + step - 1
            for piece in pieces:
                block = piece(jnp.maximum(up, 0))
                sending = jnp.logical_and(up >= 0, z < groups - 1)
                found.append((sending, z - step >= 0, links.copy(block, block, (z + 1, p, c))))
                block = piece(jnp.minimum(down, groups - 1))
                sending = jnp.logical_and(down < groups, z > 0)
                found.append((sending, z + step < groups, links.copy(block, block, (z - 1, p, c))))
            self.steps.append(found)

    def begin(self):
        for sending, _, copy in self.steps[0]:
            pl.when(sending)(copy.start)

    def advance(self):
        if self.now + 1 < len(self.steps):
            for (_, receiving, copy), (sending, _, later) in zip(self.steps[self.now], self.steps[self.now + 1]):
                pl.when(receiving)(copy.wait_recv)
                pl.when(sending)(later.start)
            self.now += 1

    def complete(self):
        while self.now + 1 < len(self.steps):
            self.advance()
        for _, receiving, copy in self.steps[-1]:
            pl.when(receiving)(copy.wait_recv)

    def finish(self):
        for found in self.steps:
            for sending, _, copy in found:
                pl.when(sending)(copy.wait_send)


class Swap:
    def __init__(self, links, shard, staging, out, lanes, width):
        self.links, self.staging, self.out, self.lanes = links, staging, out, lanes

        def source(k):
            to = lax.bitwise_xor(links.p, jnp.int32(k))
            if len(shard.shape) == 3:
                return shard.at[to]
            if shard.shape[1] == width:
                return shard
            return shard.at[:, pl.ds(pl.multiple_of(to * width, 128), width)]

        self.copies = [links.copy(source(k), staging.at[links.p], links.at(k, 0)) for k in (3, 1, 2)]
        self.keep = links.local(source(0), staging.at[links.p])

    def start(self):
        for copy in self.copies:
            copy.start()

    def settle(self):
        self.keep.wait()
        for copy in self.copies:
            copy.wait_recv()
        parts, shard, width = self.staging.shape
        rows = parts * shard
        first = self.links.z * rows if self.out.shape[0] > rows else 0
        if shard % EDGE == 0:
            for j in range(parts):
                self.out[pl.ds(pl.multiple_of(first + j * shard, EDGE), shard), self.lanes] = self.staging[j]
        else:
            block = self.staging[...].astype(F32).reshape(rows, width).astype(BF16)
            self.out[pl.ds(pl.multiple_of(first, EDGE), rows), self.lanes] = block

    def finish(self):
        for copy in self.copies:
            copy.wait_send()


class Halve:
    def __init__(self, links, grad, arrived, sums):
        self.links, self.grad, self.arrived, self.sums = links, grad, arrived, sums
        z, groups = links.z, links.groups
        self.rows, self.steps, self.now = grad.shape[0] // groups, [], 0
        first, bit = 0, 1
        while bit < groups:
            low = lax.rem(z, bit)
            mine = lax.rem(lax.div(z, bit), 2)
            device = (z + bit - 2 * bit * mine, links.p, links.c)
            found = []
            for j in range(groups // (2 * bit)):
                away = j * 2 * bit + (1 - mine) * bit + low
                kept = j * 2 * bit + mine * bit + low
                copy = links.copy(self.held(away), arrived.at[first + j], device)
                found.append((first + j, self.held(kept), copy))
            self.steps.append(found)
            self.before = (first, 2 * bit)
            first, bit = first + groups // (2 * bit), 2 * bit

    def held(self, target):
        if not self.steps:
            return self.grad.at[pl.ds(pl.multiple_of(target * self.rows, EDGE), self.rows), :]
        first, size = self.before
        return self.arrived.at[first + lax.div(target, size)]

    def begin(self):
        for _, _, copy in self.steps[0]:
            copy.start()

    def advance(self):
        for slot, held, copy in self.steps[self.now]:
            copy.wait_recv()

            def add(i, _, slot=slot, held=held):
                at = pl.ds(pl.multiple_of(i * 32, 32), 32)
                total = self.arrived[slot, at, :].astype(F32) + held[at, :].astype(F32)
                self.arrived[slot, at, :] = total.astype(BF16)
                return 0

            lax.fori_loop(0, self.rows // 32, add, 0)
        self.now += 1
        for _, _, copy in self.steps[self.now]:
            copy.start()

    def complete(self):
        while self.now + 1 < len(self.steps):
            self.advance()
        ((slot, held, copy),) = self.steps[-1]
        copy.wait_recv()
        total = self.arrived[slot].astype(F32) + held[...].astype(F32)
        shard = self.sums.shape[1]
        for j in range(GROUP):
            self.sums[j] = total[j * shard : (j + 1) * shard].astype(BF16)

    def finish(self):
        for found in self.steps:
            for _, _, copy in found:
                copy.wait_send()


class Deliver:
    def __init__(self, links, sums, out):
        self.links, self.sums, self.out = links, sums, out
        inner = sums.shape[2]
        self.mine = pl.ds(pl.multiple_of(links.p * inner, 128), inner)
        self.copies = [
            links.copy(sums.at[lax.bitwise_xor(links.p, jnp.int32(k))], out.at[:, self.mine], links.at(k, 0))
            for k in (3, 1, 2)
        ]

    def start(self):
        for copy in self.copies:
            copy.start()
        self.out[:, self.mine] = self.sums[self.links.p]

    def arrive(self):
        for copy in self.copies:
            copy.wait_recv()

    def finish(self):
        for copy in self.copies:
            copy.wait_send()


class States:
    def __init__(self, links, backward, state, decay, states, decays):
        z, groups = links.z, links.groups
        self.links, self.refs = links, (state, decay, states, decays)
        self.found = []
        for k in range(1, groups):
            to, source = (z - k, z + k) if backward else (z + k, z - k)
            sending, receiving = (to >= 0, source < groups) if backward else (to < groups, source >= 0)
            device = (jnp.clip(to, 0, groups - 1), links.p, links.c)
            pair = [links.copy(state, states.at[z], device), links.copy(decay, decays.at[z], device)]
            self.found.append((sending, receiving, pair))

    def start(self):
        for sending, _, pair in self.found:

            @pl.when(sending)
            def _(pair=pair):
                for copy in pair:
                    copy.start()

    def arrive(self):
        for _, receiving, pair in self.found:

            @pl.when(receiving)
            def _(pair=pair):
                for copy in pair:
                    copy.wait_recv()

    def finish(self):
        for sending, _, pair in self.found:

            @pl.when(sending)
            def _(pair=pair):
                for copy in pair:
                    copy.wait_send()


class Gather:
    def __init__(self, links, out, base):
        self.links, self.out, self.base = links, out, base

        def place(k, half=None):
            row = base + lax.bitwise_xor(links.p, jnp.int32(k)) * (2 * HALF) + links.c * HALF
            if half is None:
                return out.at[pl.ds(pl.multiple_of(row, EDGE), HALF), :]
            return out.at[pl.ds(pl.multiple_of(row + half * (HALF // 2), EDGE), HALF // 2), :]

        def send(k, half, to, e=0):
            return links.copy(place(k, half), place(k, half), links.at(to, e))

        self.near = {(to, half): send(0, half, to) for half in range(2) for to in (1, 2)}
        self.relays = {0: send(1, 0, 2), 1: send(2, 1, 1)}
        self.own_share = send(0, None, 0, 1)
        self.shares = {(k, half): send(k, half, 0, 1) for k in (1, 2, 3) for half in range(2)}

    def own(self, start, size):
        row = self.base + self.links.p * (2 * HALF) + self.links.c * HALF + start
        return pl.ds(pl.multiple_of(row, EDGE), size)

    def start(self):
        for which in ((1, 0), (2, 1), (1, 1), (2, 0)):
            self.near[which].start()
        self.own_share.start()

    def pass_on(self):
        for k, half in ((1, 0), (2, 1)):
            self.near[k, half].wait_recv()
            self.relays[half].start()
            self.shares[k, half].start()
        for k, half in ((1, 1), (2, 0)):
            self.near[k, half].wait_recv()
            self.shares[k, half].start()
        for half in range(2):
            self.relays[half].wait_recv()
            self.shares[3, half].start()

    def finish(self):
        shares = [self.own_share, *self.shares.values()]
        for copy in shares:
            copy.wait_recv()
        for copy in [*shares, *self.near.values(), *self.relays.values()]:
            copy.wait_send()


class EdgeForward:
    def __init__(self, links, gather):
        self.links = links
        tail = gather.out.at[gather.own(HALF - EDGE, EDGE), :]
        first = links.used
        links.used += 2 * GROUP + 1
        recv = links.recvs.at[first + 2 * GROUP]
        self.out = gather.out
        self.copies = [
            pltpu.make_async_remote_copy(
                src_ref=tail, dst_ref=gather.out.at[0:EDGE, :], send_sem=links.sends.at[first + p * 2 + c], recv_sem=recv,
                device_id=(links.z + 1, jnp.int32(p), jnp.int32(c)), device_id_type=MESH,
            )
            for p in range(GROUP)
            for c in range(2)
        ]
        self.sending = jnp.logical_and(links.last_of_plane(), links.z < links.groups - 1)

    def start(self):
        @pl.when(self.sending)
        def _():
            for copy in self.copies:
                copy.start()

        @pl.when(self.links.z == 0)
        def _():
            self.out[0:EDGE, :] = jnp.zeros((EDGE, self.out.shape[1]), self.out.dtype)

    def finish(self):
        pl.when(self.links.z > 0)(self.copies[0].wait_recv)

        @pl.when(self.sending)
        def _():
            for copy in self.copies:
                copy.wait_send()


class Scatter:
    def __init__(self, links, part, base, sib, total, peer, via):
        self.links, self.part, self.base = links, part, base
        self.sib, self.total, self.peer, self.via = sib, total, peer, via
        other = 1 - links.c
        self.to_sibling = {
            k: links.copy(part.at[self.rows(k, other, 0, HALF), :], sib.at[k], links.at(0, 1)) for k in (3, 1, 2, 0)
        }
        halves = [slice(0, HALF // 2), slice(HALF // 2, HALF)]
        self.across = [links.copy(total.at[2, halves[i]], via.at[i], links.at(i + 1, 0)) for i in range(2)]
        self.to_peer = {
            (k, i): links.copy(total.at[k - 1, halves[i]], peer.at[k - 1, halves[i]], links.at(k, 0))
            for k in (1, 2)
            for i in range(2)
        }

    def rows(self, k, c, start, size):
        row = self.base + lax.bitwise_xor(self.links.p, jnp.int32(k)) * (2 * HALF) + c * HALF + start
        return pl.ds(pl.multiple_of(row, EDGE), size)

    def pass_on(self, k):
        self.to_sibling[k].wait_recv()
        if k == 0:
            for i in (1, 0):
                self.across[i].wait_recv()

                def join(j, _, i=i):
                    at = pl.ds(pl.multiple_of(i * (HALF // 2) + j * 32, 32), 32)
                    came = self.via[i, pl.ds(pl.multiple_of(j * 32, 32), 32), :].astype(F32)
                    self.total[1 - i, at, :] = (self.total[1 - i, at, :].astype(F32) + came).astype(BF16)
                    return 0

                lax.fori_loop(0, HALF // 64, join, 0)
                self.to_peer[2 - i, i].start()
            return

        def add(i, _):
            at = pl.ds(pl.multiple_of(i * 32, 32), 32)
            mine = self.part[self.rows(k, self.links.c, i * 32, 32), :].astype(F32)
            self.total[k - 1, at, :] = (mine + self.sib[k, at, :].astype(F32)).astype(BF16)
            return 0

        lax.fori_loop(0, HALF // 32, add, 0)
        for copy in self.across if k == 3 else [self.to_peer[k, k - 1]]:
            copy.start()

    def arrive(self):
        for copy in self.to_peer.values():
            copy.wait_recv()

    def own(self, start, size):
        at = pl.ds(start, size)
        total = self.part[self.rows(0, self.links.c, start, size), :].astype(F32) + self.sib[0, at, :].astype(F32)
        for k in range(2):
            total = total + self.peer[k, at, :].astype(F32)
        return total

    def finish(self):
        for copy in [*self.to_sibling.values(), *self.across, *self.to_peer.values()]:
            copy.wait_send()


class SmallSum:
    def __init__(self, links, squares, slots):
        self.links, self.squares, self.slots = links, squares, slots
        self.copies = [
            links.copy(squares.at[:, self.lanes(k, e)], slots.at[2 * k + e - 1], links.at(k, e))
            for k in range(GROUP)
            for e in range(2)
            if k or e
        ]

    def lanes(self, k, e):
        links = self.links
        column = lax.bitwise_xor(links.p, jnp.int32(k)) * (2 * HALF) + lax.bitwise_xor(links.c, jnp.int32(e)) * HALF
        return pl.ds(pl.multiple_of(column, HALF), HALF)

    def start(self):
        for copy in self.copies:
            copy.start()

    def total(self):
        for copy in self.copies:
            copy.wait_recv()
        total = self.squares[:, self.lanes(0, 0)]
        for i in range(len(self.copies)):
            total = total + self.slots[i]
        return total

    def finish(self):
        for copy in self.copies:
            copy.wait_send()


class SmallGather:
    def __init__(self, links, out):
        self.out = out
        self.lanes = pl.ds(pl.multiple_of(links.p * (2 * HALF) + links.c * HALF, HALF), HALF)
        self.copies = [
            links.copy(out.at[:, self.lanes], out.at[:, self.lanes], links.at(k, e))
            for k in range(GROUP)
            for e in range(2)
            if k or e
        ]

    def start(self):
        for copy in self.copies:
            copy.start()

    def finish(self):
        for copy in self.copies:
            copy.wait()


def row_chunks(size=32):
    return [(start, size) for start in range(0, HALF, size)]


def rms_of(rows):
    return lax.rsqrt(jnp.mean(rows * rows, axis=-1, keepdims=True) + EPS)


def as_tile(columns):
    lane = iota((HALF, HALF), 1)
    wide = jnp.zeros((HALF, HALF), F32)
    for i, column in enumerate(columns):
        wide = jnp.where(lane == i, column, wide)
    return wide.T[0:8]


def grad_rows(links, scatter, edge_slots, grad, resid, gain, gain_out, start, size):
    at = slice(start, start + size)
    d_normed = scatter.own(start, size)
    if start + size == HALF:
        extra = edge_slots[0].astype(F32)
        for i in range(1, 2 * GROUP):
            extra = extra + edge_slots[i].astype(F32)
        used = jnp.logical_and(links.last_of_plane(), links.z < links.groups - 1)
        extra = jnp.where(used, extra, 0.0)
        d_normed = d_normed + jnp.concatenate([jnp.zeros((size - EDGE, extra.shape[1]), F32), extra])
    rows = resid[at]
    inv_rms = rms_of(rows)
    gain_sum = jnp.sum(d_normed * rows * inv_rms, axis=0, keepdims=True)
    gain_out[0:1] = gain_sum if start == 0 else gain_out[0:1] + gain_sum
    d_hidden = d_normed * gain[...]
    return (
        grad[at]
        + inv_rms * d_hidden
        - rows * (inv_rms * inv_rms * inv_rms * jnp.mean(d_hidden * rows, axis=-1, keepdims=True))
    )


class EdgeBackward:
    def __init__(self, links, part, slots):
        self.links = links
        first = links.used
        links.used += 2 * GROUP + 1
        me = links.p * 2 + links.c
        self.send = pltpu.make_async_remote_copy(
            src_ref=part.at[0:EDGE, :], dst_ref=slots.at[me], send_sem=links.sends.at[first], recv_sem=links.recvs.at[first + me],
            device_id=(links.z - 1, jnp.int32(GROUP - 1), jnp.int32(1)), device_id_type=MESH,
        )
        self.recvs = [
            pltpu.make_async_remote_copy(
                src_ref=part.at[0:EDGE, :], dst_ref=slots.at[i], send_sem=links.sends.at[first], recv_sem=links.recvs.at[first + i],
                device_id=(links.z, links.p, 1 - links.c), device_id_type=MESH,
            )
            for i in range(2 * GROUP)
        ]
        self.receiving = jnp.logical_and(links.last_of_plane(), links.z < links.groups - 1)

    def start(self):
        pl.when(self.links.z > 0)(self.send.start)

    def receive(self):
        @pl.when(self.receiving)
        def _():
            for copy in self.recvs:
                copy.wait_recv()

    def finish(self):
        pl.when(self.links.z > 0)(self.send.wait_send)


class BcSum:
    def __init__(self, links, bc, out, bufs):
        self.links, self.bc, self.out = links, bc, out
        self.sib, self.chip, self.peer, self.total, self.far = bufs
        p, c, groups = links.p, links.c, links.groups
        self.own = pl.ds(pl.multiple_of(c * STATE, STATE), STATE)
        other = pl.ds(pl.multiple_of((1 - c) * STATE, STATE), STATE)
        self.first = [links.copy(bc.at[:, :, :, other], self.sib, links.at(0, 1))]
        self.second = [
            links.copy(self.chip.at[:, lax.bitwise_xor(p, jnp.int32(k))], self.peer.at[k - 1], links.at(k, 0))
            for k in (3, 1, 2)
        ]
        self.third = []
        for k in range(1, groups):
            to = lax.rem(links.z + k, groups)
            self.third.append(links.copy(self.total.at[to], self.far.at[k - 1], (to, p, c)))
        self.fourth = [links.copy(out.at[:, self.own], out.at[:, self.own], links.at(0, 1))]

    @staticmethod
    def begin(copies):
        for copy in copies:
            copy.start()

    @staticmethod
    def arrive(copies):
        for copy in copies:
            copy.wait_recv()

    def cores(self):
        self.begin(self.first)

    def plane(self):
        self.arrive(self.first)

        def add(i, _):
            for q in range(GROUP):
                mine = self.bc[i, q, :, self.own].astype(F32)
                self.chip[i, q] = (mine + self.sib[i, q].astype(F32)).astype(BF16)
            return 0

        lax.fori_loop(0, self.links.groups, add, 0)
        self.begin(self.second)

    def groups(self):
        self.arrive(self.second)

        def add(i, _):
            total = self.chip[i, self.links.p].astype(F32)
            for k in range(GROUP - 1):
                total = total + self.peer[k, i].astype(F32)
            self.total[i] = total.astype(BF16)
            return 0

        lax.fori_loop(0, self.links.groups, add, 0)
        self.begin(self.third)

    def share(self):
        self.arrive(self.third)
        total = self.total[self.links.z].astype(F32)
        for k in range(self.links.groups - 1):
            total = total + self.far[k].astype(F32)
        self.out[:, self.own] = total.astype(BF16)
        self.begin(self.fourth)

    def finish(self):
        self.arrive(self.fourth)
        for copy in self.first + self.second + self.third + self.fourth:
            copy.wait_send()


class LaidOut:
    def __init__(self, links, dt, wide, dt_out, wide_out, dt_far, wide_far):
        self.links, self.refs = links, (dt, wide, dt_out, wide_out, dt_far, wide_far)
        z, p, c, groups = links.z, links.p, links.c, links.groups
        self.first, self.second = [], []
        for k in range(1, groups):
            to = lax.rem(z + k, groups)
            self.first.append(links.copy(dt.at[to], dt_far.at[k - 1], (to, p, c)))
            self.first.append(links.copy(wide, wide_far.at[k - 1], (to, p, c)))
        for k in range(1, GROUP):
            self.second.append(links.copy(dt_out.at[p], dt_out.at[p], links.at(k, 0)))
            self.second.append(links.copy(wide_out.at[p], wide_out.at[p], links.at(k, 0)))

    def groups(self):
        BcSum.begin(self.first)

    def plane(self):
        BcSum.arrive(self.first)
        dt, wide, dt_out, wide_out, dt_far, wide_far = self.refs
        dt_total, wide_total = dt[self.links.z].astype(F32), wide[...]
        for k in range(self.links.groups - 1):
            dt_total = dt_total + dt_far[k].astype(F32)
            wide_total = wide_total + wide_far[k]
        dt_out[self.links.p] = dt_total.astype(BF16)
        wide_out[self.links.p] = wide_total
        BcSum.begin(self.second)

    def finish(self):
        BcSum.arrive(self.second)
        for copy in self.first + self.second:
            copy.wait_send()


class VecSum:
    def __init__(self, links, vec, out, near, far):
        self.links, self.refs = links, (vec, out, near, far)
        z, p, c, groups = links.z, links.p, links.c, links.groups
        self.first, self.second, self.third = [], [], []
        for k in range(GROUP):
            for e in range(2):
                if k or e:
                    to = lax.bitwise_xor(p, jnp.int32(k)) * 2 + lax.bitwise_xor(c, jnp.int32(e))
                    self.first.append(links.copy(vec.at[to], near.at[2 * k + e - 1], links.at(k, e)))
                    self.third.append(links.copy(out.at[p * 2 + c], out.at[p * 2 + c], links.at(k, e)))
        for k in range(1, groups):
            self.second.append(links.copy(near.at[7], far.at[k - 1], (lax.rem(z + k, groups), p, c)))

    def plane(self):
        BcSum.begin(self.first)

    def groups(self):
        BcSum.arrive(self.first)
        vec, _, near, _ = self.refs
        total = vec[self.links.p * 2 + self.links.c]
        for slot in range(2 * GROUP - 1):
            total = total + near[slot]
        near[7] = total
        BcSum.begin(self.second)

    def back(self):
        BcSum.arrive(self.second)
        _, out, near, far = self.refs
        total = near[7]
        for k in range(self.links.groups - 1):
            total = total + far[k]
        out[self.links.p * 2 + self.links.c] = total
        BcSum.begin(self.third)

    def finish(self):
        BcSum.arrive(self.third)
        for copy in self.first + self.second + self.third:
            copy.wait_send()


class Refs:
    def __init__(self, refs, twins, sems):
        self.__dict__.update(refs)
        self.twins = {id(near): (far, near, sems.at[i]) for i, (far, near) in enumerate(twins)}
        self.waits = []

    def fetch(self, *refs):
        for ref in refs:
            far, near, sem = self.twins[id(ref)]
            pltpu.make_async_copy(far, near, sem).start()

    def need(self, *refs):
        for ref in refs:
            pltpu.make_async_copy(*self.twins[id(ref)]).wait()

    def flush(self, *refs):
        for ref in refs:
            far, near, sem = self.twins[id(ref)]
            self.waits.append(pltpu.make_async_copy(near, far, sem))
            self.waits[-1].start()

    def done(self):
        for copy in self.waits:
            copy.wait()


def weight_chain(links, w, steps, inner):
    rows, step_rows = w.shape[0] // links.groups, steps.shape[0] // links.groups
    cols = columns_of(inner)
    half = pl.ds(pl.multiple_of(cols.bc.start + links.c * STATE, STATE), STATE)

    def at(index):
        return pl.ds(pl.multiple_of(index * rows, EDGE), rows)

    pieces = [
        lambda i: w.at[at(i), cols.x],
        lambda i: w.at[at(i), cols.z],
        lambda i: w.at[at(i), half],
        lambda i: steps.at[pl.ds(pl.multiple_of(i * step_rows, EDGE), step_rows), :],
    ]
    return Chain(links, pieces), links.copy(w.at[:, half], w.at[:, half], links.at(0, 1))


def pack_steps(w_dt, steps_out, wide):
    heads_core, shard = w_dt.shape
    heads = heads_core // GROUP
    wide[...] = jnp.zeros_like(wide)
    wide[0:heads_core, 0:shard] = w_dt
    row, col = iota((EDGE, 128), 0), iota((EDGE, 128), 1)
    for q in range(GROUP):
        pick = jnp.logical_and(col == q * heads + row, row < heads).astype(BF16)
        steps_out[q] = dot(pick, wide[...]).astype(BF16)


def unpack_steps(steps, w, shard, inner):
    lanes = columns_of(inner).dt
    rows = GROUP * shard
    blank = jnp.zeros((128 - EDGE, 128), F32)

    def block(g, _):
        parts = []
        for j in range(GROUP):
            at = pl.ds(pl.multiple_of(g * (GROUP * EDGE) + j * EDGE, EDGE), EDGE)
            parts.append(jnp.concatenate([steps[at, :].astype(F32), blank]).T[0:shard])
        w[pl.ds(pl.multiple_of(g * rows, EDGE), rows), lanes] = jnp.concatenate(parts).astype(BF16)
        return 0

    lax.fori_loop(0, w.shape[0] // rows, block, 0)


def prepare(links, r, layer):
    inner = r.rowp.shape[1]
    heads_core = r.head_params.shape[2]
    lanes = pl.ds(pl.multiple_of(links.p * inner, 128), inner)
    r.gains[...] = r.norm_gain[...].astype(F32)
    r.headp[...] = jnp.zeros_like(r.headp)
    for i in range(3):
        r.headp[i : i + 1, 0:heads_core] = r.head_params[i, layer : layer + 1, :]
    mine = dot_exact(r.headp[...], head_pick(links.p, inner // HEADDIM).astype(F32))
    r.headp[...] = mine
    r.rowp[...] = jnp.zeros_like(r.rowp)
    r.rowp[0 : CONV + 1] = r.conv_x[:, :, lanes].astype(F32)[:, layer]
    r.rowp[5:6] = r.gated_gain[:, lanes].astype(F32)[layer : layer + 1]
    r.rowp[6:7] = dot_exact(mine, head_spread(inner).astype(F32))[2:3]
    r.bcp[...] = jnp.zeros_like(r.bcp)
    r.bcp[0 : CONV + 1] = r.conv_bc[...].astype(F32)[:, layer]


def out_chain(links, wo):
    rows = wo.shape[0] // links.groups
    return Chain(links, [lambda i: wo.at[pl.ds(pl.multiple_of(i * rows, EDGE), rows), :]])


def weight_swaps(links, r, layer, w, steps, wo):
    inner = wo.shape[1]
    cols = columns_of(inner)
    stagings = r.stagings[layer]
    here = pl.ds(pl.multiple_of(links.c * STATE, STATE), STATE)
    half = pl.ds(pl.multiple_of(cols.bc.start + links.c * STATE, STATE), STATE)
    swaps = [
        Swap(links, r.w_zx.at[layer, 1], stagings[0], w, cols.x, inner),
        Swap(links, r.w_zx.at[layer, 0], stagings[1], w, cols.z, inner),
        Swap(links, r.w_bc.at[layer, :, here], stagings[2], w, half, STATE),
        Swap(links, r.packed_steps.at[layer], stagings[3], steps, slice(0, 128), 128),
    ]
    return swaps, Swap(links, r.w_out.at[layer], stagings[4], wo, slice(0, inner), inner)


def scatter_blocks(scatter, compute):
    before = None
    for k in (3, 1, 2, 0):
        compute(lax.bitwise_xor(scatter.links.p, jnp.int32(k)))
        scatter.to_sibling[k].start()
        if before is not None:
            scatter.pass_on(before)
        before = k


def forward_layer(links, r, normed, w, wo, wo_chain, scatter, meanwhile):
    carried = States(links, False, r.state_low, r.decay_row, r.states_in, r.decays_in)
    state_sum, decay_all = project_and_convolve(
        normed, w, r.rowp, r.bcp, r.headp, r.z, r.xin, r.bcin, r.x, r.bc, r.dtraw, r.dt, r.s, r.decay, r.ext, r.local,
        lambda q: pl.when(q == 3)(wo_chain.advance),
    )
    r.state_low[...] = state_sum.astype(BF16)
    r.decay_row[...] = jnp.broadcast_to(decay_all, r.decay_row.shape)
    carried.start()
    r.flush(r.z, r.xin, r.bcin, r.x, r.bc, r.dtraw, r.dt, r.s, r.decay)
    wo_chain.advance()
    mix_within_spans(r.x, r.bc, r.s, r.dt, r.y)
    meanwhile()
    wo_chain.complete()
    r.flush(r.wo)
    carried.arrive()
    chain_states(entering_state(links.z, links.groups, r.states_in, r.decays_in, False), r.local, r.decay, r.states)
    scatter_blocks(
        scatter, lambda q: mix_out(q, r.states, r.x, r.bc, r.z, r.s, wo, r.rowp, r.y, r.part, r.squares)
    )
    r.flush(r.y, r.states)
    return carried


def first_kernel(inner_all, r):
    links = Links(r.sends, r.recvs)
    c = links.c
    inner = r.wo.shape[1]
    shard = r.w_dt.shape[2]
    links.greet(plane=True, groups=True, edge=1)
    for layer in range(2):
        pack_steps(r.w_dt[layer], r.packed_steps.at[layer], r.wide_steps)
    swaps, swap_o = weight_swaps(links, r, 0, r.w, r.dt_rows, r.wo)
    next_swaps, next_o = weight_swaps(links, r, 1, r.next_w, r.next_dt_rows, r.next_wo)
    all_swaps = swaps + [swap_o] + next_swaps + [next_o]
    gather, other = Gather(links, r.normed, EDGE), Gather(links, r.dmix, 0)
    edge = EdgeForward(links, gather)
    chain, share = weight_chain(links, r.w, r.dt_rows, inner)
    chain_o = out_chain(links, r.wo)
    next_chain, next_share = weight_chain(links, r.next_w, r.next_dt_rows, inner)
    scatter = Scatter(links, r.part, 0, r.sib, r.total, r.peer, r.via)
    small = SmallSum(links, r.squares, r.slots)
    next_gather = Gather(links, r.next_normed, EDGE)
    next_edge = EdgeForward(links, next_gather)

    prepare(links, r, 0)
    for swap in all_swaps:
        swap.keep.start()
    for start, size in row_chunks():
        at = pl.ds(pl.multiple_of(c * HALF + start, EDGE), size)
        rows_in = r.resid[at, :].astype(F32)
        r.resid_out[start : start + size] = rows_in
        r.normed[gather.own(start, size), :] = (rows_in * rms_of(rows_in) * r.gains[0:1]).astype(BF16)
        rows_in = r.cot[at, :]
        r.cot_out[start : start + size] = rows_in.astype(F32)
        r.dmix[other.own(start, size), :] = rows_in
    links.meet()
    for swap in swaps:
        swap.start()
    for swap in swaps:
        swap.settle()
    chain.begin()
    gather.start()
    edge.start()
    swap_o.start()
    chain.advance()
    gather.pass_on()
    for swap in next_swaps + [next_o]:
        swap.start()
    chain.advance()
    swap_o.settle()
    gather.finish()
    edge.finish()
    chain.complete()
    share.start()
    chain_o.begin()
    other.start()
    unpack_steps(r.dt_rows, r.w, shard, inner)
    r.flush(r.normed)
    share.wait()
    r.flush(r.w)

    def meanwhile():
        for swap in next_swaps + [next_o]:
            swap.settle()
        next_chain.begin()
        other.pass_on()

    carried = forward_layer(links, r, r.normed, r.w, r.wo, chain_o, scatter, meanwhile)
    small.start()
    scatter.pass_on(0)
    next_chain.advance()
    scatter.arrive()
    inv = lax.rsqrt(small.total() * (1.0 / inner_all) + EPS)
    r.inv_out[...] = inv
    column = inv.T[:, 0:1]
    for start, size in row_chunks():
        at = slice(start, start + size)
        mixed = scatter.own(start, size)
        r.mixed_out[at] = mixed
        fresh = r.resid_out[at] + column[at] * mixed
        r.fresh_out[at] = fresh
        r.next_normed[next_gather.own(start, size), :] = (fresh * rms_of(fresh) * r.gains[1:2]).astype(BF16)
    next_gather.start()
    next_edge.start()
    other.finish()
    r.flush(r.dmix)
    next_chain.advance()
    next_gather.pass_on()
    next_chain.complete()
    next_share.start()
    unpack_steps(r.next_dt_rows, r.next_w, shard, inner)
    scatter.finish()
    small.finish()
    next_gather.finish()
    next_edge.finish()
    carried.finish()
    for swap in all_swaps:
        swap.finish()
    for one in (chain, chain_o, next_chain):
        one.finish()
    next_share.wait()
    r.done()


def second_kernel(inner_all, r):
    links = Links(r.sends, r.recvs)
    r.fetch(r.normed, r.w)
    rows = r.wo_own.shape[0]
    keep = links.local(r.wo_own, r.wo.at[pl.ds(pl.multiple_of(links.z * rows, EDGE), rows), :])
    chain_o = out_chain(links, r.wo)
    scatter = Scatter(links, r.part, 0, r.sib, r.total, r.peer, r.via)
    small = SmallSum(links, r.squares, r.slots)
    spread = SmallGather(links, r.scalars_out)
    at = pl.ds(pl.multiple_of(links.c * HALF, HALF), HALF)
    share = links.copy(r.block_out.at[at, :], r.block_out.at[at, :], links.at(0, 1))
    keep.start()
    links.greet(plane=True, groups=True)
    prepare(links, r, 1)
    keep.wait()
    links.meet()
    chain_o.begin()
    r.need(r.normed, r.w)
    carried = forward_layer(links, r, r.normed, r.w, r.wo, chain_o, scatter, lambda: None)
    small.start()
    scatter.pass_on(0)
    scatter.arrive()
    inv = lax.rsqrt(small.total() * (1.0 / inner_all) + EPS)
    column = inv.T[:, 0:1]
    dots = []
    for start, size in row_chunks():
        at = slice(start, start + size)
        mixed = scatter.own(start, size)
        dots.append(jnp.sum(r.cot[at] * mixed, axis=-1, keepdims=True))
        r.block_out[pl.ds(pl.multiple_of(links.c * HALF + start, EDGE), size), :] = (
            r.resid[at] + column[at] * mixed
        ).astype(BF16)
    r.scalars_out[:, spread.lanes] = as_tile([column, jnp.concatenate(dots)])
    spread.start()
    share.start()
    scatter.finish()
    small.finish()
    carried.finish()
    chain_o.finish()
    spread.finish()
    share.wait()
    r.done()


def backward_layer(links, inner_all, r, at_start, before_collect, at_middle):
    carried = States(links, True, r.state_low, r.decay_row, r.states_in, r.decays_in)
    collect = Halve(links, r.gwo, r.go_in, r.go_sum)
    grad_sum, decay_all = back_through_gate(
        inner_all, r.dmix, r.wo, r.y, r.z, r.x, r.bc, r.s, r.decay, r.scalars, r.rowp,
        r.cat, r.wide, r.dy, r.prior, r.normed_out,
    )
    r.state_low[...] = grad_sum.astype(BF16)
    r.decay_row[...] = jnp.broadcast_to(decay_all, r.decay_row.shape)
    links.meet()
    carried.start()
    at_start()
    out_gradient(r.dmix, r.normed_out, r.gwo)
    before_collect()
    collect.begin()
    r.need(r.dt)
    back_within_spans(r.dy, r.x, r.bc, r.s, r.dt, r.dpre, r.flow, r.sums)
    at_middle()
    carried.arrive()
    grad = entering_state(links.z, links.groups, r.states_in, r.decays_in, True)
    r.need(r.states, r.dtraw, r.xin, r.bcin)
    back_through_states(
        grad, r.prior, r.decay, r.states, r.dy, r.x, r.bc, r.s, r.dt, r.dtraw, r.xin, r.bcin, r.rowp, r.bcp, r.headp,
        r.flow, r.sums, r.cat, r.wide, r.bc_rows, r.dpre, r.prior,
        lambda q: pl.when(q == 2)(collect.advance),
    )
    return carried, collect


def put_vector(vec, row, values):
    for i in range(values.shape[0]):
        for j in range(values.shape[1] // 128):
            vec[row // 8, row % 8 : row % 8 + 1, :] = values[i : i + 1, j * 128 : j * 128 + 128]
            row += 1


def third_kernel(inner_all, r):
    links = Links(r.sends, r.recvs)
    r.fetch(r.dt, r.states, r.dtraw, r.xin, r.bcin, r.w, r.normed, r.grad, r.resid, r.mixed)
    scatter = Scatter(links, r.part, EDGE, r.sib, r.total, r.peer, r.via)
    edge = EdgeBackward(links, r.part, r.edge_slots)
    gather = Gather(links, r.dmix_out, 0)
    spread = SmallGather(links, r.scalars_out)
    collects = [Halve(links, r.gx, r.gx_in, r.gx_sum), Halve(links, r.gwo, r.gz_in, r.gz_sum)]
    r.edge_slots[...] = jnp.zeros_like(r.edge_slots)
    links.greet(plane=True, groups=True, edge=-1)
    prepare(links, r, 1)
    carried, collect = backward_layer(links, inner_all, r, lambda: None, lambda: None, lambda: None)
    r.need(r.w, r.normed)
    x_gradient(r.cat, r.normed, r.gx)
    collects[0].begin()
    project_back_edge(r.cat, r.w, r.part)
    edge.start()
    scatter_blocks(scatter, lambda q: project_back(q, r.cat, r.w, r.part))
    scatter.pass_on(0)
    small_gradients(r.cat, r.normed, r.gbc, r.gdt)
    collect.complete()
    collect.finish()
    z_gradient(r.cat, r.normed, r.gwo)
    collects[1].begin()
    collects[0].advance()
    scatter.arrive()
    edge.receive()
    r.need(r.grad, r.resid, r.mixed)
    r.gain_row[...] = jnp.zeros_like(r.gain_row)
    dots = []
    for start, size in row_chunks():
        at = slice(start, start + size)
        fresh = grad_rows(links, scatter, r.edge_slots, r.grad, r.resid, r.gains[1:2], r.gain_row, start, size)
        r.grad_out[at] = fresh
        low = fresh.astype(BF16)
        r.dmix_out[gather.own(start, size), :] = low
        dots.append(jnp.sum(low.astype(F32) * r.mixed[at], axis=-1, keepdims=True))
    r.scalars_out[:, spread.lanes] = as_tile([r.inv[...].T[:, 0:1], jnp.concatenate(dots)])
    gather.start()
    spread.start()
    r.vec[...] = jnp.zeros_like(r.vec)
    model = r.gain_row.shape[1]
    put_vector(r.vec, model // 128, r.gain_row[0:1])
    put_vector(r.vec, 2 * (model // 128) + 2 * (CONV + 1), r.bc_rows[0 : CONV + 1])
    collects[1].advance()
    gather.pass_on()
    collects[0].complete()
    scatter.finish()
    edge.finish()
    gather.finish()
    spread.finish()
    carried.finish()
    collects[1].complete()
    for one in collects:
        one.finish()


def fourth_kernel(inner_all, r):
    links = Links(r.sends, r.recvs)
    r.fetch(r.dt, r.states, r.dtraw, r.xin, r.bcin, r.above_bc, r.above_x, r.above_z, r.above_o, r.normed, r.w, r.grad, r.resid)
    scatter = Scatter(links, r.part, EDGE, r.sib, r.total, r.peer, r.via)
    edge = EdgeBackward(links, r.part, r.edge_slots)
    at = pl.ds(pl.multiple_of(links.c * HALF, HALF), HALF)
    share = links.copy(r.out.at[at, :], r.out.at[at, :], links.at(0, 1))
    collects = [Halve(links, r.gx, r.gx_in, r.gx_sum), Halve(links, r.gwo, r.gz_in, r.gz_sum)]
    above = ((r.above_x, r.g_zx.at[1, 1]), (r.above_z, r.g_zx.at[1, 0]), (r.above_o, r.g_out.at[1]))
    own = ((r.go_sum, r.g_out.at[0]), (r.gx_sum, r.g_zx.at[0, 1]), (r.gz_sum, r.g_zx.at[0, 0]))
    delivers = [Deliver(links, parts, out) for parts, out in above]
    own_delivers = [Deliver(links, parts, out) for parts, out in own]
    bc_sums = [
        BcSum(links, bc, r.bc_out.at[i], r.bc_bufs[i])
        for i, bc in enumerate((r.gbc, r.above_bc))
    ]
    laid = LaidOut(links, r.steps_all, r.wide_all, r.dt_out, r.wide_out, r.dt_far, r.wide_far)
    vec_sum = VecSum(links, r.vec, r.vec_out, r.vec_near, r.vec_far)
    r.edge_slots[...] = jnp.zeros_like(r.edge_slots)
    links.greet(plane=True, groups=True, edge=-1)
    prepare(links, r, 0)

    def at_start():
        r.need(r.above_bc)
        bc_sums[1].cores()

    def at_middle():
        bc_sums[1].groups()
        r.need(r.above_x, r.above_z, r.above_o)
        for deliver in delivers:
            deliver.start()

    carried, collect = backward_layer(links, inner_all, r, at_start, bc_sums[1].plane, at_middle)
    r.need(r.normed)
    small_gradients(r.cat, r.normed, r.gbc, r.gdt)
    bc_sums[0].cores()
    r.steps_all[:, 0:EDGE, :] = r.gdt[...]
    r.steps_all[:, EDGE:, :] = r.above_dt[...]
    r.wide_all[0:16] = r.wide[...]
    r.wide_all[16:32] = r.above_wide[...]
    laid.groups()
    x_gradient(r.cat, r.normed, r.gx)
    collects[0].begin()
    bc_sums[0].plane()
    r.need(r.w)
    project_back_edge(r.cat, r.w, r.part)
    edge.start()
    scatter_blocks(scatter, lambda q: project_back(q, r.cat, r.w, r.part))
    scatter.pass_on(0)
    bc_sums[0].groups()
    collect.complete()
    collect.finish()
    z_gradient(r.cat, r.normed, r.gwo)
    collects[1].begin()
    collects[0].advance()
    own_delivers[0].start()
    scatter.arrive()
    edge.receive()
    r.need(r.grad, r.resid)
    r.gain_row[...] = jnp.zeros_like(r.gain_row)
    for start, size in row_chunks():
        fresh = grad_rows(links, scatter, r.edge_slots, r.grad, r.resid, r.gains[0:1], r.gain_row, start, size)
        r.out[pl.ds(pl.multiple_of(links.c * HALF + start, EDGE), size), :] = fresh.astype(BF16)
    share.start()
    r.vec[...] = r.above_vec[...]
    put_vector(r.vec, 0, r.gain_row[0:1])
    put_vector(r.vec, 2 * (r.gain_row.shape[1] // 128), r.bc_rows[0 : CONV + 1])
    vec_sum.plane()
    vec_sum.groups()
    collects[1].advance()
    bc_sums[1].share()
    laid.plane()
    collects[0].complete()
    own_delivers[1].start()
    laid.finish()
    lay_out_heads(links, r)
    bc_sums[0].share()
    vec_sum.back()
    collects[1].complete()
    own_delivers[2].start()
    for one in bc_sums + [scatter, edge, carried] + collects:
        one.finish()
    vec_sum.finish()
    lay_out_vector(r)
    share.wait()
    for deliver in delivers + own_delivers:
        deliver.arrive()
        deliver.finish()


def lay_out_heads(links, r):
    inner = r.wide.shape[1]
    heads = inner // HEADDIM
    heads_core, shard = r.g_dt.shape[1:]
    spread = head_spread(inner).astype(F32)
    row, col = iota((128, 128), 0), iota((128, 128), 1)
    blank = jnp.zeros((128 - 2 * EDGE, r.dt_out.shape[2]), F32)
    steps = [jnp.zeros((shard, 128), F32) for _ in range(2)]
    tall = [jnp.zeros((8, 128), F32) for _ in range(2)]
    for q in range(GROUP):
        lanes = slice(q * inner, q * inner + inner)
        r.step_rows[...] = jnp.concatenate([r.dt_out[q].astype(F32), blank]).T
        mine = r.step_rows[pl.ds(pl.multiple_of(links.p * shard, 8), shard), :]
        gains, taps = [], []
        for layer in range(2):
            first, second = r.wide_out[q, 16 * layer : 16 * layer + 8], r.wide_out[q, 16 * layer + 8 : 16 * layer + 16]
            taps.append(first[0 : CONV + 1])
            gains.append(first[5:6])
            place = jnp.logical_and(row - EDGE * layer == col - q * heads, jnp.logical_and(row >= EDGE * layer, row < EDGE * layer + heads))
            steps[layer] = steps[layer] + dot_exact(mine, place.astype(F32))
            place = jnp.logical_and(row == col - q * heads, row < heads).astype(F32)
            skip = dot_exact(first, spread, NT)[6:7]
            rows = jnp.concatenate([first[7:8, 0:128], second[0:1, 0:128], skip, jnp.zeros((5, 128), F32)])
            tall[layer] = tall[layer] + dot_exact(rows, place)
        for j in range(CONV + 1):
            r.g_conv_x[j, :, lanes] = jnp.concatenate([tap[j : j + 1] for tap in taps]).astype(BF16)
        r.g_gain[:, lanes] = jnp.concatenate(gains).astype(BF16)
    for layer in range(2):
        r.g_dt[layer] = steps[layer].T[0:heads_core].astype(BF16)
    for i in range(3):
        r.g_head[i] = jnp.concatenate([one[i : i + 1, 0:heads_core] for one in tall]).astype(BF16)


def lay_out_vector(r):
    def row(i):
        return r.vec_out[i // 8, i % 8 : i % 8 + 1, :]

    count = r.g_norm.shape[1] // 128
    for i in range(count):
        r.g_norm[:, i * 128 : i * 128 + 128] = jnp.concatenate([row(i), row(count + i)]).astype(BF16)
    for half in range(2):
        for j in range(CONV + 1):
            firsts = [2 * count + layer * 2 * (CONV + 1) + 2 * j + half for layer in range(2)]
            rows = jnp.concatenate([row(first) for first in firsts])
            r.g_conv_bc[j, :, half * 128 : half * 128 + 128] = rows.astype(BF16)


def flat(value):
    return [a for member in value for a in flat(member)] if isinstance(value, list) else [value]


def shaped(value, leaves):
    return [shaped(member, leaves) for member in value] if isinstance(value, list) else leaves.pop(0)


def call(body, collective, copies, outs, hbm_outs, ins, hbm_ins, scratch):
    vmem, hbm = pl.BlockSpec(memory_space=pltpu.VMEM), pl.BlockSpec(memory_space=pl.ANY)
    twins = {**{name: (a.shape, a.dtype) for name, a in hbm_ins.items()}, **hbm_outs}
    sides = [list(ins.values()), list(hbm_ins.values()), list(outs.values()), list(hbm_outs.values())]
    counts = [len(flat(side)) for side in sides]
    buffers = flat([list(scratch.values()), list(twins.values())])

    def kernel(*refs):
        refs = list(refs)
        groups = [shaped(side, refs) for side in sides]
        inner = shaped([list(scratch.values()), list(twins.values())], refs)
        sends, recvs, sems = refs
        near = dict(zip(twins, inner[1]))
        named = {**dict(zip(ins, groups[0])), **dict(zip(outs, groups[2])), **dict(zip(scratch, inner[0])), **near}
        body(Refs(dict(named, sends=sends, recvs=recvs), list(zip(groups[1] + groups[3], inner[1])), sems))

    results = pl.pallas_call(
        kernel,
        out_shape=tuple(jax.ShapeDtypeStruct(*a) for a in flat(sides[2:])),
        in_specs=[vmem] * counts[0] + [hbm] * counts[1],
        out_specs=tuple([vmem] * counts[2] + [hbm] * counts[3]),
        scratch_shapes=[pltpu.VMEM(*a) for a in buffers]
        + [pltpu.SemaphoreType.DMA((n,)) for n in (copies, copies, max(1, len(twins)))],
        compiler_params=pltpu.CompilerParams(
            vmem_limit_bytes=VMEM_BYTES, collective_id=collective, has_side_effects=True
        ),
    )(*flat(sides[:2]))
    found = shaped(sides[2:], list(results))
    return types.SimpleNamespace(**dict(zip(outs, found[0])), **dict(zip(hbm_outs, found[1])))


def on_device(resid_in, cotangent, norm_gain, w_zx, w_dt, w_bc, conv_x, conv_bc, head_params, gated_gain, w_out):
    layers, model = norm_gain.shape
    groups = lax.axis_size("z")
    shard = w_dt.shape[1]
    inner_core = conv_x.shape[2]
    inner = inner_core // GROUP
    heads_core = head_params.shape[2]
    inner_all = inner_core * lax.axis_size("head")
    length = resid_in.shape[1]
    tokens = GROUP * length
    spans = tokens // SPAN
    rows = GROUP * shard

    own_rows = ((HALF, model), F32)
    all_rows, edged_rows = ((tokens, model), BF16), ((tokens + EDGE, model), BF16)
    columns = columns_of(inner).size
    w_shape, wo_shape = ((model, columns), BF16), ((model, inner), BF16)
    scalars = ((8, tokens), F32)
    state_shape = ((spans, STATE, inner), F32)
    low_rows, steps_shape = ((tokens, inner), BF16), ((tokens, 128), F32)
    scatter_scratch = dict(
        sib=((GROUP, HALF, model), BF16),
        total=((GROUP - 1, HALF, model), BF16),
        peer=((2, HALF, model), BF16),
        via=((2, HALF // 2, model), BF16),
    )
    state_scratch = dict(
        state_low=((STATE, inner), BF16),
        decay_row=((8, inner), F32),
        states_in=((groups, STATE, inner), BF16),
        decays_in=((groups, 8, inner), F32),
    )
    saved_shapes = dict(
        y=((tokens, inner), F32),
        z=low_rows,
        x=low_rows,
        bc=((tokens, 2 * STATE), BF16),
        s=steps_shape,
        dt=steps_shape,
        dtraw=((tokens, 128), BF16),
        xin=((tokens + EDGE, inner), BF16),
        bcin=((tokens + EDGE, 2 * STATE), BF16),
        states=state_shape,
        decay=((spans, 8, inner), F32),
    )
    forward_scratch = dict(
        ext=((tokens + EDGE, inner + 2 * STATE), F32),
        local=state_shape,
        part=all_rows,
        squares=scalars,
        slots=((2 * GROUP - 1, 8, HALF), F32),
        **state_scratch,
        **scatter_scratch,
    )

    conv_x, conv_bc, head_params = [jnp.swapaxes(a, 0, 1) for a in (conv_x, conv_bc, head_params)]
    w_dt, w_out = jnp.swapaxes(w_dt, 1, 2), jnp.swapaxes(w_out, 1, 2)
    params = dict(
        norm_gain=norm_gain, conv_x=conv_x, conv_bc=conv_bc, head_params=head_params, gated_gain=gated_gain
    )
    param_scratch = dict(
        rowp=((8, inner), F32), bcp=((8, 2 * STATE), F32), headp=((8, 128), F32), gains=((layers, model), F32)
    )
    stagings = [((GROUP, rows_in, width), BF16) for rows_in, width in (
        (shard, inner), (shard, inner), (shard, STATE), (EDGE, 128), (shard, inner)
    )]
    step_rows = ((groups * GROUP * EDGE, 128), BF16)
    first = call(
        functools.partial(first_kernel, inner_all),
        0,
        200 + 14 * (groups - 1) + 2 * groups,
        dict(
            next_w=w_shape,
            next_wo=((rows, inner), BF16),
            next_normed=edged_rows,
            resid_out=own_rows,
            cot_out=own_rows,
            mixed_out=own_rows,
            fresh_out=own_rows,
            inv_out=((8, HALF), F32),
        ),
        dict(normed=edged_rows, dmix=all_rows, w=w_shape, wo=wo_shape, **saved_shapes),
        dict(
            resid=resid_in[0],
            cot=cotangent[0],
            w_zx=w_zx,
            w_dt=w_dt,
            w_bc=w_bc,
            w_out=w_out,
            **params,
        ),
        dict(),
        dict(
            **forward_scratch,
            **param_scratch,
            stagings=[stagings, stagings],
            dt_rows=step_rows,
            next_dt_rows=step_rows,
            packed_steps=((layers, GROUP, EDGE, 128), BF16),
            wide_steps=((128, 128), BF16),
        ),
    )
    second = call(
        functools.partial(second_kernel, inner_all),
        1,
        60 + 4 * groups,
        dict(block_out=((length, model), BF16), scalars_out=scalars),
        dict(wo=wo_shape, **saved_shapes),
        dict(
            wo_own=first.next_wo,
            **params,
            resid=first.fresh_out,
            cot=first.cot_out,
        ),
        dict(normed=first.next_normed, w=first.next_w),
        dict(**forward_scratch, **param_scratch),
    )
    grad_in = ((groups - 1, rows, inner), BF16)
    grad_sum = ((GROUP, shard, inner), BF16)
    bc_grad = ((groups, GROUP, shard, 2 * STATE), BF16)
    dt_grad = ((groups, EDGE, rows), BF16)
    wide_grad = ((16, inner), F32)
    vec_shape = ((2 * GROUP, 8, 128), F32)
    back_scratch = dict(
        dy=low_rows,
        gwo=wo_shape,
        normed_out=low_rows,
        prior=state_shape,
        dpre=((tokens + 2 * EDGE, inner + 2 * STATE), F32),
        flow=steps_shape,
        sums=steps_shape,
        cat=((tokens + EDGE, columns), BF16),
        bc_rows=((8, 2 * STATE), F32),
        part=edged_rows,
        gx=wo_shape,
        go_in=grad_in,
        gx_in=grad_in,
        gz_in=grad_in,
        gain_row=((8, model), F32),
        edge_slots=((2 * GROUP, EDGE, model), BF16),
        **state_scratch,
        **param_scratch,
        **scatter_scratch,
    )

    def at_once(run):
        return dict(y=run.y, z=run.z, x=run.x, bc=run.bc, s=run.s, decay=run.decay)

    def later(run):
        return dict(dt=run.dt, states=run.states, dtraw=run.dtraw, xin=run.xin, bcin=run.bcin)

    third = call(
        functools.partial(third_kernel, inner_all),
        2,
        60 + 6 * groups,
        dict(
            dmix_out=all_rows,
            scalars_out=scalars,
            grad_out=own_rows,
            go_sum=grad_sum,
            gx_sum=grad_sum,
            gz_sum=grad_sum,
            gbc=bc_grad,
            gdt=dt_grad,
            wide=wide_grad,
            vec=vec_shape,
        ),
        dict(),
        dict(
            dmix=first.dmix,
            scalars=second.scalars_out,
            wo=second.wo,
            **params,
            inv=first.inv_out,
            **at_once(second),
        ),
        dict(
            w=first.next_w,
            normed=first.next_normed,
            grad=first.cot_out,
            resid=first.fresh_out,
            mixed=first.mixed_out,
            **later(second),
        ),
        back_scratch,
    )
    far = groups - 1
    dt_shape, wide_shape = (layers * EDGE, rows), (layers * 16, inner)
    half_bc = (groups, GROUP, shard, STATE)
    bc_bufs = [
        (half_bc, BF16),
        (half_bc, BF16),
        ((GROUP - 1, groups, shard, STATE), BF16),
        ((groups, shard, STATE), BF16),
        ((far, shard, STATE), BF16),
    ]
    fourth = call(
        functools.partial(fourth_kernel, inner_all),
        3,
        130 + 14 * groups,
        dict(
            out=((length, model), BF16),
            bc_out=((layers, shard, 2 * STATE), BF16),
            g_norm=(norm_gain.shape, BF16),
            g_zx=(w_zx.shape, BF16),
            g_dt=(w_dt.shape, BF16),
            g_conv_x=(conv_x.shape, BF16),
            g_conv_bc=(conv_bc.shape, BF16),
            g_head=(head_params.shape, BF16),
            g_gain=(gated_gain.shape, BF16),
            g_out=(w_out.shape, BF16),
        ),
        dict(),
        dict(
            dmix=third.dmix_out,
            scalars=third.scalars_out,
            wo=first.wo,
            **params,
            above_dt=third.gdt,
            above_wide=third.wide,
            above_vec=third.vec,
            **at_once(first),
        ),
        dict(
            w=first.w,
            normed=first.normed,
            grad=third.grad_out,
            resid=first.resid_out,
            above_x=third.gx_sum,
            above_z=third.gz_sum,
            above_o=third.go_sum,
            above_bc=third.gbc,
            **later(first),
        ),
        dict(
            **back_scratch,
            vec_out=vec_shape,
            dt_out=((GROUP, *dt_shape), BF16),
            wide_out=((GROUP, *wide_shape), F32),
            step_rows=((rows, 128), F32),
            go_sum=grad_sum,
            gx_sum=grad_sum,
            gz_sum=grad_sum,
            gbc=bc_grad,
            gdt=dt_grad,
            wide=wide_grad,
            vec=vec_shape,
            steps_all=((groups, *dt_shape), BF16),
            wide_all=(wide_shape, F32),
            bc_bufs=[bc_bufs, bc_bufs],
            vec_near=vec_shape,
            vec_far=((far, 8, 128), F32),
            dt_far=((far, *dt_shape), BF16),
            wide_far=((far, *wide_shape), F32),
        ),
    )
    return (
        second.block_out[None],
        fourth.out[None],
        fourth.g_norm,
        fourth.g_zx,
        jnp.swapaxes(fourth.g_dt, 1, 2),
        fourth.bc_out,
        *[jnp.swapaxes(a, 0, 1) for a in (fourth.g_conv_x, fourth.g_conv_bc, fourth.g_head)],
        fourth.g_gain,
        jnp.swapaxes(fourth.g_out, 1, 2),
    )


def solution(mesh):
    seq, head = mesh.shape["seq"], mesh.shape["head"]
    split = Mesh(mesh.devices.reshape(seq // GROUP, GROUP, head), ("z", "p", "head"))
    seq_axes = ("z", "p")
    specs = (
        P(None, seq_axes, None),
        P(None, seq_axes, None),
        P(),
        P(None, None, seq_axes, "head"),
        P(None, seq_axes, "head"),
        P(None, seq_axes, None),
        P(None, None, "head"),
        P(),
        P(None, None, "head"),
        P(None, "head"),
        P(None, "head", seq_axes),
    )
    return jax.shard_map(on_device, mesh=split, in_specs=specs, out_specs=specs, check_vma=False)
```

```python
import functools
import types
import typing

import jax
import jax.numpy as jnp
from jax import lax
from jax.experimental import pallas as pl
from jax.experimental.pallas import tpu as pltpu
from jax.sharding import Mesh, PartitionSpec as P

HEADDIM = 64
STATE = 128
CONV = 4
SPAN = 256
GROUP = 4
EDGE = 16
EPS = 1e-05
HIGH = lax.Precision.HIGHEST
F32, BF16 = jnp.float32, jnp.bfloat16
NN = (((1,), (0,)), ((), ()))
NT = (((1,), (1,)), ((), ()))
TN = (((0,), (0,)), ((), ()))
VMEM_BYTES = 58 << 20


def dot(a, b, dims=NN):
    return lax.dot_general(a, b, dims, preferred_element_type=F32)


def dot_exact(a, b, dims=NN):
    return lax.dot_general(a, b, dims, precision=HIGH, preferred_element_type=F32)


def dot_split(a, b, dims=NN):
    high = a.astype(BF16)
    rest = (a - high.astype(F32)).astype(BF16)
    return dot(high, b, dims) + dot(rest, b, dims)


def sigmoid(v):
    return 1.0 / (1.0 + jnp.exp(-v))


def softplus(v):
    return jnp.maximum(v, 0.0) + jnp.log1p(jnp.exp(-jnp.abs(v)))


def silu_slope(v):
    sig = sigmoid(v)
    return sig * (1.0 + v * (1.0 - sig))


def iota(shape, dim):
    return lax.broadcasted_iota(jnp.int32, shape, dim)


def head_spread(inner):
    return (iota((128, inner), 0) == lax.shift_right_logical(iota((128, inner), 1), 6)).astype(BF16)


def triangle(lower):
    rows, cols = iota((SPAN, SPAN), 0), iota((SPAN, SPAN), 1)
    return ((cols <= rows) if lower else (cols >= rows)).astype(F32)


def half_masks():
    lane = iota((SPAN, 128), 1)
    return (lane < HEADDIM).astype(BF16), (lane >= HEADDIM).astype(BF16)


def conv_taps(window, taps):
    total = jnp.broadcast_to(taps[CONV : CONV + 1], (SPAN, window.shape[1]))
    for j in range(CONV):
        total = total + taps[j : j + 1] * window[EDGE - 3 + j : EDGE - 3 + j + SPAN]
    return total


def head_pick(place, heads):
    row, col = iota((128, 128), 0), iota((128, 128), 1)
    return jnp.logical_and(row == place * heads + col, col < heads).astype(BF16)


class Columns(typing.NamedTuple):
    x: slice
    z: slice
    dt: slice
    bc: slice
    size: int


def columns_of(inner):
    first = 2 * inner + 128
    return Columns(
        slice(0, inner), slice(inner, 2 * inner), slice(2 * inner, first), slice(first, first + 2 * STATE), first + 2 * STATE
    )


def project_and_convolve(
    normed, w, rowp, bcp, headp,
    z_out, xin_out, bcin_out, x_out, bc_out, dtraw_out, dt_out, s_out, decay_out,
    ext, local, at_block,
):
    inner = x_out.shape[1]
    spans = x_out.shape[0] // SPAN

    cols = columns_of(inner)
    edge = normed[0:EDGE]
    edge_x = dot(edge, w[:, cols.x]).astype(BF16)
    edge_bc = dot(edge, w[:, cols.bc]).astype(BF16)
    xin_out[0:EDGE] = edge_x
    bcin_out[0:EDGE] = edge_bc
    ext[0:EDGE, 0:inner] = edge_x.astype(F32)
    ext[0:EDGE, inner:] = edge_bc.astype(F32)
    spread = head_spread(inner)
    low_tri = triangle(True)
    rate = -jnp.exp(headp[0:1])
    bias = headp[1:2]

    def block(q, carry):
        state_sum, decay_all = carry
        at = pl.multiple_of(q * SPAN, SPAN)
        tok = pl.ds(at, SPAN)
        after = pl.ds(pl.multiple_of(at + EDGE, EDGE), SPAN)
        at_block(q)
        product = dot(normed[after, :], w[...]).astype(BF16)
        z_out[tok, :] = product[:, cols.z]
        xin, bcin = product[:, cols.x], product[:, cols.bc]
        dtraw = product[:, cols.dt]
        xin_out[after, :] = xin
        bcin_out[after, :] = bcin
        dtraw_out[tok, :] = dtraw
        ext[after, 0:inner] = xin.astype(F32)
        ext[after, inner:] = bcin.astype(F32)
        window = pl.ds(at, SPAN + EDGE)
        pre_x = conv_taps(ext[window, 0:inner], rowp)
        x = (pre_x * sigmoid(pre_x)).astype(BF16)
        x_out[tok, :] = x
        pre_bc = conv_taps(ext[window, inner:], bcp)
        bc = (pre_bc * sigmoid(pre_bc)).astype(BF16)
        bc_out[tok, :] = bc
        dt = softplus(dtraw.astype(F32) + bias)
        s = dot_exact(low_tri, dt * rate)
        dt_out[tok, :] = dt
        s_out[tok, :] = s
        to_end = jnp.exp(s[SPAN - 1 : SPAN] - s) * dt
        weighted = (x.astype(F32) * dot_split(to_end, spread)).astype(BF16)
        fresh = dot(bc[:, :STATE], weighted, TN)
        decay = dot_split(jnp.exp(s[SPAN - 8 : SPAN]), spread)[7:8]
        local[q] = fresh
        decay_out[q] = jnp.broadcast_to(decay, (8, inner))
        return state_sum * decay + fresh, decay_all * decay

    return lax.fori_loop(0, spans, block, (jnp.zeros((STATE, inner), F32), jnp.ones((1, inner), F32)))


def mix_within_spans(x_in, bc_in, s_in, dt_in, y_out):
    inner = x_in.shape[1]

    def block(q, _):
        tok = pl.ds(pl.multiple_of(q * SPAN, SPAN), SPAN)
        x, bc, s = x_in[tok, :], bc_in[tok, :], s_in[tok, :]
        s_row, dt_row = s.T, dt_in[tok, :].T
        cb = dot(bc[:, STATE:], bc[:, :STATE], NT)
        causal = iota((SPAN, SPAN), 1) <= iota((SPAN, SPAN), 0)
        masks = half_masks()
        for pair in range(inner // 128):
            lanes = slice(pair * 128, pair * 128 + 128)
            x_pair = x[:, lanes]
            total = None
            for e in range(2):
                h = pair * 2 + e
                gap = jnp.where(causal, s[:, h : h + 1] - s_row[h : h + 1, :], -1e30)
                scores = (cb * (jnp.exp(gap) * dt_row[h : h + 1, :])).astype(BF16)
                term = dot(scores, x_pair * masks[e])
                total = term if total is None else total + term
            y_out[tok, lanes] = total
        return 0

    lax.fori_loop(0, x_in.shape[0] // SPAN, block, 0)


def entering_state(place, count, sums, decays, backward):
    inner = sums.shape[2]
    state = jnp.zeros((STATE, inner), F32)
    for turn in range(count):
        other = count - 1 - turn if backward else turn
        ahead = (place < other) if backward else (other < place)
        state = jnp.where(ahead, decays[other, 0:1] * state + sums[other].astype(F32), state)
    return state


def chain_states(state, local, decay, states_out):
    def block(q, state):
        states_out[q] = state
        return decay[q, 0:1] * state + local[q]

    lax.fori_loop(0, local.shape[0], block, state)


def mix_out(q, states, x, bc, z, s, wo, rowp, y_out, part_out, sq_out):
    inner = x.shape[1]
    tok = pl.ds(pl.multiple_of(q * SPAN, SPAN), SPAN)
    carried = dot_split(jnp.exp(s[tok, :]), head_spread(inner)) * dot(bc[tok, STATE:], states[q].astype(BF16))
    y = y_out[tok, :] + carried + rowp[6:7] * x[tok, :].astype(F32)
    y_out[tok, :] = y
    zf = z[tok, :].astype(F32)
    gated = y * (zf * sigmoid(zf))
    sq_out[:, tok] = dot_exact(jnp.ones((8, inner), F32), gated * gated, NT)
    part_out[tok, :] = dot((gated * rowp[5:6]).astype(BF16), wo[...], NT).astype(BF16)


def back_through_gate(
    inner_all, dmix, wo, y_in, z, x, bc, s, decay, token_scalars, rowp, cat_out, wide, dy_out, prior, normed_out
):
    inner = x.shape[1]
    spans = x.shape[0] // SPAN
    spread = head_spread(inner)
    gain = rowp[5:6]
    cols = columns_of(inner)

    def block(i, carry):
        grad_sum, gain_sum, skip_sum = carry
        q = spans - 1 - i
        tok = pl.ds(pl.multiple_of(q * SPAN, SPAN), SPAN)
        columns = token_scalars[:, tok].T
        inv, total_dot = columns[:, 0:1], columns[:, 1:2]
        zf = z[tok, :].astype(F32)
        sig = sigmoid(zf)
        act = zf * sig
        y = y_in[tok, :]
        gated = y * act
        d_no = dot(dmix[tok, :], wo[...])
        scaled = gated * inv
        normed_out[tok, :] = (scaled * gain).astype(BF16)
        gain_sum = gain_sum + jnp.sum(d_no * scaled, axis=0, keepdims=True)
        d_gated = inv * (d_no * gain) - gated * (inv * inv * inv * total_dot * (1.0 / inner_all))
        after = pl.ds(pl.multiple_of(q * SPAN + EDGE, EDGE), SPAN)
        cat_out[after, cols.z] = (d_gated * y * (sig * (1.0 + zf * (1.0 - sig)))).astype(BF16)
        dy = d_gated * act
        xf = x[tok, :].astype(F32)
        skip_sum = skip_sum + jnp.sum(dy * xf, axis=0, keepdims=True)
        dy_low = dy.astype(BF16)
        dy_out[tok, :] = dy_low
        scaled_dy = (dy_low.astype(F32) * dot_split(jnp.exp(s[tok, :]), spread)).astype(BF16)
        fresh = dot(bc[tok, STATE:], scaled_dy, TN)
        prior[q] = fresh
        return fresh + decay[q, 0:1] * grad_sum, gain_sum, skip_sum

    zero = jnp.zeros((1, inner), F32)
    grad_sum, gain_sum, skip_sum = lax.fori_loop(
        0, spans, block, (jnp.zeros((STATE, inner), F32), zero, zero)
    )
    decay_all = decay[0, 0:1]
    for q in range(1, spans):
        decay_all = decay_all * decay[q, 0:1]
    wide[...] = jnp.zeros_like(wide)
    wide[5:6] = gain_sum
    wide[6:7] = skip_sum
    return grad_sum, decay_all


def out_gradient(dmix, normed_out, gwo_out):
    def rows_of(i, _):
        rows = pl.ds(pl.multiple_of(i * SPAN, SPAN), SPAN)
        gwo_out[rows, :] = dot(dmix[:, rows], normed_out[...], TN).astype(BF16)
        return 0

    lax.fori_loop(0, dmix.shape[1] // SPAN, rows_of, 0)


def back_within_spans(dy_in, x_in, bc_in, s_in, dt_in, dpre, flow_out, sum_out):
    inner = x_in.shape[1]

    def block(q, _):
        at = pl.multiple_of(q * SPAN, SPAN)
        tok = pl.ds(at, SPAN)
        after = pl.ds(pl.multiple_of(at + EDGE, EDGE), SPAN)
        x_low, dy = x_in[tok, :], dy_in[tok, :]
        b, c = bc_in[tok, :STATE], bc_in[tok, STATE:]
        s, dt = s_in[tok, :], dt_in[tok, :]
        s_row = s.T
        cb = dot(b, c, NT)
        seen = iota((SPAN, SPAN), 0) <= iota((SPAN, SPAN), 1)
        masks = half_masks()
        d_cb = jnp.zeros((SPAN, SPAN), F32)
        lane = iota((SPAN, 128), 1)
        row_id = iota((128, SPAN), 0)
        sum_k = jnp.zeros((128, SPAN), F32)
        sum_t = jnp.zeros((SPAN, 128), F32)
        for pair in range(inner // 128):
            lanes = slice(pair * 128, pair * 128 + 128)
            x_pair, dy_pair = x_low[:, lanes], dy[:, lanes]
            total = None
            for e in range(2):
                h = pair * 2 + e
                d_scores = dot(x_pair * masks[e], dy_pair, NT)
                fade = jnp.exp(jnp.where(seen, s_row[h : h + 1, :] - s[:, h : h + 1], -1e30))
                dt_h = dt[:, h : h + 1]
                fade_cb = cb * fade
                term = dot((fade_cb * dt_h).astype(BF16), dy_pair * masks[e])
                total = term if total is None else total + term
                d_cb = d_cb + d_scores * (fade * dt_h)
                flow = d_scores * fade_cb
                sum_t = jnp.where(lane == h, jnp.sum(flow, axis=1, keepdims=True), sum_t)
                sum_k = jnp.where(row_id == h, jnp.sum(flow * dt_h, axis=0, keepdims=True), sum_k)
            dpre[after, lanes] = total
        d_cb_low = d_cb.astype(BF16)
        dpre[after, inner : inner + STATE] = dot(d_cb_low, c)
        dpre[after, inner + STATE :] = dot(d_cb_low, b, TN)
        flow_out[tok, :] = sum_k.T - sum_t * dt
        sum_out[tok, :] = sum_t
        return 0

    lax.fori_loop(0, x_in.shape[0] // SPAN, block, 0)


def back_through_states(
    grad, prior, decay, states, dy_in, x, bc, s_in, dt_in, dtraw, xin, bcin, rowp, bcp, headp, flow_in, sum_in,
    cat_out, row_out, bcrow_out,
    dpre, dend,
):
    inner = x.shape[1]
    spans = x.shape[0] // SPAN
    spread = head_spread(inner)
    up_tri = triangle(False)
    skip = rowp[6:7]
    rate = -jnp.exp(headp[0:1])
    bias = headp[1:2]
    width = inner + 2 * STATE

    def chain(i, grad):
        q = spans - 1 - i
        before = prior[q] + decay[q, 0:1] * grad
        dend[q] = grad
        return before

    lax.fori_loop(0, spans, chain, grad)
    dpre[0:EDGE] = jnp.zeros((EDGE, width), F32)
    dpre[EDGE + spans * SPAN :] = jnp.zeros((EDGE, width), F32)
    bcrow_out[...] = jnp.zeros_like(bcrow_out)
    cols = columns_of(inner)
    cat_out[0:EDGE, cols.z] = jnp.zeros((EDGE, inner), BF16)
    cat_out[0:EDGE, cols.dt] = jnp.zeros((EDGE, 128), BF16)

    def block(q, _):
        at = pl.multiple_of(q * SPAN, SPAN)
        tok = pl.ds(at, SPAN)
        after = pl.ds(pl.multiple_of(at + EDGE, EDGE), SPAN)
        window = pl.ds(at, SPAN + EDGE)
        x_low, dy = x[tok, :], dy_in[tok, :]
        xf, dyf = x_low.astype(F32), dy.astype(F32)
        b, c = bc[tok, :STATE], bc[tok, STATE:]
        s, dt = s_in[tok, :], dt_in[tok, :]
        exp_s = jnp.exp(s)
        to_end = jnp.exp(s[SPAN - 1 : SPAN] - s)
        w = to_end * dt
        w_all, s_all = dot_split(w, spread), dot_split(exp_s, spread)
        state, grad = states[q], dend[q]
        state_low, grad_low = state.astype(BF16), grad.astype(BF16)
        carried = s_all * dot(c, state_low)
        ds = dot_split(dyf * carried, spread, NT)
        d_c = dot((dyf * s_all).astype(BF16), state_low, NT)
        d_w = dot(b, grad_low)
        d_b = dot((xf * w_all).astype(BF16), grad_low, NT)
        dx = dpre[after, 0:inner] + dyf * skip + d_w * w_all
        dsw = dot_split(d_w * xf, spread, NT)
        end = dsw * w
        ds = ds + flow_in[tok, :] - end
        held = dot_split(jnp.broadcast_to(jnp.sum(grad * state, axis=0, keepdims=True), (8, inner)), spread, NT)[0:1]
        last = jnp.sum(end, axis=0, keepdims=True) + held * exp_s[SPAN - 1 : SPAN]
        ds = ds + jnp.where(iota((SPAN, 128), 0) == SPAN - 1, last, 0.0)
        da = dot_exact(up_tri, ds)
        d_dt = sum_in[tok, :] + dsw * to_end + da * rate
        d_raw = d_dt * sigmoid(dtraw[tok, :].astype(F32) + bias)
        d_raw = jnp.where(iota((SPAN, 128), 1) < inner // HEADDIM, d_raw, 0.0)
        row_out[7:8, 0:128] += jnp.sum(da * (dt * rate), axis=0, keepdims=True)
        row_out[8:9, 0:128] += jnp.sum(d_raw, axis=0, keepdims=True)
        d_low = d_raw.astype(BF16)
        cat_out[after, cols.dt] = d_low

        win_x = xin[window, :].astype(F32)
        d_x = dx * silu_slope(conv_taps(win_x, rowp))
        dpre[after, 0:inner] = d_x
        for j in range(CONV):
            row_out[j : j + 1] += jnp.sum(d_x * win_x[EDGE - 3 + j : EDGE - 3 + j + SPAN], axis=0, keepdims=True)
        row_out[CONV : CONV + 1] += jnp.sum(d_x, axis=0, keepdims=True)
        win_bc = bcin[window, :].astype(F32)
        d_bc = dpre[after, inner:] + jnp.concatenate([d_b, d_c], axis=1)
        d_bc = d_bc * silu_slope(conv_taps(win_bc, bcp))
        dpre[after, inner:] = d_bc
        for j in range(CONV):
            bcrow_out[j : j + 1] += jnp.sum(d_bc * win_bc[EDGE - 3 + j : EDGE - 3 + j + SPAN], axis=0, keepdims=True)
        bcrow_out[CONV : CONV + 1] += jnp.sum(d_bc, axis=0, keepdims=True)
        return 0

    lax.fori_loop(0, spans, block, 0)

    def back(window, taps, rows):
        total = None
        for j in range(CONV):
            term = taps[j : j + 1] * window[CONV - 1 - j : CONV - 1 - j + rows]
            total = term if total is None else total + term
        return total.astype(BF16)

    cat_out[0:EDGE, cols.x] = back(dpre[0 : 2 * EDGE, 0:inner], rowp, EDGE)
    cat_out[0:EDGE, cols.bc] = back(dpre[0 : 2 * EDGE, inner:], bcp, EDGE)

    def conv_block(q, _):
        after = pl.ds(pl.multiple_of(q * SPAN + EDGE, EDGE), SPAN)
        window = pl.ds(pl.multiple_of(q * SPAN + EDGE, EDGE), SPAN + EDGE)
        cat_out[after, cols.x] = back(dpre[window, 0:inner], rowp, SPAN)
        cat_out[after, cols.bc] = back(dpre[window, inner:], bcp, SPAN)
        return 0

    lax.fori_loop(0, spans, conv_block, 0)


def project_back_edge(cat, w, dn_out):
    cols = columns_of((w.shape[1] - 3 * STATE) // 2)
    dn_out[0:EDGE] = (
        dot(cat[0:EDGE, cols.x], w[:, cols.x], NT) + dot(cat[0:EDGE, cols.bc], w[:, cols.bc], NT)
    ).astype(BF16)


def project_back(q, cat, w, dn_out):
    after = pl.ds(pl.multiple_of(q * SPAN + EDGE, EDGE), SPAN)
    dn_out[after, :] = dot(cat[after, :], w[...], NT).astype(BF16)


def for_row_blocks(grad, body):
    groups, rows = grad

    def one(g, _):
        body(pl.ds(pl.multiple_of(g * rows, 128), rows) if rows % 128 == 0 else pl.ds(g * rows, rows), g)
        return 0

    if rows % 128 == 0:
        lax.fori_loop(0, groups, one, 0)
    else:
        for g in range(groups):
            one(g, 0)


def x_gradient(cat, normed, gx_out):
    cols = columns_of(gx_out.shape[1])

    def body(at, _):
        total = dot(normed[EDGE:, at], cat[EDGE:, cols.x], TN) + dot(normed[0:EDGE, at], cat[0:EDGE, cols.x], TN)
        gx_out[at, :] = total.astype(BF16)

    for_row_blocks((normed.shape[1] // SPAN, SPAN), body)


def z_gradient(cat, normed, gz_out):
    cols = columns_of(gz_out.shape[1])

    def body(at, _):
        gz_out[at, :] = dot(normed[EDGE:, at], cat[EDGE:, cols.z], TN).astype(BF16)

    for_row_blocks((normed.shape[1] // SPAN, SPAN), body)


def small_gradients(cat, normed, gbc_out, gdt_out):
    groups, parts, shard, _ = gbc_out.shape
    cols = columns_of((cat.shape[1] - 3 * STATE) // 2)

    def body(at, g):
        edge, tokens = normed[0:EDGE, at], normed[EDGE:, at]
        bc = dot(tokens, cat[EDGE:, cols.bc], TN) + dot(edge, cat[0:EDGE, cols.bc], TN)
        gbc_out[g] = bc.reshape(parts, shard, 2 * STATE).astype(BF16)
        gdt_out[g] = dot(cat[EDGE:, cols.dt], tokens, TN)[0:EDGE].astype(BF16)

    for_row_blocks((groups, parts * shard), body)


HALF = 128
MESH = pl.DeviceIdType.MESH


class Links:
    def __init__(self, sends, recvs):
        self.z, self.p, self.c = lax.axis_index("z"), lax.axis_index("p"), lax.axis_index("head")
        self.groups = lax.axis_size("z")
        self.sends, self.recvs, self.used = sends, recvs, 0

    def copy(self, src, dst, device):
        i = self.used
        self.used += 1
        return pltpu.make_async_remote_copy(
            src_ref=src, dst_ref=dst, send_sem=self.sends.at[i], recv_sem=self.recvs.at[i],
            device_id=device, device_id_type=MESH,
        )

    def local(self, src, dst):
        i = self.used
        self.used += 1
        return pltpu.make_async_copy(src, dst, self.sends.at[i])

    def at(self, k, e):
        return (self.z, lax.bitwise_xor(self.p, jnp.int32(k)), lax.bitwise_xor(self.c, jnp.int32(e)))

    def last_of_plane(self):
        return jnp.logical_and(self.p == GROUP - 1, self.c == 1)

    def greet(self, plane=False, sibling=False, groups=False, edge=0):
        barrier = pltpu.get_barrier_semaphore()
        z, count = self.z, self.groups
        above = z < count - 1

        def signal(device):
            pl.semaphore_signal(barrier, 1, device_id=device, device_id_type=MESH)

        self.expected = jnp.int32(0)
        for k in range(GROUP):
            for e in range(2):
                if (k or e) if plane else (sibling and e and not k):
                    signal(self.at(k, e))
                    self.expected = self.expected + 1
        if groups:
            for k in range(1, count):
                signal((lax.rem(z + k, count), self.p, self.c))
            self.expected = self.expected + (count - 1)
        sending = jnp.logical_and(self.last_of_plane(), above)
        if edge == 1:
            pl.when(z > 0)(lambda: signal((z - 1, jnp.int32(GROUP - 1), jnp.int32(1))))
            self.expected = self.expected + 2 * GROUP * sending.astype(jnp.int32)
        if edge == -1:

            @pl.when(sending)
            def _():
                for p in range(GROUP):
                    for c in range(2):
                        signal((z + 1, jnp.int32(p), jnp.int32(c)))

            self.expected = self.expected + (z > 0).astype(jnp.int32)

    def meet(self):
        pl.semaphore_wait(pltpu.get_barrier_semaphore(), self.expected)

    def start_barrier(self, **who):
        self.greet(**who)
        self.meet()


class Chain:
    def __init__(self, links, pieces):
        z, p, c, groups = links.z, links.p, links.c, links.groups
        self.steps, self.now = [], 0
        for step in range(1, groups):
            found = []
            up, down = z - step + 1, z + step - 1
            for piece in pieces:
                block = piece(jnp.maximum(up, 0))
                sending = jnp.logical_and(up >= 0, z < groups - 1)
                found.append((sending, z - step >= 0, links.copy(block, block, (z + 1, p, c))))
                block = piece(jnp.minimum(down, groups - 1))
                sending = jnp.logical_and(down < groups, z > 0)
                found.append((sending, z + step < groups, links.copy(block, block, (z - 1, p, c))))
            self.steps.append(found)

    def begin(self):
        for sending, _, copy in self.steps[0]:
            pl.when(sending)(copy.start)

    def advance(self):
        if self.now + 1 < len(self.steps):
            for (_, receiving, copy), (sending, _, later) in zip(self.steps[self.now], self.steps[self.now + 1]):
                pl.when(receiving)(copy.wait_recv)
                pl.when(sending)(later.start)
            self.now += 1

    def complete(self):
        while self.now + 1 < len(self.steps):
            self.advance()
        for _, receiving, copy in self.steps[-1]:
            pl.when(receiving)(copy.wait_recv)

    def finish(self):
        for found in self.steps:
            for sending, _, copy in found:
                pl.when(sending)(copy.wait_send)


class Swap:
    def __init__(self, links, shard, staging, out, lanes, width):
        self.links, self.staging, self.out, self.lanes = links, staging, out, lanes

        def source(k):
            to = lax.bitwise_xor(links.p, jnp.int32(k))
            if len(shard.shape) == 3:
                return shard.at[to]
            if shard.shape[1] == width:
                return shard
            return shard.at[:, pl.ds(pl.multiple_of(to * width, 128), width)]

        self.copies = [links.copy(source(k), staging.at[links.p], links.at(k, 0)) for k in (3, 1, 2)]
        self.keep = links.local(source(0), staging.at[links.p])

    def start(self):
        for copy in self.copies:
            copy.start()

    def settle(self):
        self.keep.wait()
        for copy in self.copies:
            copy.wait_recv()
        parts, shard, width = self.staging.shape
        rows = parts * shard
        first = self.links.z * rows if self.out.shape[0] > rows else 0
        if shard % EDGE == 0:
            for j in range(parts):
                self.out[pl.ds(pl.multiple_of(first + j * shard, EDGE), shard), self.lanes] = self.staging[j]
        else:
            block = self.staging[...].astype(F32).reshape(rows, width).astype(BF16)
            self.out[pl.ds(pl.multiple_of(first, EDGE), rows), self.lanes] = block

    def finish(self):
        for copy in self.copies:
            copy.wait_send()


class Halve:
    def __init__(self, links, grad, arrived, sums):
        self.links, self.grad, self.arrived, self.sums = links, grad, arrived, sums
        z, groups = links.z, links.groups
        self.rows, self.steps, self.now = grad.shape[0] // groups, [], 0
        first, bit = 0, 1
        while bit < groups:
            low = lax.rem(z, bit)
            mine = lax.rem(lax.div(z, bit), 2)
            device = (z + bit - 2 * bit * mine, links.p, links.c)
            found = []
            for j in range(groups // (2 * bit)):
                away = j * 2 * bit + (1 - mine) * bit + low
                kept = j * 2 * bit + mine * bit + low
                copy = links.copy(self.held(away), arrived.at[first + j], device)
                found.append((first + j, self.held(kept), copy))
            self.steps.append(found)
            self.before = (first, 2 * bit)
            first, bit = first + groups // (2 * bit), 2 * bit

    def held(self, target):
        if not self.steps:
            return self.grad.at[pl.ds(pl.multiple_of(target * self.rows, EDGE), self.rows), :]
        first, size = self.before
        return self.arrived.at[first + lax.div(target, size)]

    def begin(self):
        for _, _, copy in self.steps[0]:
            copy.start()

    def advance(self):
        for slot, held, copy in self.steps[self.now]:
            copy.wait_recv()

            def add(i, _, slot=slot, held=held):
                at = pl.ds(pl.multiple_of(i * 32, 32), 32)
                total = self.arrived[slot, at, :].astype(F32) + held[at, :].astype(F32)
                self.arrived[slot, at, :] = total.astype(BF16)
                return 0

            lax.fori_loop(0, self.rows // 32, add, 0)
        self.now += 1
        for _, _, copy in self.steps[self.now]:
            copy.start()

    def complete(self):
        while self.now + 1 < len(self.steps):
            self.advance()
        ((slot, held, copy),) = self.steps[-1]
        copy.wait_recv()
        total = self.arrived[slot].astype(F32) + held[...].astype(F32)
        shard = self.sums.shape[1]
        for j in range(GROUP):
            self.sums[j] = total[j * shard : (j + 1) * shard].astype(BF16)

    def finish(self):
        for found in self.steps:
            for _, _, copy in found:
                copy.wait_send()


class Deliver:
    def __init__(self, links, sums, out):
        self.links, self.sums, self.out = links, sums, out
        inner = sums.shape[2]
        self.mine = pl.ds(pl.multiple_of(links.p * inner, 128), inner)
        self.copies = [
            links.copy(sums.at[lax.bitwise_xor(links.p, jnp.int32(k))], out.at[:, self.mine], links.at(k, 0))
            for k in (3, 1, 2)
        ]

    def start(self):
        for copy in self.copies:
            copy.start()
        self.out[:, self.mine] = self.sums[self.links.p]

    def arrive(self):
        for copy in self.copies:
            copy.wait_recv()

    def finish(self):
        for copy in self.copies:
            copy.wait_send()


class States:
    def __init__(self, links, backward, state, decay, states, decays):
        z, groups = links.z, links.groups
        self.links, self.refs = links, (state, decay, states, decays)
        self.found = []
        for k in range(1, groups):
            to, source = (z - k, z + k) if backward else (z + k, z - k)
            sending, receiving = (to >= 0, source < groups) if backward else (to < groups, source >= 0)
            device = (jnp.clip(to, 0, groups - 1), links.p, links.c)
            pair = [links.copy(state, states.at[z], device), links.copy(decay, decays.at[z], device)]
            self.found.append((sending, receiving, pair))

    def start(self):
        for sending, _, pair in self.found:

            @pl.when(sending)
            def _(pair=pair):
                for copy in pair:
                    copy.start()

    def arrive(self):
        for _, receiving, pair in self.found:

            @pl.when(receiving)
            def _(pair=pair):
                for copy in pair:
                    copy.wait_recv()

    def finish(self):
        for sending, _, pair in self.found:

            @pl.when(sending)
            def _(pair=pair):
                for copy in pair:
                    copy.wait_send()


class Gather:
    def __init__(self, links, out, base):
        self.links, self.out, self.base = links, out, base

        def place(k, half=None):
            row = base + lax.bitwise_xor(links.p, jnp.int32(k)) * (2 * HALF) + links.c * HALF
            if half is None:
                return out.at[pl.ds(pl.multiple_of(row, EDGE), HALF), :]
            return out.at[pl.ds(pl.multiple_of(row + half * (HALF // 2), EDGE), HALF // 2), :]

        def send(k, half, to, e=0):
            return links.copy(place(k, half), place(k, half), links.at(to, e))

        self.near = {(to, half): send(0, half, to) for half in range(2) for to in (1, 2)}
        self.relays = {0: send(1, 0, 2), 1: send(2, 1, 1)}
        self.own_share = send(0, None, 0, 1)
        self.shares = {(k, half): send(k, half, 0, 1) for k in (1, 2, 3) for half in range(2)}

    def own(self, start, size):
        row = self.base + self.links.p * (2 * HALF) + self.links.c * HALF + start
        return pl.ds(pl.multiple_of(row, EDGE), size)

    def start(self):
        for which in ((1, 0), (2, 1), (1, 1), (2, 0)):
            self.near[which].start()
        self.own_share.start()

    def pass_on(self):
        for k, half in ((1, 0), (2, 1)):
            self.near[k, half].wait_recv()
            self.relays[half].start()
            self.shares[k, half].start()
        for k, half in ((1, 1), (2, 0)):
            self.near[k, half].wait_recv()
            self.shares[k, half].start()
        for half in range(2):
            self.relays[half].wait_recv()
            self.shares[3, half].start()

    def finish(self):
        shares = [self.own_share, *self.shares.values()]
        for copy in shares:
            copy.wait_recv()
        for copy in [*shares, *self.near.values(), *self.relays.values()]:
            copy.wait_send()


class EdgeForward:
    def __init__(self, links, gather):
        self.links = links
        tail = gather.out.at[gather.own(HALF - EDGE, EDGE), :]
        first = links.used
        links.used += 2 * GROUP + 1
        recv = links.recvs.at[first + 2 * GROUP]
        self.out = gather.out
        self.copies = [
            pltpu.make_async_remote_copy(
                src_ref=tail, dst_ref=gather.out.at[0:EDGE, :], send_sem=links.sends.at[first + p * 2 + c], recv_sem=recv,
                device_id=(links.z + 1, jnp.int32(p), jnp.int32(c)), device_id_type=MESH,
            )
            for p in range(GROUP)
            for c in range(2)
        ]
        self.sending = jnp.logical_and(links.last_of_plane(), links.z < links.groups - 1)

    def start(self):
        @pl.when(self.sending)
        def _():
            for copy in self.copies:
                copy.start()

        @pl.when(self.links.z == 0)
        def _():
            self.out[0:EDGE, :] = jnp.zeros((EDGE, self.out.shape[1]), self.out.dtype)

    def finish(self):
        pl.when(self.links.z > 0)(self.copies[0].wait_recv)

        @pl.when(self.sending)
        def _():
            for copy in self.copies:
                copy.wait_send()


class Scatter:
    def __init__(self, links, part, base, sib, total, peer, via):
        self.links, self.part, self.base = links, part, base
        self.sib, self.total, self.peer, self.via = sib, total, peer, via
        other = 1 - links.c
        self.to_sibling = {
            k: links.copy(part.at[self.rows(k, other, 0, HALF), :], sib.at[k], links.at(0, 1)) for k in (3, 1, 2, 0)
        }
        halves = [slice(0, HALF // 2), slice(HALF // 2, HALF)]
        self.across = [links.copy(total.at[2, halves[i]], via.at[i], links.at(i + 1, 0)) for i in range(2)]
        self.to_peer = {
            (k, i): links.copy(total.at[k - 1, halves[i]], peer.at[k - 1, halves[i]], links.at(k, 0))
            for k in (1, 2)
            for i in range(2)
        }

    def rows(self, k, c, start, size):
        row = self.base + lax.bitwise_xor(self.links.p, jnp.int32(k)) * (2 * HALF) + c * HALF + start
        return pl.ds(pl.multiple_of(row, EDGE), size)

    def pass_on(self, k):
        self.to_sibling[k].wait_recv()
        if k == 0:
            for i in (1, 0):
                self.across[i].wait_recv()

                def join(j, _, i=i):
                    at = pl.ds(pl.multiple_of(i * (HALF // 2) + j * 32, 32), 32)
                    came = self.via[i, pl.ds(pl.multiple_of(j * 32, 32), 32), :].astype(F32)
                    self.total[1 - i, at, :] = (self.total[1 - i, at, :].astype(F32) + came).astype(BF16)
                    return 0

                lax.fori_loop(0, HALF // 64, join, 0)
                self.to_peer[2 - i, i].start()
            return

        def add(i, _):
            at = pl.ds(pl.multiple_of(i * 32, 32), 32)
            mine = self.part[self.rows(k, self.links.c, i * 32, 32), :].astype(F32)
            self.total[k - 1, at, :] = (mine + self.sib[k, at, :].astype(F32)).astype(BF16)
            return 0

        lax.fori_loop(0, HALF // 32, add, 0)
        for copy in self.across if k == 3 else [self.to_peer[k, k - 1]]:
            copy.start()

    def arrive(self):
        for copy in self.to_peer.values():
            copy.wait_recv()

    def own(self, start, size):
        at = pl.ds(start, size)
        total = self.part[self.rows(0, self.links.c, start, size), :].astype(F32) + self.sib[0, at, :].astype(F32)
        for k in range(2):
            total = total + self.peer[k, at, :].astype(F32)
        return total

    def finish(self):
        for copy in [*self.to_sibling.values(), *self.across, *self.to_peer.values()]:
            copy.wait_send()


class SmallSum:
    def __init__(self, links, squares, slots):
        self.links, self.squares, self.slots = links, squares, slots
        self.copies = [
            links.copy(squares.at[:, self.lanes(k, e)], slots.at[2 * k + e - 1], links.at(k, e))
            for k in range(GROUP)
            for e in range(2)
            if k or e
        ]

    def lanes(self, k, e):
        links = self.links
        column = lax.bitwise_xor(links.p, jnp.int32(k)) * (2 * HALF) + lax.bitwise_xor(links.c, jnp.int32(e)) * HALF
        return pl.ds(pl.multiple_of(column, HALF), HALF)

    def start(self):
        for copy in self.copies:
            copy.start()

    def total(self):
        for copy in self.copies:
            copy.wait_recv()
        total = self.squares[:, self.lanes(0, 0)]
        for i in range(len(self.copies)):
            total = total + self.slots[i]
        return total

    def finish(self):
        for copy in self.copies:
            copy.wait_send()


class SmallGather:
    def __init__(self, links, out):
        self.out = out
        self.lanes = pl.ds(pl.multiple_of(links.p * (2 * HALF) + links.c * HALF, HALF), HALF)
        self.copies = [
            links.copy(out.at[:, self.lanes], out.at[:, self.lanes], links.at(k, e))
            for k in range(GROUP)
            for e in range(2)
            if k or e
        ]

    def start(self):
        for copy in self.copies:
            copy.start()

    def finish(self):
        for copy in self.copies:
            copy.wait()


def row_chunks(size=32):
    return [(start, size) for start in range(0, HALF, size)]


def rms_of(rows):
    return lax.rsqrt(jnp.mean(rows * rows, axis=-1, keepdims=True) + EPS)


def as_tile(columns):
    lane = iota((HALF, HALF), 1)
    wide = jnp.zeros((HALF, HALF), F32)
    for i, column in enumerate(columns):
        wide = jnp.where(lane == i, column, wide)
    return wide.T[0:8]


def grad_rows(links, scatter, edge_slots, grad, resid, gain, gain_out, start, size):
    at = slice(start, start + size)
    d_normed = scatter.own(start, size)
    if start + size == HALF:
        extra = edge_slots[0].astype(F32)
        for i in range(1, 2 * GROUP):
            extra = extra + edge_slots[i].astype(F32)
        used = jnp.logical_and(links.last_of_plane(), links.z < links.groups - 1)
        extra = jnp.where(used, extra, 0.0)
        d_normed = d_normed + jnp.concatenate([jnp.zeros((size - EDGE, extra.shape[1]), F32), extra])
    rows = resid[at]
    inv_rms = rms_of(rows)
    gain_sum = jnp.sum(d_normed * rows * inv_rms, axis=0, keepdims=True)
    gain_out[0:1] = gain_sum if start == 0 else gain_out[0:1] + gain_sum
    d_hidden = d_normed * gain[...]
    return (
        grad[at]
        + inv_rms * d_hidden
        - rows * (inv_rms * inv_rms * inv_rms * jnp.mean(d_hidden * rows, axis=-1, keepdims=True))
    )


class EdgeBackward:
    def __init__(self, links, part, slots):
        self.links = links
        first = links.used
        links.used += 2 * GROUP + 1
        me = links.p * 2 + links.c
        self.send = pltpu.make_async_remote_copy(
            src_ref=part.at[0:EDGE, :], dst_ref=slots.at[me], send_sem=links.sends.at[first], recv_sem=links.recvs.at[first + me],
            device_id=(links.z - 1, jnp.int32(GROUP - 1), jnp.int32(1)), device_id_type=MESH,
        )
        self.recvs = [
            pltpu.make_async_remote_copy(
                src_ref=part.at[0:EDGE, :], dst_ref=slots.at[i], send_sem=links.sends.at[first], recv_sem=links.recvs.at[first + i],
                device_id=(links.z, links.p, 1 - links.c), device_id_type=MESH,
            )
            for i in range(2 * GROUP)
        ]
        self.receiving = jnp.logical_and(links.last_of_plane(), links.z < links.groups - 1)

    def start(self):
        pl.when(self.links.z > 0)(self.send.start)

    def receive(self):
        @pl.when(self.receiving)
        def _():
            for copy in self.recvs:
                copy.wait_recv()

    def finish(self):
        pl.when(self.links.z > 0)(self.send.wait_send)


class BcSum:
    def __init__(self, links, bc, out, bufs):
        self.links, self.bc, self.out = links, bc, out
        self.sib, self.chip, self.peer, self.total, self.far = bufs
        p, c, groups = links.p, links.c, links.groups
        self.own = pl.ds(pl.multiple_of(c * STATE, STATE), STATE)
        other = pl.ds(pl.multiple_of((1 - c) * STATE, STATE), STATE)
        self.first = [links.copy(bc.at[:, :, :, other], self.sib, links.at(0, 1))]
        self.second = [
            links.copy(self.chip.at[:, lax.bitwise_xor(p, jnp.int32(k))], self.peer.at[k - 1], links.at(k, 0))
            for k in (3, 1, 2)
        ]
        self.third = []
        for k in range(1, groups):
            to = lax.rem(links.z + k, groups)
            self.third.append(links.copy(self.total.at[to], self.far.at[k - 1], (to, p, c)))
        self.fourth = [links.copy(out.at[:, self.own], out.at[:, self.own], links.at(0, 1))]

    @staticmethod
    def begin(copies):
        for copy in copies:
            copy.start()

    @staticmethod
    def arrive(copies):
        for copy in copies:
            copy.wait_recv()

    def cores(self):
        self.begin(self.first)

    def plane(self):
        self.arrive(self.first)

        def add(i, _):
            for q in range(GROUP):
                mine = self.bc[i, q, :, self.own].astype(F32)
                self.chip[i, q] = (mine + self.sib[i, q].astype(F32)).astype(BF16)
            return 0

        lax.fori_loop(0, self.links.groups, add, 0)
        self.begin(self.second)

    def groups(self):
        self.arrive(self.second)

        def add(i, _):
            total = self.chip[i, self.links.p].astype(F32)
            for k in range(GROUP - 1):
                total = total + self.peer[k, i].astype(F32)
            self.total[i] = total.astype(BF16)
            return 0

        lax.fori_loop(0, self.links.groups, add, 0)
        self.begin(self.third)

    def share(self):
        self.arrive(self.third)
        total = self.total[self.links.z].astype(F32)
        for k in range(self.links.groups - 1):
            total = total + self.far[k].astype(F32)
        self.out[:, self.own] = total.astype(BF16)
        self.begin(self.fourth)

    def finish(self):
        self.arrive(self.fourth)
        for copy in self.first + self.second + self.third + self.fourth:
            copy.wait_send()


class LaidOut:
    def __init__(self, links, dt, wide, dt_out, wide_out, dt_far, wide_far):
        self.links, self.refs = links, (dt, wide, dt_out, wide_out, dt_far, wide_far)
        z, p, c, groups = links.z, links.p, links.c, links.groups
        self.first, self.second = [], []
        for k in range(1, groups):
            to = lax.rem(z + k, groups)
            self.first.append(links.copy(dt.at[to], dt_far.at[k - 1], (to, p, c)))
            self.first.append(links.copy(wide, wide_far.at[k - 1], (to, p, c)))
        for k in range(1, GROUP):
            self.second.append(links.copy(dt_out.at[p], dt_out.at[p], links.at(k, 0)))
            self.second.append(links.copy(wide_out.at[p], wide_out.at[p], links.at(k, 0)))

    def groups(self):
        BcSum.begin(self.first)

    def plane(self):
        BcSum.arrive(self.first)
        dt, wide, dt_out, wide_out, dt_far, wide_far = self.refs
        dt_total, wide_total = dt[self.links.z].astype(F32), wide[...]
        for k in range(self.links.groups - 1):
            dt_total = dt_total + dt_far[k].astype(F32)
            wide_total = wide_total + wide_far[k]
        dt_out[self.links.p] = dt_total.astype(BF16)
        wide_out[self.links.p] = wide_total
        BcSum.begin(self.second)

    def finish(self):
        BcSum.arrive(self.second)
        for copy in self.first + self.second:
            copy.wait_send()


class VecSum:
    def __init__(self, links, vec, out, near, far):
        self.links, self.refs = links, (vec, out, near, far)
        z, p, c, groups = links.z, links.p, links.c, links.groups
        self.first, self.second, self.third = [], [], []
        for k in range(GROUP):
            for e in range(2):
                if k or e:
                    to = lax.bitwise_xor(p, jnp.int32(k)) * 2 + lax.bitwise_xor(c, jnp.int32(e))
                    self.first.append(links.copy(vec.at[to], near.at[2 * k + e - 1], links.at(k, e)))
                    self.third.append(links.copy(out.at[p * 2 + c], out.at[p * 2 + c], links.at(k, e)))
        for k in range(1, groups):
            self.second.append(links.copy(near.at[7], far.at[k - 1], (lax.rem(z + k, groups), p, c)))

    def plane(self):
        BcSum.begin(self.first)

    def groups(self):
        BcSum.arrive(self.first)
        vec, _, near, _ = self.refs
        total = vec[self.links.p * 2 + self.links.c]
        for slot in range(2 * GROUP - 1):
            total = total + near[slot]
        near[7] = total
        BcSum.begin(self.second)

    def back(self):
        BcSum.arrive(self.second)
        _, out, near, far = self.refs
        total = near[7]
        for k in range(self.links.groups - 1):
            total = total + far[k]
        out[self.links.p * 2 + self.links.c] = total
        BcSum.begin(self.third)

    def finish(self):
        BcSum.arrive(self.third)
        for copy in self.first + self.second + self.third:
            copy.wait_send()


class Refs:
    def __init__(self, refs, twins, sems):
        self.__dict__.update(refs)
        self.twins = {id(near): (far, near, sems.at[i]) for i, (far, near) in enumerate(twins)}
        self.waits = []

    def fetch(self, *refs):
        for ref in refs:
            far, near, sem = self.twins[id(ref)]
            pltpu.make_async_copy(far, near, sem).start()

    def need(self, *refs):
        for ref in refs:
            pltpu.make_async_copy(*self.twins[id(ref)]).wait()

    def flush(self, *refs):
        for ref in refs:
            far, near, sem = self.twins[id(ref)]
            self.waits.append(pltpu.make_async_copy(near, far, sem))
            self.waits[-1].start()

    def done(self):
        for copy in self.waits:
            copy.wait()


def weight_chain(links, w, steps, inner):
    rows, step_rows = w.shape[0] // links.groups, steps.shape[0] // links.groups
    cols = columns_of(inner)
    half = pl.ds(pl.multiple_of(cols.bc.start + links.c * STATE, STATE), STATE)

    def at(index):
        return pl.ds(pl.multiple_of(index * rows, EDGE), rows)

    pieces = [
        lambda i: w.at[at(i), cols.x],
        lambda i: w.at[at(i), cols.z],
        lambda i: w.at[at(i), half],
        lambda i: steps.at[pl.ds(pl.multiple_of(i * step_rows, EDGE), step_rows), :],
    ]
    return Chain(links, pieces), links.copy(w.at[:, half], w.at[:, half], links.at(0, 1))


def pack_steps(w_dt, steps_out, wide):
    heads_core, shard = w_dt.shape
    heads = heads_core // GROUP
    wide[...] = jnp.zeros_like(wide)
    wide[0:heads_core, 0:shard] = w_dt
    row, col = iota((EDGE, 128), 0), iota((EDGE, 128), 1)
    for q in range(GROUP):
        pick = jnp.logical_and(col == q * heads + row, row < heads).astype(BF16)
        steps_out[q] = dot(pick, wide[...]).astype(BF16)


def unpack_steps(steps, w, shard, inner):
    lanes = columns_of(inner).dt
    rows = GROUP * shard
    blank = jnp.zeros((128 - EDGE, 128), F32)

    def block(g, _):
        parts = []
        for j in range(GROUP):
            at = pl.ds(pl.multiple_of(g * (GROUP * EDGE) + j * EDGE, EDGE), EDGE)
            parts.append(jnp.concatenate([steps[at, :].astype(F32), blank]).T[0:shard])
        w[pl.ds(pl.multiple_of(g * rows, EDGE), rows), lanes] = jnp.concatenate(parts).astype(BF16)
        return 0

    lax.fori_loop(0, w.shape[0] // rows, block, 0)


def prepare(links, r, layer):
    inner = r.rowp.shape[1]
    heads_core = r.head_params.shape[2]
    lanes = pl.ds(pl.multiple_of(links.p * inner, 128), inner)
    r.gains[...] = r.norm_gain[...].astype(F32)
    r.headp[...] = jnp.zeros_like(r.headp)
    for i in range(3):
        r.headp[i : i + 1, 0:heads_core] = r.head_params[i, layer : layer + 1, :]
    mine = dot_exact(r.headp[...], head_pick(links.p, inner // HEADDIM).astype(F32))
    r.headp[...] = mine
    r.rowp[...] = jnp.zeros_like(r.rowp)
    r.rowp[0 : CONV + 1] = r.conv_x[:, :, lanes].astype(F32)[:, layer]
    r.rowp[5:6] = r.gated_gain[:, lanes].astype(F32)[layer : layer + 1]
    r.rowp[6:7] = dot_exact(mine, head_spread(inner).astype(F32))[2:3]
    r.bcp[...] = jnp.zeros_like(r.bcp)
    r.bcp[0 : CONV + 1] = r.conv_bc[...].astype(F32)[:, layer]


def out_chain(links, wo):
    rows = wo.shape[0] // links.groups
    return Chain(links, [lambda i: wo.at[pl.ds(pl.multiple_of(i * rows, EDGE), rows), :]])


def weight_swaps(links, r, layer, w, steps, wo):
    inner = wo.shape[1]
    cols = columns_of(inner)
    stagings = r.stagings[layer]
    here = pl.ds(pl.multiple_of(links.c * STATE, STATE), STATE)
    half = pl.ds(pl.multiple_of(cols.bc.start + links.c * STATE, STATE), STATE)
    swaps = [
        Swap(links, r.w_zx.at[layer, 1], stagings[0], w, cols.x, inner),
        Swap(links, r.w_zx.at[layer, 0], stagings[1], w, cols.z, inner),
        Swap(links, r.w_bc.at[layer, :, here], stagings[2], w, half, STATE),
        Swap(links, r.packed_steps.at[layer], stagings[3], steps, slice(0, 128), 128),
    ]
    return swaps, Swap(links, r.w_out.at[layer], stagings[4], wo, slice(0, inner), inner)


def scatter_blocks(scatter, compute):
    before = None
    for k in (3, 1, 2, 0):
        compute(lax.bitwise_xor(scatter.links.p, jnp.int32(k)))
        scatter.to_sibling[k].start()
        if before is not None:
            scatter.pass_on(before)
        before = k


def forward_layer(links, r, normed, w, wo, wo_chain, scatter, meanwhile):
    carried = States(links, False, r.state_low, r.decay_row, r.states_in, r.decays_in)
    state_sum, decay_all = project_and_convolve(
        normed, w, r.rowp, r.bcp, r.headp, r.z, r.xin, r.bcin, r.x, r.bc, r.dtraw, r.dt, r.s, r.decay, r.ext, r.local,
        lambda q: pl.when(q == 2)(wo_chain.advance),
    )
    r.state_low[...] = state_sum.astype(BF16)
    r.decay_row[...] = jnp.broadcast_to(decay_all, r.decay_row.shape)
    carried.start()
    r.flush(r.z, r.xin, r.bcin, r.x, r.bc, r.dtraw, r.dt, r.s, r.decay)
    wo_chain.advance()
    mix_within_spans(r.x, r.bc, r.s, r.dt, r.y)
    meanwhile()
    wo_chain.complete()
    r.flush(r.wo)
    carried.arrive()
    chain_states(entering_state(links.z, links.groups, r.states_in, r.decays_in, False), r.local, r.decay, r.states)
    scatter_blocks(
        scatter, lambda q: mix_out(q, r.states, r.x, r.bc, r.z, r.s, wo, r.rowp, r.y, r.part, r.squares)
    )
    r.flush(r.y, r.states)
    return carried


def first_kernel(inner_all, r):
    links = Links(r.sends, r.recvs)
    c = links.c
    inner = r.wo.shape[1]
    shard = r.w_dt.shape[2]
    links.greet(plane=True, groups=True, edge=1)
    for layer in range(2):
        pack_steps(r.w_dt[layer], r.packed_steps.at[layer], r.wide_steps)
    swaps, swap_o = weight_swaps(links, r, 0, r.w, r.dt_rows, r.wo)
    next_swaps, next_o = weight_swaps(links, r, 1, r.next_w, r.next_dt_rows, r.next_wo)
    all_swaps = swaps + [swap_o] + next_swaps + [next_o]
    gather, other = Gather(links, r.normed, EDGE), Gather(links, r.dmix, 0)
    edge = EdgeForward(links, gather)
    chain, share = weight_chain(links, r.w, r.dt_rows, inner)
    chain_o = out_chain(links, r.wo)
    next_chain, next_share = weight_chain(links, r.next_w, r.next_dt_rows, inner)
    scatter = Scatter(links, r.part, 0, r.sib, r.total, r.peer, r.via)
    small = SmallSum(links, r.squares, r.slots)
    next_gather = Gather(links, r.next_normed, EDGE)
    next_edge = EdgeForward(links, next_gather)

    prepare(links, r, 0)
    for swap in all_swaps:
        swap.keep.start()
    for start, size in row_chunks():
        at = pl.ds(pl.multiple_of(c * HALF + start, EDGE), size)
        rows_in = r.resid[at, :].astype(F32)
        r.resid_out[start : start + size] = rows_in
        r.normed[gather.own(start, size), :] = (rows_in * rms_of(rows_in) * r.gains[0:1]).astype(BF16)
        rows_in = r.cot[at, :]
        r.cot_out[start : start + size] = rows_in.astype(F32)
        r.dmix[other.own(start, size), :] = rows_in
    links.meet()
    for swap in swaps:
        swap.start()
    for swap in swaps:
        swap.settle()
    chain.begin()
    gather.start()
    edge.start()
    swap_o.start()
    chain.advance()
    gather.pass_on()
    for swap in next_swaps + [next_o]:
        swap.start()
    chain.advance()
    swap_o.settle()
    gather.finish()
    edge.finish()
    chain.complete()
    share.start()
    chain_o.begin()
    other.start()
    unpack_steps(r.dt_rows, r.w, shard, inner)
    r.flush(r.normed)
    share.wait()
    r.flush(r.w)

    def meanwhile():
        for swap in next_swaps + [next_o]:
            swap.settle()
        next_chain.begin()
        other.pass_on()

    carried = forward_layer(links, r, r.normed, r.w, r.wo, chain_o, scatter, meanwhile)
    small.start()
    scatter.pass_on(0)
    next_chain.advance()
    scatter.arrive()
    inv = lax.rsqrt(small.total() * (1.0 / inner_all) + EPS)
    r.inv_out[...] = inv
    column = inv.T[:, 0:1]
    for start, size in row_chunks():
        at = slice(start, start + size)
        mixed = scatter.own(start, size)
        r.mixed_out[at] = mixed
        fresh = r.resid_out[at] + column[at] * mixed
        r.fresh_out[at] = fresh
        r.next_normed[next_gather.own(start, size), :] = (fresh * rms_of(fresh) * r.gains[1:2]).astype(BF16)
    next_gather.start()
    next_edge.start()
    other.finish()
    r.flush(r.dmix)
    next_chain.advance()
    next_gather.pass_on()
    next_chain.complete()
    next_share.start()
    unpack_steps(r.next_dt_rows, r.next_w, shard, inner)
    scatter.finish()
    small.finish()
    next_gather.finish()
    next_edge.finish()
    carried.finish()
    for swap in all_swaps:
        swap.finish()
    for one in (chain, chain_o, next_chain):
        one.finish()
    next_share.wait()
    r.done()


def second_kernel(inner_all, r):
    links = Links(r.sends, r.recvs)
    r.fetch(r.normed, r.w)
    rows = r.wo_own.shape[0]
    keep = links.local(r.wo_own, r.wo.at[pl.ds(pl.multiple_of(links.z * rows, EDGE), rows), :])
    chain_o = out_chain(links, r.wo)
    scatter = Scatter(links, r.part, 0, r.sib, r.total, r.peer, r.via)
    small = SmallSum(links, r.squares, r.slots)
    spread = SmallGather(links, r.scalars_out)
    at = pl.ds(pl.multiple_of(links.c * HALF, HALF), HALF)
    share = links.copy(r.block_out.at[at, :], r.block_out.at[at, :], links.at(0, 1))
    keep.start()
    links.greet(plane=True, groups=True)
    prepare(links, r, 1)
    keep.wait()
    links.meet()
    chain_o.begin()
    r.need(r.normed, r.w)
    carried = forward_layer(links, r, r.normed, r.w, r.wo, chain_o, scatter, lambda: None)
    small.start()
    scatter.pass_on(0)
    scatter.arrive()
    inv = lax.rsqrt(small.total() * (1.0 / inner_all) + EPS)
    column = inv.T[:, 0:1]
    dots = []
    for start, size in row_chunks():
        at = slice(start, start + size)
        mixed = scatter.own(start, size)
        dots.append(jnp.sum(r.cot[at] * mixed, axis=-1, keepdims=True))
        r.block_out[pl.ds(pl.multiple_of(links.c * HALF + start, EDGE), size), :] = (
            r.resid[at] + column[at] * mixed
        ).astype(BF16)
    r.scalars_out[:, spread.lanes] = as_tile([column, jnp.concatenate(dots)])
    spread.start()
    share.start()
    scatter.finish()
    small.finish()
    carried.finish()
    chain_o.finish()
    spread.finish()
    share.wait()
    r.done()


def backward_layer(links, inner_all, r, z_collect, at_start, before_collect, at_middle):
    carried = States(links, True, r.state_low, r.decay_row, r.states_in, r.decays_in)
    collect = Halve(links, r.gwo, r.go_in, r.go_sum)
    grad_sum, decay_all = back_through_gate(
        inner_all, r.dmix, r.wo, r.y, r.z, r.x, r.bc, r.s, r.decay, r.scalars, r.rowp,
        r.cat, r.wide, r.dy, r.prior, r.normed_out,
    )
    r.state_low[...] = grad_sum.astype(BF16)
    r.decay_row[...] = jnp.broadcast_to(decay_all, r.decay_row.shape)
    links.meet()
    carried.start()
    at_start()
    out_gradient(r.dmix, r.normed_out, r.gwo)
    before_collect()
    collect.begin()
    r.need(r.normed)
    z_gradient(r.cat, r.normed, r.gz)
    z_collect.begin()
    r.need(r.dt)
    back_within_spans(r.dy, r.x, r.bc, r.s, r.dt, r.dpre, r.flow, r.sums)
    at_middle()
    carried.arrive()
    grad = entering_state(links.z, links.groups, r.states_in, r.decays_in, True)
    r.need(r.states, r.dtraw, r.xin, r.bcin)
    back_through_states(
        grad, r.prior, r.decay, r.states, r.dy, r.x, r.bc, r.s, r.dt, r.dtraw, r.xin, r.bcin, r.rowp, r.bcp, r.headp,
        r.flow, r.sums, r.cat, r.wide, r.bc_rows, r.dpre, r.prior,
    )
    collect.advance()
    return carried, collect


def put_vector(vec, row, values):
    for i in range(values.shape[0]):
        for j in range(values.shape[1] // 128):
            vec[row // 8, row % 8 : row % 8 + 1, :] = values[i : i + 1, j * 128 : j * 128 + 128]
            row += 1


def third_kernel(inner_all, r):
    links = Links(r.sends, r.recvs)
    r.fetch(r.dt, r.states, r.dtraw, r.xin, r.bcin, r.w, r.normed, r.grad, r.resid, r.mixed)
    scatter = Scatter(links, r.part, EDGE, r.sib, r.total, r.peer, r.via)
    edge = EdgeBackward(links, r.part, r.edge_slots)
    gather = Gather(links, r.dmix_out, 0)
    spread = SmallGather(links, r.scalars_out)
    collects = [Halve(links, r.gx, r.gx_in, r.gx_sum), Halve(links, r.gz, r.gz_in, r.gz_sum)]
    r.edge_slots[...] = jnp.zeros_like(r.edge_slots)
    links.greet(plane=True, groups=True, edge=-1)
    prepare(links, r, 1)
    carried, collect = backward_layer(links, inner_all, r, collects[1], lambda: None, lambda: None, lambda: None)
    r.need(r.w)
    x_gradient(r.cat, r.normed, r.gx)
    collects[0].begin()
    project_back_edge(r.cat, r.w, r.part)
    edge.start()
    scatter_blocks(scatter, lambda q: project_back(q, r.cat, r.w, r.part))
    scatter.pass_on(0)
    small_gradients(r.cat, r.normed, r.gbc, r.gdt)
    collect.complete()
    collects[1].advance()
    scatter.arrive()
    edge.receive()
    r.need(r.grad, r.resid, r.mixed)
    r.gain_row[...] = jnp.zeros_like(r.gain_row)
    dots = []
    for start, size in row_chunks():
        at = slice(start, start + size)
        fresh = grad_rows(links, scatter, r.edge_slots, r.grad, r.resid, r.gains[1:2], r.gain_row, start, size)
        r.grad_out[at] = fresh
        low = fresh.astype(BF16)
        r.dmix_out[gather.own(start, size), :] = low
        dots.append(jnp.sum(low.astype(F32) * r.mixed[at], axis=-1, keepdims=True))
    r.scalars_out[:, spread.lanes] = as_tile([r.inv[...].T[:, 0:1], jnp.concatenate(dots)])
    gather.start()
    spread.start()
    r.vec[...] = jnp.zeros_like(r.vec)
    model = r.gain_row.shape[1]
    put_vector(r.vec, model // 128, r.gain_row[0:1])
    put_vector(r.vec, 2 * (model // 128) + 2 * (CONV + 1), r.bc_rows[0 : CONV + 1])
    collects[0].advance()
    gather.pass_on()
    collects[1].complete()
    scatter.finish()
    edge.finish()
    gather.finish()
    spread.finish()
    carried.finish()
    collects[0].complete()
    for one in [collect] + collects:
        one.finish()


def fourth_kernel(inner_all, r):
    links = Links(r.sends, r.recvs)
    r.fetch(r.dt, r.states, r.dtraw, r.xin, r.bcin, r.above_bc, r.above_x, r.above_z, r.above_o, r.normed, r.w, r.grad, r.resid)
    scatter = Scatter(links, r.part, EDGE, r.sib, r.total, r.peer, r.via)
    edge = EdgeBackward(links, r.part, r.edge_slots)
    at = pl.ds(pl.multiple_of(links.c * HALF, HALF), HALF)
    share = links.copy(r.out.at[at, :], r.out.at[at, :], links.at(0, 1))
    collects = [Halve(links, r.gx, r.gx_in, r.gx_sum), Halve(links, r.gz, r.gz_in, r.gz_sum)]
    above = ((r.above_x, r.g_zx.at[1, 1]), (r.above_z, r.g_zx.at[1, 0]), (r.above_o, r.g_out.at[1]))
    own = ((r.go_sum, r.g_out.at[0]), (r.gx_sum, r.g_zx.at[0, 1]), (r.gz_sum, r.g_zx.at[0, 0]))
    delivers = [Deliver(links, parts, out) for parts, out in above]
    own_delivers = [Deliver(links, parts, out) for parts, out in own]
    bc_sums = [
        BcSum(links, bc, r.bc_out.at[i], r.bc_bufs[i])
        for i, bc in enumerate((r.gbc, r.above_bc))
    ]
    laid = LaidOut(links, r.steps_all, r.wide_all, r.dt_out, r.wide_out, r.dt_far, r.wide_far)
    vec_sum = VecSum(links, r.vec, r.vec_out, r.vec_near, r.vec_far)
    r.edge_slots[...] = jnp.zeros_like(r.edge_slots)
    links.greet(plane=True, groups=True, edge=-1)
    prepare(links, r, 0)

    def at_start():
        r.need(r.above_bc)
        bc_sums[1].cores()

    def at_middle():
        bc_sums[1].groups()
        r.need(r.above_x, r.above_z, r.above_o)
        for deliver in delivers:
            deliver.start()

    carried, collect = backward_layer(links, inner_all, r, collects[1], at_start, bc_sums[1].plane, at_middle)
    small_gradients(r.cat, r.normed, r.gbc, r.gdt)
    bc_sums[0].cores()
    r.steps_all[:, 0:EDGE, :] = r.gdt[...]
    r.steps_all[:, EDGE:, :] = r.above_dt[...]
    r.wide_all[0:16] = r.wide[...]
    r.wide_all[16:32] = r.above_wide[...]
    laid.groups()
    x_gradient(r.cat, r.normed, r.gx)
    collects[0].begin()
    bc_sums[0].plane()
    r.need(r.w)
    project_back_edge(r.cat, r.w, r.part)
    edge.start()
    scatter_blocks(scatter, lambda q: project_back(q, r.cat, r.w, r.part))
    scatter.pass_on(0)
    bc_sums[0].groups()
    collect.complete()
    own_delivers[0].start()
    collects[1].advance()
    scatter.arrive()
    edge.receive()
    r.need(r.grad, r.resid)
    r.gain_row[...] = jnp.zeros_like(r.gain_row)
    for start, size in row_chunks():
        fresh = grad_rows(links, scatter, r.edge_slots, r.grad, r.resid, r.gains[0:1], r.gain_row, start, size)
        r.out[pl.ds(pl.multiple_of(links.c * HALF + start, EDGE), size), :] = fresh.astype(BF16)
    share.start()
    r.vec[...] = r.above_vec[...]
    put_vector(r.vec, 0, r.gain_row[0:1])
    put_vector(r.vec, 2 * (r.gain_row.shape[1] // 128), r.bc_rows[0 : CONV + 1])
    vec_sum.plane()
    vec_sum.groups()
    collects[0].advance()
    bc_sums[1].share()
    laid.plane()
    collects[1].complete()
    own_delivers[2].start()
    laid.finish()
    lay_out_heads(links, r)
    bc_sums[0].share()
    vec_sum.back()
    collects[0].complete()
    own_delivers[1].start()
    for one in bc_sums + [scatter, edge, carried, collect] + collects:
        one.finish()
    vec_sum.finish()
    lay_out_vector(r)
    share.wait()
    for deliver in delivers + own_delivers:
        deliver.arrive()
        deliver.finish()


def lay_out_heads(links, r):
    inner = r.wide.shape[1]
    heads = inner // HEADDIM
    heads_core, shard = r.g_dt.shape[1:]
    spread = head_spread(inner).astype(F32)
    row, col = iota((128, 128), 0), iota((128, 128), 1)
    blank = jnp.zeros((128 - 2 * EDGE, r.dt_out.shape[2]), F32)
    steps = [jnp.zeros((shard, 128), F32) for _ in range(2)]
    tall = [jnp.zeros((8, 128), F32) for _ in range(2)]
    for q in range(GROUP):
        lanes = slice(q * inner, q * inner + inner)
        r.step_rows[...] = jnp.concatenate([r.dt_out[q].astype(F32), blank]).T
        mine = r.step_rows[pl.ds(pl.multiple_of(links.p * shard, 8), shard), :]
        gains, taps = [], []
        for layer in range(2):
            first, second = r.wide_out[q, 16 * layer : 16 * layer + 8], r.wide_out[q, 16 * layer + 8 : 16 * layer + 16]
            taps.append(first[0 : CONV + 1])
            gains.append(first[5:6])
            place = jnp.logical_and(row - EDGE * layer == col - q * heads, jnp.logical_and(row >= EDGE * layer, row < EDGE * layer + heads))
            steps[layer] = steps[layer] + dot_exact(mine, place.astype(F32))
            place = jnp.logical_and(row == col - q * heads, row < heads).astype(F32)
            skip = dot_exact(first, spread, NT)[6:7]
            rows = jnp.concatenate([first[7:8, 0:128], second[0:1, 0:128], skip, jnp.zeros((5, 128), F32)])
            tall[layer] = tall[layer] + dot_exact(rows, place)
        for j in range(CONV + 1):
            r.g_conv_x[j, :, lanes] = jnp.concatenate([tap[j : j + 1] for tap in taps]).astype(BF16)
        r.g_gain[:, lanes] = jnp.concatenate(gains).astype(BF16)
    for layer in range(2):
        r.g_dt[layer] = steps[layer].T[0:heads_core].astype(BF16)
    for i in range(3):
        r.g_head[i] = jnp.concatenate([one[i : i + 1, 0:heads_core] for one in tall]).astype(BF16)


def lay_out_vector(r):
    def row(i):
        return r.vec_out[i // 8, i % 8 : i % 8 + 1, :]

    count = r.g_norm.shape[1] // 128
    for i in range(count):
        r.g_norm[:, i * 128 : i * 128 + 128] = jnp.concatenate([row(i), row(count + i)]).astype(BF16)
    for half in range(2):
        for j in range(CONV + 1):
            firsts = [2 * count + layer * 2 * (CONV + 1) + 2 * j + half for layer in range(2)]
            rows = jnp.concatenate([row(first) for first in firsts])
            r.g_conv_bc[j, :, half * 128 : half * 128 + 128] = rows.astype(BF16)


def flat(value):
    return [a for member in value for a in flat(member)] if isinstance(value, list) else [value]


def shaped(value, leaves):
    return [shaped(member, leaves) for member in value] if isinstance(value, list) else leaves.pop(0)


def call(body, collective, copies, outs, hbm_outs, ins, hbm_ins, scratch):
    vmem, hbm = pl.BlockSpec(memory_space=pltpu.VMEM), pl.BlockSpec(memory_space=pl.ANY)
    twins = {**{name: (a.shape, a.dtype) for name, a in hbm_ins.items()}, **hbm_outs}
    sides = [list(ins.values()), list(hbm_ins.values()), list(outs.values()), list(hbm_outs.values())]
    counts = [len(flat(side)) for side in sides]
    buffers = flat([list(scratch.values()), list(twins.values())])

    def kernel(*refs):
        refs = list(refs)
        groups = [shaped(side, refs) for side in sides]
        inner = shaped([list(scratch.values()), list(twins.values())], refs)
        sends, recvs, sems = refs
        near = dict(zip(twins, inner[1]))
        named = {**dict(zip(ins, groups[0])), **dict(zip(outs, groups[2])), **dict(zip(scratch, inner[0])), **near}
        body(Refs(dict(named, sends=sends, recvs=recvs), list(zip(groups[1] + groups[3], inner[1])), sems))

    results = pl.pallas_call(
        kernel,
        out_shape=tuple(jax.ShapeDtypeStruct(*a) for a in flat(sides[2:])),
        in_specs=[vmem] * counts[0] + [hbm] * counts[1],
        out_specs=tuple([vmem] * counts[2] + [hbm] * counts[3]),
        scratch_shapes=[pltpu.VMEM(*a) for a in buffers]
        + [pltpu.SemaphoreType.DMA((n,)) for n in (copies, copies, max(1, len(twins)))],
        compiler_params=pltpu.CompilerParams(
            vmem_limit_bytes=VMEM_BYTES, collective_id=collective, has_side_effects=True
        ),
    )(*flat(sides[:2]))
    found = shaped(sides[2:], list(results))
    return types.SimpleNamespace(**dict(zip(outs, found[0])), **dict(zip(hbm_outs, found[1])))


def on_device(resid_in, cotangent, norm_gain, w_zx, w_dt, w_bc, conv_x, conv_bc, head_params, gated_gain, w_out):
    layers, model = norm_gain.shape
    groups = lax.axis_size("z")
    shard = w_dt.shape[1]
    inner_core = conv_x.shape[2]
    inner = inner_core // GROUP
    heads_core = head_params.shape[2]
    inner_all = inner_core * lax.axis_size("head")
    length = resid_in.shape[1]
    tokens = GROUP * length
    spans = tokens // SPAN
    rows = GROUP * shard

    own_rows = ((HALF, model), F32)
    all_rows, edged_rows = ((tokens, model), BF16), ((tokens + EDGE, model), BF16)
    columns = columns_of(inner).size
    w_shape, wo_shape = ((model, columns), BF16), ((model, inner), BF16)
    scalars = ((8, tokens), F32)
    state_shape = ((spans, STATE, inner), F32)
    low_rows, steps_shape = ((tokens, inner), BF16), ((tokens, 128), F32)
    scatter_scratch = dict(
        sib=((GROUP, HALF, model), BF16),
        total=((GROUP - 1, HALF, model), BF16),
        peer=((2, HALF, model), BF16),
        via=((2, HALF // 2, model), BF16),
    )
    state_scratch = dict(
        state_low=((STATE, inner), BF16),
        decay_row=((8, inner), F32),
        states_in=((groups, STATE, inner), BF16),
        decays_in=((groups, 8, inner), F32),
    )
    saved_shapes = dict(
        y=((tokens, inner), F32),
        z=low_rows,
        x=low_rows,
        bc=((tokens, 2 * STATE), BF16),
        s=steps_shape,
        dt=steps_shape,
        dtraw=((tokens, 128), BF16),
        xin=((tokens + EDGE, inner), BF16),
        bcin=((tokens + EDGE, 2 * STATE), BF16),
        states=state_shape,
        decay=((spans, 8, inner), F32),
    )
    forward_scratch = dict(
        ext=((tokens + EDGE, inner + 2 * STATE), F32),
        local=state_shape,
        part=all_rows,
        squares=scalars,
        slots=((2 * GROUP - 1, 8, HALF), F32),
        **state_scratch,
        **scatter_scratch,
    )

    conv_x, conv_bc, head_params = [jnp.swapaxes(a, 0, 1) for a in (conv_x, conv_bc, head_params)]
    w_dt, w_out = jnp.swapaxes(w_dt, 1, 2), jnp.swapaxes(w_out, 1, 2)
    params = dict(
        norm_gain=norm_gain, conv_x=conv_x, conv_bc=conv_bc, head_params=head_params, gated_gain=gated_gain
    )
    param_scratch = dict(
        rowp=((8, inner), F32), bcp=((8, 2 * STATE), F32), headp=((8, 128), F32), gains=((layers, model), F32)
    )
    stagings = [((GROUP, rows_in, width), BF16) for rows_in, width in (
        (shard, inner), (shard, inner), (shard, STATE), (EDGE, 128), (shard, inner)
    )]
    step_rows = ((groups * GROUP * EDGE, 128), BF16)
    first = call(
        functools.partial(first_kernel, inner_all),
        0,
        200 + 14 * (groups - 1) + 2 * groups,
        dict(
            next_w=w_shape,
            next_wo=((rows, inner), BF16),
            next_normed=edged_rows,
            resid_out=own_rows,
            cot_out=own_rows,
            mixed_out=own_rows,
            fresh_out=own_rows,
            inv_out=((8, HALF), F32),
        ),
        dict(normed=edged_rows, dmix=all_rows, w=w_shape, wo=wo_shape, **saved_shapes),
        dict(
            resid=resid_in[0],
            cot=cotangent[0],
            w_zx=w_zx,
            w_dt=w_dt,
            w_bc=w_bc,
            w_out=w_out,
            **params,
        ),
        dict(),
        dict(
            **forward_scratch,
            **param_scratch,
            stagings=[stagings, stagings],
            dt_rows=step_rows,
            next_dt_rows=step_rows,
            packed_steps=((layers, GROUP, EDGE, 128), BF16),
            wide_steps=((128, 128), BF16),
        ),
    )
    second = call(
        functools.partial(second_kernel, inner_all),
        1,
        60 + 4 * groups,
        dict(block_out=((length, model), BF16), scalars_out=scalars),
        dict(wo=wo_shape, **saved_shapes),
        dict(
            wo_own=first.next_wo,
            **params,
            resid=first.fresh_out,
            cot=first.cot_out,
        ),
        dict(normed=first.next_normed, w=first.next_w),
        dict(**forward_scratch, **param_scratch),
    )
    grad_in = ((groups - 1, rows, inner), BF16)
    grad_sum = ((GROUP, shard, inner), BF16)
    bc_grad = ((groups, GROUP, shard, 2 * STATE), BF16)
    dt_grad = ((groups, EDGE, rows), BF16)
    wide_grad = ((16, inner), F32)
    vec_shape = ((2 * GROUP, 8, 128), F32)
    back_scratch = dict(
        dy=low_rows,
        gwo=wo_shape,
        normed_out=low_rows,
        prior=state_shape,
        dpre=((tokens + 2 * EDGE, inner + 2 * STATE), F32),
        flow=steps_shape,
        sums=steps_shape,
        cat=((tokens + EDGE, columns), BF16),
        bc_rows=((8, 2 * STATE), F32),
        part=edged_rows,
        gx=wo_shape,
        gz=wo_shape,
        go_in=grad_in,
        gx_in=grad_in,
        gz_in=grad_in,
        gain_row=((8, model), F32),
        edge_slots=((2 * GROUP, EDGE, model), BF16),
        **state_scratch,
        **param_scratch,
        **scatter_scratch,
    )

    def at_once(run):
        return dict(y=run.y, z=run.z, x=run.x, bc=run.bc, s=run.s, decay=run.decay)

    def later(run):
        return dict(dt=run.dt, states=run.states, dtraw=run.dtraw, xin=run.xin, bcin=run.bcin)

    third = call(
        functools.partial(third_kernel, inner_all),
        2,
        60 + 6 * groups,
        dict(
            dmix_out=all_rows,
            scalars_out=scalars,
            grad_out=own_rows,
            go_sum=grad_sum,
            gx_sum=grad_sum,
            gz_sum=grad_sum,
            gbc=bc_grad,
            gdt=dt_grad,
            wide=wide_grad,
            vec=vec_shape,
        ),
        dict(),
        dict(
            dmix=first.dmix,
            scalars=second.scalars_out,
            wo=second.wo,
            **params,
            inv=first.inv_out,
            **at_once(second),
        ),
        dict(
            w=first.next_w,
            normed=first.next_normed,
            grad=first.cot_out,
            resid=first.fresh_out,
            mixed=first.mixed_out,
            **later(second),
        ),
        back_scratch,
    )
    far = groups - 1
    dt_shape, wide_shape = (layers * EDGE, rows), (layers * 16, inner)
    half_bc = (groups, GROUP, shard, STATE)
    bc_bufs = [
        (half_bc, BF16),
        (half_bc, BF16),
        ((GROUP - 1, groups, shard, STATE), BF16),
        ((groups, shard, STATE), BF16),
        ((far, shard, STATE), BF16),
    ]
    fourth = call(
        functools.partial(fourth_kernel, inner_all),
        3,
        130 + 14 * groups,
        dict(
            out=((length, model), BF16),
            bc_out=((layers, shard, 2 * STATE), BF16),
            g_norm=(norm_gain.shape, BF16),
            g_zx=(w_zx.shape, BF16),
            g_dt=(w_dt.shape, BF16),
            g_conv_x=(conv_x.shape, BF16),
            g_conv_bc=(conv_bc.shape, BF16),
            g_head=(head_params.shape, BF16),
            g_gain=(gated_gain.shape, BF16),
            g_out=(w_out.shape, BF16),
        ),
        dict(),
        dict(
            dmix=third.dmix_out,
            scalars=third.scalars_out,
            wo=first.wo,
            **params,
            above_dt=third.gdt,
            above_wide=third.wide,
            above_vec=third.vec,
            **at_once(first),
        ),
        dict(
            w=first.w,
            normed=first.normed,
            grad=third.grad_out,
            resid=first.resid_out,
            above_x=third.gx_sum,
            above_z=third.gz_sum,
            above_o=third.go_sum,
            above_bc=third.gbc,
            **later(first),
        ),
        dict(
            **back_scratch,
            vec_out=vec_shape,
            dt_out=((GROUP, *dt_shape), BF16),
            wide_out=((GROUP, *wide_shape), F32),
            step_rows=((rows, 128), F32),
            go_sum=grad_sum,
            gx_sum=grad_sum,
            gz_sum=grad_sum,
            gbc=bc_grad,
            gdt=dt_grad,
            wide=wide_grad,
            vec=vec_shape,
            steps_all=((groups, *dt_shape), BF16),
            wide_all=(wide_shape, F32),
            bc_bufs=[bc_bufs, bc_bufs],
            vec_near=vec_shape,
            vec_far=((far, 8, 128), F32),
            dt_far=((far, *dt_shape), BF16),
            wide_far=((far, *wide_shape), F32),
        ),
    )
    return (
        second.block_out[None],
        fourth.out[None],
        fourth.g_norm,
        fourth.g_zx,
        jnp.swapaxes(fourth.g_dt, 1, 2),
        fourth.bc_out,
        *[jnp.swapaxes(a, 0, 1) for a in (fourth.g_conv_x, fourth.g_conv_bc, fourth.g_head)],
        fourth.g_gain,
        jnp.swapaxes(fourth.g_out, 1, 2),
    )


def solution(mesh):
    seq, head = mesh.shape["seq"], mesh.shape["head"]
    split = Mesh(mesh.devices.reshape(seq // GROUP, GROUP, head), ("z", "p", "head"))
    seq_axes = ("z", "p")
    specs = (
        P(None, seq_axes, None),
        P(None, seq_axes, None),
        P(),
        P(None, None, seq_axes, "head"),
        P(None, seq_axes, "head"),
        P(None, seq_axes, None),
        P(None, None, "head"),
        P(),
        P(None, None, "head"),
        P(None, "head"),
        P(None, "head", seq_axes),
    )
    return jax.shard_map(on_device, mesh=split, in_specs=specs, out_specs=specs, check_vma=False)
```

```python
import functools
import types
import typing

import jax
import jax.numpy as jnp
from jax import lax
from jax.experimental import pallas as pl
from jax.experimental.pallas import tpu as pltpu
from jax.sharding import Mesh, PartitionSpec as P

HEADDIM = 64
STATE = 128
CONV = 4
SPAN = 256
GROUP = 4
EDGE = 16
EPS = 1e-05
HIGH = lax.Precision.HIGHEST
F32, BF16 = jnp.float32, jnp.bfloat16
NN = (((1,), (0,)), ((), ()))
NT = (((1,), (1,)), ((), ()))
TN = (((0,), (0,)), ((), ()))
VMEM_BYTES = 58 << 20


def dot(a, b, dims=NN):
    return lax.dot_general(a, b, dims, preferred_element_type=F32)


def dot_exact(a, b, dims=NN):
    return lax.dot_general(a, b, dims, precision=HIGH, preferred_element_type=F32)


def dot_split(a, b, dims=NN):
    high = a.astype(BF16)
    rest = (a - high.astype(F32)).astype(BF16)
    return dot(high, b, dims) + dot(rest, b, dims)


def sigmoid(v):
    return 1.0 / (1.0 + jnp.exp(-v))


def softplus(v):
    return jnp.maximum(v, 0.0) + jnp.log1p(jnp.exp(-jnp.abs(v)))


def silu_slope(v):
    sig = sigmoid(v)
    return sig * (1.0 + v * (1.0 - sig))


def iota(shape, dim):
    return lax.broadcasted_iota(jnp.int32, shape, dim)


def head_spread(inner):
    return (iota((128, inner), 0) == lax.shift_right_logical(iota((128, inner), 1), 6)).astype(BF16)


def triangle(lower):
    rows, cols = iota((SPAN, SPAN), 0), iota((SPAN, SPAN), 1)
    return ((cols <= rows) if lower else (cols >= rows)).astype(F32)


def half_masks():
    lane = iota((SPAN, 128), 1)
    return (lane < HEADDIM).astype(BF16), (lane >= HEADDIM).astype(BF16)


def conv_taps(window, taps):
    total = jnp.broadcast_to(taps[CONV : CONV + 1], (SPAN, window.shape[1]))
    for j in range(CONV):
        total = total + taps[j : j + 1] * window[EDGE - 3 + j : EDGE - 3 + j + SPAN]
    return total


def head_pick(place, heads):
    row, col = iota((128, 128), 0), iota((128, 128), 1)
    return jnp.logical_and(row == place * heads + col, col < heads).astype(BF16)


class Columns(typing.NamedTuple):
    x: slice
    z: slice
    dt: slice
    bc: slice
    size: int


def columns_of(inner):
    first = 2 * inner + 128
    return Columns(
        slice(0, inner), slice(inner, 2 * inner), slice(2 * inner, first), slice(first, first + 2 * STATE), first + 2 * STATE
    )


def project_and_convolve(
    normed, w, rowp, bcp, headp,
    z_out, xin_out, bcin_out, x_out, bc_out, dtraw_out, dt_out, s_out, decay_out,
    ext, local, at_block,
):
    inner = x_out.shape[1]
    spans = x_out.shape[0] // SPAN

    cols = columns_of(inner)
    edge = normed[0:EDGE]
    edge_x = dot(edge, w[:, cols.x]).astype(BF16)
    edge_bc = dot(edge, w[:, cols.bc]).astype(BF16)
    xin_out[0:EDGE] = edge_x
    bcin_out[0:EDGE] = edge_bc
    ext[0:EDGE, 0:inner] = edge_x.astype(F32)
    ext[0:EDGE, inner:] = edge_bc.astype(F32)
    spread = head_spread(inner)
    low_tri = triangle(True)
    rate = -jnp.exp(headp[0:1])
    bias = headp[1:2]

    def block(q, carry):
        state_sum, decay_all = carry
        at = pl.multiple_of(q * SPAN, SPAN)
        tok = pl.ds(at, SPAN)
        after = pl.ds(pl.multiple_of(at + EDGE, EDGE), SPAN)
        at_block(q)
        product = dot(normed[after, :], w[...]).astype(BF16)
        z_out[tok, :] = product[:, cols.z]
        xin, bcin = product[:, cols.x], product[:, cols.bc]
        dtraw = product[:, cols.dt]
        xin_out[after, :] = xin
        bcin_out[after, :] = bcin
        dtraw_out[tok, :] = dtraw
        ext[after, 0:inner] = xin.astype(F32)
        ext[after, inner:] = bcin.astype(F32)
        window = pl.ds(at, SPAN + EDGE)
        pre_x = conv_taps(ext[window, 0:inner], rowp)
        x = (pre_x * sigmoid(pre_x)).astype(BF16)
        x_out[tok, :] = x
        pre_bc = conv_taps(ext[window, inner:], bcp)
        bc = (pre_bc * sigmoid(pre_bc)).astype(BF16)
        bc_out[tok, :] = bc
        dt = softplus(dtraw.astype(F32) + bias)
        s = dot_exact(low_tri, dt * rate)
        dt_out[tok, :] = dt
        s_out[tok, :] = s
        to_end = jnp.exp(s[SPAN - 1 : SPAN] - s) * dt
        weighted = (x.astype(F32) * dot_split(to_end, spread)).astype(BF16)
        fresh = dot(bc[:, :STATE], weighted, TN)
        decay = dot_split(jnp.exp(s[SPAN - 8 : SPAN]), spread)[7:8]
        local[q] = fresh
        decay_out[q] = jnp.broadcast_to(decay, (8, inner))
        return state_sum * decay + fresh, decay_all * decay

    return lax.fori_loop(0, spans, block, (jnp.zeros((STATE, inner), F32), jnp.ones((1, inner), F32)))


def mix_within_spans(x_in, bc_in, s_in, dt_in, y_out):
    inner = x_in.shape[1]

    def block(q, _):
        tok = pl.ds(pl.multiple_of(q * SPAN, SPAN), SPAN)
        x, bc, s = x_in[tok, :], bc_in[tok, :], s_in[tok, :]
        s_row, dt_row = s.T, dt_in[tok, :].T
        cb = dot(bc[:, STATE:], bc[:, :STATE], NT)
        causal = iota((SPAN, SPAN), 1) <= iota((SPAN, SPAN), 0)
        masks = half_masks()
        for pair in range(inner // 128):
            lanes = slice(pair * 128, pair * 128 + 128)
            x_pair = x[:, lanes]
            total = None
            for e in range(2):
                h = pair * 2 + e
                gap = jnp.where(causal, s[:, h : h + 1] - s_row[h : h + 1, :], -1e30)
                scores = (cb * (jnp.exp(gap) * dt_row[h : h + 1, :])).astype(BF16)
                term = dot(scores, x_pair * masks[e])
                total = term if total is None else total + term
            y_out[tok, lanes] = total
        return 0

    lax.fori_loop(0, x_in.shape[0] // SPAN, block, 0)


def entering_state(place, count, sums, decays, backward):
    inner = sums.shape[2]
    state = jnp.zeros((STATE, inner), F32)
    for turn in range(count):
        other = count - 1 - turn if backward else turn
        ahead = (place < other) if backward else (other < place)
        state = jnp.where(ahead, decays[other, 0:1] * state + sums[other].astype(F32), state)
    return state


def chain_states(state, local, decay, states_out):
    def block(q, state):
        states_out[q] = state
        return decay[q, 0:1] * state + local[q]

    lax.fori_loop(0, local.shape[0], block, state)


def mix_out(q, states, x, bc, z, s, wo, rowp, y_out, part_out, sq_out):
    inner = x.shape[1]
    tok = pl.ds(pl.multiple_of(q * SPAN, SPAN), SPAN)
    carried = dot_split(jnp.exp(s[tok, :]), head_spread(inner)) * dot(bc[tok, STATE:], states[q].astype(BF16))
    y = y_out[tok, :] + carried + rowp[6:7] * x[tok, :].astype(F32)
    y_out[tok, :] = y
    zf = z[tok, :].astype(F32)
    gated = y * (zf * sigmoid(zf))
    sq_out[:, tok] = dot_exact(jnp.ones((8, inner), F32), gated * gated, NT)
    part_out[tok, :] = dot((gated * rowp[5:6]).astype(BF16), wo[...], NT).astype(BF16)


def back_through_gate(
    inner_all, dmix, wo, y_in, z, x, bc, s, decay, token_scalars, rowp, cat_out, wide, dy_out, prior, normed_out
):
    inner = x.shape[1]
    spans = x.shape[0] // SPAN
    spread = head_spread(inner)
    gain = rowp[5:6]
    cols = columns_of(inner)

    def block(i, carry):
        grad_sum, gain_sum, skip_sum = carry
        q = spans - 1 - i
        tok = pl.ds(pl.multiple_of(q * SPAN, SPAN), SPAN)
        columns = token_scalars[:, tok].T
        inv, total_dot = columns[:, 0:1], columns[:, 1:2]
        zf = z[tok, :].astype(F32)
        sig = sigmoid(zf)
        act = zf * sig
        y = y_in[tok, :]
        gated = y * act
        d_no = dot(dmix[tok, :], wo[...])
        scaled = gated * inv
        normed_out[tok, :] = (scaled * gain).astype(BF16)
        gain_sum = gain_sum + jnp.sum(d_no * scaled, axis=0, keepdims=True)
        d_gated = inv * (d_no * gain) - gated * (inv * inv * inv * total_dot * (1.0 / inner_all))
        after = pl.ds(pl.multiple_of(q * SPAN + EDGE, EDGE), SPAN)
        cat_out[after, cols.z] = (d_gated * y * (sig * (1.0 + zf * (1.0 - sig)))).astype(BF16)
        dy = d_gated * act
        xf = x[tok, :].astype(F32)
        skip_sum = skip_sum + jnp.sum(dy * xf, axis=0, keepdims=True)
        dy_low = dy.astype(BF16)
        dy_out[tok, :] = dy_low
        scaled_dy = (dy_low.astype(F32) * dot_split(jnp.exp(s[tok, :]), spread)).astype(BF16)
        fresh = dot(bc[tok, STATE:], scaled_dy, TN)
        prior[q] = fresh
        return fresh + decay[q, 0:1] * grad_sum, gain_sum, skip_sum

    zero = jnp.zeros((1, inner), F32)
    grad_sum, gain_sum, skip_sum = lax.fori_loop(
        0, spans, block, (jnp.zeros((STATE, inner), F32), zero, zero)
    )
    decay_all = decay[0, 0:1]
    for q in range(1, spans):
        decay_all = decay_all * decay[q, 0:1]
    wide[...] = jnp.zeros_like(wide)
    wide[5:6] = gain_sum
    wide[6:7] = skip_sum
    return grad_sum, decay_all


def out_gradient(dmix, normed_out, gwo_out):
    def rows_of(i, _):
        rows = pl.ds(pl.multiple_of(i * SPAN, SPAN), SPAN)
        gwo_out[rows, :] = dot(dmix[:, rows], normed_out[...], TN).astype(BF16)
        return 0

    lax.fori_loop(0, dmix.shape[1] // SPAN, rows_of, 0)


def back_within_spans(dy_in, x_in, bc_in, s_in, dt_in, dpre, flow_out, sum_out):
    inner = x_in.shape[1]

    def block(q, _):
        at = pl.multiple_of(q * SPAN, SPAN)
        tok = pl.ds(at, SPAN)
        after = pl.ds(pl.multiple_of(at + EDGE, EDGE), SPAN)
        x_low, dy = x_in[tok, :], dy_in[tok, :]
        b, c = bc_in[tok, :STATE], bc_in[tok, STATE:]
        s, dt = s_in[tok, :], dt_in[tok, :]
        s_row = s.T
        cb = dot(b, c, NT)
        seen = iota((SPAN, SPAN), 0) <= iota((SPAN, SPAN), 1)
        masks = half_masks()
        d_cb = jnp.zeros((SPAN, SPAN), F32)
        lane = iota((SPAN, 128), 1)
        row_id = iota((128, SPAN), 0)
        sum_k = jnp.zeros((128, SPAN), F32)
        sum_t = jnp.zeros((SPAN, 128), F32)
        for pair in range(inner // 128):
            lanes = slice(pair * 128, pair * 128 + 128)
            x_pair, dy_pair = x_low[:, lanes], dy[:, lanes]
            total = None
            for e in range(2):
                h = pair * 2 + e
                d_scores = dot(x_pair * masks[e], dy_pair, NT)
                fade = jnp.exp(jnp.where(seen, s_row[h : h + 1, :] - s[:, h : h + 1], -1e30))
                dt_h = dt[:, h : h + 1]
                fade_cb = cb * fade
                term = dot((fade_cb * dt_h).astype(BF16), dy_pair * masks[e])
                total = term if total is None else total + term
                d_cb = d_cb + d_scores * (fade * dt_h)
                flow = d_scores * fade_cb
                sum_t = jnp.where(lane == h, jnp.sum(flow, axis=1, keepdims=True), sum_t)
                sum_k = jnp.where(row_id == h, jnp.sum(flow * dt_h, axis=0, keepdims=True), sum_k)
            dpre[after, lanes] = total
        d_cb_low = d_cb.astype(BF16)
        dpre[after, inner : inner + STATE] = dot(d_cb_low, c)
        dpre[after, inner + STATE :] = dot(d_cb_low, b, TN)
        flow_out[tok, :] = sum_k.T - sum_t * dt
        sum_out[tok, :] = sum_t
        return 0

    lax.fori_loop(0, x_in.shape[0] // SPAN, block, 0)


def back_through_states(
    grad, prior, decay, states, dy_in, x, bc, s_in, dt_in, dtraw, xin, bcin, rowp, bcp, headp, flow_in, sum_in,
    cat_out, row_out, bcrow_out,
    dpre, dend,
):
    inner = x.shape[1]
    spans = x.shape[0] // SPAN
    spread = head_spread(inner)
    up_tri = triangle(False)
    skip = rowp[6:7]
    rate = -jnp.exp(headp[0:1])
    bias = headp[1:2]
    width = inner + 2 * STATE

    def chain(i, grad):
        q = spans - 1 - i
        before = prior[q] + decay[q, 0:1] * grad
        dend[q] = grad
        return before

    lax.fori_loop(0, spans, chain, grad)
    dpre[0:EDGE] = jnp.zeros((EDGE, width), F32)
    dpre[EDGE + spans * SPAN :] = jnp.zeros((EDGE, width), F32)
    bcrow_out[...] = jnp.zeros_like(bcrow_out)
    cols = columns_of(inner)
    cat_out[0:EDGE, cols.z] = jnp.zeros((EDGE, inner), BF16)
    cat_out[0:EDGE, cols.dt] = jnp.zeros((EDGE, 128), BF16)

    def block(q, _):
        at = pl.multiple_of(q * SPAN, SPAN)
        tok = pl.ds(at, SPAN)
        after = pl.ds(pl.multiple_of(at + EDGE, EDGE), SPAN)
        window = pl.ds(at, SPAN + EDGE)
        x_low, dy = x[tok, :], dy_in[tok, :]
        xf, dyf = x_low.astype(F32), dy.astype(F32)
        b, c = bc[tok, :STATE], bc[tok, STATE:]
        s, dt = s_in[tok, :], dt_in[tok, :]
        exp_s = jnp.exp(s)
        to_end = jnp.exp(s[SPAN - 1 : SPAN] - s)
        w = to_end * dt
        w_all, s_all = dot_split(w, spread), dot_split(exp_s, spread)
        state, grad = states[q], dend[q]
        state_low, grad_low = state.astype(BF16), grad.astype(BF16)
        carried = s_all * dot(c, state_low)
        ds = dot_split(dyf * carried, spread, NT)
        d_c = dot((dyf * s_all).astype(BF16), state_low, NT)
        d_w = dot(b, grad_low)
        d_b = dot((xf * w_all).astype(BF16), grad_low, NT)
        dx = dpre[after, 0:inner] + dyf * skip + d_w * w_all
        dsw = dot_split(d_w * xf, spread, NT)
        end = dsw * w
        ds = ds + flow_in[tok, :] - end
        held = dot_split(jnp.broadcast_to(jnp.sum(grad * state, axis=0, keepdims=True), (8, inner)), spread, NT)[0:1]
        last = jnp.sum(end, axis=0, keepdims=True) + held * exp_s[SPAN - 1 : SPAN]
        ds = ds + jnp.where(iota((SPAN, 128), 0) == SPAN - 1, last, 0.0)
        da = dot_exact(up_tri, ds)
        d_dt = sum_in[tok, :] + dsw * to_end + da * rate
        d_raw = d_dt * sigmoid(dtraw[tok, :].astype(F32) + bias)
        d_raw = jnp.where(iota((SPAN, 128), 1) < inner // HEADDIM, d_raw, 0.0)
        row_out[7:8, 0:128] += jnp.sum(da * (dt * rate), axis=0, keepdims=True)
        row_out[8:9, 0:128] += jnp.sum(d_raw, axis=0, keepdims=True)
        d_low = d_raw.astype(BF16)
        cat_out[after, cols.dt] = d_low

        win_x = xin[window, :].astype(F32)
        d_x = dx * silu_slope(conv_taps(win_x, rowp))
        dpre[after, 0:inner] = d_x
        for j in range(CONV):
            row_out[j : j + 1] += jnp.sum(d_x * win_x[EDGE - 3 + j : EDGE - 3 + j + SPAN], axis=0, keepdims=True)
        row_out[CONV : CONV + 1] += jnp.sum(d_x, axis=0, keepdims=True)
        win_bc = bcin[window, :].astype(F32)
        d_bc = dpre[after, inner:] + jnp.concatenate([d_b, d_c], axis=1)
        d_bc = d_bc * silu_slope(conv_taps(win_bc, bcp))
        dpre[after, inner:] = d_bc
        for j in range(CONV):
            bcrow_out[j : j + 1] += jnp.sum(d_bc * win_bc[EDGE - 3 + j : EDGE - 3 + j + SPAN], axis=0, keepdims=True)
        bcrow_out[CONV : CONV + 1] += jnp.sum(d_bc, axis=0, keepdims=True)
        return 0

    lax.fori_loop(0, spans, block, 0)

    def back(window, taps, rows):
        total = None
        for j in range(CONV):
            term = taps[j : j + 1] * window[CONV - 1 - j : CONV - 1 - j + rows]
            total = term if total is None else total + term
        return total.astype(BF16)

    cat_out[0:EDGE, cols.x] = back(dpre[0 : 2 * EDGE, 0:inner], rowp, EDGE)
    cat_out[0:EDGE, cols.bc] = back(dpre[0 : 2 * EDGE, inner:], bcp, EDGE)

    def conv_block(q, _):
        after = pl.ds(pl.multiple_of(q * SPAN + EDGE, EDGE), SPAN)
        window = pl.ds(pl.multiple_of(q * SPAN + EDGE, EDGE), SPAN + EDGE)
        cat_out[after, cols.x] = back(dpre[window, 0:inner], rowp, SPAN)
        cat_out[after, cols.bc] = back(dpre[window, inner:], bcp, SPAN)
        return 0

    lax.fori_loop(0, spans, conv_block, 0)


def project_back_edge(cat, w, dn_out):
    cols = columns_of((w.shape[1] - 3 * STATE) // 2)
    dn_out[0:EDGE] = (
        dot(cat[0:EDGE, cols.x], w[:, cols.x], NT) + dot(cat[0:EDGE, cols.bc], w[:, cols.bc], NT)
    ).astype(BF16)


def project_back(q, cat, w, dn_out):
    after = pl.ds(pl.multiple_of(q * SPAN + EDGE, EDGE), SPAN)
    dn_out[after, :] = dot(cat[after, :], w[...], NT).astype(BF16)


def for_row_blocks(grad, body):
    groups, rows = grad

    def one(g, _):
        body(pl.ds(pl.multiple_of(g * rows, 128), rows) if rows % 128 == 0 else pl.ds(g * rows, rows), g)
        return 0

    if rows % 128 == 0:
        lax.fori_loop(0, groups, one, 0)
    else:
        for g in range(groups):
            one(g, 0)


def x_gradient(cat, normed, gx_out):
    cols = columns_of(gx_out.shape[1])

    def body(at, _):
        total = dot(normed[EDGE:, at], cat[EDGE:, cols.x], TN) + dot(normed[0:EDGE, at], cat[0:EDGE, cols.x], TN)
        gx_out[at, :] = total.astype(BF16)

    for_row_blocks((normed.shape[1] // SPAN, SPAN), body)


def z_gradient(cat, normed, gz_out):
    cols = columns_of(gz_out.shape[1])

    def body(at, _):
        gz_out[at, :] = dot(normed[EDGE:, at], cat[EDGE:, cols.z], TN).astype(BF16)

    for_row_blocks((normed.shape[1] // SPAN, SPAN), body)


def small_gradients(cat, normed, gbc_out, gdt_out):
    groups, parts, shard, _ = gbc_out.shape
    cols = columns_of((cat.shape[1] - 3 * STATE) // 2)

    def body(at, g):
        edge, tokens = normed[0:EDGE, at], normed[EDGE:, at]
        bc = dot(tokens, cat[EDGE:, cols.bc], TN) + dot(edge, cat[0:EDGE, cols.bc], TN)
        gbc_out[g] = bc.reshape(parts, shard, 2 * STATE).astype(BF16)
        gdt_out[g] = dot(cat[EDGE:, cols.dt], tokens, TN)[0:EDGE].astype(BF16)

    for_row_blocks((groups, parts * shard), body)


HALF = 128
MESH = pl.DeviceIdType.MESH


class Links:
    def __init__(self, sends, recvs):
        self.z, self.p, self.c = lax.axis_index("z"), lax.axis_index("p"), lax.axis_index("head")
        self.groups = lax.axis_size("z")
        self.sends, self.recvs, self.used = sends, recvs, 0

    def copy(self, src, dst, device):
        i = self.used
        self.used += 1
        return pltpu.make_async_remote_copy(
            src_ref=src, dst_ref=dst, send_sem=self.sends.at[i], recv_sem=self.recvs.at[i],
            device_id=device, device_id_type=MESH,
        )

    def local(self, src, dst):
        i = self.used
        self.used += 1
        return pltpu.make_async_copy(src, dst, self.sends.at[i])

    def at(self, k, e):
        return (self.z, lax.bitwise_xor(self.p, jnp.int32(k)), lax.bitwise_xor(self.c, jnp.int32(e)))

    def last_of_plane(self):
        return jnp.logical_and(self.p == GROUP - 1, self.c == 1)

    def greet(self, plane=False, sibling=False, groups=False, edge=0):
        barrier = pltpu.get_barrier_semaphore()
        z, count = self.z, self.groups
        above = z < count - 1

        def signal(device):
            pl.semaphore_signal(barrier, 1, device_id=device, device_id_type=MESH)

        self.expected = jnp.int32(0)
        for k in range(GROUP):
            for e in range(2):
                if (k or e) if plane else (sibling and e and not k):
                    signal(self.at(k, e))
                    self.expected = self.expected + 1
        if groups:
            for k in range(1, count):
                signal((lax.rem(z + k, count), self.p, self.c))
            self.expected = self.expected + (count - 1)
        sending = jnp.logical_and(self.last_of_plane(), above)
        if edge == 1:
            pl.when(z > 0)(lambda: signal((z - 1, jnp.int32(GROUP - 1), jnp.int32(1))))
            self.expected = self.expected + 2 * GROUP * sending.astype(jnp.int32)
        if edge == -1:

            @pl.when(sending)
            def _():
                for p in range(GROUP):
                    for c in range(2):
                        signal((z + 1, jnp.int32(p), jnp.int32(c)))

            self.expected = self.expected + (z > 0).astype(jnp.int32)

    def meet(self):
        pl.semaphore_wait(pltpu.get_barrier_semaphore(), self.expected)

    def start_barrier(self, **who):
        self.greet(**who)
        self.meet()


class Chain:
    def __init__(self, links, pieces):
        z, p, c, groups = links.z, links.p, links.c, links.groups
        self.steps, self.now = [], 0
        for step in range(1, groups):
            found = []
            up, down = z - step + 1, z + step - 1
            for piece in pieces:
                block = piece(jnp.maximum(up, 0))
                sending = jnp.logical_and(up >= 0, z < groups - 1)
                found.append((sending, z - step >= 0, links.copy(block, block, (z + 1, p, c))))
                block = piece(jnp.minimum(down, groups - 1))
                sending = jnp.logical_and(down < groups, z > 0)
                found.append((sending, z + step < groups, links.copy(block, block, (z - 1, p, c))))
            self.steps.append(found)

    def begin(self, piece=None):
        for sending, _, copy in self.steps[0] if piece is None else self.steps[0][2 * piece : 2 * piece + 2]:
            pl.when(sending)(copy.start)

    def advance(self):
        if self.now + 1 < len(self.steps):
            for (_, receiving, copy), (sending, _, later) in zip(self.steps[self.now], self.steps[self.now + 1]):
                pl.when(receiving)(copy.wait_recv)
                pl.when(sending)(later.start)
            self.now += 1

    def complete(self):
        while self.now + 1 < len(self.steps):
            self.advance()
        for _, receiving, copy in self.steps[-1]:
            pl.when(receiving)(copy.wait_recv)

    def finish(self):
        for found in self.steps:
            for sending, _, copy in found:
                pl.when(sending)(copy.wait_send)


class Swap:
    def __init__(self, links, shard, staging, out, lanes, width):
        self.links, self.staging, self.out, self.lanes = links, staging, out, lanes

        def source(k):
            to = lax.bitwise_xor(links.p, jnp.int32(k))
            if len(shard.shape) == 3:
                return shard.at[to]
            if shard.shape[1] == width:
                return shard
            return shard.at[:, pl.ds(pl.multiple_of(to * width, 128), width)]

        self.copies = [links.copy(source(k), staging.at[links.p], links.at(k, 0)) for k in (3, 1, 2)]
        self.keep = links.local(source(0), staging.at[links.p])

    def start(self):
        for copy in self.copies:
            copy.start()

    def settle(self):
        self.keep.wait()
        for copy in self.copies:
            copy.wait_recv()
        parts, shard, width = self.staging.shape
        rows = parts * shard
        first = self.links.z * rows if self.out.shape[0] > rows else 0
        if shard % EDGE == 0:
            for j in range(parts):
                self.out[pl.ds(pl.multiple_of(first + j * shard, EDGE), shard), self.lanes] = self.staging[j]
        else:
            block = self.staging[...].astype(F32).reshape(rows, width).astype(BF16)
            self.out[pl.ds(pl.multiple_of(first, EDGE), rows), self.lanes] = block

    def finish(self):
        for copy in self.copies:
            copy.wait_send()


class Halve:
    def __init__(self, links, grad, arrived, sums):
        self.links, self.grad, self.arrived, self.sums = links, grad, arrived, sums
        z, groups = links.z, links.groups
        self.rows, self.steps, self.now = grad.shape[0] // groups, [], 0
        first, bit = 0, 1
        while bit < groups:
            low = lax.rem(z, bit)
            mine = lax.rem(lax.div(z, bit), 2)
            device = (z + bit - 2 * bit * mine, links.p, links.c)
            found = []
            for j in range(groups // (2 * bit)):
                away = j * 2 * bit + (1 - mine) * bit + low
                kept = j * 2 * bit + mine * bit + low
                copy = links.copy(self.held(away), arrived.at[first + j], device)
                found.append((first + j, self.held(kept), copy))
            self.steps.append(found)
            self.before = (first, 2 * bit)
            first, bit = first + groups // (2 * bit), 2 * bit

    def held(self, target):
        if not self.steps:
            return self.grad.at[pl.ds(pl.multiple_of(target * self.rows, EDGE), self.rows), :]
        first, size = self.before
        return self.arrived.at[first + lax.div(target, size)]

    def begin(self):
        for _, _, copy in self.steps[0]:
            copy.start()

    def advance(self):
        for slot, held, copy in self.steps[self.now]:
            copy.wait_recv()

            def add(i, _, slot=slot, held=held):
                at = pl.ds(pl.multiple_of(i * 32, 32), 32)
                total = self.arrived[slot, at, :].astype(F32) + held[at, :].astype(F32)
                self.arrived[slot, at, :] = total.astype(BF16)
                return 0

            lax.fori_loop(0, self.rows // 32, add, 0)
        self.now += 1
        for _, _, copy in self.steps[self.now]:
            copy.start()

    def complete(self):
        while self.now + 1 < len(self.steps):
            self.advance()
        ((slot, held, copy),) = self.steps[-1]
        copy.wait_recv()
        total = self.arrived[slot].astype(F32) + held[...].astype(F32)
        shard = self.sums.shape[1]
        for j in range(GROUP):
            self.sums[j] = total[j * shard : (j + 1) * shard].astype(BF16)

    def finish(self):
        for found in self.steps:
            for _, _, copy in found:
                copy.wait_send()


class Deliver:
    def __init__(self, links, sums, out):
        self.links, self.sums, self.out = links, sums, out
        inner = sums.shape[2]
        self.mine = pl.ds(pl.multiple_of(links.p * inner, 128), inner)
        self.copies = [
            links.copy(sums.at[lax.bitwise_xor(links.p, jnp.int32(k))], out.at[:, self.mine], links.at(k, 0))
            for k in (3, 1, 2)
        ]

    def start(self):
        for copy in self.copies:
            copy.start()
        self.out[:, self.mine] = self.sums[self.links.p]

    def arrive(self):
        for copy in self.copies:
            copy.wait_recv()

    def finish(self):
        for copy in self.copies:
            copy.wait_send()


class States:
    def __init__(self, links, backward, state, decay, states, decays):
        z, groups = links.z, links.groups
        self.links, self.refs = links, (state, decay, states, decays)
        self.found = []
        for k in range(1, groups):
            to, source = (z - k, z + k) if backward else (z + k, z - k)
            sending, receiving = (to >= 0, source < groups) if backward else (to < groups, source >= 0)
            device = (jnp.clip(to, 0, groups - 1), links.p, links.c)
            pair = [links.copy(state, states.at[z], device), links.copy(decay, decays.at[z], device)]
            self.found.append((sending, receiving, pair))

    def start(self):
        for sending, _, pair in self.found:

            @pl.when(sending)
            def _(pair=pair):
                for copy in pair:
                    copy.start()

    def arrive(self):
        for _, receiving, pair in self.found:

            @pl.when(receiving)
            def _(pair=pair):
                for copy in pair:
                    copy.wait_recv()

    def finish(self):
        for sending, _, pair in self.found:

            @pl.when(sending)
            def _(pair=pair):
                for copy in pair:
                    copy.wait_send()


class Gather:
    def __init__(self, links, out, base):
        self.links, self.out, self.base = links, out, base

        def place(k, half=None):
            row = base + lax.bitwise_xor(links.p, jnp.int32(k)) * (2 * HALF) + links.c * HALF
            if half is None:
                return out.at[pl.ds(pl.multiple_of(row, EDGE), HALF), :]
            return out.at[pl.ds(pl.multiple_of(row + half * (HALF // 2), EDGE), HALF // 2), :]

        def send(k, half, to, e=0):
            return links.copy(place(k, half), place(k, half), links.at(to, e))

        self.near = {(to, half): send(0, half, to) for half in range(2) for to in (1, 2)}
        self.relays = {0: send(1, 0, 2), 1: send(2, 1, 1)}
        self.own_share = send(0, None, 0, 1)
        self.shares = {(k, half): send(k, half, 0, 1) for k in (1, 2, 3) for half in range(2)}

    def own(self, start, size):
        row = self.base + self.links.p * (2 * HALF) + self.links.c * HALF + start
        return pl.ds(pl.multiple_of(row, EDGE), size)

    def start(self):
        for which in ((1, 0), (2, 1), (1, 1), (2, 0)):
            self.near[which].start()
        self.own_share.start()

    def pass_on(self):
        for k, half in ((1, 0), (2, 1)):
            self.near[k, half].wait_recv()
            self.relays[half].start()
            self.shares[k, half].start()
        for k, half in ((1, 1), (2, 0)):
            self.near[k, half].wait_recv()
            self.shares[k, half].start()
        for half in range(2):
            self.relays[half].wait_recv()
            self.shares[3, half].start()

    def finish(self):
        shares = [self.own_share, *self.shares.values()]
        for copy in shares:
            copy.wait_recv()
        for copy in [*shares, *self.near.values(), *self.relays.values()]:
            copy.wait_send()


class EdgeForward:
    def __init__(self, links, gather):
        self.links = links
        tail = gather.out.at[gather.own(HALF - EDGE, EDGE), :]
        first = links.used
        links.used += 2 * GROUP + 1
        recv = links.recvs.at[first + 2 * GROUP]
        self.out = gather.out
        self.copies = [
            pltpu.make_async_remote_copy(
                src_ref=tail, dst_ref=gather.out.at[0:EDGE, :], send_sem=links.sends.at[first + p * 2 + c], recv_sem=recv,
                device_id=(links.z + 1, jnp.int32(p), jnp.int32(c)), device_id_type=MESH,
            )
            for p in range(GROUP)
            for c in range(2)
        ]
        self.sending = jnp.logical_and(links.last_of_plane(), links.z < links.groups - 1)

    def start(self):
        @pl.when(self.sending)
        def _():
            for copy in self.copies:
                copy.start()

        @pl.when(self.links.z == 0)
        def _():
            self.out[0:EDGE, :] = jnp.zeros((EDGE, self.out.shape[1]), self.out.dtype)

    def finish(self):
        pl.when(self.links.z > 0)(self.copies[0].wait_recv)

        @pl.when(self.sending)
        def _():
            for copy in self.copies:
                copy.wait_send()


class Scatter:
    def __init__(self, links, part, base, sib, total, peer, via):
        self.links, self.part, self.base = links, part, base
        self.sib, self.total, self.peer, self.via = sib, total, peer, via
        other = 1 - links.c
        self.to_sibling = {
            k: links.copy(part.at[self.rows(k, other, 0, HALF), :], sib.at[k], links.at(0, 1)) for k in (3, 1, 2, 0)
        }
        halves = [slice(0, HALF // 2), slice(HALF // 2, HALF)]
        self.across = [links.copy(total.at[2, halves[i]], via.at[i], links.at(i + 1, 0)) for i in range(2)]
        self.to_peer = {
            (k, i): links.copy(total.at[k - 1, halves[i]], peer.at[k - 1, halves[i]], links.at(k, 0))
            for k in (1, 2)
            for i in range(2)
        }

    def rows(self, k, c, start, size):
        row = self.base + lax.bitwise_xor(self.links.p, jnp.int32(k)) * (2 * HALF) + c * HALF + start
        return pl.ds(pl.multiple_of(row, EDGE), size)

    def pass_on(self, k):
        self.to_sibling[k].wait_recv()
        if k == 0:
            for i in (1, 0):
                self.across[i].wait_recv()

                def join(j, _, i=i):
                    at = pl.ds(pl.multiple_of(i * (HALF // 2) + j * 32, 32), 32)
                    came = self.via[i, pl.ds(pl.multiple_of(j * 32, 32), 32), :].astype(F32)
                    self.total[1 - i, at, :] = (self.total[1 - i, at, :].astype(F32) + came).astype(BF16)
                    return 0

                lax.fori_loop(0, HALF // 64, join, 0)
                self.to_peer[2 - i, i].start()
            return

        def add(i, _):
            at = pl.ds(pl.multiple_of(i * 32, 32), 32)
            mine = self.part[self.rows(k, self.links.c, i * 32, 32), :].astype(F32)
            self.total[k - 1, at, :] = (mine + self.sib[k, at, :].astype(F32)).astype(BF16)
            return 0

        lax.fori_loop(0, HALF // 32, add, 0)
        for copy in self.across if k == 3 else [self.to_peer[k, k - 1]]:
            copy.start()

    def arrive(self):
        for copy in self.to_peer.values():
            copy.wait_recv()

    def own(self, start, size):
        at = pl.ds(start, size)
        total = self.part[self.rows(0, self.links.c, start, size), :].astype(F32) + self.sib[0, at, :].astype(F32)
        for k in range(2):
            total = total + self.peer[k, at, :].astype(F32)
        return total

    def finish(self):
        for copy in [*self.to_sibling.values(), *self.across, *self.to_peer.values()]:
            copy.wait_send()


class SmallSum:
    def __init__(self, links, squares, slots):
        self.links, self.squares, self.slots = links, squares, slots
        self.copies = [
            links.copy(squares.at[:, self.lanes(k, e)], slots.at[2 * k + e - 1], links.at(k, e))
            for k in range(GROUP)
            for e in range(2)
            if k or e
        ]

    def lanes(self, k, e):
        links = self.links
        column = lax.bitwise_xor(links.p, jnp.int32(k)) * (2 * HALF) + lax.bitwise_xor(links.c, jnp.int32(e)) * HALF
        return pl.ds(pl.multiple_of(column, HALF), HALF)

    def start(self):
        for copy in self.copies:
            copy.start()

    def total(self):
        for copy in self.copies:
            copy.wait_recv()
        total = self.squares[:, self.lanes(0, 0)]
        for i in range(len(self.copies)):
            total = total + self.slots[i]
        return total

    def finish(self):
        for copy in self.copies:
            copy.wait_send()


class SmallGather:
    def __init__(self, links, out):
        self.out = out
        self.lanes = pl.ds(pl.multiple_of(links.p * (2 * HALF) + links.c * HALF, HALF), HALF)
        self.copies = [
            links.copy(out.at[:, self.lanes], out.at[:, self.lanes], links.at(k, e))
            for k in range(GROUP)
            for e in range(2)
            if k or e
        ]

    def start(self):
        for copy in self.copies:
            copy.start()

    def finish(self):
        for copy in self.copies:
            copy.wait()


def row_chunks(size=32):
    return [(start, size) for start in range(0, HALF, size)]


def rms_of(rows):
    return lax.rsqrt(jnp.mean(rows * rows, axis=-1, keepdims=True) + EPS)


def as_tile(columns):
    lane = iota((HALF, HALF), 1)
    wide = jnp.zeros((HALF, HALF), F32)
    for i, column in enumerate(columns):
        wide = jnp.where(lane == i, column, wide)
    return wide.T[0:8]


def grad_rows(links, scatter, edge_slots, grad, resid, gain, gain_out, start, size):
    at = slice(start, start + size)
    d_normed = scatter.own(start, size)
    if start + size == HALF:
        extra = edge_slots[0].astype(F32)
        for i in range(1, 2 * GROUP):
            extra = extra + edge_slots[i].astype(F32)
        used = jnp.logical_and(links.last_of_plane(), links.z < links.groups - 1)
        extra = jnp.where(used, extra, 0.0)
        d_normed = d_normed + jnp.concatenate([jnp.zeros((size - EDGE, extra.shape[1]), F32), extra])
    rows = resid[at]
    inv_rms = rms_of(rows)
    gain_sum = jnp.sum(d_normed * rows * inv_rms, axis=0, keepdims=True)
    gain_out[0:1] = gain_sum if start == 0 else gain_out[0:1] + gain_sum
    d_hidden = d_normed * gain[...]
    return (
        grad[at]
        + inv_rms * d_hidden
        - rows * (inv_rms * inv_rms * inv_rms * jnp.mean(d_hidden * rows, axis=-1, keepdims=True))
    )


class EdgeBackward:
    def __init__(self, links, part, slots):
        self.links = links
        first = links.used
        links.used += 2 * GROUP + 1
        me = links.p * 2 + links.c
        self.send = pltpu.make_async_remote_copy(
            src_ref=part.at[0:EDGE, :], dst_ref=slots.at[me], send_sem=links.sends.at[first], recv_sem=links.recvs.at[first + me],
            device_id=(links.z - 1, jnp.int32(GROUP - 1), jnp.int32(1)), device_id_type=MESH,
        )
        self.recvs = [
            pltpu.make_async_remote_copy(
                src_ref=part.at[0:EDGE, :], dst_ref=slots.at[i], send_sem=links.sends.at[first], recv_sem=links.recvs.at[first + i],
                device_id=(links.z, links.p, 1 - links.c), device_id_type=MESH,
            )
            for i in range(2 * GROUP)
        ]
        self.receiving = jnp.logical_and(links.last_of_plane(), links.z < links.groups - 1)

    def start(self):
        pl.when(self.links.z > 0)(self.send.start)

    def receive(self):
        @pl.when(self.receiving)
        def _():
            for copy in self.recvs:
                copy.wait_recv()

    def finish(self):
        pl.when(self.links.z > 0)(self.send.wait_send)


class BcSum:
    def __init__(self, links, bc, out, bufs):
        self.links, self.bc, self.out = links, bc, out
        self.sib, self.chip, self.peer, self.total, self.far = bufs
        p, c, groups = links.p, links.c, links.groups
        self.own = pl.ds(pl.multiple_of(c * STATE, STATE), STATE)
        other = pl.ds(pl.multiple_of((1 - c) * STATE, STATE), STATE)
        self.first = [links.copy(bc.at[:, :, :, other], self.sib, links.at(0, 1))]
        self.second = [
            links.copy(self.chip.at[:, lax.bitwise_xor(p, jnp.int32(k))], self.peer.at[k - 1], links.at(k, 0))
            for k in (3, 1, 2)
        ]
        self.third = []
        for k in range(1, groups):
            to = lax.rem(links.z + k, groups)
            self.third.append(links.copy(self.total.at[to], self.far.at[k - 1], (to, p, c)))
        self.fourth = [links.copy(out.at[:, self.own], out.at[:, self.own], links.at(0, 1))]

    @staticmethod
    def begin(copies):
        for copy in copies:
            copy.start()

    @staticmethod
    def arrive(copies):
        for copy in copies:
            copy.wait_recv()

    def cores(self):
        self.begin(self.first)

    def plane(self):
        self.arrive(self.first)

        def add(i, _):
            for q in range(GROUP):
                mine = self.bc[i, q, :, self.own].astype(F32)
                self.chip[i, q] = (mine + self.sib[i, q].astype(F32)).astype(BF16)
            return 0

        lax.fori_loop(0, self.links.groups, add, 0)
        self.begin(self.second)

    def groups(self):
        self.arrive(self.second)

        def add(i, _):
            total = self.chip[i, self.links.p].astype(F32)
            for k in range(GROUP - 1):
                total = total + self.peer[k, i].astype(F32)
            self.total[i] = total.astype(BF16)
            return 0

        lax.fori_loop(0, self.links.groups, add, 0)
        self.begin(self.third)

    def share(self):
        self.arrive(self.third)
        total = self.total[self.links.z].astype(F32)
        for k in range(self.links.groups - 1):
            total = total + self.far[k].astype(F32)
        self.out[:, self.own] = total.astype(BF16)
        self.begin(self.fourth)

    def finish(self):
        self.arrive(self.fourth)
        for copy in self.first + self.second + self.third + self.fourth:
            copy.wait_send()


class LaidOut:
    def __init__(self, links, dt, wide, dt_out, wide_out, dt_far, wide_far):
        self.links, self.refs = links, (dt, wide, dt_out, wide_out, dt_far, wide_far)
        z, p, c, groups = links.z, links.p, links.c, links.groups
        self.first, self.second = [], []
        for k in range(1, groups):
            to = lax.rem(z + k, groups)
            self.first.append(links.copy(dt.at[to], dt_far.at[k - 1], (to, p, c)))
            self.first.append(links.copy(wide, wide_far.at[k - 1], (to, p, c)))
        for k in range(1, GROUP):
            self.second.append(links.copy(dt_out.at[p], dt_out.at[p], links.at(k, 0)))
            self.second.append(links.copy(wide_out.at[p], wide_out.at[p], links.at(k, 0)))

    def groups(self):
        BcSum.begin(self.first)

    def plane(self):
        BcSum.arrive(self.first)
        dt, wide, dt_out, wide_out, dt_far, wide_far = self.refs
        dt_total, wide_total = dt[self.links.z].astype(F32), wide[...]
        for k in range(self.links.groups - 1):
            dt_total = dt_total + dt_far[k].astype(F32)
            wide_total = wide_total + wide_far[k]
        dt_out[self.links.p] = dt_total.astype(BF16)
        wide_out[self.links.p] = wide_total
        BcSum.begin(self.second)

    def finish(self):
        BcSum.arrive(self.second)
        for copy in self.first + self.second:
            copy.wait_send()


class VecSum:
    def __init__(self, links, vec, out, near, far):
        self.links, self.refs = links, (vec, out, near, far)
        z, p, c, groups = links.z, links.p, links.c, links.groups
        self.first, self.second, self.third = [], [], []
        for k in range(GROUP):
            for e in range(2):
                if k or e:
                    to = lax.bitwise_xor(p, jnp.int32(k)) * 2 + lax.bitwise_xor(c, jnp.int32(e))
                    self.first.append(links.copy(vec.at[to], near.at[2 * k + e - 1], links.at(k, e)))
                    self.third.append(links.copy(out.at[p * 2 + c], out.at[p * 2 + c], links.at(k, e)))
        for k in range(1, groups):
            self.second.append(links.copy(near.at[7], far.at[k - 1], (lax.rem(z + k, groups), p, c)))

    def plane(self):
        BcSum.begin(self.first)

    def groups(self):
        BcSum.arrive(self.first)
        vec, _, near, _ = self.refs
        total = vec[self.links.p * 2 + self.links.c]
        for slot in range(2 * GROUP - 1):
            total = total + near[slot]
        near[7] = total
        BcSum.begin(self.second)

    def back(self):
        BcSum.arrive(self.second)
        _, out, near, far = self.refs
        total = near[7]
        for k in range(self.links.groups - 1):
            total = total + far[k]
        out[self.links.p * 2 + self.links.c] = total
        BcSum.begin(self.third)

    def finish(self):
        BcSum.arrive(self.third)
        for copy in self.first + self.second + self.third:
            copy.wait_send()


class Refs:
    def __init__(self, refs, twins, sems):
        self.__dict__.update(refs)
        self.twins = {id(near): (far, near, sems.at[i]) for i, (far, near) in enumerate(twins)}
        self.waits = []

    def fetch(self, *refs):
        for ref in refs:
            far, near, sem = self.twins[id(ref)]
            pltpu.make_async_copy(far, near, sem).start()

    def need(self, *refs):
        for ref in refs:
            pltpu.make_async_copy(*self.twins[id(ref)]).wait()

    def flush(self, *refs):
        for ref in refs:
            far, near, sem = self.twins[id(ref)]
            self.waits.append(pltpu.make_async_copy(near, far, sem))
            self.waits[-1].start()

    def done(self):
        for copy in self.waits:
            copy.wait()


def weight_chain(links, w, steps, inner):
    rows, step_rows = w.shape[0] // links.groups, steps.shape[0] // links.groups
    cols = columns_of(inner)
    half = pl.ds(pl.multiple_of(cols.bc.start + links.c * STATE, STATE), STATE)

    def at(index):
        return pl.ds(pl.multiple_of(index * rows, EDGE), rows)

    pieces = [
        lambda i: w.at[at(i), cols.x],
        lambda i: w.at[at(i), cols.z],
        lambda i: w.at[at(i), half],
        lambda i: steps.at[pl.ds(pl.multiple_of(i * step_rows, EDGE), step_rows), :],
    ]
    return Chain(links, pieces), links.copy(w.at[:, half], w.at[:, half], links.at(0, 1))


def pack_steps(w_dt, steps_out, wide):
    heads_core, shard = w_dt.shape
    heads = heads_core // GROUP
    wide[...] = jnp.zeros_like(wide)
    wide[0:heads_core, 0:shard] = w_dt
    row, col = iota((EDGE, 128), 0), iota((EDGE, 128), 1)
    for q in range(GROUP):
        pick = jnp.logical_and(col == q * heads + row, row < heads).astype(BF16)
        steps_out[q] = dot(pick, wide[...]).astype(BF16)


def unpack_steps(steps, w, shard, inner):
    lanes = columns_of(inner).dt
    rows = GROUP * shard
    blank = jnp.zeros((128 - EDGE, 128), F32)

    def block(g, _):
        parts = []
        for j in range(GROUP):
            at = pl.ds(pl.multiple_of(g * (GROUP * EDGE) + j * EDGE, EDGE), EDGE)
            parts.append(jnp.concatenate([steps[at, :].astype(F32), blank]).T[0:shard])
        w[pl.ds(pl.multiple_of(g * rows, EDGE), rows), lanes] = jnp.concatenate(parts).astype(BF16)
        return 0

    lax.fori_loop(0, w.shape[0] // rows, block, 0)


def prepare(links, r, layer):
    inner = r.rowp.shape[1]
    heads_core = r.head_params.shape[2]
    lanes = pl.ds(pl.multiple_of(links.p * inner, 128), inner)
    r.gains[...] = r.norm_gain[...].astype(F32)
    r.headp[...] = jnp.zeros_like(r.headp)
    for i in range(3):
        r.headp[i : i + 1, 0:heads_core] = r.head_params[i, layer : layer + 1, :]
    mine = dot_exact(r.headp[...], head_pick(links.p, inner // HEADDIM).astype(F32))
    r.headp[...] = mine
    r.rowp[...] = jnp.zeros_like(r.rowp)
    r.rowp[0 : CONV + 1] = r.conv_x[:, :, lanes].astype(F32)[:, layer]
    r.rowp[5:6] = r.gated_gain[:, lanes].astype(F32)[layer : layer + 1]
    r.rowp[6:7] = dot_exact(mine, head_spread(inner).astype(F32))[2:3]
    r.bcp[...] = jnp.zeros_like(r.bcp)
    r.bcp[0 : CONV + 1] = r.conv_bc[...].astype(F32)[:, layer]


def out_chain(links, wo):
    rows = wo.shape[0] // links.groups
    return Chain(links, [lambda i: wo.at[pl.ds(pl.multiple_of(i * rows, EDGE), rows), :]])


def weight_swaps(links, r, layer, w, steps, wo):
    inner = wo.shape[1]
    cols = columns_of(inner)
    stagings = r.stagings[layer]
    here = pl.ds(pl.multiple_of(links.c * STATE, STATE), STATE)
    half = pl.ds(pl.multiple_of(cols.bc.start + links.c * STATE, STATE), STATE)
    swaps = [
        Swap(links, r.w_zx.at[layer, 1], stagings[0], w, cols.x, inner),
        Swap(links, r.w_zx.at[layer, 0], stagings[1], w, cols.z, inner),
        Swap(links, r.w_bc.at[layer, :, here], stagings[2], w, half, STATE),
        Swap(links, r.packed_steps.at[layer], stagings[3], steps, slice(0, 128), 128),
    ]
    return swaps, Swap(links, r.w_out.at[layer], stagings[4], wo, slice(0, inner), inner)


def scatter_blocks(scatter, compute):
    before = None
    for k in (3, 1, 2, 0):
        compute(lax.bitwise_xor(scatter.links.p, jnp.int32(k)))
        scatter.to_sibling[k].start()
        if before is not None:
            scatter.pass_on(before)
        before = k


def forward_layer(links, r, normed, w, wo, wo_chain, scatter, meanwhile):
    carried = States(links, False, r.state_low, r.decay_row, r.states_in, r.decays_in)
    state_sum, decay_all = project_and_convolve(
        normed, w, r.rowp, r.bcp, r.headp, r.z, r.xin, r.bcin, r.x, r.bc, r.dtraw, r.dt, r.s, r.decay, r.ext, r.local,
        lambda q: pl.when(q == 2)(wo_chain.advance),
    )
    r.state_low[...] = state_sum.astype(BF16)
    r.decay_row[...] = jnp.broadcast_to(decay_all, r.decay_row.shape)
    carried.start()
    r.flush(r.z, r.xin, r.bcin, r.x, r.bc, r.dtraw, r.dt, r.s, r.decay)
    wo_chain.advance()
    mix_within_spans(r.x, r.bc, r.s, r.dt, r.y)
    meanwhile()
    wo_chain.complete()
    r.flush(r.wo)
    carried.arrive()
    chain_states(entering_state(links.z, links.groups, r.states_in, r.decays_in, False), r.local, r.decay, r.states)
    scatter_blocks(
        scatter, lambda q: mix_out(q, r.states, r.x, r.bc, r.z, r.s, wo, r.rowp, r.y, r.part, r.squares)
    )
    r.flush(r.y, r.states)
    return carried


def first_kernel(inner_all, r):
    links = Links(r.sends, r.recvs)
    c = links.c
    inner = r.wo.shape[1]
    shard = r.w_dt.shape[2]
    links.greet(plane=True, groups=True, edge=1)
    for layer in range(2):
        pack_steps(r.w_dt[layer], r.packed_steps.at[layer], r.wide_steps)
    swaps, swap_o = weight_swaps(links, r, 0, r.w, r.dt_rows, r.wo)
    next_swaps, next_o = weight_swaps(links, r, 1, r.next_w, r.next_dt_rows, r.next_wo)
    all_swaps = swaps + [swap_o] + next_swaps + [next_o]
    gather, other = Gather(links, r.normed, EDGE), Gather(links, r.dmix, 0)
    edge = EdgeForward(links, gather)
    chain, share = weight_chain(links, r.w, r.dt_rows, inner)
    chain_o = out_chain(links, r.wo)
    next_chain, next_share = weight_chain(links, r.next_w, r.next_dt_rows, inner)
    scatter = Scatter(links, r.part, 0, r.sib, r.total, r.peer, r.via)
    small = SmallSum(links, r.squares, r.slots)
    next_gather = Gather(links, r.next_normed, EDGE)
    next_edge = EdgeForward(links, next_gather)

    prepare(links, r, 0)
    for swap in all_swaps:
        swap.keep.start()
    for start, size in row_chunks():
        at = pl.ds(pl.multiple_of(c * HALF + start, EDGE), size)
        rows_in = r.resid[at, :].astype(F32)
        r.resid_out[start : start + size] = rows_in
        r.normed[gather.own(start, size), :] = (rows_in * rms_of(rows_in) * r.gains[0:1]).astype(BF16)
        rows_in = r.cot[at, :]
        r.cot_out[start : start + size] = rows_in.astype(F32)
        r.dmix[other.own(start, size), :] = rows_in
    links.meet()
    for swap in swaps:
        swap.start()
    for i, swap in enumerate(swaps):
        swap.settle()
        chain.begin(i)
    gather.start()
    edge.start()
    swap_o.start()
    chain.advance()
    gather.pass_on()
    for swap in next_swaps + [next_o]:
        swap.start()
    chain.advance()
    swap_o.settle()
    gather.finish()
    edge.finish()
    chain.complete()
    share.start()
    chain_o.begin()
    other.start()
    unpack_steps(r.dt_rows, r.w, shard, inner)
    r.flush(r.normed)
    share.wait()
    r.flush(r.w)

    def meanwhile():
        for swap in next_swaps + [next_o]:
            swap.settle()
        next_chain.begin()
        other.pass_on()

    carried = forward_layer(links, r, r.normed, r.w, r.wo, chain_o, scatter, meanwhile)
    small.start()
    scatter.pass_on(0)
    next_chain.advance()
    scatter.arrive()
    inv = lax.rsqrt(small.total() * (1.0 / inner_all) + EPS)
    r.inv_out[...] = inv
    column = inv.T[:, 0:1]
    for start, size in row_chunks():
        at = slice(start, start + size)
        mixed = scatter.own(start, size)
        r.mixed_out[at] = mixed
        fresh = r.resid_out[at] + column[at] * mixed
        r.fresh_out[at] = fresh
        r.next_normed[next_gather.own(start, size), :] = (fresh * rms_of(fresh) * r.gains[1:2]).astype(BF16)
    next_gather.start()
    next_edge.start()
    other.finish()
    r.flush(r.dmix)
    next_chain.advance()
    next_gather.pass_on()
    next_chain.complete()
    next_share.start()
    unpack_steps(r.next_dt_rows, r.next_w, shard, inner)
    scatter.finish()
    small.finish()
    next_gather.finish()
    next_edge.finish()
    carried.finish()
    for swap in all_swaps:
        swap.finish()
    for one in (chain, chain_o, next_chain):
        one.finish()
    next_share.wait()
    r.done()


def second_kernel(inner_all, r):
    links = Links(r.sends, r.recvs)
    r.fetch(r.normed, r.w)
    rows = r.wo_own.shape[0]
    keep = links.local(r.wo_own, r.wo.at[pl.ds(pl.multiple_of(links.z * rows, EDGE), rows), :])
    chain_o = out_chain(links, r.wo)
    scatter = Scatter(links, r.part, 0, r.sib, r.total, r.peer, r.via)
    small = SmallSum(links, r.squares, r.slots)
    spread = SmallGather(links, r.scalars_out)
    at = pl.ds(pl.multiple_of(links.c * HALF, HALF), HALF)
    share = links.copy(r.block_out.at[at, :], r.block_out.at[at, :], links.at(0, 1))
    keep.start()
    links.greet(plane=True, groups=True)
    prepare(links, r, 1)
    keep.wait()
    links.meet()
    chain_o.begin()
    r.need(r.normed, r.w)
    carried = forward_layer(links, r, r.normed, r.w, r.wo, chain_o, scatter, lambda: None)
    small.start()
    scatter.pass_on(0)
    scatter.arrive()
    inv = lax.rsqrt(small.total() * (1.0 / inner_all) + EPS)
    column = inv.T[:, 0:1]
    dots = []
    for start, size in row_chunks():
        at = slice(start, start + size)
        mixed = scatter.own(start, size)
        dots.append(jnp.sum(r.cot[at] * mixed, axis=-1, keepdims=True))
        r.block_out[pl.ds(pl.multiple_of(links.c * HALF + start, EDGE), size), :] = (
            r.resid[at] + column[at] * mixed
        ).astype(BF16)
    r.scalars_out[:, spread.lanes] = as_tile([column, jnp.concatenate(dots)])
    spread.start()
    share.start()
    scatter.finish()
    small.finish()
    carried.finish()
    chain_o.finish()
    spread.finish()
    share.wait()
    r.done()


def backward_layer(links, inner_all, r, z_collect, at_start, before_collect, at_middle):
    carried = States(links, True, r.state_low, r.decay_row, r.states_in, r.decays_in)
    collect = Halve(links, r.gwo, r.go_in, r.go_sum)
    grad_sum, decay_all = back_through_gate(
        inner_all, r.dmix, r.wo, r.y, r.z, r.x, r.bc, r.s, r.decay, r.scalars, r.rowp,
        r.cat, r.wide, r.dy, r.prior, r.normed_out,
    )
    r.state_low[...] = grad_sum.astype(BF16)
    r.decay_row[...] = jnp.broadcast_to(decay_all, r.decay_row.shape)
    links.meet()
    carried.start()
    at_start()
    out_gradient(r.dmix, r.normed_out, r.gwo)
    before_collect()
    collect.begin()
    r.need(r.normed)
    z_gradient(r.cat, r.normed, r.gz)
    z_collect.begin()
    r.need(r.dt)
    back_within_spans(r.dy, r.x, r.bc, r.s, r.dt, r.dpre, r.flow, r.sums)
    at_middle()
    carried.arrive()
    grad = entering_state(links.z, links.groups, r.states_in, r.decays_in, True)
    r.need(r.states, r.dtraw, r.xin, r.bcin)
    back_through_states(
        grad, r.prior, r.decay, r.states, r.dy, r.x, r.bc, r.s, r.dt, r.dtraw, r.xin, r.bcin, r.rowp, r.bcp, r.headp,
        r.flow, r.sums, r.cat, r.wide, r.bc_rows, r.dpre, r.prior,
    )
    collect.advance()
    return carried, collect


def put_vector(vec, row, values):
    for i in range(values.shape[0]):
        for j in range(values.shape[1] // 128):
            vec[row // 8, row % 8 : row % 8 + 1, :] = values[i : i + 1, j * 128 : j * 128 + 128]
            row += 1


def third_kernel(inner_all, r):
    links = Links(r.sends, r.recvs)
    r.fetch(r.dt, r.states, r.dtraw, r.xin, r.bcin, r.w, r.normed, r.grad, r.resid, r.mixed)
    scatter = Scatter(links, r.part, EDGE, r.sib, r.total, r.peer, r.via)
    edge = EdgeBackward(links, r.part, r.edge_slots)
    gather = Gather(links, r.dmix_out, 0)
    spread = SmallGather(links, r.scalars_out)
    collects = [Halve(links, r.gx, r.gx_in, r.gx_sum), Halve(links, r.gz, r.gz_in, r.gz_sum)]
    r.edge_slots[...] = jnp.zeros_like(r.edge_slots)
    links.greet(plane=True, groups=True, edge=-1)
    prepare(links, r, 1)
    carried, collect = backward_layer(links, inner_all, r, collects[1], lambda: None, lambda: None, lambda: None)
    r.need(r.w)
    x_gradient(r.cat, r.normed, r.gx)
    collects[0].begin()
    project_back_edge(r.cat, r.w, r.part)
    edge.start()
    scatter_blocks(scatter, lambda q: project_back(q, r.cat, r.w, r.part))
    scatter.pass_on(0)
    small_gradients(r.cat, r.normed, r.gbc, r.gdt)
    collect.complete()
    collects[1].advance()
    scatter.arrive()
    edge.receive()
    r.need(r.grad, r.resid, r.mixed)
    r.gain_row[...] = jnp.zeros_like(r.gain_row)
    dots = []
    for start, size in row_chunks():
        at = slice(start, start + size)
        fresh = grad_rows(links, scatter, r.edge_slots, r.grad, r.resid, r.gains[1:2], r.gain_row, start, size)
        r.grad_out[at] = fresh
        low = fresh.astype(BF16)
        r.dmix_out[gather.own(start, size), :] = low
        dots.append(jnp.sum(low.astype(F32) * r.mixed[at], axis=-1, keepdims=True))
    r.scalars_out[:, spread.lanes] = as_tile([r.inv[...].T[:, 0:1], jnp.concatenate(dots)])
    gather.start()
    spread.start()
    r.vec[...] = jnp.zeros_like(r.vec)
    model = r.gain_row.shape[1]
    put_vector(r.vec, model // 128, r.gain_row[0:1])
    put_vector(r.vec, 2 * (model // 128) + 2 * (CONV + 1), r.bc_rows[0 : CONV + 1])
    collects[0].advance()
    gather.pass_on()
    collects[1].complete()
    scatter.finish()
    edge.finish()
    gather.finish()
    spread.finish()
    carried.finish()
    collects[0].complete()
    for one in [collect] + collects:
        one.finish()


def fourth_kernel(inner_all, r):
    links = Links(r.sends, r.recvs)
    r.fetch(r.dt, r.states, r.dtraw, r.xin, r.bcin, r.above_bc, r.above_x, r.above_z, r.above_o, r.normed, r.w, r.grad, r.resid)
    scatter = Scatter(links, r.part, EDGE, r.sib, r.total, r.peer, r.via)
    edge = EdgeBackward(links, r.part, r.edge_slots)
    at = pl.ds(pl.multiple_of(links.c * HALF, HALF), HALF)
    share = links.copy(r.out.at[at, :], r.out.at[at, :], links.at(0, 1))
    collects = [Halve(links, r.gx, r.gx_in, r.gx_sum), Halve(links, r.gz, r.gz_in, r.gz_sum)]
    above = ((r.above_x, r.g_zx.at[1, 1]), (r.above_z, r.g_zx.at[1, 0]), (r.above_o, r.g_out.at[1]))
    own = ((r.go_sum, r.g_out.at[0]), (r.gx_sum, r.g_zx.at[0, 1]), (r.gz_sum, r.g_zx.at[0, 0]))
    delivers = [Deliver(links, parts, out) for parts, out in above]
    own_delivers = [Deliver(links, parts, out) for parts, out in own]
    bc_sums = [
        BcSum(links, bc, r.bc_out.at[i], r.bc_bufs[i])
        for i, bc in enumerate((r.gbc, r.above_bc))
    ]
    laid = LaidOut(links, r.steps_all, r.wide_all, r.dt_out, r.wide_out, r.dt_far, r.wide_far)
    vec_sum = VecSum(links, r.vec, r.vec_out, r.vec_near, r.vec_far)
    r.edge_slots[...] = jnp.zeros_like(r.edge_slots)
    links.greet(plane=True, groups=True, edge=-1)
    prepare(links, r, 0)

    def at_start():
        r.need(r.above_bc)
        bc_sums[1].cores()

    def at_middle():
        bc_sums[1].groups()
        r.need(r.above_x, r.above_z, r.above_o)
        for deliver in delivers:
            deliver.start()

    carried, collect = backward_layer(links, inner_all, r, collects[1], at_start, bc_sums[1].plane, at_middle)
    small_gradients(r.cat, r.normed, r.gbc, r.gdt)
    bc_sums[0].cores()
    r.steps_all[:, 0:EDGE, :] = r.gdt[...]
    r.steps_all[:, EDGE:, :] = r.above_dt[...]
    r.wide_all[0:16] = r.wide[...]
    r.wide_all[16:32] = r.above_wide[...]
    laid.groups()
    x_gradient(r.cat, r.normed, r.gx)
    collects[0].begin()
    bc_sums[0].plane()
    r.need(r.w)
    project_back_edge(r.cat, r.w, r.part)
    edge.start()
    scatter_blocks(scatter, lambda q: project_back(q, r.cat, r.w, r.part))
    scatter.pass_on(0)
    bc_sums[0].groups()
    collect.complete()
    own_delivers[0].start()
    collects[1].advance()
    scatter.arrive()
    edge.receive()
    r.need(r.grad, r.resid)
    r.gain_row[...] = jnp.zeros_like(r.gain_row)
    for start, size in row_chunks():
        fresh = grad_rows(links, scatter, r.edge_slots, r.grad, r.resid, r.gains[0:1], r.gain_row, start, size)
        r.out[pl.ds(pl.multiple_of(links.c * HALF + start, EDGE), size), :] = fresh.astype(BF16)
    share.start()
    r.vec[...] = r.above_vec[...]
    put_vector(r.vec, 0, r.gain_row[0:1])
    put_vector(r.vec, 2 * (r.gain_row.shape[1] // 128), r.bc_rows[0 : CONV + 1])
    vec_sum.plane()
    vec_sum.groups()
    collects[0].advance()
    bc_sums[1].share()
    laid.plane()
    collects[1].complete()
    own_delivers[2].start()
    laid.finish()
    lay_out_heads(links, r)
    bc_sums[0].share()
    vec_sum.back()
    collects[0].complete()
    own_delivers[1].start()
    for one in bc_sums + [scatter, edge, carried, collect] + collects:
        one.finish()
    vec_sum.finish()
    lay_out_vector(r)
    share.wait()
    for deliver in delivers + own_delivers:
        deliver.arrive()
        deliver.finish()


def lay_out_heads(links, r):
    inner = r.wide.shape[1]
    heads = inner // HEADDIM
    heads_core, shard = r.g_dt.shape[1:]
    spread = head_spread(inner).astype(F32)
    row, col = iota((128, 128), 0), iota((128, 128), 1)
    blank = jnp.zeros((128 - 2 * EDGE, r.dt_out.shape[2]), F32)
    steps = [jnp.zeros((shard, 128), F32) for _ in range(2)]
    tall = [jnp.zeros((8, 128), F32) for _ in range(2)]
    for q in range(GROUP):
        lanes = slice(q * inner, q * inner + inner)
        r.step_rows[...] = jnp.concatenate([r.dt_out[q].astype(F32), blank]).T
        mine = r.step_rows[pl.ds(pl.multiple_of(links.p * shard, 8), shard), :]
        gains, taps = [], []
        for layer in range(2):
            first, second = r.wide_out[q, 16 * layer : 16 * layer + 8], r.wide_out[q, 16 * layer + 8 : 16 * layer + 16]
            taps.append(first[0 : CONV + 1])
            gains.append(first[5:6])
            place = jnp.logical_and(row - EDGE * layer == col - q * heads, jnp.logical_and(row >= EDGE * layer, row < EDGE * layer + heads))
            steps[layer] = steps[layer] + dot_exact(mine, place.astype(F32))
            place = jnp.logical_and(row == col - q * heads, row < heads).astype(F32)
            skip = dot_exact(first, spread, NT)[6:7]
            rows = jnp.concatenate([first[7:8, 0:128], second[0:1, 0:128], skip, jnp.zeros((5, 128), F32)])
            tall[layer] = tall[layer] + dot_exact(rows, place)
        for j in range(CONV + 1):
            r.g_conv_x[j, :, lanes] = jnp.concatenate([tap[j : j + 1] for tap in taps]).astype(BF16)
        r.g_gain[:, lanes] = jnp.concatenate(gains).astype(BF16)
    for layer in range(2):
        r.g_dt[layer] = steps[layer].T[0:heads_core].astype(BF16)
    for i in range(3):
        r.g_head[i] = jnp.concatenate([one[i : i + 1, 0:heads_core] for one in tall]).astype(BF16)


def lay_out_vector(r):
    def row(i):
        return r.vec_out[i // 8, i % 8 : i % 8 + 1, :]

    count = r.g_norm.shape[1] // 128
    for i in range(count):
        r.g_norm[:, i * 128 : i * 128 + 128] = jnp.concatenate([row(i), row(count + i)]).astype(BF16)
    for half in range(2):
        for j in range(CONV + 1):
            firsts = [2 * count + layer * 2 * (CONV + 1) + 2 * j + half for layer in range(2)]
            rows = jnp.concatenate([row(first) for first in firsts])
            r.g_conv_bc[j, :, half * 128 : half * 128 + 128] = rows.astype(BF16)


def flat(value):
    return [a for member in value for a in flat(member)] if isinstance(value, list) else [value]


def shaped(value, leaves):
    return [shaped(member, leaves) for member in value] if isinstance(value, list) else leaves.pop(0)


def call(body, collective, copies, outs, hbm_outs, ins, hbm_ins, scratch):
    vmem, hbm = pl.BlockSpec(memory_space=pltpu.VMEM), pl.BlockSpec(memory_space=pl.ANY)
    twins = {**{name: (a.shape, a.dtype) for name, a in hbm_ins.items()}, **hbm_outs}
    sides = [list(ins.values()), list(hbm_ins.values()), list(outs.values()), list(hbm_outs.values())]
    counts = [len(flat(side)) for side in sides]
    buffers = flat([list(scratch.values()), list(twins.values())])

    def kernel(*refs):
        refs = list(refs)
        groups = [shaped(side, refs) for side in sides]
        inner = shaped([list(scratch.values()), list(twins.values())], refs)
        sends, recvs, sems = refs
        near = dict(zip(twins, inner[1]))
        named = {**dict(zip(ins, groups[0])), **dict(zip(outs, groups[2])), **dict(zip(scratch, inner[0])), **near}
        body(Refs(dict(named, sends=sends, recvs=recvs), list(zip(groups[1] + groups[3], inner[1])), sems))

    results = pl.pallas_call(
        kernel,
        out_shape=tuple(jax.ShapeDtypeStruct(*a) for a in flat(sides[2:])),
        in_specs=[vmem] * counts[0] + [hbm] * counts[1],
        out_specs=tuple([vmem] * counts[2] + [hbm] * counts[3]),
        scratch_shapes=[pltpu.VMEM(*a) for a in buffers]
        + [pltpu.SemaphoreType.DMA((n,)) for n in (copies, copies, max(1, len(twins)))],
        compiler_params=pltpu.CompilerParams(
            vmem_limit_bytes=VMEM_BYTES, collective_id=collective, has_side_effects=True
        ),
    )(*flat(sides[:2]))
    found = shaped(sides[2:], list(results))
    return types.SimpleNamespace(**dict(zip(outs, found[0])), **dict(zip(hbm_outs, found[1])))


def on_device(resid_in, cotangent, norm_gain, w_zx, w_dt, w_bc, conv_x, conv_bc, head_params, gated_gain, w_out):
    layers, model = norm_gain.shape
    groups = lax.axis_size("z")
    shard = w_dt.shape[1]
    inner_core = conv_x.shape[2]
    inner = inner_core // GROUP
    heads_core = head_params.shape[2]
    inner_all = inner_core * lax.axis_size("head")
    length = resid_in.shape[1]
    tokens = GROUP * length
    spans = tokens // SPAN
    rows = GROUP * shard

    own_rows = ((HALF, model), F32)
    all_rows, edged_rows = ((tokens, model), BF16), ((tokens + EDGE, model), BF16)
    columns = columns_of(inner).size
    w_shape, wo_shape = ((model, columns), BF16), ((model, inner), BF16)
    scalars = ((8, tokens), F32)
    state_shape = ((spans, STATE, inner), F32)
    low_rows, steps_shape = ((tokens, inner), BF16), ((tokens, 128), F32)
    scatter_scratch = dict(
        sib=((GROUP, HALF, model), BF16),
        total=((GROUP - 1, HALF, model), BF16),
        peer=((2, HALF, model), BF16),
        via=((2, HALF // 2, model), BF16),
    )
    state_scratch = dict(
        state_low=((STATE, inner), BF16),
        decay_row=((8, inner), F32),
        states_in=((groups, STATE, inner), BF16),
        decays_in=((groups, 8, inner), F32),
    )
    saved_shapes = dict(
        y=((tokens, inner), F32),
        z=low_rows,
        x=low_rows,
        bc=((tokens, 2 * STATE), BF16),
        s=steps_shape,
        dt=steps_shape,
        dtraw=((tokens, 128), BF16),
        xin=((tokens + EDGE, inner), BF16),
        bcin=((tokens + EDGE, 2 * STATE), BF16),
        states=state_shape,
        decay=((spans, 8, inner), F32),
    )
    forward_scratch = dict(
        ext=((tokens + EDGE, inner + 2 * STATE), F32),
        local=state_shape,
        part=all_rows,
        squares=scalars,
        slots=((2 * GROUP - 1, 8, HALF), F32),
        **state_scratch,
        **scatter_scratch,
    )

    conv_x, conv_bc, head_params = [jnp.swapaxes(a, 0, 1) for a in (conv_x, conv_bc, head_params)]
    w_dt, w_out = jnp.swapaxes(w_dt, 1, 2), jnp.swapaxes(w_out, 1, 2)
    params = dict(
        norm_gain=norm_gain, conv_x=conv_x, conv_bc=conv_bc, head_params=head_params, gated_gain=gated_gain
    )
    param_scratch = dict(
        rowp=((8, inner), F32), bcp=((8, 2 * STATE), F32), headp=((8, 128), F32), gains=((layers, model), F32)
    )
    stagings = [((GROUP, rows_in, width), BF16) for rows_in, width in (
        (shard, inner), (shard, inner), (shard, STATE), (EDGE, 128), (shard, inner)
    )]
    step_rows = ((groups * GROUP * EDGE, 128), BF16)
    first = call(
        functools.partial(first_kernel, inner_all),
        0,
        200 + 14 * (groups - 1) + 2 * groups,
        dict(
            next_w=w_shape,
            next_wo=((rows, inner), BF16),
            next_normed=edged_rows,
            resid_out=own_rows,
            cot_out=own_rows,
            mixed_out=own_rows,
            fresh_out=own_rows,
            inv_out=((8, HALF), F32),
        ),
        dict(normed=edged_rows, dmix=all_rows, w=w_shape, wo=wo_shape, **saved_shapes),
        dict(
            resid=resid_in[0],
            cot=cotangent[0],
            w_zx=w_zx,
            w_dt=w_dt,
            w_bc=w_bc,
            w_out=w_out,
            **params,
        ),
        dict(),
        dict(
            **forward_scratch,
            **param_scratch,
            stagings=[stagings, stagings],
            dt_rows=step_rows,
            next_dt_rows=step_rows,
            packed_steps=((layers, GROUP, EDGE, 128), BF16),
            wide_steps=((128, 128), BF16),
        ),
    )
    second = call(
        functools.partial(second_kernel, inner_all),
        1,
        60 + 4 * groups,
        dict(block_out=((length, model), BF16), scalars_out=scalars),
        dict(wo=wo_shape, **saved_shapes),
        dict(
            wo_own=first.next_wo,
            **params,
            resid=first.fresh_out,
            cot=first.cot_out,
        ),
        dict(normed=first.next_normed, w=first.next_w),
        dict(**forward_scratch, **param_scratch),
    )
    grad_in = ((groups - 1, rows, inner), BF16)
    grad_sum = ((GROUP, shard, inner), BF16)
    bc_grad = ((groups, GROUP, shard, 2 * STATE), BF16)
    dt_grad = ((groups, EDGE, rows), BF16)
    wide_grad = ((16, inner), F32)
    vec_shape = ((2 * GROUP, 8, 128), F32)
    back_scratch = dict(
        dy=low_rows,
        gwo=wo_shape,
        normed_out=low_rows,
        prior=state_shape,
        dpre=((tokens + 2 * EDGE, inner + 2 * STATE), F32),
        flow=steps_shape,
        sums=steps_shape,
        cat=((tokens + EDGE, columns), BF16),
        bc_rows=((8, 2 * STATE), F32),
        part=edged_rows,
        gx=wo_shape,
        gz=wo_shape,
        go_in=grad_in,
        gx_in=grad_in,
        gz_in=grad_in,
        gain_row=((8, model), F32),
        edge_slots=((2 * GROUP, EDGE, model), BF16),
        **state_scratch,
        **param_scratch,
        **scatter_scratch,
    )

    def at_once(run):
        return dict(y=run.y, z=run.z, x=run.x, bc=run.bc, s=run.s, decay=run.decay)

    def later(run):
        return dict(dt=run.dt, states=run.states, dtraw=run.dtraw, xin=run.xin, bcin=run.bcin)

    third = call(
        functools.partial(third_kernel, inner_all),
        2,
        60 + 6 * groups,
        dict(
            dmix_out=all_rows,
            scalars_out=scalars,
            grad_out=own_rows,
            go_sum=grad_sum,
            gx_sum=grad_sum,
            gz_sum=grad_sum,
            gbc=bc_grad,
            gdt=dt_grad,
            wide=wide_grad,
            vec=vec_shape,
        ),
        dict(),
        dict(
            dmix=first.dmix,
            scalars=second.scalars_out,
            wo=second.wo,
            **params,
            inv=first.inv_out,
            **at_once(second),
        ),
        dict(
            w=first.next_w,
            normed=first.next_normed,
            grad=first.cot_out,
            resid=first.fresh_out,
            mixed=first.mixed_out,
            **later(second),
        ),
        back_scratch,
    )
    far = groups - 1
    dt_shape, wide_shape = (layers * EDGE, rows), (layers * 16, inner)
    half_bc = (groups, GROUP, shard, STATE)
    bc_bufs = [
        (half_bc, BF16),
        (half_bc, BF16),
        ((GROUP - 1, groups, shard, STATE), BF16),
        ((groups, shard, STATE), BF16),
        ((far, shard, STATE), BF16),
    ]
    fourth = call(
        functools.partial(fourth_kernel, inner_all),
        3,
        130 + 14 * groups,
        dict(
            out=((length, model), BF16),
            bc_out=((layers, shard, 2 * STATE), BF16),
            g_norm=(norm_gain.shape, BF16),
            g_zx=(w_zx.shape, BF16),
            g_dt=(w_dt.shape, BF16),
            g_conv_x=(conv_x.shape, BF16),
            g_conv_bc=(conv_bc.shape, BF16),
            g_head=(head_params.shape, BF16),
            g_gain=(gated_gain.shape, BF16),
            g_out=(w_out.shape, BF16),
        ),
        dict(),
        dict(
            dmix=third.dmix_out,
            scalars=third.scalars_out,
            wo=first.wo,
            **params,
            above_dt=third.gdt,
            above_wide=third.wide,
            above_vec=third.vec,
            **at_once(first),
        ),
        dict(
            w=first.w,
            normed=first.normed,
            grad=third.grad_out,
            resid=first.resid_out,
            above_x=third.gx_sum,
            above_z=third.gz_sum,
            above_o=third.go_sum,
            above_bc=third.gbc,
            **later(first),
        ),
        dict(
            **back_scratch,
            vec_out=vec_shape,
            dt_out=((GROUP, *dt_shape), BF16),
            wide_out=((GROUP, *wide_shape), F32),
            step_rows=((rows, 128), F32),
            go_sum=grad_sum,
            gx_sum=grad_sum,
            gz_sum=grad_sum,
            gbc=bc_grad,
            gdt=dt_grad,
            wide=wide_grad,
            vec=vec_shape,
            steps_all=((groups, *dt_shape), BF16),
            wide_all=(wide_shape, F32),
            bc_bufs=[bc_bufs, bc_bufs],
            vec_near=vec_shape,
            vec_far=((far, 8, 128), F32),
            dt_far=((far, *dt_shape), BF16),
            wide_far=((far, *wide_shape), F32),
        ),
    )
    return (
        second.block_out[None],
        fourth.out[None],
        fourth.g_norm,
        fourth.g_zx,
        jnp.swapaxes(fourth.g_dt, 1, 2),
        fourth.bc_out,
        *[jnp.swapaxes(a, 0, 1) for a in (fourth.g_conv_x, fourth.g_conv_bc, fourth.g_head)],
        fourth.g_gain,
        jnp.swapaxes(fourth.g_out, 1, 2),
    )


def solution(mesh):
    seq, head = mesh.shape["seq"], mesh.shape["head"]
    split = Mesh(mesh.devices.reshape(seq // GROUP, GROUP, head), ("z", "p", "head"))
    seq_axes = ("z", "p")
    specs = (
        P(None, seq_axes, None),
        P(None, seq_axes, None),
        P(),
        P(None, None, seq_axes, "head"),
        P(None, seq_axes, "head"),
        P(None, seq_axes, None),
        P(None, None, "head"),
        P(),
        P(None, None, "head"),
        P(None, "head"),
        P(None, "head", seq_axes),
    )
    return jax.shard_map(on_device, mesh=split, in_specs=specs, out_specs=specs, check_vma=False)
```
